32 devices in a mesh: dp: 8 (over z, x), group: 4 (over y, core).
Axes of the slice: x: 2, y: 2, z: 4, core: 2. Of those that a mesh axis runs over, the one named last changes fastest.
Arguments:
- fine_features: bfloat16 [65536, 128], P(('dp', 'group')), may hold values from -6 to 6
- down_map: int32 [16384, 8], P(('dp', 'group')), may hold values from 0 to 2048, as said below
- neighbours: int32 [16384, 27], P(('dp', 'group')), may hold values from 0 to 512, as said below
- voxel_counts: int32 [32], P(('dp', 'group')), may hold values from 1 to 512, as said below
- down_weight: bfloat16 [8, 128, 256], replicated, may hold values from -0.1875 to 0.1875
- mid_weight: bfloat16 [27, 256, 256], replicated, may hold values from -0.078125 to 0.078125
- out_weight: bfloat16 [27, 256, 256], replicated, may hold values from -0.078125 to 0.078125
- norm_gain: float32 [3, 256], replicated, may hold values from 0.5 to 1.5
- norm_bias: float32 [3, 256], replicated, may hold values from -2 to 2
- cotangent: bfloat16 [16384, 256], P(('dp', 'group')), may hold values from -6 to 6
Outputs:
- features: bfloat16 [16384, 256], P(('dp', 'group'))
- fine_grad: bfloat16 [65536, 128], P(('dp', 'group'))
- down_weight_grad: float32 [8, 128, 256], replicated
- mid_weight_grad: float32 [27, 256, 256], replicated
- out_weight_grad: float32 [27, 256, 256], replicated
- gain_grad: float32 [3, 256], replicated
- bias_grad: float32 [3, 256], replicated
The draws below stay inside these ranges and needn't reach their ends.
Inputs may be any that keep to these rules, and one draw needn't show every extreme that they name: The live coarse rows of a device are its first voxel_counts rows; one device in every draw has all 512 rows live. `down_map`: entry k of coarse row r of a device is 4 * r + (k mod 4) of that device's fine block or the empty mark 2048; of entries k and k + 4 at most one is not empty; rows that are not live hold only the empty mark. `neighbours`: entries are live rows of the same device's block or the empty mark 512; entry 13 of a live row is the row itself; rows that are not live hold only the empty mark.
All inputs are finite; a program needn't handle non-finite values.
Results may differ from the reference program's by a relative error of at most 0.013.
Values sent between devices are 32-bit elements; how exact they have to be, the bound alone decides.
A program may use at most 128 MiB of HBM per device.

```python
import jax
import jax.numpy as jnp
from jax import lax

CIN = 128
COUT = 256
KDOWN = 8
KERNEL = 27
VOX_DEV = 512
VIN_DEV = 2048
DEVICE_TOTAL = 32
VOXELS = 16384
FINE = 65536


def live_numbers(key):
    count_key = jax.random.fold_in(key, 101)
    order_key = jax.random.fold_in(key, 202)
    places = jnp.arange(DEVICE_TOTAL, dtype=jnp.int32)
    floor_part = VOX_DEV // 3
    rising = floor_part + (VOX_DEV - floor_part) * places // max(DEVICE_TOTAL - 1, 1)
    cuts = jax.random.randint(count_key, (DEVICE_TOTAL,), 0, VOX_DEV // 8 + 1)
    numbers = jnp.where(places == DEVICE_TOTAL - 1, VOX_DEV, rising - cuts)
    order = jax.random.permutation(order_key, DEVICE_TOTAL)
    return numbers[order].astype(jnp.int32)


def draw_voxel_counts(key, part):
    return live_numbers(key)


def draw_neighbours(key, part):
    numbers = live_numbers(key)
    key = jax.random.fold_in(key, 7)
    pick_key, keep_key = jax.random.split(key)
    shape = (DEVICE_TOTAL, VOX_DEV, KERNEL)
    slots = jnp.arange(VOX_DEV, dtype=jnp.int32)[None, :, None]
    alive = slots < numbers[:, None, None]
    target = jax.random.randint(pick_key, shape, 0, VOX_DEV) % numbers[:, None, None]
    present = jax.random.randint(keep_key, shape, 0, 2) == 1
    offsets = jnp.arange(KERNEL, dtype=jnp.int32)[None, None, :]
    chosen = jnp.where(offsets == KERNEL // 2, slots, jnp.where(present, target, VOX_DEV))
    chosen = jnp.where(alive, chosen, VOX_DEV)
    return chosen.reshape(VOXELS, KERNEL).astype(jnp.int32)


def draw_down_map(key, part):
    numbers = live_numbers(key)
    key = jax.random.fold_in(key, 11)
    side_key, keep_key = jax.random.split(key)
    half = KDOWN // 2
    shape = (DEVICE_TOTAL, VOX_DEV, half)
    slots = jnp.arange(VOX_DEV, dtype=jnp.int32)[None, :, None]
    alive = slots < numbers[:, None, None]
    sides = jax.random.randint(side_key, shape, 0, 2)
    present = jax.random.randint(keep_key, shape, 0, 4) > 0
    sides_full = jnp.concatenate([sides, sides], axis=2)
    present_full = jnp.concatenate([present, present], axis=2)
    offsets = jnp.arange(KDOWN, dtype=jnp.int32)[None, None, :]
    taken = present_full & (sides_full == offsets // half) & alive
    chosen = jnp.where(taken, slots * half + offsets % half, VIN_DEV)
    return chosen.reshape(VOXELS, KDOWN).astype(jnp.int32)


def shard_levels(own_key, dims, shards, least, top_value):
    level = 1.0
    for axis_at, shards_of in shards:
        heights = jax.random.uniform(jax.random.fold_in(jax.random.fold_in(own_key, 6), axis_at), (shards_of,), jnp.float32, least / len(shards), top_value / len(shards))
        level = level * jnp.repeat(jnp.exp(heights), dims[axis_at] // shards_of).reshape((-1,) + (1,) * (len(dims) - 1 - axis_at))
    return level


def scatter_about(rng, shape, deviation, reach, pieces=(), held_as=jnp.bfloat16):
    level = shard_levels(rng, shape, pieces, -0.22, 0.18) if pieces else 1.0
    values = jax.random.normal(rng, shape, jnp.float32) * deviation * level
    return jnp.minimum(jnp.maximum(values, -reach), reach).astype(held_as)


def setup_inputs(seed: int = 0) -> dict:
    seeds = jax.random.split(jax.random.key(seed), 11)
    fine_features = scatter_about(seeds[0], (FINE, CIN), 1.0, 6.0, ((0, 32),))
    down_map = draw_down_map(jax.random.fold_in(seeds[10], 71), 0)
    neighbours = draw_neighbours(jax.random.fold_in(seeds[10], 71), 0)
    voxel_counts = draw_voxel_counts(jax.random.fold_in(seeds[10], 71), 0)
    down_weight = scatter_about(seeds[4], (KDOWN, CIN, COUT), (KDOWN * CIN) ** -0.5, 0.1875)
    mid_weight = scatter_about(seeds[5], (KERNEL, COUT, COUT), (KERNEL * COUT) ** -0.5, 0.078125)
    out_weight = scatter_about(seeds[6], (KERNEL, COUT, COUT), (KERNEL * COUT) ** -0.5, 0.078125)
    norm_gain = jnp.clip(1.0 + 0.1 * jax.random.normal(seeds[7], (3, COUT), jnp.float32), 0.5, 1.5)
    norm_bias = scatter_about(seeds[8], (3, COUT), 0.5, 2.0, (), jnp.float32)
    cotangent = scatter_about(seeds[9], (VOXELS, COUT), 1.0, 6.0, ((0, 32),))
    return {"fine_features": fine_features, "down_map": down_map, "neighbours": neighbours, "voxel_counts": voxel_counts, "down_weight": down_weight, "mid_weight": mid_weight, "out_weight": out_weight, "norm_gain": norm_gain, "norm_bias": norm_bias, "cotangent": cotangent}


eps_norm = 1e-05

@jax.custom_vjp
def low(v):
    return lax.optimization_barrier(v.astype(jnp.bfloat16)).astype(jnp.float32)

@jax.custom_vjp
def low_back(v):
    return v

def low_keep(v):
    return (low(v), None)

def low_pass(kept, grad):
    return (grad,)

def back_keep(v):
    return (v, None)

def back_low(kept, grad):
    return (low(grad),)
low.defvjp(low_keep, low_pass)
low_back.defvjp(back_keep, back_low)

def convolve(source, index_map, weight, block):
    blocks = source.reshape(DEVICE_TOTAL, block, source.shape[1])
    tables = index_map.reshape(DEVICE_TOTAL, VOX_DEV, index_map.shape[1])

    def local(pair):
        piece, table = pair
        padded = jnp.concatenate([piece, jnp.zeros((1, piece.shape[1]), piece.dtype)], axis=0)
        return jnp.einsum('vkc,kcd->vd', padded[table], weight, precision=lax.Precision.HIGHEST)
    return lax.map(jax.checkpoint(local), (blocks, tables)).reshape(VOXELS, weight.shape[2])

def normalize(hidden, gain, shift, live_mask, live_total):
    center = lax.optimization_barrier(jnp.sum(hidden * live_mask, axis=0)) / live_total
    centered = (hidden - center) * live_mask
    spread = lax.optimization_barrier(jnp.sum(centered * centered, axis=0)) / live_total
    return (hidden - center) * lax.rsqrt(spread + eps_norm) * gain + shift

def reference(fine_features, down_map, neighbours, voxel_counts, down_weight, mid_weight, out_weight, norm_gain, norm_bias, cotangent):
    slots = jnp.arange(VOX_DEV, dtype=jnp.int32)
    live_mask = (slots[None, :] < voxel_counts[:, None]).astype(jnp.float32).reshape(VOXELS, 1)
    live_total = jnp.sum(live_mask)

    def forward(feats, w_down, w_mid, w_out, gains, shifts):
        first = low_back(convolve(feats, down_map, w_down, VIN_DEV))
        act_one = jax.nn.silu(normalize(first, gains[0], shifts[0], live_mask, live_total)) * live_mask
        second = low_back(convolve(low(act_one), neighbours, w_mid, VOX_DEV))
        act_two = jax.nn.silu(normalize(second, gains[1], shifts[1], live_mask, live_total)) * live_mask
        third = low_back(convolve(low(act_two), neighbours, w_out, VOX_DEV))
        summed = normalize(third, gains[2], shifts[2], live_mask, live_total) * live_mask + act_one
        return jax.nn.silu(summed) * live_mask
    primals = (fine_features.astype(jnp.float32), down_weight.astype(jnp.float32), mid_weight.astype(jnp.float32), out_weight.astype(jnp.float32), norm_gain.astype(jnp.float32), norm_bias.astype(jnp.float32))
    result, pullback = jax.vjp(forward, *primals)
    grads = pullback(cotangent.astype(jnp.float32))
    return (result.astype(jnp.bfloat16), grads[0].astype(jnp.bfloat16), grads[1], grads[2], grads[3], grads[4], grads[5])
```

```python
import functools

import jax
import jax.numpy as jnp
from jax import lax
from jax.experimental import pallas as pl
from jax.experimental.pallas import tpu as pltpu
from jax.sharding import PartitionSpec as P

eps_norm = 1e-05
MESH = pl.DeviceIdType.MESH
GROUP = 3


def sigmoid(value):
    return 1.0 / (1.0 + jnp.exp(-value))


def silu_slope(value):
    sigma = sigmoid(value)
    return sigma * (1.0 + value * (1.0 - sigma))


def dot(left, right):
    return jnp.dot(left, right, preferred_element_type=jnp.float32)


def dot_last(left, right):
    return lax.dot_general(
        left, right, (((1,), (1,)), ((), ())), preferred_element_type=jnp.float32
    )


def kernel(
    dp_size,
    group_size,
    fine_ref,
    down_map_ref,
    neighbours_ref,
    count_ref,
    down_hbm,
    mid_hbm,
    out_hbm,
    gain_ref,
    bias_ref,
    cotangent_ref,
    features_ref,
    fine_grad_ref,
    grad_down_hbm,
    grad_mid_hbm,
    grad_out_hbm,
    gain_grad_ref,
    bias_grad_ref,
    w_down,
    w_mid,
    w_out,
    spread_fine,
    cols_down,
    nb_cols,
    nb_rows,
    act_one,
    act_one_b,
    act_two_b,
    hid_one,
    hid_two,
    hid_three,
    grad_hidden,
    grad_act,
    side,
    grad_down,
    grad_mid,
    grad_out,
    near,
    far,
    load_sem,
    store_sem,
    near_send,
    near_recv,
    far_send,
    far_recv,
):
    rows, width = cotangent_ref.shape
    offsets = neighbours_ref.shape[1]
    fine_rows, in_width = fine_ref.shape
    children = fine_rows // rows
    down_offsets = down_map_ref.shape[1]
    dp_me = lax.axis_index("dp")
    group_me = lax.axis_index("group")

    loads = [
        pltpu.make_async_copy(source, target, load_sem.at[at])
        for at, (source, target) in enumerate(
            ((down_hbm, w_down), (mid_hbm, w_mid), (out_hbm, w_out))
        )
    ]
    for load in loads:
        load.start()

    barrier = pltpu.get_barrier_semaphore()
    for step in range(1, group_size):
        pl.semaphore_signal(
            barrier,
            inc=1,
            device_id={"group": lax.rem(group_me + step, group_size)},
            device_id_type=MESH,
        )
    for step in range(1, dp_size):
        pl.semaphore_signal(
            barrier,
            inc=1,
            device_id={"dp": lax.rem(dp_me + step, dp_size)},
            device_id_type=MESH,
        )
    pl.semaphore_wait(barrier, group_size + dp_size - 2)

    def share(at, axis, me, size, slots, send, recv):
        copies = []
        for step in range(1, size):
            copies.append(
                pltpu.make_async_remote_copy(
                    src_ref=slots.at[at, me],
                    dst_ref=slots.at[at, me],
                    send_sem=send.at[at, step - 1],
                    recv_sem=recv.at[at, step - 1],
                    device_id={axis: lax.rem(me + step, size)},
                    device_id_type=MESH,
                )
            )
        for copy in copies:
            copy.start()
        return copies

    def exchange(at, block, combine, meanwhile=None):
        near[at, group_me] = block
        copies = share(at, "group", group_me, group_size, near, near_send, near_recv)
        if meanwhile is not None:
            meanwhile()
        for copy in copies:
            copy.wait()
        far[at, dp_me] = combine([near[at, slot] for slot in range(group_size)])
        copies = share(at, "dp", dp_me, dp_size, far, far_send, far_recv)
        for copy in copies:
            copy.wait()
        return combine([far[at, slot] for slot in range(dp_size)])

    place = lax.broadcasted_iota(jnp.int32, (8, width), 0)

    def stack(first, second, third):
        return jnp.where(
            place == 0, first, jnp.where(place == 1, second, jnp.where(place == 2, third, 0.0))
        )

    def add_all(blocks):
        total = blocks[0]
        for block in blocks[1:]:
            total = total + block
        return total

    def merge_all(blocks):
        count = add_all([block[2:3] for block in blocks])
        center = add_all([block[2:3] * block[0:1] for block in blocks]) / count
        squares = add_all(
            [
                block[1:2] + block[2:3] * (block[0:1] - center) * (block[0:1] - center)
                for block in blocks
            ]
        )
        return stack(center, squares, count)

    count = count_ref[0]
    own_count = jnp.full((1, width), count.astype(jnp.float32))
    live = lax.broadcasted_iota(jnp.int32, (rows, width), 0) < count

    def norm_stats(at, hidden, meanwhile=None):
        center = jnp.sum(hidden, axis=0, keepdims=True) / own_count
        centered = jnp.where(live, hidden - center, 0.0)
        squares = jnp.sum(centered * centered, axis=0, keepdims=True)
        merged = exchange(at, stack(center, squares, own_count), merge_all, meanwhile)
        total = merged[2:3]
        scale = lax.rsqrt(merged[1:2] / total + eps_norm)
        return merged[0:1], scale, total

    def norm_grad(at, norm, incoming, normed, scale, total, meanwhile=None):
        shift_sum = jnp.sum(incoming, axis=0, keepdims=True)
        scale_sum = jnp.sum(incoming * normed, axis=0, keepdims=True)
        summed = exchange(
            at, stack(shift_sum, scale_sum, jnp.zeros_like(shift_sum)), add_all, meanwhile
        )
        bias_grad_ref[norm : norm + 1, :] = summed[0:1]
        gain_grad_ref[norm : norm + 1, :] = summed[1:2]
        hidden_grad = (
            scale
            * gain_ref[norm : norm + 1, :]
            * (incoming - summed[0:1] / total - normed * (summed[1:2] / total))
        )
        return jnp.where(live, hidden_grad, 0.0).astype(jnp.bfloat16)

    def convolve(source, weight, hidden):
        lanes = lax.broadcasted_iota(jnp.int32, (rows, rows), 1)
        hidden[...] = jnp.zeros_like(hidden)

        def step(at, carry):
            total = None
            for part in range(GROUP):
                k = at * GROUP + part
                wanted = jnp.concatenate([nb_cols[k]] * (rows // 128), axis=1)
                picker = jnp.where(wanted == lanes, 1.0, 0.0).astype(jnp.bfloat16)
                columns = dot(picker, source[...]).astype(jnp.bfloat16)
                term = dot(columns, weight[k])
                total = term if total is None else total + term
            hidden[...] += total
            return carry

        lax.fori_loop(0, offsets // GROUP, step, 0)

    def convolve_back(source_t, weight, hidden_grad, act_grad, weight_grad, weight_grad_hbm, sems):
        places = lax.broadcasted_iota(jnp.int32, (rows, rows), 0)

        def step(at, carry):
            total = None
            for part in range(GROUP):
                k = at * GROUP + part
                picker = jnp.where(nb_rows[pl.ds(k, 1), :] == places, 1.0, 0.0).astype(
                    jnp.bfloat16
                )
                spread = dot(picker, hidden_grad[...]).astype(jnp.bfloat16)
                term = dot_last(spread, weight[k])
                total = term if total is None else total + term
                weight_grad[k] = dot(source_t[...], spread)
                pltpu.make_async_copy(
                    weight_grad.at[k], weight_grad_hbm.at[k], sems.at[k]
                ).start()
            act_grad[...] += total
            return carry

        lax.fori_loop(0, offsets // GROUP, step, 0)

    spread_fine[...] = fine_ref[...].astype(jnp.float32)
    for k in range(down_offsets):
        child = spread_fine[pl.ds(k % children, rows, stride=children), :]
        there = down_map_ref[:, k : k + 1] < fine_rows
        cols_down[:, k * in_width : (k + 1) * in_width] = jnp.where(there, child, 0.0).astype(
            jnp.bfloat16
        )
    loads[0].wait()
    hid_one[...] = dot(cols_down[...], w_down[...].reshape(down_offsets * in_width, width))

    def spread_neighbours():
        for k in range(offsets):
            nb_cols[k] = jnp.broadcast_to(neighbours_ref[:, k : k + 1], (rows, 128))
        side[...] = jnp.zeros_like(side)
        side[:, :offsets] = neighbours_ref[...]
        nb_rows[...] = side[...].T

    center_one, scale_one, total = norm_stats(0, hid_one[...], spread_neighbours)

    def pre_one():
        normed = (hid_one[...] - center_one) * scale_one
        return normed, normed * gain_ref[0:1, :] + bias_ref[0:1, :]

    _, pre = pre_one()
    act_one[...] = jnp.where(live, pre * sigmoid(pre), 0.0)
    act_one_b[...] = act_one[...].astype(jnp.bfloat16)
    loads[1].wait()
    convolve(act_one_b, w_mid, hid_two)
    center_two, scale_two, _ = norm_stats(1, hid_two[...])

    def pre_two():
        normed = (hid_two[...] - center_two) * scale_two
        return normed, normed * gain_ref[1:2, :] + bias_ref[1:2, :]

    _, pre = pre_two()
    act_two_b[...] = jnp.where(live, pre * sigmoid(pre), 0.0).astype(jnp.bfloat16)
    loads[2].wait()
    convolve(act_two_b, w_out, hid_three)
    center_three, scale_three, _ = norm_stats(2, hid_three[...])
    normed_three = (hid_three[...] - center_three) * scale_three
    summed = (
        jnp.where(live, normed_three * gain_ref[2:3, :] + bias_ref[2:3, :], 0.0) + act_one[...]
    )
    sigma = sigmoid(summed)
    features_ref[...] = jnp.where(live, summed * sigma, 0.0).astype(jnp.bfloat16)

    slope = sigma * (1.0 + summed * (1.0 - sigma))
    act_one[...] = jnp.where(live, cotangent_ref[...].astype(jnp.float32) * slope, 0.0)
    grad_hidden[...] = norm_grad(3, 2, act_one[...], normed_three, scale_three, total)
    grad_act[...] = jnp.zeros_like(grad_act)
    convolve_back(
        act_two_b[...].T, w_out, grad_hidden, grad_act, grad_out, grad_out_hbm, store_sem.at[0]
    )
    normed, pre = pre_two()
    incoming = jnp.where(live, grad_act[...] * silu_slope(pre), 0.0)
    grad_hidden[...] = norm_grad(4, 1, incoming, normed, scale_two, total)
    grad_act[...] = act_one[...]
    convolve_back(
        act_one_b[...].T, w_mid, grad_hidden, grad_act, grad_mid, grad_mid_hbm, store_sem.at[1]
    )
    normed, pre = pre_one()
    incoming = jnp.where(live, grad_act[...] * silu_slope(pre), 0.0)
    grad_hidden[...] = norm_grad(5, 0, incoming, normed, scale_one, total)
    grad_down[...] = dot(cols_down[...].T, grad_hidden[...]).reshape(grad_down.shape)
    down_store = pltpu.make_async_copy(grad_down, grad_down_hbm, store_sem.at[2, 0])
    down_store.start()
    for child in range(children):
        total_child = jnp.zeros((rows, in_width), jnp.float32)
        for k in range(child, down_offsets, children):
            there = down_map_ref[:, k : k + 1] < fine_rows
            total_child += jnp.where(there, dot_last(grad_hidden[...], w_down[k]), 0.0)
        spread_fine[pl.ds(child, rows, stride=children), :] = total_child
    fine_grad_ref[...] = spread_fine[...].astype(jnp.bfloat16)

    def finish(k, carry):
        pltpu.make_async_copy(grad_out.at[k], grad_out_hbm.at[k], store_sem.at[0, k]).wait()
        pltpu.make_async_copy(grad_mid.at[k], grad_mid_hbm.at[k], store_sem.at[1, k]).wait()
        return carry

    lax.fori_loop(0, offsets, finish, 0)
    down_store.wait()


def per_device(
    dp_size,
    group_size,
    fine_features,
    down_map,
    neighbours,
    voxel_counts,
    down_weight,
    mid_weight,
    out_weight,
    norm_gain,
    norm_bias,
    cotangent,
):
    rows, width = cotangent.shape
    fine_rows, in_width = fine_features.shape
    offsets = neighbours.shape[1]
    down_offsets = down_map.shape[1]
    f32, bf16, i32 = jnp.float32, jnp.bfloat16, jnp.int32
    vmem = pl.BlockSpec(memory_space=pltpu.VMEM)
    smem = pl.BlockSpec(memory_space=pltpu.SMEM)
    hbm = pl.BlockSpec(memory_space=pl.ANY)
    shape = jax.ShapeDtypeStruct
    features, fine_grad, grad_down, grad_mid, grad_out, gain_grad, bias_grad = pl.pallas_call(
        functools.partial(kernel, dp_size, group_size),
        out_shape=(
            shape((rows, width), bf16),
            shape((fine_rows, in_width), bf16),
            shape(down_weight.shape, f32),
            shape(mid_weight.shape, f32),
            shape(out_weight.shape, f32),
            shape(norm_gain.shape, f32),
            shape(norm_bias.shape, f32),
        ),
        in_specs=[vmem, vmem, vmem, smem, hbm, hbm, hbm, vmem, vmem, vmem],
        out_specs=(vmem, vmem, hbm, hbm, hbm, vmem, vmem),
        scratch_shapes=[
            pltpu.VMEM(down_weight.shape, bf16),
            pltpu.VMEM(mid_weight.shape, bf16),
            pltpu.VMEM(out_weight.shape, bf16),
            pltpu.VMEM((fine_rows, in_width), f32),
            pltpu.VMEM((rows, down_offsets * in_width), bf16),
            pltpu.VMEM((offsets, rows, 128), i32),
            pltpu.VMEM((128, rows), i32),
            pltpu.VMEM((rows, width), f32),
            pltpu.VMEM((rows, width), bf16),
            pltpu.VMEM((rows, width), bf16),
            pltpu.VMEM((rows, width), f32),
            pltpu.VMEM((rows, width), f32),
            pltpu.VMEM((rows, width), f32),
            pltpu.VMEM((rows, width), bf16),
            pltpu.VMEM((rows, width), f32),
            pltpu.VMEM((rows, 128), i32),
            pltpu.VMEM(down_weight.shape, f32),
            pltpu.VMEM(mid_weight.shape, f32),
            pltpu.VMEM(out_weight.shape, f32),
            pltpu.VMEM((6, group_size, 8, width), f32),
            pltpu.VMEM((6, dp_size, 8, width), f32),
            pltpu.SemaphoreType.DMA((3,)),
            pltpu.SemaphoreType.DMA((3, offsets)),
            pltpu.SemaphoreType.DMA((6, group_size - 1)),
            pltpu.SemaphoreType.DMA((6, group_size - 1)),
            pltpu.SemaphoreType.DMA((6, dp_size - 1)),
            pltpu.SemaphoreType.DMA((6, dp_size - 1)),
        ],
        compiler_params=pltpu.CompilerParams(
            collective_id=0, has_side_effects=True, vmem_limit_bytes=56 * 1024 * 1024
        ),
    )(
        fine_features,
        down_map,
        neighbours,
        voxel_counts,
        down_weight,
        mid_weight,
        out_weight,
        norm_gain,
        norm_bias,
        cotangent,
    )
    axes = ("dp", "group")
    grad_out = lax.psum(grad_out, axes)
    grad_mid = lax.psum(grad_mid, axes)
    grad_down = lax.psum(grad_down, axes)
    return (features, fine_grad, grad_down, grad_mid, grad_out, gain_grad, bias_grad)


def solution(mesh):
    in_specs = (
        P(("dp", "group"), None),
        P(("dp", "group"), None),
        P(("dp", "group"), None),
        P(("dp", "group")),
        P(),
        P(),
        P(),
        P(),
        P(),
        P(("dp", "group"), None),
    )
    out_specs = (P(("dp", "group"), None), P(("dp", "group"), None), P(), P(), P(), P(), P())
    return jax.shard_map(
        functools.partial(per_device, mesh.shape["dp"], mesh.shape["group"]),
        mesh=mesh,
        in_specs=in_specs,
        out_specs=out_specs,
        check_vma=False,
    )
```

```python
import functools

import jax
import jax.numpy as jnp
from jax import lax
from jax.experimental import pallas as pl
from jax.experimental.pallas import tpu as pltpu
from jax.sharding import PartitionSpec as P

eps_norm = 1e-05
MESH = pl.DeviceIdType.MESH
GROUP = 3
CHUNK = 512
STAGES = 8
RING = 8


def sigmoid(value):
    return 1.0 / (1.0 + jnp.exp(-value))


def silu_slope(value):
    sigma = sigmoid(value)
    return sigma * (1.0 + value * (1.0 - sigma))


def dot(left, right):
    return jnp.dot(left, right, preferred_element_type=jnp.float32)


def dot_last(left, right):
    return lax.dot_general(
        left, right, (((1,), (1,)), ((), ())), preferred_element_type=jnp.float32
    )


def kernel(
    dp_size,
    group_size,
    reduce_here,
    fine_ref,
    down_rows_ref,
    nb_rows,
    count_ref,
    down_hbm,
    mid_hbm,
    out_hbm,
    gain_ref,
    bias_ref,
    cotangent_ref,
    features_ref,
    fine_grad_ref,
    grads_hbm,
    gain_grad_ref,
    bias_grad_ref,
    w_down,
    w_mid,
    w_out,
    spread_fine,
    cols_down,
    nb_cols,
    act_one,
    act_one_b,
    act_two_b,
    hid_one,
    hid_two,
    hid_three,
    grad_hidden,
    source_t,
    grad_act,
    side,
    side_cols,
    grads,
    from_core,
    from_first_a,
    from_first_b,
    from_second_a,
    from_second_b,
    from_line_a,
    from_line_b,
    near,
    far,
    load_sem,
    store_sem,
    sum_send,
    sum_recv,
    near_send,
    near_recv,
    far_send,
    far_recv,
):
    rows, width = cotangent_ref.shape
    offsets = nb_rows.shape[0]
    fine_rows, in_width = fine_ref.shape
    children = fine_rows // rows
    down_offsets = down_rows_ref.shape[0]
    chunks = grads.shape[0] // CHUNK
    dp_me = lax.axis_index("dp")
    group_me = lax.axis_index("group")

    loads = [
        pltpu.make_async_copy(source, target, load_sem.at[at])
        for at, (source, target) in enumerate(
            ((down_hbm, w_down), (mid_hbm, w_mid), (out_hbm, w_out))
        )
    ]
    for load in loads:
        load.start()

    barrier = pltpu.get_barrier_semaphore()
    for step in range(1, group_size):
        pl.semaphore_signal(
            barrier,
            inc=1,
            device_id={"group": lax.rem(group_me + step, group_size)},
            device_id_type=MESH,
        )
    for step in range(1, dp_size):
        pl.semaphore_signal(
            barrier,
            inc=1,
            device_id={"dp": lax.rem(dp_me + step, dp_size)},
            device_id_type=MESH,
        )
    pl.semaphore_wait(barrier, group_size + dp_size - 2)

    def share(at, axis, me, size, slots, send, recv):
        copies = []
        for step in range(1, size):
            copies.append(
                pltpu.make_async_remote_copy(
                    src_ref=slots.at[at, me],
                    dst_ref=slots.at[at, me],
                    send_sem=send.at[at, step - 1],
                    recv_sem=recv.at[at, step - 1],
                    device_id={axis: lax.rem(me + step, size)},
                    device_id_type=MESH,
                )
            )
        for copy in copies:
            copy.start()
        return copies

    def exchange(at, block, combine, meanwhile=None):
        near[at, group_me] = block
        copies = share(at, "group", group_me, group_size, near, near_send, near_recv)
        if meanwhile is not None:
            meanwhile()
        for copy in copies:
            copy.wait()
        far[at, dp_me] = combine([near[at, slot] for slot in range(group_size)])
        copies = share(at, "dp", dp_me, dp_size, far, far_send, far_recv)
        for copy in copies:
            copy.wait()
        return combine([far[at, slot] for slot in range(dp_size)])

    place = lax.broadcasted_iota(jnp.int32, (8, width), 0)

    def stack(first, second, third):
        return jnp.where(
            place == 0, first, jnp.where(place == 1, second, jnp.where(place == 2, third, 0.0))
        )

    def add_all(blocks):
        total = blocks[0]
        for block in blocks[1:]:
            total = total + block
        return total

    def merge_all(blocks):
        count = add_all([block[2:3] for block in blocks])
        center = add_all([block[2:3] * block[0:1] for block in blocks]) / count
        squares = add_all(
            [
                block[1:2] + block[2:3] * (block[0:1] - center) * (block[0:1] - center)
                for block in blocks
            ]
        )
        return stack(center, squares, count)

    count = count_ref[0]
    own_count = jnp.full((1, width), count.astype(jnp.float32))
    live = lax.broadcasted_iota(jnp.int32, (rows, width), 0) < count

    def norm_stats(at, hidden, meanwhile=None):
        center = jnp.sum(hidden, axis=0, keepdims=True) / own_count
        centered = jnp.where(live, hidden - center, 0.0)
        squares = jnp.sum(centered * centered, axis=0, keepdims=True)
        merged = exchange(at, stack(center, squares, own_count), merge_all, meanwhile)
        total = merged[2:3]
        scale = lax.rsqrt(merged[1:2] / total + eps_norm)
        return merged[0:1], scale, total

    def norm_grad(at, norm, incoming, normed, scale, total, meanwhile=None):
        shift_sum = jnp.sum(incoming, axis=0, keepdims=True)
        scale_sum = jnp.sum(incoming * normed, axis=0, keepdims=True)
        summed = exchange(
            at, stack(shift_sum, scale_sum, jnp.zeros_like(shift_sum)), add_all, meanwhile
        )
        bias_grad_ref[norm : norm + 1, :] = summed[0:1]
        gain_grad_ref[norm : norm + 1, :] = summed[1:2]
        hidden_grad = (
            scale
            * gain_ref[norm : norm + 1, :]
            * (incoming - summed[0:1] / total - normed * (summed[1:2] / total))
        )
        return jnp.where(live, hidden_grad, 0.0).astype(jnp.bfloat16)

    def convolve(source, weight, hidden):
        lanes = lax.broadcasted_iota(jnp.int32, (rows, rows), 1)
        hidden[...] = jnp.zeros_like(hidden)

        def step(at, carry):
            total = None
            for part in range(GROUP):
                k = at * GROUP + part
                wanted = jnp.concatenate([nb_cols[k]] * (rows // 128), axis=1)
                picker = jnp.where(wanted == lanes, 1.0, 0.0).astype(jnp.bfloat16)
                columns = dot(picker, source[...]).astype(jnp.bfloat16)
                term = dot(columns, weight[k])
                total = term if total is None else total + term
            hidden[...] += total
            return carry

        lax.fori_loop(0, offsets // GROUP, step, 0)

    def convolve_back(source_t, weight, hidden_grad, act_grad, first_unit, first_slot):
        places = lax.broadcasted_iota(jnp.int32, (rows, rows), 0)

        def step(at, carry):
            total = None
            for part in range(GROUP):
                k = at * GROUP + part
                picker = jnp.where(nb_rows[pl.ds(k, 1), :] == places, 1.0, 0.0).astype(
                    jnp.bfloat16
                )
                spread = dot(picker, hidden_grad[...]).astype(jnp.bfloat16)
                term = dot_last(spread, weight[k])
                total = term if total is None else total + term
                unit = pl.multiple_of((first_unit + k) * width, width)
                grads[pl.ds(unit, width), :] = dot(source_t[...], spread)
            act_grad[...] += total

            @pl.when(lax.rem(at, 2) == 0)
            def _():
                slot(first_slot + at // 2)

            return carry

        lax.fori_loop(0, offsets // GROUP, step, 0)

    core, row = lax.rem(group_me, 2), group_me // 2
    column, plane = lax.rem(dp_me, 2), dp_me // 2
    planes = dp_size // 2
    core_peer = {"group": group_me + 1 - 2 * core}
    row_peer = {"group": group_me + 2 - 4 * row}
    column_peer = {"dp": dp_me + 1 - 2 * column}
    half, quarter, eighth, part_rows = CHUNK // 2, CHUNK // 8, CHUNK // 16, CHUNK // 64

    def places_of(c):
        base = c * CHUNK
        own, other = base + half * core, base + half * (1 - core)
        keep_a, give_a = own + quarter * column, own + quarter * (1 - column)
        keep_b = own + 2 * quarter + quarter * row
        give_b = own + 2 * quarter + quarter * (1 - row)
        keep_aa, give_aa = keep_a + eighth * row, keep_a + eighth * (1 - row)
        keep_bb, give_bb = keep_b + eighth * column, keep_b + eighth * (1 - column)
        return own, other, keep_a, give_a, keep_b, give_b, keep_aa, give_aa, keep_bb, give_bb

    def at_rows(ref, first, count, step):
        return ref.at[pl.ds(pl.multiple_of(first, step), count), :]

    def send(c, number, source, target, peer):
        turn = lax.rem(c, RING)
        return pltpu.make_async_remote_copy(
            src_ref=source,
            dst_ref=target,
            send_sem=sum_send.at[turn, number],
            recv_sem=sum_recv.at[turn, number],
            device_id=peer,
            device_id_type=MESH,
        )

    def copies_of(c, stage):
        own, other, keep_a, give_a, keep_b, give_b, keep_aa, give_aa, keep_bb, give_bb = places_of(c)
        if stage == 0:
            return [
                send(
                    c,
                    0,
                    at_rows(grads, other, half, half),
                    at_rows(from_core, c * half, half, half),
                    core_peer,
                )
            ]
        if stage == 1:
            return [
                send(
                    c,
                    1,
                    at_rows(grads, give_a, quarter, quarter),
                    at_rows(from_first_a, c * quarter, quarter, quarter),
                    column_peer,
                ),
                send(
                    c,
                    2,
                    at_rows(grads, give_b, quarter, quarter),
                    at_rows(from_first_b, c * quarter, quarter, quarter),
                    row_peer,
                ),
            ]
        if stage == 2:
            return [
                send(
                    c,
                    3,
                    at_rows(grads, give_aa, eighth, eighth),
                    at_rows(from_second_a, c * eighth, eighth, eighth),
                    row_peer,
                ),
                send(
                    c,
                    4,
                    at_rows(grads, give_bb, eighth, eighth),
                    at_rows(from_second_b, c * eighth, eighth, eighth),
                    column_peer,
                ),
            ]
        if stage in (3, 4):
            copies = []
            for lane, (keep, landing) in enumerate(((keep_aa, from_line_a), (keep_bb, from_line_b))):
                for step in range(1, planes):
                    there = lax.rem(plane + step, planes)
                    number = 5 + ((stage - 3) * 2 + lane) * (planes - 1) + step - 1
                    if stage == 3:
                        source = at_rows(grads, keep + part_rows * there, part_rows, part_rows)
                        target = landing.at[c, step - 1]
                    else:
                        piece = keep + part_rows * plane
                        source = at_rows(grads, piece, part_rows, part_rows)
                        target = at_rows(grads_hbm, piece, part_rows, part_rows)
                    copies.append(
                        send(c, number, source, target, {"dp": 2 * there + column})
                    )
            return copies
        first = 5 + 4 * (planes - 1)
        if stage == 5:
            block_a, block_b = (at_rows(grads_hbm, keep, eighth, eighth) for keep in (keep_aa, keep_bb))
            return [
                send(c, first, block_a, block_a, row_peer),
                send(c, first + 1, block_b, block_b, column_peer),
            ]
        if stage == 6:
            block_a, block_b = (at_rows(grads_hbm, keep, quarter, quarter) for keep in (keep_a, keep_b))
            return [
                send(c, first + 2, block_a, block_a, column_peer),
                send(c, first + 3, block_b, block_b, row_peer),
            ]
        block = at_rows(grads_hbm, own, half, half)
        return [send(c, first + 4, block, block, core_peer)]

    def store_of(c, lane):
        _, _, _, _, _, _, keep_aa, _, keep_bb, _ = places_of(c)
        piece = (keep_aa, keep_bb)[lane] + part_rows * plane
        return pltpu.make_async_copy(
            at_rows(grads, piece, part_rows, part_rows),
            at_rows(grads_hbm, piece, part_rows, part_rows),
            store_sem.at[lax.rem(c, RING), lane],
        )

    def add_rows(first, count, landing):
        here = pl.ds(pl.multiple_of(first, count), count)
        grads[here, :] = grads[here, :] + landing

    def stage_of(c, stage):
        if stage > 0:
            for copy in copies_of(c, stage - 1):
                copy.wait()
        own, _, keep_a, _, keep_b, _, keep_aa, _, keep_bb, _ = places_of(c)
        if stage == 1:
            add_rows(own, half, from_core[pl.ds(pl.multiple_of(c * half, half), half), :])
        if stage == 2:
            landed = pl.ds(pl.multiple_of(c * quarter, quarter), quarter)
            add_rows(keep_a, quarter, from_first_a[landed, :])
            add_rows(keep_b, quarter, from_first_b[landed, :])
        if stage == 3:
            landed = pl.ds(pl.multiple_of(c * eighth, eighth), eighth)
            add_rows(keep_aa, eighth, from_second_a[landed, :])
            add_rows(keep_bb, eighth, from_second_b[landed, :])
        if stage == 4:
            for keep, landing in ((keep_aa, from_line_a), (keep_bb, from_line_b)):
                add_rows(
                    keep + part_rows * plane,
                    part_rows,
                    add_all([landing[c, step] for step in range(planes - 1)]),
                )
            for lane in range(2):
                store_of(c, lane).start()
        if stage == 5:
            for lane in range(2):
                store_of(c, lane).wait()
        if stage < STAGES:
            for copy in copies_of(c, stage):
                copy.start()

    def slot(at):
        if not reduce_here:
            return
        for stage in range(STAGES + 1):
            c = at - stage

            @pl.when((c >= 0) & (c < chunks))
            def _():
                stage_of(c, stage)

    side[...] = jnp.zeros_like(side)
    side[:offsets, :] = nb_rows[...]
    side[offsets : offsets + down_offsets, :] = down_rows_ref[...]
    side_cols[...] = side[...].T

    spread_fine[...] = fine_ref[...].astype(jnp.float32)
    for k in range(down_offsets):
        child = spread_fine[pl.ds(k % children, rows, stride=children), :]
        there = side_cols[:, offsets + k : offsets + k + 1] < fine_rows
        cols_down[:, k * in_width : (k + 1) * in_width] = jnp.where(there, child, 0.0).astype(
            jnp.bfloat16
        )
    loads[0].wait()
    hid_one[...] = dot(cols_down[...], w_down[...].reshape(down_offsets * in_width, width))

    def spread_neighbours():
        for k in range(offsets):
            nb_cols[k] = jnp.broadcast_to(side_cols[:, k : k + 1], (rows, 128))

    center_one, scale_one, total = norm_stats(0, hid_one[...], spread_neighbours)

    def pre_one():
        normed = (hid_one[...] - center_one) * scale_one
        return normed, normed * gain_ref[0:1, :] + bias_ref[0:1, :]

    _, pre = pre_one()
    act_one[...] = jnp.where(live, pre * sigmoid(pre), 0.0)
    act_one_b[...] = act_one[...].astype(jnp.bfloat16)
    loads[1].wait()
    convolve(act_one_b, w_mid, hid_two)
    center_two, scale_two, _ = norm_stats(1, hid_two[...])

    def pre_two():
        normed = (hid_two[...] - center_two) * scale_two
        return normed, normed * gain_ref[1:2, :] + bias_ref[1:2, :]

    _, pre = pre_two()
    act_two_b[...] = jnp.where(live, pre * sigmoid(pre), 0.0).astype(jnp.bfloat16)
    loads[2].wait()
    convolve(act_two_b, w_out, hid_three)
    center_three, scale_three, _ = norm_stats(2, hid_three[...])
    normed_three = (hid_three[...] - center_three) * scale_three
    summed = (
        jnp.where(live, normed_three * gain_ref[2:3, :] + bias_ref[2:3, :], 0.0) + act_one[...]
    )
    sigma = sigmoid(summed)
    features_ref[...] = jnp.where(live, summed * sigma, 0.0).astype(jnp.bfloat16)

    slope = sigma * (1.0 + summed * (1.0 - sigma))
    act_one[...] = jnp.where(live, cotangent_ref[...].astype(jnp.float32) * slope, 0.0)
    grad_hidden[...] = norm_grad(3, 2, act_one[...], normed_three, scale_three, total)
    grad_act[...] = jnp.zeros_like(grad_act)
    steps = offsets // GROUP
    slots = (steps + 1) // 2
    source_t[...] = act_two_b[...].T
    convolve_back(source_t, w_out, grad_hidden, grad_act, 0, 0)
    normed, pre = pre_two()
    incoming = jnp.where(live, grad_act[...] * silu_slope(pre), 0.0)
    grad_hidden[...] = norm_grad(4, 1, incoming, normed, scale_two, total)
    grad_act[...] = act_one[...]
    source_t[...] = act_one_b[...].T
    convolve_back(source_t, w_mid, grad_hidden, grad_act, offsets, slots)
    normed, pre = pre_one()
    incoming = jnp.where(live, grad_act[...] * silu_slope(pre), 0.0)
    grad_hidden[...] = norm_grad(5, 0, incoming, normed, scale_one, total)
    grads[2 * offsets * width :, :] = dot(cols_down[...].T, grad_hidden[...])
    slot(2 * slots)
    for child in range(children):
        total_child = jnp.zeros((rows, in_width), jnp.float32)
        for k in range(child, down_offsets, children):
            there = side_cols[:, offsets + k : offsets + k + 1] < fine_rows
            total_child += jnp.where(there, dot_last(grad_hidden[...], w_down[k]), 0.0)
        spread_fine[pl.ds(child, rows, stride=children), :] = total_child
    fine_grad_ref[...] = spread_fine[...].astype(jnp.bfloat16)

    if reduce_here:

        def rest(at, carry):
            slot(at)
            return carry

        lax.fori_loop(2 * slots + 1, chunks + STAGES, rest, 0)
    else:
        store = pltpu.make_async_copy(grads, grads_hbm, store_sem.at[0, 0])
        store.start()
        store.wait()


def per_device(
    dp_size,
    group_size,
    fine_features,
    down_map,
    neighbours,
    voxel_counts,
    down_weight,
    mid_weight,
    out_weight,
    norm_gain,
    norm_bias,
    cotangent,
):
    rows, width = cotangent.shape
    fine_rows, in_width = fine_features.shape
    offsets = neighbours.shape[1]
    down_offsets = down_map.shape[1]
    f32, bf16, i32 = jnp.float32, jnp.bfloat16, jnp.int32
    vmem = pl.BlockSpec(memory_space=pltpu.VMEM)
    smem = pl.BlockSpec(memory_space=pltpu.SMEM)
    hbm = pl.BlockSpec(memory_space=pl.ANY)
    shape = jax.ShapeDtypeStruct
    reduce_here = dp_size == 8 and group_size == 4
    grad_rows = 2 * offsets * width + down_offsets * in_width
    chunks = grad_rows // CHUNK
    planes = dp_size // 2 if reduce_here else 2
    copies = 10 + 4 * (planes - 1)
    features, fine_grad, grads, gain_grad, bias_grad = pl.pallas_call(
        functools.partial(kernel, dp_size, group_size, reduce_here),
        out_shape=(
            shape((rows, width), bf16),
            shape((fine_rows, in_width), bf16),
            shape((grad_rows, width), f32),
            shape(norm_gain.shape, f32),
            shape(norm_bias.shape, f32),
        ),
        in_specs=[vmem, vmem, vmem, smem, hbm, hbm, hbm, vmem, vmem, vmem],
        out_specs=(vmem, vmem, hbm, vmem, vmem),
        scratch_shapes=[
            pltpu.VMEM(down_weight.shape, bf16),
            pltpu.VMEM(mid_weight.shape, bf16),
            pltpu.VMEM(out_weight.shape, bf16),
            pltpu.VMEM((fine_rows, in_width), f32),
            pltpu.VMEM((rows, down_offsets * in_width), bf16),
            pltpu.VMEM((offsets, rows, 128), i32),
            pltpu.VMEM((rows, width), f32),
            pltpu.VMEM((rows, width), bf16),
            pltpu.VMEM((rows, width), bf16),
            pltpu.VMEM((rows, width), f32),
            pltpu.VMEM((rows, width), f32),
            pltpu.VMEM((rows, width), f32),
            pltpu.VMEM((rows, width), bf16),
            pltpu.VMEM((width, rows), bf16),
            pltpu.VMEM((rows, width), f32),
            pltpu.VMEM((128, rows), i32),
            pltpu.VMEM((rows, 128), i32),
            pltpu.VMEM((grad_rows, width), f32),
            pltpu.VMEM((grad_rows // 2, width), f32),
            pltpu.VMEM((grad_rows // 8, width), f32),
            pltpu.VMEM((grad_rows // 8, width), f32),
            pltpu.VMEM((grad_rows // 16, width), f32),
            pltpu.VMEM((grad_rows // 16, width), f32),
            pltpu.VMEM((chunks, planes - 1, CHUNK // 64, width), f32),
            pltpu.VMEM((chunks, planes - 1, CHUNK // 64, width), f32),
            pltpu.VMEM((6, group_size, 8, width), f32),
            pltpu.VMEM((6, dp_size, 8, width), f32),
            pltpu.SemaphoreType.DMA((3,)),
            pltpu.SemaphoreType.DMA((RING, 2)),
            pltpu.SemaphoreType.DMA((RING, copies)),
            pltpu.SemaphoreType.DMA((RING, copies)),
            pltpu.SemaphoreType.DMA((6, group_size - 1)),
            pltpu.SemaphoreType.DMA((6, group_size - 1)),
            pltpu.SemaphoreType.DMA((6, dp_size - 1)),
            pltpu.SemaphoreType.DMA((6, dp_size - 1)),
        ],
        compiler_params=pltpu.CompilerParams(
            collective_id=0, has_side_effects=True, vmem_limit_bytes=60 * 1024 * 1024
        ),
    )(
        fine_features,
        down_map.T,
        neighbours.T,
        voxel_counts,
        down_weight,
        mid_weight,
        out_weight,
        norm_gain,
        norm_bias,
        cotangent,
    )
    if not reduce_here:
        grads = lax.psum(grads, ("dp", "group"))
    middle, end = offsets * width, 2 * offsets * width
    grad_out = grads[:middle].reshape(out_weight.shape)
    grad_mid = grads[middle:end].reshape(mid_weight.shape)
    grad_down = grads[end:].reshape(down_weight.shape)
    return (features, fine_grad, grad_down, grad_mid, grad_out, gain_grad, bias_grad)


def solution(mesh):
    in_specs = (
        P(("dp", "group"), None),
        P(("dp", "group"), None),
        P(("dp", "group"), None),
        P(("dp", "group")),
        P(),
        P(),
        P(),
        P(),
        P(),
        P(("dp", "group"), None),
    )
    out_specs = (P(("dp", "group"), None), P(("dp", "group"), None), P(), P(), P(), P(), P())
    return jax.shard_map(
        functools.partial(per_device, mesh.shape["dp"], mesh.shape["group"]),
        mesh=mesh,
        in_specs=in_specs,
        out_specs=out_specs,
        check_vma=False,
    )
```

```python
import functools

import jax
import jax.numpy as jnp
from jax import lax
from jax.experimental import pallas as pl
from jax.experimental.pallas import tpu as pltpu
from jax.sharding import PartitionSpec as P

eps_norm = 1e-05
MESH = pl.DeviceIdType.MESH
GROUP = 3
CHUNK = 512
STAGES = 8
RING = 8


def sigmoid(value):
    return 1.0 / (1.0 + jnp.exp(-value))


def silu_slope(value):
    sigma = sigmoid(value)
    return sigma * (1.0 + value * (1.0 - sigma))


def dot(left, right):
    return jnp.dot(left, right, preferred_element_type=jnp.float32)


def dot_last(left, right):
    return lax.dot_general(
        left, right, (((1,), (1,)), ((), ())), preferred_element_type=jnp.float32
    )


def kernel(
    dp_size,
    group_size,
    reduce_here,
    fine_ref,
    down_rows_ref,
    nb_rows,
    count_ref,
    down_hbm,
    mid_hbm,
    out_hbm,
    gain_ref,
    bias_ref,
    cotangent_ref,
    features_ref,
    fine_grad_ref,
    grads_hbm,
    gain_grad_ref,
    bias_grad_ref,
    w_down,
    w_mid,
    w_out,
    spread_fine,
    cols_down,
    nb_cols,
    act_one,
    act_one_b,
    act_two_b,
    hid_one,
    hid_two,
    hid_three,
    grad_hidden,
    source_t,
    grad_act,
    side,
    side_cols,
    grads,
    from_core,
    from_first_a,
    from_first_b,
    from_second_a,
    from_second_b,
    from_line_a,
    from_line_b,
    near,
    far,
    load_sem,
    store_sem,
    sum_send,
    sum_recv,
    near_send,
    near_recv,
    far_send,
    far_recv,
):
    rows, width = cotangent_ref.shape
    offsets = nb_rows.shape[0]
    fine_rows, in_width = fine_ref.shape
    children = fine_rows // rows
    down_offsets = down_rows_ref.shape[0]
    chunks = grads.shape[0] // CHUNK
    dp_me = lax.axis_index("dp")
    group_me = lax.axis_index("group")

    loads = [
        pltpu.make_async_copy(source, target, load_sem.at[at])
        for at, (source, target) in enumerate(
            ((down_hbm, w_down), (mid_hbm, w_mid), (out_hbm, w_out))
        )
    ]
    for load in loads:
        load.start()

    barrier = pltpu.get_barrier_semaphore()
    for step in range(1, group_size):
        pl.semaphore_signal(
            barrier,
            inc=1,
            device_id={"group": lax.rem(group_me + step, group_size)},
            device_id_type=MESH,
        )
    for step in range(1, dp_size):
        pl.semaphore_signal(
            barrier,
            inc=1,
            device_id={"dp": lax.rem(dp_me + step, dp_size)},
            device_id_type=MESH,
        )
    pl.semaphore_wait(barrier, group_size + dp_size - 2)

    def share(at, axis, me, size, slots, send, recv):
        copies = []
        for step in range(1, size):
            copies.append(
                pltpu.make_async_remote_copy(
                    src_ref=slots.at[at, me],
                    dst_ref=slots.at[at, me],
                    send_sem=send.at[at, step - 1],
                    recv_sem=recv.at[at, step - 1],
                    device_id={axis: lax.rem(me + step, size)},
                    device_id_type=MESH,
                )
            )
        for copy in copies:
            copy.start()
        return copies

    def exchange(at, block, combine, meanwhile=(None, None)):
        near[at, group_me] = block
        copies = share(at, "group", group_me, group_size, near, near_send, near_recv)
        if meanwhile[0] is not None:
            meanwhile[0]()
        for copy in copies:
            copy.wait()
        far[at, dp_me] = combine([near[at, slot] for slot in range(group_size)])
        copies = share(at, "dp", dp_me, dp_size, far, far_send, far_recv)
        if meanwhile[1] is not None:
            meanwhile[1]()
        for copy in copies:
            copy.wait()
        return combine([far[at, slot] for slot in range(dp_size)])

    place = lax.broadcasted_iota(jnp.int32, (8, width), 0)

    def stack(first, second, third):
        return jnp.where(
            place == 0, first, jnp.where(place == 1, second, jnp.where(place == 2, third, 0.0))
        )

    def add_all(blocks):
        total = blocks[0]
        for block in blocks[1:]:
            total = total + block
        return total

    def merge_all(blocks):
        count = add_all([block[2:3] for block in blocks])
        center = add_all([block[2:3] * block[0:1] for block in blocks]) / count
        squares = add_all(
            [
                block[1:2] + block[2:3] * (block[0:1] - center) * (block[0:1] - center)
                for block in blocks
            ]
        )
        return stack(center, squares, count)

    count = count_ref[0]
    own_count = jnp.full((1, width), count.astype(jnp.float32))
    live = lax.broadcasted_iota(jnp.int32, (rows, width), 0) < count

    def norm_stats(at, hidden, meanwhile=(None, None)):
        center = jnp.sum(hidden, axis=0, keepdims=True) / own_count
        centered = jnp.where(live, hidden - center, 0.0)
        squares = jnp.sum(centered * centered, axis=0, keepdims=True)
        merged = exchange(at, stack(center, squares, own_count), merge_all, meanwhile)
        total = merged[2:3]
        scale = lax.rsqrt(merged[1:2] / total + eps_norm)
        return merged[0:1], scale, total

    def norm_grad(at, norm, incoming, normed, scale, total, meanwhile=(None, None)):
        shift_sum = jnp.sum(incoming, axis=0, keepdims=True)
        scale_sum = jnp.sum(incoming * normed, axis=0, keepdims=True)
        summed = exchange(
            at, stack(shift_sum, scale_sum, jnp.zeros_like(shift_sum)), add_all, meanwhile
        )
        bias_grad_ref[norm : norm + 1, :] = summed[0:1]
        gain_grad_ref[norm : norm + 1, :] = summed[1:2]
        hidden_grad = (
            scale
            * gain_ref[norm : norm + 1, :]
            * (incoming - summed[0:1] / total - normed * (summed[1:2] / total))
        )
        return jnp.where(live, hidden_grad, 0.0).astype(jnp.bfloat16)

    def convolve(source, weight, hidden):
        lanes = lax.broadcasted_iota(jnp.int32, (GROUP * rows, rows), 1)
        hidden[...] = jnp.zeros_like(hidden)

        def step(at, carry):
            wanted = jnp.concatenate(
                [
                    jnp.concatenate([nb_cols[at * GROUP + part]] * (rows // 128), axis=1)
                    for part in range(GROUP)
                ],
                axis=0,
            )
            picker = jnp.where(wanted == lanes, 1.0, 0.0).astype(jnp.bfloat16)
            picked = dot(picker, source[...]).astype(jnp.bfloat16)
            columns = jnp.concatenate(
                [picked[part * rows : (part + 1) * rows] for part in range(GROUP)], axis=1
            )
            weights = weight[pl.ds(at * GROUP, GROUP)].reshape(GROUP * width, width)
            total = dot(columns, weights)
            hidden[...] += total
            return carry

        lax.fori_loop(0, offsets // GROUP, step, 0)

    def convolve_back(source_t, weight, hidden_grad, act_grad, first_unit, first_slot):
        places = lax.broadcasted_iota(jnp.int32, (rows, rows), 0)

        def step(at, carry):
            picker = jnp.concatenate(
                [
                    jnp.where(nb_rows[pl.ds(at * GROUP + part, 1), :] == places, 1.0, 0.0)
                    for part in range(GROUP)
                ],
                axis=0,
            ).astype(jnp.bfloat16)
            picked = dot(picker, hidden_grad[...]).astype(jnp.bfloat16)
            spread = jnp.concatenate(
                [picked[part * rows : (part + 1) * rows] for part in range(GROUP)], axis=1
            )
            weights = jnp.concatenate(
                [weight[at * GROUP + part] for part in range(GROUP)], axis=1
            )
            act_grad[...] += dot_last(spread, weights)
            product = dot(source_t[...], spread)
            for part in range(GROUP):
                unit = pl.multiple_of((first_unit + at * GROUP + part) * width, width)
                grads[pl.ds(unit, width), :] = product[:, part * width : (part + 1) * width]
            slot(first_slot + at)
            return carry

        lax.fori_loop(0, offsets // GROUP, step, 0)

    core, row = lax.rem(group_me, 2), group_me // 2
    column, plane = lax.rem(dp_me, 2), dp_me // 2
    planes = dp_size // 2
    core_peer = {"group": group_me + 1 - 2 * core}
    row_peer = {"group": group_me + 2 - 4 * row}
    column_peer = {"dp": dp_me + 1 - 2 * column}
    half, quarter, eighth, part_rows = CHUNK // 2, CHUNK // 8, CHUNK // 16, CHUNK // 64

    def places_of(c):
        base = c * CHUNK
        own, other = base + half * core, base + half * (1 - core)
        keep_a, give_a = own + quarter * column, own + quarter * (1 - column)
        keep_b = own + 2 * quarter + quarter * row
        give_b = own + 2 * quarter + quarter * (1 - row)
        keep_aa, give_aa = keep_a + eighth * row, keep_a + eighth * (1 - row)
        keep_bb, give_bb = keep_b + eighth * column, keep_b + eighth * (1 - column)
        return own, other, keep_a, give_a, keep_b, give_b, keep_aa, give_aa, keep_bb, give_bb

    def at_rows(ref, first, count, step):
        return ref.at[pl.ds(pl.multiple_of(first, step), count), :]

    def send(c, number, source, target, peer):
        turn = lax.rem(c, RING)
        return pltpu.make_async_remote_copy(
            src_ref=source,
            dst_ref=target,
            send_sem=sum_send.at[turn, number],
            recv_sem=sum_recv.at[turn, number],
            device_id=peer,
            device_id_type=MESH,
        )

    def copies_of(c, stage):
        own, other, keep_a, give_a, keep_b, give_b, keep_aa, give_aa, keep_bb, give_bb = places_of(c)
        if stage == 0:
            return [
                send(
                    c,
                    0,
                    at_rows(grads, other, half, half),
                    at_rows(from_core, c * half, half, half),
                    core_peer,
                )
            ]
        if stage == 1:
            return [
                send(
                    c,
                    1,
                    at_rows(grads, give_a, quarter, quarter),
                    at_rows(from_first_a, c * quarter, quarter, quarter),
                    column_peer,
                ),
                send(
                    c,
                    2,
                    at_rows(grads, give_b, quarter, quarter),
                    at_rows(from_first_b, c * quarter, quarter, quarter),
                    row_peer,
                ),
            ]
        if stage == 2:
            return [
                send(
                    c,
                    3,
                    at_rows(grads, give_aa, eighth, eighth),
                    at_rows(from_second_a, c * eighth, eighth, eighth),
                    row_peer,
                ),
                send(
                    c,
                    4,
                    at_rows(grads, give_bb, eighth, eighth),
                    at_rows(from_second_b, c * eighth, eighth, eighth),
                    column_peer,
                ),
            ]
        if stage in (3, 4):
            copies = []
            for lane, (keep, landing) in enumerate(((keep_aa, from_line_a), (keep_bb, from_line_b))):
                for step in range(1, planes):
                    there = lax.rem(plane + step, planes)
                    number = 5 + ((stage - 3) * 2 + lane) * (planes - 1) + step - 1
                    if stage == 3:
                        source = at_rows(grads, keep + part_rows * there, part_rows, part_rows)
                        target = landing.at[c, step - 1]
                    else:
                        piece = keep + part_rows * plane
                        source = at_rows(grads, piece, part_rows, part_rows)
                        target = at_rows(grads_hbm, piece, part_rows, part_rows)
                    copies.append(
                        send(c, number, source, target, {"dp": 2 * there + column})
                    )
            return copies
        first = 5 + 4 * (planes - 1)
        if stage == 5:
            block_a, block_b = (at_rows(grads_hbm, keep, eighth, eighth) for keep in (keep_aa, keep_bb))
            return [
                send(c, first, block_a, block_a, row_peer),
                send(c, first + 1, block_b, block_b, column_peer),
            ]
        if stage == 6:
            block_a, block_b = (at_rows(grads_hbm, keep, quarter, quarter) for keep in (keep_a, keep_b))
            return [
                send(c, first + 2, block_a, block_a, column_peer),
                send(c, first + 3, block_b, block_b, row_peer),
            ]
        block = at_rows(grads_hbm, own, half, half)
        return [send(c, first + 4, block, block, core_peer)]

    def store_of(c, lane):
        _, _, _, _, _, _, keep_aa, _, keep_bb, _ = places_of(c)
        piece = (keep_aa, keep_bb)[lane] + part_rows * plane
        return pltpu.make_async_copy(
            at_rows(grads, piece, part_rows, part_rows),
            at_rows(grads_hbm, piece, part_rows, part_rows),
            store_sem.at[lax.rem(c, RING), lane],
        )

    def add_rows(first, count, landing):
        here = pl.ds(pl.multiple_of(first, count), count)
        grads[here, :] = grads[here, :] + landing

    def stage_of(c, stage):
        if stage > 0:
            for copy in copies_of(c, stage - 1):
                copy.wait()
        own, _, keep_a, _, keep_b, _, keep_aa, _, keep_bb, _ = places_of(c)
        if stage == 1:
            add_rows(own, half, from_core[pl.ds(pl.multiple_of(c * half, half), half), :])
        if stage == 2:
            landed = pl.ds(pl.multiple_of(c * quarter, quarter), quarter)
            add_rows(keep_a, quarter, from_first_a[landed, :])
            add_rows(keep_b, quarter, from_first_b[landed, :])
        if stage == 3:
            landed = pl.ds(pl.multiple_of(c * eighth, eighth), eighth)
            add_rows(keep_aa, eighth, from_second_a[landed, :])
            add_rows(keep_bb, eighth, from_second_b[landed, :])
        if stage == 4:
            for keep, landing in ((keep_aa, from_line_a), (keep_bb, from_line_b)):
                add_rows(
                    keep + part_rows * plane,
                    part_rows,
                    add_all([landing[c, step] for step in range(planes - 1)]),
                )
            for lane in range(2):
                store_of(c, lane).start()
        if stage == 5:
            for lane in range(2):
                store_of(c, lane).wait()
        if stage < STAGES:
            for copy in copies_of(c, stage):
                copy.start()

    def slot(at):
        if not reduce_here:
            return
        for stage in range(STAGES + 1):
            c = at - stage

            @pl.when((c >= 0) & (c < chunks))
            def _():
                stage_of(c, stage)

    side[...] = jnp.zeros_like(side)
    side[:offsets, :] = nb_rows[...]
    side[offsets : offsets + down_offsets, :] = down_rows_ref[...]
    side_cols[...] = side[...].T

    spread_fine[...] = fine_ref[...].astype(jnp.float32)
    for k in range(down_offsets):
        child = spread_fine[pl.ds(k % children, rows, stride=children), :]
        there = side_cols[:, offsets + k : offsets + k + 1] < fine_rows
        cols_down[:, k * in_width : (k + 1) * in_width] = jnp.where(there, child, 0.0).astype(
            jnp.bfloat16
        )
    loads[0].wait()
    hid_one[...] = dot(cols_down[...], w_down[...].reshape(down_offsets * in_width, width))

    def spread_neighbours():
        for k in range(offsets):
            nb_cols[k] = jnp.broadcast_to(side_cols[:, k : k + 1], (rows, 128))

    center_one, scale_one, total = norm_stats(0, hid_one[...], (spread_neighbours, None))

    def pre_one():
        normed = (hid_one[...] - center_one) * scale_one
        return normed, normed * gain_ref[0:1, :] + bias_ref[0:1, :]

    _, pre = pre_one()
    act_one[...] = jnp.where(live, pre * sigmoid(pre), 0.0)
    act_one_b[...] = act_one[...].astype(jnp.bfloat16)
    loads[1].wait()
    convolve(act_one_b, w_mid, hid_two)
    center_two, scale_two, _ = norm_stats(1, hid_two[...])

    def pre_two():
        normed = (hid_two[...] - center_two) * scale_two
        return normed, normed * gain_ref[1:2, :] + bias_ref[1:2, :]

    _, pre = pre_two()
    act_two_b[...] = jnp.where(live, pre * sigmoid(pre), 0.0).astype(jnp.bfloat16)
    loads[2].wait()
    convolve(act_two_b, w_out, hid_three)
    center_three, scale_three, _ = norm_stats(2, hid_three[...])
    normed_three = (hid_three[...] - center_three) * scale_three
    summed = (
        jnp.where(live, normed_three * gain_ref[2:3, :] + bias_ref[2:3, :], 0.0) + act_one[...]
    )
    sigma = sigmoid(summed)
    features_ref[...] = jnp.where(live, summed * sigma, 0.0).astype(jnp.bfloat16)

    slope = sigma * (1.0 + summed * (1.0 - sigma))
    act_one[...] = jnp.where(live, cotangent_ref[...].astype(jnp.float32) * slope, 0.0)
    grad_hidden[...] = norm_grad(3, 2, act_one[...], normed_three, scale_three, total)
    grad_act[...] = jnp.zeros_like(grad_act)
    steps = offsets // GROUP

    def slots_from(at):
        return (lambda: slot(at), lambda: slot(at + 1))

    source_t[...] = act_two_b[...].T
    convolve_back(source_t, w_out, grad_hidden, grad_act, 0, 0)
    normed, pre = pre_two()
    incoming = jnp.where(live, grad_act[...] * silu_slope(pre), 0.0)
    grad_hidden[...] = norm_grad(
        4, 1, incoming, normed, scale_two, total, slots_from(steps)
    )
    grad_act[...] = act_one[...]
    source_t[...] = act_one_b[...].T
    convolve_back(source_t, w_mid, grad_hidden, grad_act, offsets, steps + 2)
    normed, pre = pre_one()
    incoming = jnp.where(live, grad_act[...] * silu_slope(pre), 0.0)
    grad_hidden[...] = norm_grad(
        5, 0, incoming, normed, scale_one, total, slots_from(2 * steps + 2)
    )
    grads[2 * offsets * width :, :] = dot(cols_down[...].T, grad_hidden[...])
    slot(2 * steps + 4)
    for child in range(children):
        total_child = jnp.zeros((rows, in_width), jnp.float32)
        for k in range(child, down_offsets, children):
            there = side_cols[:, offsets + k : offsets + k + 1] < fine_rows
            total_child += jnp.where(there, dot_last(grad_hidden[...], w_down[k]), 0.0)
        spread_fine[pl.ds(child, rows, stride=children), :] = total_child
    fine_grad_ref[...] = spread_fine[...].astype(jnp.bfloat16)

    if reduce_here:

        def rest(at, carry):
            slot(at)
            return carry

        lax.fori_loop(2 * steps + 5, chunks + STAGES, rest, 0)
    else:
        store = pltpu.make_async_copy(grads, grads_hbm, store_sem.at[0, 0])
        store.start()
        store.wait()


def per_device(
    dp_size,
    group_size,
    fine_features,
    down_map,
    neighbours,
    voxel_counts,
    down_weight,
    mid_weight,
    out_weight,
    norm_gain,
    norm_bias,
    cotangent,
):
    rows, width = cotangent.shape
    fine_rows, in_width = fine_features.shape
    offsets = neighbours.shape[1]
    down_offsets = down_map.shape[1]
    f32, bf16, i32 = jnp.float32, jnp.bfloat16, jnp.int32
    vmem = pl.BlockSpec(memory_space=pltpu.VMEM)
    smem = pl.BlockSpec(memory_space=pltpu.SMEM)
    hbm = pl.BlockSpec(memory_space=pl.ANY)
    shape = jax.ShapeDtypeStruct
    reduce_here = dp_size == 8 and group_size == 4
    grad_rows = 2 * offsets * width + down_offsets * in_width
    chunks = grad_rows // CHUNK
    planes = dp_size // 2 if reduce_here else 2
    copies = 10 + 4 * (planes - 1)
    features, fine_grad, grads, gain_grad, bias_grad = pl.pallas_call(
        functools.partial(kernel, dp_size, group_size, reduce_here),
        out_shape=(
            shape((rows, width), bf16),
            shape((fine_rows, in_width), bf16),
            shape((grad_rows, width), f32),
            shape(norm_gain.shape, f32),
            shape(norm_bias.shape, f32),
        ),
        in_specs=[vmem, vmem, vmem, smem, hbm, hbm, hbm, vmem, vmem, vmem],
        out_specs=(vmem, vmem, hbm, vmem, vmem),
        scratch_shapes=[
            pltpu.VMEM(down_weight.shape, bf16),
            pltpu.VMEM(mid_weight.shape, bf16),
            pltpu.VMEM(out_weight.shape, bf16),
            pltpu.VMEM((fine_rows, in_width), f32),
            pltpu.VMEM((rows, down_offsets * in_width), bf16),
            pltpu.VMEM((offsets, rows, 128), i32),
            pltpu.VMEM((rows, width), f32),
            pltpu.VMEM((rows, width), bf16),
            pltpu.VMEM((rows, width), bf16),
            pltpu.VMEM((rows, width), f32),
            pltpu.VMEM((rows, width), f32),
            pltpu.VMEM((rows, width), f32),
            pltpu.VMEM((rows, width), bf16),
            pltpu.VMEM((width, rows), bf16),
            pltpu.VMEM((rows, width), f32),
            pltpu.VMEM((128, rows), i32),
            pltpu.VMEM((rows, 128), i32),
            pltpu.VMEM((grad_rows, width), f32),
            pltpu.VMEM((grad_rows // 2, width), f32),
            pltpu.VMEM((grad_rows // 8, width), f32),
            pltpu.VMEM((grad_rows // 8, width), f32),
            pltpu.VMEM((grad_rows // 16, width), f32),
            pltpu.VMEM((grad_rows // 16, width), f32),
            pltpu.VMEM((chunks, planes - 1, CHUNK // 64, width), f32),
            pltpu.VMEM((chunks, planes - 1, CHUNK // 64, width), f32),
            pltpu.VMEM((6, group_size, 8, width), f32),
            pltpu.VMEM((6, dp_size, 8, width), f32),
            pltpu.SemaphoreType.DMA((3,)),
            pltpu.SemaphoreType.DMA((RING, 2)),
            pltpu.SemaphoreType.DMA((RING, copies)),
            pltpu.SemaphoreType.DMA((RING, copies)),
            pltpu.SemaphoreType.DMA((6, group_size - 1)),
            pltpu.SemaphoreType.DMA((6, group_size - 1)),
            pltpu.SemaphoreType.DMA((6, dp_size - 1)),
            pltpu.SemaphoreType.DMA((6, dp_size - 1)),
        ],
        compiler_params=pltpu.CompilerParams(
            collective_id=0, has_side_effects=True, vmem_limit_bytes=60 * 1024 * 1024
        ),
    )(
        fine_features,
        down_map.T,
        neighbours.T,
        voxel_counts,
        down_weight,
        mid_weight,
        out_weight,
        norm_gain,
        norm_bias,
        cotangent,
    )
    if not reduce_here:
        grads = lax.psum(grads, ("dp", "group"))
    middle, end = offsets * width, 2 * offsets * width
    grad_out = grads[:middle].reshape(out_weight.shape)
    grad_mid = grads[middle:end].reshape(mid_weight.shape)
    grad_down = grads[end:].reshape(down_weight.shape)
    return (features, fine_grad, grad_down, grad_mid, grad_out, gain_grad, bias_grad)


def solution(mesh):
    in_specs = (
        P(("dp", "group"), None),
        P(("dp", "group"), None),
        P(("dp", "group"), None),
        P(("dp", "group")),
        P(),
        P(),
        P(),
        P(),
        P(),
        P(("dp", "group"), None),
    )
    out_specs = (P(("dp", "group"), None), P(("dp", "group"), None), P(), P(), P(), P(), P())
    return jax.shard_map(
        functools.partial(per_device, mesh.shape["dp"], mesh.shape["group"]),
        mesh=mesh,
        in_specs=in_specs,
        out_specs=out_specs,
        check_vma=False,
    )
```

```python
import functools

import jax
import jax.numpy as jnp
from jax import lax
from jax.experimental import pallas as pl
from jax.experimental.pallas import tpu as pltpu
from jax.sharding import PartitionSpec as P

eps_norm = 1e-05
MESH = pl.DeviceIdType.MESH
GROUP = 3
BLOCK = 256
CHUNK = 512
STAGES = 8
RING = 8


def sigmoid(value):
    return 1.0 / (1.0 + jnp.exp(-value))


def silu_slope(value):
    sigma = sigmoid(value)
    return sigma * (1.0 + value * (1.0 - sigma))


def dot(left, right):
    return jnp.dot(left, right, preferred_element_type=jnp.float32)


def dot_last(left, right):
    return lax.dot_general(
        left, right, (((1,), (1,)), ((), ())), preferred_element_type=jnp.float32
    )


def kernel(
    dp_size,
    group_size,
    reduce_here,
    fine_ref,
    down_rows_ref,
    nb_rows,
    count_ref,
    down_hbm,
    mid_hbm,
    out_hbm,
    gain_ref,
    bias_ref,
    cotangent_ref,
    features_ref,
    fine_grad_ref,
    grads_hbm,
    gain_grad_ref,
    bias_grad_ref,
    w_down,
    w_mid,
    w_out,
    spread_fine,
    cols_down,
    nb_cols,
    columns,
    act_one,
    act_one_b,
    act_two_b,
    hid_one,
    hid_two,
    hid_three,
    grad_hidden,
    source_t,
    grad_act,
    side,
    side_cols,
    grads,
    from_core,
    from_first_a,
    from_first_b,
    from_second_a,
    from_second_b,
    from_line_a,
    from_line_b,
    near,
    far,
    load_sem,
    store_sem,
    sum_send,
    sum_recv,
    near_send,
    near_recv,
    far_send,
    far_recv,
):
    rows, width = cotangent_ref.shape
    offsets = nb_rows.shape[0]
    fine_rows, in_width = fine_ref.shape
    children = fine_rows // rows
    down_offsets = down_rows_ref.shape[0]
    chunks = grads.shape[0] // CHUNK
    dp_me = lax.axis_index("dp")
    group_me = lax.axis_index("group")

    loads = [
        pltpu.make_async_copy(source, target, load_sem.at[at])
        for at, (source, target) in enumerate(
            ((down_hbm, w_down), (mid_hbm, w_mid), (out_hbm, w_out))
        )
    ]
    for load in loads:
        load.start()

    barrier = pltpu.get_barrier_semaphore()
    for step in range(1, group_size):
        pl.semaphore_signal(
            barrier,
            inc=1,
            device_id={"group": lax.rem(group_me + step, group_size)},
            device_id_type=MESH,
        )
    for step in range(1, dp_size):
        pl.semaphore_signal(
            barrier,
            inc=1,
            device_id={"dp": lax.rem(dp_me + step, dp_size)},
            device_id_type=MESH,
        )
    pl.semaphore_wait(barrier, group_size + dp_size - 2)

    def share(at, axis, me, size, slots, send, recv):
        copies = []
        for step in range(1, size):
            copies.append(
                pltpu.make_async_remote_copy(
                    src_ref=slots.at[at, me],
                    dst_ref=slots.at[at, me],
                    send_sem=send.at[at, step - 1],
                    recv_sem=recv.at[at, step - 1],
                    device_id={axis: lax.rem(me + step, size)},
                    device_id_type=MESH,
                )
            )
        for copy in copies:
            copy.start()
        return copies

    def exchange(at, block, combine, meanwhile=(None, None)):
        near[at, group_me] = block
        copies = share(at, "group", group_me, group_size, near, near_send, near_recv)
        if meanwhile[0] is not None:
            meanwhile[0]()
        for copy in copies:
            copy.wait()
        far[at, dp_me] = combine([near[at, slot] for slot in range(group_size)])
        copies = share(at, "dp", dp_me, dp_size, far, far_send, far_recv)
        if meanwhile[1] is not None:
            meanwhile[1]()
        for copy in copies:
            copy.wait()
        return combine([far[at, slot] for slot in range(dp_size)])

    place = lax.broadcasted_iota(jnp.int32, (8, width), 0)

    def stack(first, second, third):
        return jnp.where(
            place == 0, first, jnp.where(place == 1, second, jnp.where(place == 2, third, 0.0))
        )

    def add_all(blocks):
        total = blocks[0]
        for block in blocks[1:]:
            total = total + block
        return total

    def merge_all(blocks):
        count = add_all([block[2:3] for block in blocks])
        center = add_all([block[2:3] * block[0:1] for block in blocks]) / count
        squares = add_all(
            [
                block[1:2] + block[2:3] * (block[0:1] - center) * (block[0:1] - center)
                for block in blocks
            ]
        )
        return stack(center, squares, count)

    count = count_ref[0]
    own_count = jnp.full((1, width), count.astype(jnp.float32))
    live = lax.broadcasted_iota(jnp.int32, (rows, width), 0) < count

    def norm_stats(at, hidden, meanwhile=(None, None)):
        center = jnp.sum(hidden, axis=0, keepdims=True) / own_count
        centered = jnp.where(live, hidden - center, 0.0)
        squares = jnp.sum(centered * centered, axis=0, keepdims=True)
        merged = exchange(at, stack(center, squares, own_count), merge_all, meanwhile)
        total = merged[2:3]
        scale = lax.rsqrt(merged[1:2] / total + eps_norm)
        return merged[0:1], scale, total

    def norm_grad(at, norm, incoming, normed, scale, total, meanwhile=(None, None)):
        shift_sum = jnp.sum(incoming, axis=0, keepdims=True)
        scale_sum = jnp.sum(incoming * normed, axis=0, keepdims=True)
        summed = exchange(
            at, stack(shift_sum, scale_sum, jnp.zeros_like(shift_sum)), add_all, meanwhile
        )
        bias_grad_ref[norm : norm + 1, :] = summed[0:1]
        gain_grad_ref[norm : norm + 1, :] = summed[1:2]
        hidden_grad = (
            scale
            * gain_ref[norm : norm + 1, :]
            * (incoming - summed[0:1] / total - normed * (summed[1:2] / total))
        )
        return jnp.where(live, hidden_grad, 0.0).astype(jnp.bfloat16)

    def pick(mask):
        return jnp.where(mask, jnp.bfloat16(1), jnp.bfloat16(0))

    def counting(shape, axis):
        return lax.broadcasted_iota(jnp.int32, shape, axis).astype(jnp.float32).astype(jnp.bfloat16)

    def convolve(source, weight, hidden):
        lanes = counting((BLOCK, BLOCK), 1)
        hidden[...] = jnp.zeros_like(hidden)

        def step(at, carry):
            for part in range(GROUP):
                k = at * GROUP + part
                for first in range(0, rows, BLOCK):
                    picker = jnp.concatenate(
                        [
                            pick(
                                jnp.concatenate(
                                    [nb_cols[block, k, first : first + BLOCK, :]] * (BLOCK // 128),
                                    axis=1,
                                )
                                == lanes
                            )
                            for block in range(rows // BLOCK)
                        ],
                        axis=1,
                    )
                    columns[first : first + BLOCK, part * width : (part + 1) * width] = dot(
                        picker, source[...]
                    ).astype(jnp.bfloat16)
            weights = weight[pl.ds(at * GROUP, GROUP)].reshape(GROUP * width, width)
            hidden[...] += dot(columns[...], weights)
            return carry

        lax.fori_loop(0, offsets // GROUP, step, 0)

    def convolve_back(source_t, weight, hidden_grad, act_grad, first_unit, first_slot):
        places = counting((BLOCK, rows), 0)

        def step(at, carry):
            for part in range(GROUP):
                wanted = nb_rows[pl.ds(at * GROUP + part, 1), :].astype(jnp.float32)
                for first in range(0, rows, BLOCK):
                    here = jnp.broadcast_to(wanted - first, (16, rows)).astype(jnp.bfloat16)
                    picker = pick(jnp.concatenate([here] * (BLOCK // 16), axis=0) == places)
                    columns[first : first + BLOCK, part * width : (part + 1) * width] = dot(
                        picker, hidden_grad[...]
                    ).astype(jnp.bfloat16)
            weights = jnp.concatenate(
                [weight[at * GROUP + part] for part in range(GROUP)], axis=1
            )
            act_grad[...] += dot_last(columns[...], weights)
            product = dot(source_t[...], columns[...])
            for part in range(GROUP):
                unit = pl.multiple_of((first_unit + at * GROUP + part) * width, width)
                grads[pl.ds(unit, width), :] = product[:, part * width : (part + 1) * width]
            slot(first_slot + at)
            return carry

        lax.fori_loop(0, offsets // GROUP, step, 0)

    core, row = lax.rem(group_me, 2), group_me // 2
    column, plane = lax.rem(dp_me, 2), dp_me // 2
    planes = dp_size // 2
    core_peer = {"group": group_me + 1 - 2 * core}
    row_peer = {"group": group_me + 2 - 4 * row}
    column_peer = {"dp": dp_me + 1 - 2 * column}
    half, quarter, eighth, part_rows = CHUNK // 2, CHUNK // 8, CHUNK // 16, CHUNK // 64

    def places_of(c):
        base = c * CHUNK
        own, other = base + half * core, base + half * (1 - core)
        keep_a, give_a = own + quarter * column, own + quarter * (1 - column)
        keep_b = own + 2 * quarter + quarter * row
        give_b = own + 2 * quarter + quarter * (1 - row)
        keep_aa, give_aa = keep_a + eighth * row, keep_a + eighth * (1 - row)
        keep_bb, give_bb = keep_b + eighth * column, keep_b + eighth * (1 - column)
        return own, other, keep_a, give_a, keep_b, give_b, keep_aa, give_aa, keep_bb, give_bb

    def at_rows(ref, first, count, step):
        return ref.at[pl.ds(pl.multiple_of(first, step), count), :]

    def send(c, number, source, target, peer):
        turn = lax.rem(c, RING)
        return pltpu.make_async_remote_copy(
            src_ref=source,
            dst_ref=target,
            send_sem=sum_send.at[turn, number],
            recv_sem=sum_recv.at[turn, number],
            device_id=peer,
            device_id_type=MESH,
        )

    def copies_of(c, stage):
        own, other, keep_a, give_a, keep_b, give_b, keep_aa, give_aa, keep_bb, give_bb = places_of(c)
        if stage == 0:
            return [
                send(
                    c,
                    0,
                    at_rows(grads, other, half, half),
                    at_rows(from_core, c * half, half, half),
                    core_peer,
                )
            ]
        if stage == 1:
            return [
                send(
                    c,
                    1,
                    at_rows(grads, give_a, quarter, quarter),
                    at_rows(from_first_a, c * quarter, quarter, quarter),
                    column_peer,
                ),
                send(
                    c,
                    2,
                    at_rows(grads, give_b, quarter, quarter),
                    at_rows(from_first_b, c * quarter, quarter, quarter),
                    row_peer,
                ),
            ]
        if stage == 2:
            return [
                send(
                    c,
                    3,
                    at_rows(grads, give_aa, eighth, eighth),
                    at_rows(from_second_a, c * eighth, eighth, eighth),
                    row_peer,
                ),
                send(
                    c,
                    4,
                    at_rows(grads, give_bb, eighth, eighth),
                    at_rows(from_second_b, c * eighth, eighth, eighth),
                    column_peer,
                ),
            ]
        if stage in (3, 4):
            copies = []
            for lane, (keep, landing) in enumerate(((keep_aa, from_line_a), (keep_bb, from_line_b))):
                for step in range(1, planes):
                    there = lax.rem(plane + step, planes)
                    number = 5 + ((stage - 3) * 2 + lane) * (planes - 1) + step - 1
                    if stage == 3:
                        source = at_rows(grads, keep + part_rows * there, part_rows, part_rows)
                        target = landing.at[c, step - 1]
                    else:
                        piece = keep + part_rows * plane
                        source = at_rows(grads, piece, part_rows, part_rows)
                        target = at_rows(grads_hbm, piece, part_rows, part_rows)
                    copies.append(
                        send(c, number, source, target, {"dp": 2 * there + column})
                    )
            return copies
        first = 5 + 4 * (planes - 1)
        if stage == 5:
            block_a, block_b = (at_rows(grads_hbm, keep, eighth, eighth) for keep in (keep_aa, keep_bb))
            return [
                send(c, first, block_a, block_a, row_peer),
                send(c, first + 1, block_b, block_b, column_peer),
            ]
        if stage == 6:
            block_a, block_b = (at_rows(grads_hbm, keep, quarter, quarter) for keep in (keep_a, keep_b))
            return [
                send(c, first + 2, block_a, block_a, column_peer),
                send(c, first + 3, block_b, block_b, row_peer),
            ]
        block = at_rows(grads_hbm, own, half, half)
        return [send(c, first + 4, block, block, core_peer)]

    def store_of(c, lane):
        _, _, _, _, _, _, keep_aa, _, keep_bb, _ = places_of(c)
        piece = (keep_aa, keep_bb)[lane] + part_rows * plane
        return pltpu.make_async_copy(
            at_rows(grads, piece, part_rows, part_rows),
            at_rows(grads_hbm, piece, part_rows, part_rows),
            store_sem.at[lax.rem(c, RING), lane],
        )

    def add_rows(first, count, landing):
        here = pl.ds(pl.multiple_of(first, count), count)
        grads[here, :] = grads[here, :] + landing

    def stage_of(c, stage):
        if stage > 0:
            for copy in copies_of(c, stage - 1):
                copy.wait()
        own, _, keep_a, _, keep_b, _, keep_aa, _, keep_bb, _ = places_of(c)
        if stage == 1:
            add_rows(own, half, from_core[pl.ds(pl.multiple_of(c * half, half), half), :])
        if stage == 2:
            landed = pl.ds(pl.multiple_of(c * quarter, quarter), quarter)
            add_rows(keep_a, quarter, from_first_a[landed, :])
            add_rows(keep_b, quarter, from_first_b[landed, :])
        if stage == 3:
            landed = pl.ds(pl.multiple_of(c * eighth, eighth), eighth)
            add_rows(keep_aa, eighth, from_second_a[landed, :])
            add_rows(keep_bb, eighth, from_second_b[landed, :])
        if stage == 4:
            for keep, landing in ((keep_aa, from_line_a), (keep_bb, from_line_b)):
                add_rows(
                    keep + part_rows * plane,
                    part_rows,
                    add_all([landing[c, step] for step in range(planes - 1)]),
                )
            for lane in range(2):
                store_of(c, lane).start()
        if stage == 5:
            for lane in range(2):
                store_of(c, lane).wait()
        if stage < STAGES:
            for copy in copies_of(c, stage):
                copy.start()

    def slot(at):
        if not reduce_here:
            return
        for stage in range(STAGES + 1):
            c = at - stage

            @pl.when((c >= 0) & (c < chunks))
            def _():
                stage_of(c, stage)

    side[...] = jnp.zeros_like(side)
    side[:offsets, :] = nb_rows[...]
    side[offsets : offsets + down_offsets, :] = down_rows_ref[...]
    side_cols[...] = side[...].T

    spread_fine[...] = fine_ref[...].astype(jnp.float32)
    for k in range(down_offsets):
        child = spread_fine[pl.ds(k % children, rows, stride=children), :]
        there = side_cols[:, offsets + k : offsets + k + 1] < fine_rows
        cols_down[:, k * in_width : (k + 1) * in_width] = jnp.where(there, child, 0.0).astype(
            jnp.bfloat16
        )
    loads[0].wait()
    hid_one[...] = dot(cols_down[...], w_down[...].reshape(down_offsets * in_width, width))

    def spread_neighbours():
        for k in range(offsets):
            wanted = jnp.broadcast_to(side_cols[:, k : k + 1], (rows, 128)).astype(jnp.float32)
            for block in range(rows // BLOCK):
                nb_cols[block, k] = (wanted - block * BLOCK).astype(jnp.bfloat16)

    center_one, scale_one, total = norm_stats(0, hid_one[...], (spread_neighbours, None))

    def pre_one():
        normed = (hid_one[...] - center_one) * scale_one
        return normed, normed * gain_ref[0:1, :] + bias_ref[0:1, :]

    _, pre = pre_one()
    act_one[...] = jnp.where(live, pre * sigmoid(pre), 0.0)
    act_one_b[...] = act_one[...].astype(jnp.bfloat16)
    loads[1].wait()
    convolve(act_one_b, w_mid, hid_two)
    center_two, scale_two, _ = norm_stats(1, hid_two[...])

    def pre_two():
        normed = (hid_two[...] - center_two) * scale_two
        return normed, normed * gain_ref[1:2, :] + bias_ref[1:2, :]

    _, pre = pre_two()
    act_two_b[...] = jnp.where(live, pre * sigmoid(pre), 0.0).astype(jnp.bfloat16)
    loads[2].wait()
    convolve(act_two_b, w_out, hid_three)
    center_three, scale_three, _ = norm_stats(2, hid_three[...])
    normed_three = (hid_three[...] - center_three) * scale_three
    summed = (
        jnp.where(live, normed_three * gain_ref[2:3, :] + bias_ref[2:3, :], 0.0) + act_one[...]
    )
    sigma = sigmoid(summed)
    features_ref[...] = jnp.where(live, summed * sigma, 0.0).astype(jnp.bfloat16)

    slope = sigma * (1.0 + summed * (1.0 - sigma))
    act_one[...] = jnp.where(live, cotangent_ref[...].astype(jnp.float32) * slope, 0.0)
    grad_hidden[...] = norm_grad(3, 2, act_one[...], normed_three, scale_three, total)
    grad_act[...] = jnp.zeros_like(grad_act)
    steps = offsets // GROUP

    def slots_from(at):
        return (lambda: slot(at), lambda: slot(at + 1))

    source_t[...] = act_two_b[...].T
    convolve_back(source_t, w_out, grad_hidden, grad_act, 0, 0)
    normed, pre = pre_two()
    incoming = jnp.where(live, grad_act[...] * silu_slope(pre), 0.0)
    grad_hidden[...] = norm_grad(
        4, 1, incoming, normed, scale_two, total, slots_from(steps)
    )
    grad_act[...] = act_one[...]
    source_t[...] = act_one_b[...].T
    convolve_back(source_t, w_mid, grad_hidden, grad_act, offsets, steps + 2)
    normed, pre = pre_one()
    incoming = jnp.where(live, grad_act[...] * silu_slope(pre), 0.0)
    grad_hidden[...] = norm_grad(
        5, 0, incoming, normed, scale_one, total, slots_from(2 * steps + 2)
    )
    grads[2 * offsets * width :, :] = dot(cols_down[...].T, grad_hidden[...])
    slot(2 * steps + 4)
    for child in range(children):
        total_child = jnp.zeros((rows, in_width), jnp.float32)
        for k in range(child, down_offsets, children):
            there = side_cols[:, offsets + k : offsets + k + 1] < fine_rows
            total_child += jnp.where(there, dot_last(grad_hidden[...], w_down[k]), 0.0)
        spread_fine[pl.ds(child, rows, stride=children), :] = total_child
    fine_grad_ref[...] = spread_fine[...].astype(jnp.bfloat16)

    if reduce_here:

        def rest(at, carry):
            slot(at)
            return carry

        lax.fori_loop(2 * steps + 5, chunks + STAGES, rest, 0)
    else:
        store = pltpu.make_async_copy(grads, grads_hbm, store_sem.at[0, 0])
        store.start()
        store.wait()


def per_device(
    dp_size,
    group_size,
    fine_features,
    down_map,
    neighbours,
    voxel_counts,
    down_weight,
    mid_weight,
    out_weight,
    norm_gain,
    norm_bias,
    cotangent,
):
    rows, width = cotangent.shape
    fine_rows, in_width = fine_features.shape
    offsets = neighbours.shape[1]
    down_offsets = down_map.shape[1]
    f32, bf16, i32 = jnp.float32, jnp.bfloat16, jnp.int32
    vmem = pl.BlockSpec(memory_space=pltpu.VMEM)
    smem = pl.BlockSpec(memory_space=pltpu.SMEM)
    hbm = pl.BlockSpec(memory_space=pl.ANY)
    shape = jax.ShapeDtypeStruct
    reduce_here = dp_size == 8 and group_size == 4
    grad_rows = 2 * offsets * width + down_offsets * in_width
    chunks = grad_rows // CHUNK
    planes = dp_size // 2 if reduce_here else 2
    copies = 10 + 4 * (planes - 1)
    features, fine_grad, grads, gain_grad, bias_grad = pl.pallas_call(
        functools.partial(kernel, dp_size, group_size, reduce_here),
        out_shape=(
            shape((rows, width), bf16),
            shape((fine_rows, in_width), bf16),
            shape((grad_rows, width), f32),
            shape(norm_gain.shape, f32),
            shape(norm_bias.shape, f32),
        ),
        in_specs=[vmem, vmem, vmem, smem, hbm, hbm, hbm, vmem, vmem, vmem],
        out_specs=(vmem, vmem, hbm, vmem, vmem),
        scratch_shapes=[
            pltpu.VMEM(down_weight.shape, bf16),
            pltpu.VMEM(mid_weight.shape, bf16),
            pltpu.VMEM(out_weight.shape, bf16),
            pltpu.VMEM((fine_rows, in_width), f32),
            pltpu.VMEM((rows, down_offsets * in_width), bf16),
            pltpu.VMEM((rows // BLOCK, offsets, rows, 128), bf16),
            pltpu.VMEM((rows, GROUP * width), bf16),
            pltpu.VMEM((rows, width), f32),
            pltpu.VMEM((rows, width), bf16),
            pltpu.VMEM((rows, width), bf16),
            pltpu.VMEM((rows, width), f32),
            pltpu.VMEM((rows, width), f32),
            pltpu.VMEM((rows, width), f32),
            pltpu.VMEM((rows, width), bf16),
            pltpu.VMEM((width, rows), bf16),
            pltpu.VMEM((rows, width), f32),
            pltpu.VMEM((128, rows), i32),
            pltpu.VMEM((rows, 128), i32),
            pltpu.VMEM((grad_rows, width), f32),
            pltpu.VMEM((grad_rows // 2, width), f32),
            pltpu.VMEM((grad_rows // 8, width), f32),
            pltpu.VMEM((grad_rows // 8, width), f32),
            pltpu.VMEM((grad_rows // 16, width), f32),
            pltpu.VMEM((grad_rows // 16, width), f32),
            pltpu.VMEM((chunks, planes - 1, CHUNK // 64, width), f32),
            pltpu.VMEM((chunks, planes - 1, CHUNK // 64, width), f32),
            pltpu.VMEM((6, group_size, 8, width), f32),
            pltpu.VMEM((6, dp_size, 8, width), f32),
            pltpu.SemaphoreType.DMA((3,)),
            pltpu.SemaphoreType.DMA((RING, 2)),
            pltpu.SemaphoreType.DMA((RING, copies)),
            pltpu.SemaphoreType.DMA((RING, copies)),
            pltpu.SemaphoreType.DMA((6, group_size - 1)),
            pltpu.SemaphoreType.DMA((6, group_size - 1)),
            pltpu.SemaphoreType.DMA((6, dp_size - 1)),
            pltpu.SemaphoreType.DMA((6, dp_size - 1)),
        ],
        compiler_params=pltpu.CompilerParams(
            collective_id=0, has_side_effects=True, vmem_limit_bytes=60 * 1024 * 1024
        ),
    )(
        fine_features,
        down_map.T,
        neighbours.T,
        voxel_counts,
        down_weight,
        mid_weight,
        out_weight,
        norm_gain,
        norm_bias,
        cotangent,
    )
    if not reduce_here:
        grads = lax.psum(grads, ("dp", "group"))
    middle, end = offsets * width, 2 * offsets * width
    grad_out = grads[:middle].reshape(out_weight.shape)
    grad_mid = grads[middle:end].reshape(mid_weight.shape)
    grad_down = grads[end:].reshape(down_weight.shape)
    return (features, fine_grad, grad_down, grad_mid, grad_out, gain_grad, bias_grad)


def solution(mesh):
    in_specs = (
        P(("dp", "group"), None),
        P(("dp", "group"), None),
        P(("dp", "group"), None),
        P(("dp", "group")),
        P(),
        P(),
        P(),
        P(),
        P(),
        P(("dp", "group"), None),
    )
    out_specs = (P(("dp", "group"), None), P(("dp", "group"), None), P(), P(), P(), P(), P())
    return jax.shard_map(
        functools.partial(per_device, mesh.shape["dp"], mesh.shape["group"]),
        mesh=mesh,
        in_specs=in_specs,
        out_specs=out_specs,
        check_vma=False,
    )
```

```python
import functools

import jax
import jax.numpy as jnp
from jax import lax
from jax.experimental import pallas as pl
from jax.experimental.pallas import tpu as pltpu
from jax.sharding import PartitionSpec as P

eps_norm = 1e-05
MESH = pl.DeviceIdType.MESH
GROUP = 3
BLOCK = 256
PAIR = 2
COPIES = 18
STAGES = 8
RING = 8


def sigmoid(value):
    return 1.0 / (1.0 + jnp.exp(-value))


def silu_slope(value):
    sigma = sigmoid(value)
    return sigma * (1.0 + value * (1.0 - sigma))


def dot(left, right):
    return jnp.dot(left, right, preferred_element_type=jnp.float32)


def dot_last(left, right):
    return lax.dot_general(
        left, right, (((1,), (1,)), ((), ())), preferred_element_type=jnp.float32
    )


def kernel(
    dp_size,
    group_size,
    reduce_here,
    fine_ref,
    down_rows_ref,
    nb_rows,
    count_ref,
    down_hbm,
    mid_hbm,
    out_hbm,
    gain_ref,
    bias_ref,
    cotangent_ref,
    features_ref,
    fine_grad_ref,
    grads_hbm,
    gain_grad_ref,
    bias_grad_ref,
    w_down,
    w_mid,
    w_out,
    spread_fine,
    cols_down,
    nb_cols,
    columns,
    act_one,
    act_one_b,
    act_two_b,
    hid_one,
    hid_two,
    hid_three,
    grad_hidden,
    pair_hidden,
    source_t,
    pair_source_t,
    grad_act,
    side,
    side_cols,
    nb_own,
    nb_pair,
    swap_out,
    swap_in,
    down_all,
    down_got,
    grads,
    from_core,
    from_first_a,
    from_first_b,
    from_second_a,
    from_second_b,
    from_line_a,
    from_line_b,
    near,
    far,
    load_sem,
    store_sem,
    sum_send,
    sum_recv,
    swap_send,
    swap_recv,
    near_send,
    near_recv,
    far_send,
    far_recv,
):
    rows, width = cotangent_ref.shape
    offsets = nb_rows.shape[0]
    fine_rows, in_width = fine_ref.shape
    children = fine_rows // rows
    down_offsets = down_rows_ref.shape[0]
    units = (offsets + 1) // 2 * (1 if reduce_here else 2)
    chunks = 2 * units + down_offsets * in_width // (2 * width)
    dp_me = lax.axis_index("dp")
    group_me = lax.axis_index("group")

    loads = [
        pltpu.make_async_copy(source, target, load_sem.at[at])
        for at, (source, target) in enumerate(
            (
                (down_hbm, w_down),
                (mid_hbm, w_mid.at[pl.ds(0, offsets)]),
                (out_hbm, w_out.at[pl.ds(0, offsets)]),
            )
        )
    ]
    for load in loads:
        load.start()

    barrier = pltpu.get_barrier_semaphore()
    for step in range(1, group_size):
        pl.semaphore_signal(
            barrier,
            inc=1,
            device_id={"group": lax.rem(group_me + step, group_size)},
            device_id_type=MESH,
        )
    for step in range(1, dp_size):
        pl.semaphore_signal(
            barrier,
            inc=1,
            device_id={"dp": lax.rem(dp_me + step, dp_size)},
            device_id_type=MESH,
        )
    pl.semaphore_wait(barrier, group_size + dp_size - 2)

    def share(at, axis, me, size, slots, send, recv):
        copies = []
        for step in range(1, size):
            copies.append(
                pltpu.make_async_remote_copy(
                    src_ref=slots.at[at, me],
                    dst_ref=slots.at[at, me],
                    send_sem=send.at[at, step - 1],
                    recv_sem=recv.at[at, step - 1],
                    device_id={axis: lax.rem(me + step, size)},
                    device_id_type=MESH,
                )
            )
        for copy in copies:
            copy.start()
        return copies

    def exchange(at, block, combine, meanwhile=(None, None)):
        near[at, group_me] = block
        copies = share(at, "group", group_me, group_size, near, near_send, near_recv)
        if meanwhile[0] is not None:
            meanwhile[0]()
        for copy in copies:
            copy.wait()
        far[at, dp_me] = combine([near[at, slot] for slot in range(group_size)])
        copies = share(at, "dp", dp_me, dp_size, far, far_send, far_recv)
        if meanwhile[1] is not None:
            meanwhile[1]()
        for copy in copies:
            copy.wait()
        return combine([far[at, slot] for slot in range(dp_size)])

    place = lax.broadcasted_iota(jnp.int32, (8, width), 0)

    def stack(first, second, third):
        return jnp.where(
            place == 0, first, jnp.where(place == 1, second, jnp.where(place == 2, third, 0.0))
        )

    def add_all(blocks):
        total = blocks[0]
        for block in blocks[1:]:
            total = total + block
        return total

    def merge_all(blocks):
        count = add_all([block[2:3] for block in blocks])
        center = add_all([block[2:3] * block[0:1] for block in blocks]) / count
        squares = add_all(
            [
                block[1:2] + block[2:3] * (block[0:1] - center) * (block[0:1] - center)
                for block in blocks
            ]
        )
        return stack(center, squares, count)

    count = count_ref[0]
    own_count = jnp.full((1, width), count.astype(jnp.float32))
    live = lax.broadcasted_iota(jnp.int32, (rows, width), 0) < count

    def norm_stats(at, hidden, meanwhile=(None, None)):
        center = jnp.sum(hidden, axis=0, keepdims=True) / own_count
        centered = jnp.where(live, hidden - center, 0.0)
        squares = jnp.sum(centered * centered, axis=0, keepdims=True)
        merged = exchange(at, stack(center, squares, own_count), merge_all, meanwhile)
        total = merged[2:3]
        scale = lax.rsqrt(merged[1:2] / total + eps_norm)
        return merged[0:1], scale, total

    def norm_grad(at, norm, incoming, normed, scale, total, meanwhile=(None, None)):
        shift_sum = jnp.sum(incoming, axis=0, keepdims=True)
        scale_sum = jnp.sum(incoming * normed, axis=0, keepdims=True)
        summed = exchange(
            at, stack(shift_sum, scale_sum, jnp.zeros_like(shift_sum)), add_all, meanwhile
        )
        bias_grad_ref[norm : norm + 1, :] = summed[0:1]
        gain_grad_ref[norm : norm + 1, :] = summed[1:2]
        hidden_grad = (
            scale
            * gain_ref[norm : norm + 1, :]
            * (incoming - summed[0:1] / total - normed * (summed[1:2] / total))
        )
        return jnp.where(live, hidden_grad, 0.0).astype(jnp.bfloat16)

    def pick(mask):
        return jnp.where(mask, jnp.bfloat16(1), jnp.bfloat16(0))

    def counting(shape, axis):
        return lax.broadcasted_iota(jnp.int32, shape, axis).astype(jnp.float32).astype(jnp.bfloat16)

    def convolve(source, weight, hidden):
        lanes = counting((BLOCK, BLOCK), 1)
        hidden[...] = jnp.zeros_like(hidden)

        def step(at, carry):
            for part in range(GROUP):
                k = at * GROUP + part
                for first in range(0, rows, BLOCK):
                    picker = jnp.concatenate(
                        [
                            pick(
                                jnp.concatenate(
                                    [nb_cols[block, k, first : first + BLOCK, :]] * (BLOCK // 128),
                                    axis=1,
                                )
                                == lanes
                            )
                            for block in range(rows // BLOCK)
                        ],
                        axis=1,
                    )
                    columns[first : first + BLOCK, part * width : (part + 1) * width] = dot(
                        picker, source[...]
                    ).astype(jnp.bfloat16)
            weights = weight[pl.ds(at * GROUP, GROUP)].reshape(GROUP * width, width)
            hidden[...] += dot(columns[...], weights)
            return carry

        lax.fori_loop(0, offsets // GROUP, step, 0)

    def spread_rows(neighbours, hidden_grad, first_offset):
        places = counting((BLOCK, rows), 0)
        for part in range(PAIR):
            wanted = neighbours[pl.ds(first_offset + part, 1), :].astype(jnp.float32)
            for first in range(0, rows, BLOCK):
                here = jnp.broadcast_to(wanted - first, (16, rows)).astype(jnp.bfloat16)
                picker = pick(jnp.concatenate([here] * (BLOCK // 16), axis=0) == places)
                columns[first : first + BLOCK, part * width : (part + 1) * width] = dot(
                    picker, hidden_grad[...]
                ).astype(jnp.bfloat16)
        return columns[:, : PAIR * width]

    def unit_rows(unit):
        return pl.ds(pl.multiple_of(unit * width, width), width)

    def convolve_back(weight, act_grad, first_unit, own_slot, other_slot):
        def step(first_offset, at, weigh):
            spread = spread_rows(nb_own, grad_hidden, first_offset)
            weights = jnp.concatenate(
                [weight[first_offset + part] for part in range(PAIR)], axis=1
            )
            act_grad[...] += dot_last(spread, weights)
            if weigh:
                product = dot(source_t[...], spread)
                for part in range(PAIR):
                    grads[unit_rows(first_unit + PAIR * at + part), :] = product[
                        :, part * width : (part + 1) * width
                    ]

        def own(at, carry):
            step(own_offset + PAIR * at, at, True)
            own_slot(at)
            return carry

        def other(at, carry):
            step(other_offset + PAIR * at, at, False)
            other_slot(at)
            return carry

        lax.fori_loop(0, units // PAIR, own, 0)
        if reduce_here:
            lax.fori_loop(0, units // PAIR, other, 0)

    def convolve_pair(first_unit, at_slot):
        def step(at, carry):
            spread = spread_rows(nb_pair, pair_hidden, own_offset + PAIR * at)
            product = dot(pair_source_t[...], spread)
            for part in range(PAIR):
                here = unit_rows(first_unit + PAIR * at + part)
                grads[here, :] = grads[here, :] + product[:, part * width : (part + 1) * width]
            at_slot(at)
            return carry

        lax.fori_loop(0, units // PAIR, step, 0)

    core, row = lax.rem(group_me, 2), group_me // 2
    column, plane = lax.rem(dp_me, 2), dp_me // 2
    pair, high = lax.rem(plane, 2), plane // 2
    planes = 4
    core_peer = {"group": group_me + 1 - 2 * core}
    row_peer = {"group": group_me + 2 - 4 * row}
    column_peer = {"dp": dp_me + 1 - 2 * column}
    pair_peer = {"dp": dp_me + 2 - 4 * pair}
    cross_peer = {"dp": dp_me + 4 - 8 * high}
    own_offset = units * pair if reduce_here else 0
    other_offset = units * (1 - pair)
    half, fourth, eighth, piece = width // 2, width // 8, width // 16, width // 32

    def keep_rows():
        own = half * core
        a, b = own + fourth * column, own + 2 * fourth + fourth * row
        aa, bb = a + eighth * row, b + eighth * column
        return own, (a, b), (aa, bb), (aa + piece * high, bb + piece * high)

    def give_rows():
        _, (a, b), (aa, bb), _ = keep_rows()
        return (
            half * (1 - core),
            (a + fourth * (1 - 2 * column), b + fourth * (1 - 2 * row)),
            (aa + eighth * (1 - 2 * row), bb + eighth * (1 - 2 * column)),
            (aa + piece * (1 - high), bb + piece * (1 - high)),
        )

    def at_rows(ref, c, first, count):
        start = pl.multiple_of(c * width + first, count)
        return ref.at[pl.ds(start, count), :]

    def landing(ref, c, count):
        return ref.at[pl.ds(pl.multiple_of(c * count, count), count), :]

    def place_of(c, first, count):
        return grads_hbm.at[:, c, pl.ds(pl.multiple_of(first, count), count), :]

    def send(c, number, source, target, peer):
        turn = lax.rem(c, RING)
        return pltpu.make_async_remote_copy(
            src_ref=source,
            dst_ref=target,
            send_sem=sum_send.at[turn, number],
            recv_sem=sum_recv.at[turn, number],
            device_id=peer,
            device_id_type=MESH,
        )

    def own_place(c, lane):
        first = keep_rows()[3][lane]
        return (
            at_rows(grads, c, first, piece),
            grads_hbm.at[pair, c, pl.ds(pl.multiple_of(first, piece), piece), :],
        )

    def copies_of(c, stage):
        keep, give = keep_rows(), give_rows()
        if stage == 0:
            target = landing(from_core, c, half)
            return [send(c, 0, at_rows(grads, c, give[0], half), target, core_peer)]
        if stage < 4:
            count = (fourth, eighth, piece)[stage - 1]
            targets = (
                (from_first_a, from_first_b),
                (from_second_a, from_second_b),
                (from_line_a, from_line_b),
            )[stage - 1]
            peers = (
                (column_peer, row_peer),
                (row_peer, column_peer),
                (cross_peer, cross_peer),
            )[stage - 1]
            return [
                send(
                    c,
                    2 * stage - 1 + lane,
                    at_rows(grads, c, give[stage][lane], count),
                    landing(targets[lane], c, count),
                    peers[lane],
                )
                for lane in range(2)
            ]
        if stage == 4:
            return [
                send(
                    c,
                    7 + (planes - 1) * lane + step - 1,
                    *own_place(c, lane),
                    {"dp": 2 * lax.rem(plane + step, planes) + column},
                )
                for lane in range(2)
                for step in range(1, planes)
            ]
        first = 7 + 2 * (planes - 1)
        if stage < 7:
            level, count = ((2, eighth), (1, fourth))[stage - 5]
            peers = ((row_peer, column_peer), (column_peer, row_peer))[stage - 5]
            blocks = [place_of(c, keep[level][lane], count) for lane in range(2)]
            return [
                send(c, first + 2 * (stage - 5) + lane, blocks[lane], blocks[lane], peers[lane])
                for lane in range(2)
            ]
        block = place_of(c, keep[0], half)
        return [send(c, first + 4, block, block, core_peer)]

    def store_of(c, lane):
        source, target = own_place(c, lane)
        return pltpu.make_async_copy(source, target, store_sem.at[lax.rem(c, RING), lane])

    def stage_of(c, stage):
        if stage > 0:
            for copy in copies_of(c, stage - 1):
                copy.wait()
        keep = keep_rows()
        if 1 <= stage <= 4:
            count = (half, fourth, eighth, piece)[stage - 1]
            firsts = ((keep[0],), *keep[1:])[stage - 1]
            landings = (
                (from_core,),
                (from_first_a, from_first_b),
                (from_second_a, from_second_b),
                (from_line_a, from_line_b),
            )[stage - 1]
            for first, landed in zip(firsts, landings):
                here = pl.ds(pl.multiple_of(c * width + first, count), count)
                there = pl.ds(pl.multiple_of(c * count, count), count)
                grads[here, :] = grads[here, :] + landed[there, :]
        for lane in range(2):
            if stage == 4:
                store_of(c, lane).start()
            if stage == 5:
                store_of(c, lane).wait()
        if stage < STAGES:
            for copy in copies_of(c, stage):
                copy.start()

    def slot(at):
        if not reduce_here:
            return
        for stage in range(STAGES + 1):
            c = at - stage

            @pl.when((c >= 0) & (c < chunks))
            def _():
                stage_of(c, stage)

    def slot_when(condition, at):
        @pl.when(condition)
        def _():
            slot(at)

    def no_slot(at):
        pass

    def swap(at, source, target):
        return pltpu.make_async_remote_copy(
            src_ref=source,
            dst_ref=target,
            send_sem=swap_send.at[at],
            recv_sem=swap_recv.at[at],
            device_id=pair_peer,
            device_id_type=MESH,
        )

    def swap_rows(at):
        return swap(at, swap_out.at[at], swap_in.at[at])

    def start_rows(at, value):
        if reduce_here:
            swap_out[at] = value.astype(jnp.float32)
            swap_rows(at).start()

    side[...] = jnp.zeros_like(side)
    side[:offsets, :] = nb_rows[...]
    side[offsets : offsets + down_offsets, :] = down_rows_ref[...]
    side_cols[...] = side[...].T
    nb_own[...] = jnp.full_like(nb_own, rows)
    nb_own[:offsets, :] = nb_rows[...]
    swap_neighbours = swap(4, nb_own, nb_pair)
    if reduce_here:
        swap_neighbours.start()
    for weight in (w_mid, w_out):
        weight[offsets:] = jnp.zeros_like(weight[offsets:])

    spread_fine[...] = fine_ref[...].astype(jnp.float32)
    for k in range(down_offsets):
        child = spread_fine[pl.ds(k % children, rows, stride=children), :]
        there = side_cols[:, offsets + k : offsets + k + 1] < fine_rows
        cols_down[:, k * in_width : (k + 1) * in_width] = jnp.where(there, child, 0.0).astype(
            jnp.bfloat16
        )
    loads[0].wait()
    hid_one[...] = dot(cols_down[...], w_down[...].reshape(down_offsets * in_width, width))

    def spread_neighbours():
        for k in range(offsets):
            wanted = jnp.broadcast_to(side_cols[:, k : k + 1], (rows, 128)).astype(jnp.float32)
            for block in range(rows // BLOCK):
                nb_cols[block, k] = (wanted - block * BLOCK).astype(jnp.bfloat16)

    center_one, scale_one, total = norm_stats(0, hid_one[...], (spread_neighbours, None))

    def pre_one():
        normed = (hid_one[...] - center_one) * scale_one
        return normed, normed * gain_ref[0:1, :] + bias_ref[0:1, :]

    _, pre = pre_one()
    act_one[...] = jnp.where(live, pre * sigmoid(pre), 0.0)
    act_one_b[...] = act_one[...].astype(jnp.bfloat16)
    start_rows(0, act_one_b[...])
    loads[1].wait()
    convolve(act_one_b, w_mid, hid_two)
    center_two, scale_two, _ = norm_stats(1, hid_two[...])

    def pre_two():
        normed = (hid_two[...] - center_two) * scale_two
        return normed, normed * gain_ref[1:2, :] + bias_ref[1:2, :]

    _, pre = pre_two()
    act_two_b[...] = jnp.where(live, pre * sigmoid(pre), 0.0).astype(jnp.bfloat16)
    start_rows(1, act_two_b[...])
    loads[2].wait()
    convolve(act_two_b, w_out, hid_three)
    center_three, scale_three, _ = norm_stats(2, hid_three[...])
    normed_three = (hid_three[...] - center_three) * scale_three
    summed = (
        jnp.where(live, normed_three * gain_ref[2:3, :] + bias_ref[2:3, :], 0.0) + act_one[...]
    )
    sigma = sigmoid(summed)
    features_ref[...] = jnp.where(live, summed * sigma, 0.0).astype(jnp.bfloat16)

    slope = sigma * (1.0 + summed * (1.0 - sigma))
    act_one[...] = jnp.where(live, cotangent_ref[...].astype(jnp.float32) * slope, 0.0)
    grad_hidden[...] = norm_grad(3, 2, act_one[...], normed_three, scale_three, total)
    start_rows(2, grad_hidden[...])
    grad_act[...] = jnp.zeros_like(grad_act)
    steps = units // PAIR

    def receive(source_at, hidden_at):
        swap_rows(source_at).wait()
        pair_source_t[...] = swap_in[source_at].astype(jnp.bfloat16).T
        swap_rows(hidden_at).wait()
        pair_hidden[...] = swap_in[hidden_at].astype(jnp.bfloat16)

    def slots_from(at):
        return (lambda: slot(at), lambda: slot(at + 1))

    source_t[...] = act_two_b[...].T
    convolve_back(w_out, grad_act, 0, no_slot, no_slot)
    if reduce_here:
        swap_neighbours.wait()
        receive(1, 2)
        convolve_pair(0, slot)
    normed, pre = pre_two()
    incoming = jnp.where(live, grad_act[...] * silu_slope(pre), 0.0)
    grad_hidden[...] = norm_grad(
        4, 1, incoming, normed, scale_two, total, slots_from(steps)
    )
    start_rows(3, grad_hidden[...])
    grad_act[...] = act_one[...]
    source_t[...] = act_one_b[...].T
    done = steps + 2
    convolve_back(
        w_mid,
        grad_act,
        units,
        lambda at: slot_when(lax.rem(at, 3) == 0, done + at // 3),
        lambda at: slot_when(lax.rem(at, 4) == 0, done + 3 + at // 4),
    )
    done = units
    if reduce_here:
        receive(0, 3)
        convolve_pair(units, lambda at: slot(done + at))
    done = units + steps
    normed, pre = pre_one()
    incoming = jnp.where(live, grad_act[...] * silu_slope(pre), 0.0)
    grad_hidden[...] = norm_grad(5, 0, incoming, normed, scale_one, total, slots_from(done))
    down_rows = down_offsets * in_width
    if reduce_here:
        down_all[...] = dot(cols_down[...].T, grad_hidden[...])
        kept = down_rows // 2
        swap_down = swap(
            5, down_all.at[pl.ds(pl.multiple_of(kept * (1 - pair), kept), kept), :], down_got
        )
        swap_down.start()
    else:
        grads[2 * units * width :, :] = dot(cols_down[...].T, grad_hidden[...])
    slot(done + 2)
    for child in range(children):
        total_child = jnp.zeros((rows, in_width), jnp.float32)
        for k in range(child, down_offsets, children):
            there = side_cols[:, offsets + k : offsets + k + 1] < fine_rows
            total_child += jnp.where(there, dot_last(grad_hidden[...], w_down[k]), 0.0)
        spread_fine[pl.ds(child, rows, stride=children), :] = total_child
    fine_grad_ref[...] = spread_fine[...].astype(jnp.bfloat16)

    if reduce_here:

        def rest(at, carry):
            slot(at)
            return carry

        lax.fori_loop(done + 3, 2 * units, rest, 0)
        swap_down.wait()
        grads[2 * units * width :, :] = (
            down_all[pl.ds(pl.multiple_of(kept * pair, kept), kept), :] + down_got[...]
        )
        lax.fori_loop(2 * units, chunks + STAGES, rest, 0)
    else:
        store = pltpu.make_async_copy(grads, grads_hbm, store_sem.at[0, 0])
        store.start()
        store.wait()


def place_kernel(
    features_ref,
    fine_grad_ref,
    grads_ref,
    gain_ref,
    bias_ref,
    features_out,
    fine_grad_out,
    grad_down_out,
    grad_mid_out,
    grad_out_out,
    gain_out,
    bias_out,
    sem,
):
    offsets, width = grad_mid_out.shape[:2]
    units = (offsets + 1) // 2
    moves = [(features_ref, features_out), (fine_grad_ref, fine_grad_out)]
    for at, target in enumerate((grad_out_out, grad_mid_out)):
        for pair in range(2):
            for first in range(0, units, (units + 1) // 2):
                count = min((units + 1) // 2, offsets - units * pair - first, units - first)
                moves.append(
                    (
                        grads_ref.at[pair, pl.ds(at * units + first, count)],
                        target.at[pl.ds(units * pair + first, count)],
                    )
                )
    down_units = grad_down_out.shape[0] // width // 2
    for pair in range(2):
        for at in range(down_units):
            moves.append(
                (
                    grads_ref.at[pair, 2 * units + at],
                    grad_down_out.at[pl.ds((pair * down_units + at) * width, width), :],
                )
            )
    copies = [
        pltpu.make_async_copy(source, target, sem.at[at])
        for at, (source, target) in enumerate(moves)
    ]
    for copy in copies:
        copy.start()
    gain_out[...] = gain_ref[...]
    bias_out[...] = bias_ref[...]
    for copy in copies:
        copy.wait()


def per_device(
    dp_size,
    group_size,
    fine_features,
    down_map,
    neighbours,
    voxel_counts,
    down_weight,
    mid_weight,
    out_weight,
    norm_gain,
    norm_bias,
    cotangent,
):
    rows, width = cotangent.shape
    fine_rows, in_width = fine_features.shape
    offsets = neighbours.shape[1]
    down_offsets = down_map.shape[1]
    f32, bf16, i32 = jnp.float32, jnp.bfloat16, jnp.int32
    vmem = pl.BlockSpec(memory_space=pltpu.VMEM)
    smem = pl.BlockSpec(memory_space=pltpu.SMEM)
    hbm = pl.BlockSpec(memory_space=pl.ANY)
    shape = jax.ShapeDtypeStruct
    reduce_here = dp_size == 8 and group_size == 4
    share = 2 if reduce_here else 1
    units = (offsets + 1) // 2 * 2 // share
    chunks = 2 * units + down_offsets * in_width // (share * width)
    grad_rows = chunks * width
    padded = (offsets + 1) // 2 * 2
    features, fine_grad, grads, gain_grad, bias_grad = pl.pallas_call(
        functools.partial(kernel, dp_size, group_size, reduce_here),
        out_shape=(
            shape((rows, width), bf16),
            shape((fine_rows, in_width), bf16),
            shape((share, chunks, width, width) if reduce_here else (grad_rows, width), f32),
            shape(norm_gain.shape, f32),
            shape(norm_bias.shape, f32),
        ),
        in_specs=[vmem, vmem, vmem, smem, hbm, hbm, hbm, vmem, vmem, vmem],
        out_specs=(vmem, vmem, hbm, vmem, vmem),
        scratch_shapes=[
            pltpu.VMEM(down_weight.shape, bf16),
            pltpu.VMEM((padded, width, width), bf16),
            pltpu.VMEM((padded, width, width), bf16),
            pltpu.VMEM((fine_rows, in_width), f32),
            pltpu.VMEM((rows, down_offsets * in_width), bf16),
            pltpu.VMEM((rows // BLOCK, offsets, rows, 128), bf16),
            pltpu.VMEM((rows, GROUP * width), bf16),
            pltpu.VMEM((rows, width), f32),
            pltpu.VMEM((rows, width), bf16),
            pltpu.VMEM((rows, width), bf16),
            pltpu.VMEM((rows, width), f32),
            pltpu.VMEM((rows, width), f32),
            pltpu.VMEM((rows, width), f32),
            pltpu.VMEM((rows, width), bf16),
            pltpu.VMEM((rows, width), bf16),
            pltpu.VMEM((width, rows), bf16),
            pltpu.VMEM((width, rows), bf16),
            pltpu.VMEM((rows, width), f32),
            pltpu.VMEM((128, rows), i32),
            pltpu.VMEM((rows, 128), i32),
            pltpu.VMEM((padded, rows), i32),
            pltpu.VMEM((padded, rows), i32),
            pltpu.VMEM((4, rows, width), f32),
            pltpu.VMEM((4, rows, width), f32),
            pltpu.VMEM((down_offsets * in_width, width), f32),
            pltpu.VMEM((down_offsets * in_width // 2, width), f32),
            pltpu.VMEM((grad_rows, width), f32),
            pltpu.VMEM((chunks * width // 2, width), f32),
            pltpu.VMEM((chunks * width // 8, width), f32),
            pltpu.VMEM((chunks * width // 8, width), f32),
            pltpu.VMEM((chunks * width // 16, width), f32),
            pltpu.VMEM((chunks * width // 16, width), f32),
            pltpu.VMEM((chunks * width // 32, width), f32),
            pltpu.VMEM((chunks * width // 32, width), f32),
            pltpu.VMEM((6, group_size, 8, width), f32),
            pltpu.VMEM((6, dp_size, 8, width), f32),
            pltpu.SemaphoreType.DMA((3,)),
            pltpu.SemaphoreType.DMA((RING, 2)),
            pltpu.SemaphoreType.DMA((RING, COPIES)),
            pltpu.SemaphoreType.DMA((RING, COPIES)),
            pltpu.SemaphoreType.DMA((6,)),
            pltpu.SemaphoreType.DMA((6,)),
            pltpu.SemaphoreType.DMA((6, group_size - 1)),
            pltpu.SemaphoreType.DMA((6, group_size - 1)),
            pltpu.SemaphoreType.DMA((6, dp_size - 1)),
            pltpu.SemaphoreType.DMA((6, dp_size - 1)),
        ],
        compiler_params=pltpu.CompilerParams(
            collective_id=0, has_side_effects=True, vmem_limit_bytes=60 * 1024 * 1024
        ),
    )(
        fine_features,
        down_map.T,
        neighbours.T,
        voxel_counts,
        down_weight,
        mid_weight,
        out_weight,
        norm_gain,
        norm_bias,
        cotangent,
    )
    if not reduce_here:
        grads = lax.psum(grads, ("dp", "group"))
        middle, end = offsets * width, 2 * padded * width
        grad_out = grads[:middle].reshape(out_weight.shape)
        grad_mid = grads[padded * width : padded * width + middle].reshape(mid_weight.shape)
        grad_down = grads[end:].reshape(down_weight.shape)
        return (features, fine_grad, grad_down, grad_mid, grad_out, gain_grad, bias_grad)
    features, fine_grad, grad_down, grad_mid, grad_out, gain_grad, bias_grad = pl.pallas_call(
        place_kernel,
        out_shape=(
            shape(features.shape, bf16),
            shape(fine_grad.shape, bf16),
            shape((down_offsets * in_width, width), f32),
            shape(mid_weight.shape, f32),
            shape(out_weight.shape, f32),
            shape(norm_gain.shape, f32),
            shape(norm_bias.shape, f32),
        ),
        in_specs=[hbm, hbm, hbm, vmem, vmem],
        out_specs=(hbm, hbm, hbm, hbm, hbm, vmem, vmem),
        scratch_shapes=[pltpu.SemaphoreType.DMA((16,))],
    )(features, fine_grad, grads, gain_grad, bias_grad)
    grad_down = grad_down.reshape(down_weight.shape)
    return (features, fine_grad, grad_down, grad_mid, grad_out, gain_grad, bias_grad)


def solution(mesh):
    in_specs = (
        P(("dp", "group"), None),
        P(("dp", "group"), None),
        P(("dp", "group"), None),
        P(("dp", "group")),
        P(),
        P(),
        P(),
        P(),
        P(),
        P(("dp", "group"), None),
    )
    out_specs = (P(("dp", "group"), None), P(("dp", "group"), None), P(), P(), P(), P(), P())
    return jax.shard_map(
        functools.partial(per_device, mesh.shape["dp"], mesh.shape["group"]),
        mesh=mesh,
        in_specs=in_specs,
        out_specs=out_specs,
        check_vma=False,
    )
```

```python
import functools

import jax
import jax.numpy as jnp
from jax import lax
from jax.experimental import pallas as pl
from jax.experimental.pallas import tpu as pltpu
from jax.sharding import PartitionSpec as P

eps_norm = 1e-05
MESH = pl.DeviceIdType.MESH
GROUP = 3
BLOCK = 256
PAIR = 2
COPIES = 18
STAGES = 8
RING = 8


def sigmoid(value):
    return 1.0 / (1.0 + jnp.exp(-value))


def silu_slope(value):
    sigma = sigmoid(value)
    return sigma * (1.0 + value * (1.0 - sigma))


def dot(left, right):
    return jnp.dot(left, right, preferred_element_type=jnp.float32)


def dot_last(left, right):
    return lax.dot_general(
        left, right, (((1,), (1,)), ((), ())), preferred_element_type=jnp.float32
    )


def kernel(
    dp_size,
    group_size,
    reduce_here,
    fine_ref,
    down_rows_ref,
    nb_rows,
    count_ref,
    down_hbm,
    mid_hbm,
    out_hbm,
    gain_ref,
    bias_ref,
    cotangent_ref,
    features_ref,
    fine_grad_ref,
    grads_hbm,
    gain_grad_ref,
    bias_grad_ref,
    w_down,
    w_mid,
    w_out,
    spread_fine,
    cols_down,
    nb_cols,
    columns,
    act_one,
    act_one_b,
    act_two_b,
    hid_one,
    hid_two,
    hid_three,
    grad_hidden,
    pair_hidden,
    source_t,
    pair_source_t,
    grad_act,
    side,
    side_cols,
    nb_own,
    nb_pair,
    swap_out,
    swap_in,
    down_all,
    down_got,
    grads,
    results,
    from_core,
    from_first_a,
    from_first_b,
    from_second_a,
    from_second_b,
    from_line_a,
    from_line_b,
    near,
    far,
    load_sem,
    store_sem,
    sum_send,
    sum_recv,
    swap_send,
    swap_recv,
    near_send,
    near_recv,
    far_send,
    far_recv,
):
    rows, width = cotangent_ref.shape
    offsets = nb_rows.shape[0]
    fine_rows, in_width = fine_ref.shape
    children = fine_rows // rows
    down_offsets = down_rows_ref.shape[0]
    units = (offsets + 1) // 2 * (1 if reduce_here else 2)
    chunks = 2 * units + down_offsets * in_width // (2 * width)
    dp_me = lax.axis_index("dp")
    group_me = lax.axis_index("group")

    loads = [
        pltpu.make_async_copy(source, target, load_sem.at[at])
        for at, (source, target) in enumerate(
            (
                (down_hbm, w_down),
                (mid_hbm, w_mid.at[pl.ds(0, offsets)]),
                (out_hbm, w_out.at[pl.ds(0, offsets)]),
            )
        )
    ]
    for load in loads:
        load.start()

    barrier = pltpu.get_barrier_semaphore()
    for step in range(1, group_size):
        pl.semaphore_signal(
            barrier,
            inc=1,
            device_id={"group": lax.rem(group_me + step, group_size)},
            device_id_type=MESH,
        )
    for step in range(1, dp_size):
        pl.semaphore_signal(
            barrier,
            inc=1,
            device_id={"dp": lax.rem(dp_me + step, dp_size)},
            device_id_type=MESH,
        )
    pl.semaphore_wait(barrier, group_size + dp_size - 2)

    def share(at, axis, me, size, slots, send, recv):
        copies = []
        for step in range(1, size):
            copies.append(
                pltpu.make_async_remote_copy(
                    src_ref=slots.at[at, me],
                    dst_ref=slots.at[at, me],
                    send_sem=send.at[at, step - 1],
                    recv_sem=recv.at[at, step - 1],
                    device_id={axis: lax.rem(me + step, size)},
                    device_id_type=MESH,
                )
            )
        for copy in copies:
            copy.start()
        return copies

    def exchange(at, block, combine, meanwhile=(None, None)):
        near[at, group_me] = block
        copies = share(at, "group", group_me, group_size, near, near_send, near_recv)
        if meanwhile[0] is not None:
            meanwhile[0]()
        for copy in copies:
            copy.wait()
        far[at, dp_me] = combine([near[at, slot] for slot in range(group_size)])
        copies = share(at, "dp", dp_me, dp_size, far, far_send, far_recv)
        if meanwhile[1] is not None:
            meanwhile[1]()
        for copy in copies:
            copy.wait()
        return combine([far[at, slot] for slot in range(dp_size)])

    place = lax.broadcasted_iota(jnp.int32, (8, width), 0)

    def stack(first, second, third):
        return jnp.where(
            place == 0, first, jnp.where(place == 1, second, jnp.where(place == 2, third, 0.0))
        )

    def add_all(blocks):
        total = blocks[0]
        for block in blocks[1:]:
            total = total + block
        return total

    def merge_all(blocks):
        count = add_all([block[2:3] for block in blocks])
        center = add_all([block[2:3] * block[0:1] for block in blocks]) / count
        squares = add_all(
            [
                block[1:2] + block[2:3] * (block[0:1] - center) * (block[0:1] - center)
                for block in blocks
            ]
        )
        return stack(center, squares, count)

    count = count_ref[0]
    own_count = jnp.full((1, width), count.astype(jnp.float32))
    live = lax.broadcasted_iota(jnp.int32, (rows, width), 0) < count

    def norm_stats(at, hidden, meanwhile=(None, None)):
        center = jnp.sum(hidden, axis=0, keepdims=True) / own_count
        centered = jnp.where(live, hidden - center, 0.0)
        squares = jnp.sum(centered * centered, axis=0, keepdims=True)
        merged = exchange(at, stack(center, squares, own_count), merge_all, meanwhile)
        total = merged[2:3]
        scale = lax.rsqrt(merged[1:2] / total + eps_norm)
        return merged[0:1], scale, total

    def norm_grad(at, norm, incoming, normed, scale, total, meanwhile=(None, None)):
        shift_sum = jnp.sum(incoming, axis=0, keepdims=True)
        scale_sum = jnp.sum(incoming * normed, axis=0, keepdims=True)
        summed = exchange(
            at, stack(shift_sum, scale_sum, jnp.zeros_like(shift_sum)), add_all, meanwhile
        )
        bias_grad_ref[norm : norm + 1, :] = summed[0:1]
        gain_grad_ref[norm : norm + 1, :] = summed[1:2]
        hidden_grad = (
            scale
            * gain_ref[norm : norm + 1, :]
            * (incoming - summed[0:1] / total - normed * (summed[1:2] / total))
        )
        return jnp.where(live, hidden_grad, 0.0).astype(jnp.bfloat16)

    def pick(mask):
        return jnp.where(mask, jnp.bfloat16(1), jnp.bfloat16(0))

    def counting(shape, axis):
        return lax.broadcasted_iota(jnp.int32, shape, axis).astype(jnp.float32).astype(jnp.bfloat16)

    def convolve(source, weight, hidden):
        lanes = counting((BLOCK, BLOCK), 1)
        hidden[...] = jnp.zeros_like(hidden)

        def step(at, carry):
            for part in range(GROUP):
                k = at * GROUP + part
                for first in range(0, rows, BLOCK):
                    picker = jnp.concatenate(
                        [
                            pick(
                                jnp.concatenate(
                                    [nb_cols[block, k, first : first + BLOCK, :]] * (BLOCK // 128),
                                    axis=1,
                                )
                                == lanes
                            )
                            for block in range(rows // BLOCK)
                        ],
                        axis=1,
                    )
                    columns[first : first + BLOCK, part * width : (part + 1) * width] = dot(
                        picker, source[...]
                    ).astype(jnp.bfloat16)
            weights = weight[pl.ds(at * GROUP, GROUP)].reshape(GROUP * width, width)
            hidden[...] += dot(columns[...], weights)
            return carry

        lax.fori_loop(0, offsets // GROUP, step, 0)

    def spread_rows(neighbours, hidden_grad, first_offset):
        places = counting((BLOCK, rows), 0)
        for part in range(PAIR):
            wanted = neighbours[pl.ds(first_offset + part, 1), :].astype(jnp.float32)
            for first in range(0, rows, BLOCK):
                here = jnp.broadcast_to(wanted - first, (16, rows)).astype(jnp.bfloat16)
                picker = pick(jnp.concatenate([here] * (BLOCK // 16), axis=0) == places)
                columns[first : first + BLOCK, part * width : (part + 1) * width] = dot(
                    picker, hidden_grad[...]
                ).astype(jnp.bfloat16)
        return columns[:, : PAIR * width]

    def unit_rows(unit):
        return pl.ds(pl.multiple_of(unit * width, width), width)

    def convolve_back(weight, act_grad, first_unit, own_slot, other_slot):
        def step(first_offset, at, weigh):
            spread = spread_rows(nb_own, grad_hidden, first_offset)
            weights = jnp.concatenate(
                [weight[first_offset + part] for part in range(PAIR)], axis=1
            )
            act_grad[...] += dot_last(spread, weights)
            if weigh:
                product = dot(source_t[...], spread)
                for part in range(PAIR):
                    grads[unit_rows(first_unit + PAIR * at + part), :] = product[
                        :, part * width : (part + 1) * width
                    ]

        def own(at, carry):
            step(own_offset + PAIR * at, at, True)
            own_slot(at)
            return carry

        def other(at, carry):
            step(other_offset + PAIR * at, at, False)
            other_slot(at)
            return carry

        lax.fori_loop(0, units // PAIR, own, 0)
        if reduce_here:
            lax.fori_loop(0, units // PAIR, other, 0)

    def convolve_pair(first_unit, at_slot):
        def step(at, carry):
            spread = spread_rows(nb_pair, pair_hidden, own_offset + PAIR * at)
            product = dot(pair_source_t[...], spread)
            for part in range(PAIR):
                here = unit_rows(first_unit + PAIR * at + part)
                grads[here, :] = grads[here, :] + product[:, part * width : (part + 1) * width]
            at_slot(at)
            return carry

        lax.fori_loop(0, units // PAIR, step, 0)

    core, row = lax.rem(group_me, 2), group_me // 2
    column, plane = lax.rem(dp_me, 2), dp_me // 2
    pair, high = lax.rem(plane, 2), plane // 2
    planes = 4
    core_peer = {"group": group_me + 1 - 2 * core}
    row_peer = {"group": group_me + 2 - 4 * row}
    column_peer = {"dp": dp_me + 1 - 2 * column}
    pair_peer = {"dp": dp_me + 2 - 4 * pair}
    cross_peer = {"dp": dp_me + 4 - 8 * high}
    own_offset = units * pair if reduce_here else 0
    other_offset = units * (1 - pair)
    half, fourth, eighth, piece = width // 2, width // 8, width // 16, width // 32

    def keep_rows():
        own = half * core
        a, b = own + fourth * column, own + 2 * fourth + fourth * row
        aa, bb = a + eighth * row, b + eighth * column
        return own, (a, b), (aa, bb), (aa + piece * high, bb + piece * high)

    def give_rows():
        _, (a, b), (aa, bb), _ = keep_rows()
        return (
            half * (1 - core),
            (a + fourth * (1 - 2 * column), b + fourth * (1 - 2 * row)),
            (aa + eighth * (1 - 2 * row), bb + eighth * (1 - 2 * column)),
            (aa + piece * (1 - high), bb + piece * (1 - high)),
        )

    def at_rows(ref, c, first, count):
        start = pl.multiple_of(c * width + first, count)
        return ref.at[pl.ds(start, count), :]

    def landing(ref, c, count):
        return ref.at[pl.ds(pl.multiple_of(c * count, count), count), :]

    def place_of(c, first, count):
        return results.at[:, c, pl.ds(pl.multiple_of(first, count), count), :]

    def send(c, number, source, target, peer):
        turn = lax.rem(c, RING)
        return pltpu.make_async_remote_copy(
            src_ref=source,
            dst_ref=target,
            send_sem=sum_send.at[turn, number],
            recv_sem=sum_recv.at[turn, number],
            device_id=peer,
            device_id_type=MESH,
        )

    def own_place(c, lane):
        first = keep_rows()[3][lane]
        return (
            at_rows(grads, c, first, piece),
            results.at[pair, c, pl.ds(pl.multiple_of(first, piece), piece), :],
        )

    def copies_of(c, stage):
        keep, give = keep_rows(), give_rows()
        if stage == 0:
            target = landing(from_core, lax.rem(c, RING), half)
            return [send(c, 0, at_rows(grads, c, give[0], half), target, core_peer)]
        if stage < 4:
            count = (fourth, eighth, piece)[stage - 1]
            targets = (
                (from_first_a, from_first_b),
                (from_second_a, from_second_b),
                (from_line_a, from_line_b),
            )[stage - 1]
            peers = (
                (column_peer, row_peer),
                (row_peer, column_peer),
                (cross_peer, cross_peer),
            )[stage - 1]
            return [
                send(
                    c,
                    2 * stage - 1 + lane,
                    at_rows(grads, c, give[stage][lane], count),
                    landing(targets[lane], c, count),
                    peers[lane],
                )
                for lane in range(2)
            ]
        if stage == 4:
            return [
                send(
                    c,
                    7 + (planes - 1) * lane + step - 1,
                    *own_place(c, lane),
                    {"dp": 2 * lax.rem(plane + step, planes) + column},
                )
                for lane in range(2)
                for step in range(1, planes)
            ]
        first = 7 + 2 * (planes - 1)
        if stage < 7:
            level, count = ((2, eighth), (1, fourth))[stage - 5]
            peers = ((row_peer, column_peer), (column_peer, row_peer))[stage - 5]
            blocks = [place_of(c, keep[level][lane], count) for lane in range(2)]
            return [
                send(c, first + 2 * (stage - 5) + lane, blocks[lane], blocks[lane], peers[lane])
                for lane in range(2)
            ]
        block = place_of(c, keep[0], half)
        return [send(c, first + 4, block, block, core_peer)]

    def store_of(c):
        return pltpu.make_async_copy(results.at[:, c], grads_hbm.at[:, c], store_sem.at[c])

    def stage_of(c, stage):
        if stage > 0:
            for copy in copies_of(c, stage - 1):
                copy.wait()
        keep = keep_rows()
        if 1 <= stage <= 4:
            count = (half, fourth, eighth, piece)[stage - 1]
            firsts = ((keep[0],), *keep[1:])[stage - 1]
            landings = (
                (from_core,),
                (from_first_a, from_first_b),
                (from_second_a, from_second_b),
                (from_line_a, from_line_b),
            )[stage - 1]
            turn = lax.rem(c, RING) if stage == 1 else c
            for first, landed in zip(firsts, landings):
                here = pl.ds(pl.multiple_of(c * width + first, count), count)
                there = pl.ds(pl.multiple_of(turn * count, count), count)
                grads[here, :] = grads[here, :] + landed[there, :]
        if stage == 4:
            for lane in range(2):
                first = pl.ds(pl.multiple_of(keep[3][lane], piece), piece)
                here = pl.ds(pl.multiple_of(c * width + keep[3][lane], piece), piece)
                results[pair, c, first, :] = grads[here, :]
        if stage == STAGES:
            store_of(c).start()
        else:
            for copy in copies_of(c, stage):
                copy.start()

    def slot(at):
        if not reduce_here:
            return
        for stage in range(STAGES + 1):
            c = at - stage

            @pl.when((c >= 0) & (c < chunks))
            def _():
                stage_of(c, stage)

    def slot_when(condition, at):
        @pl.when(condition)
        def _():
            slot(at)

    def no_slot(at):
        pass

    def swap(at, source, target):
        return pltpu.make_async_remote_copy(
            src_ref=source,
            dst_ref=target,
            send_sem=swap_send.at[at],
            recv_sem=swap_recv.at[at],
            device_id=pair_peer,
            device_id_type=MESH,
        )

    def swap_rows(at):
        return swap(at, swap_out.at[at], swap_in.at[at])

    def start_rows(at, value):
        if reduce_here:
            swap_out[at] = value.astype(jnp.float32)
            swap_rows(at).start()

    side[...] = jnp.zeros_like(side)
    side[:offsets, :] = nb_rows[...]
    side[offsets : offsets + down_offsets, :] = down_rows_ref[...]
    side_cols[...] = side[...].T
    nb_own[...] = jnp.full_like(nb_own, rows)
    nb_own[:offsets, :] = nb_rows[...]
    swap_neighbours = swap(4, nb_own, nb_pair)
    if reduce_here:
        swap_neighbours.start()
    for weight in (w_mid, w_out):
        weight[offsets:] = jnp.zeros_like(weight[offsets:])

    spread_fine[...] = fine_ref[...].astype(jnp.float32)
    for k in range(down_offsets):
        child = spread_fine[pl.ds(k % children, rows, stride=children), :]
        there = side_cols[:, offsets + k : offsets + k + 1] < fine_rows
        cols_down[:, k * in_width : (k + 1) * in_width] = jnp.where(there, child, 0.0).astype(
            jnp.bfloat16
        )
    loads[0].wait()
    hid_one[...] = dot(cols_down[...], w_down[...].reshape(down_offsets * in_width, width))

    def spread_neighbours():
        for k in range(offsets):
            wanted = jnp.broadcast_to(side_cols[:, k : k + 1], (rows, 128)).astype(jnp.float32)
            for block in range(rows // BLOCK):
                nb_cols[block, k] = (wanted - block * BLOCK).astype(jnp.bfloat16)

    center_one, scale_one, total = norm_stats(0, hid_one[...], (spread_neighbours, None))

    def pre_one():
        normed = (hid_one[...] - center_one) * scale_one
        return normed, normed * gain_ref[0:1, :] + bias_ref[0:1, :]

    _, pre = pre_one()
    act_one[...] = jnp.where(live, pre * sigmoid(pre), 0.0)
    act_one_b[...] = act_one[...].astype(jnp.bfloat16)
    start_rows(0, act_one_b[...])
    loads[1].wait()
    convolve(act_one_b, w_mid, hid_two)
    center_two, scale_two, _ = norm_stats(1, hid_two[...])

    def pre_two():
        normed = (hid_two[...] - center_two) * scale_two
        return normed, normed * gain_ref[1:2, :] + bias_ref[1:2, :]

    _, pre = pre_two()
    act_two_b[...] = jnp.where(live, pre * sigmoid(pre), 0.0).astype(jnp.bfloat16)
    start_rows(1, act_two_b[...])
    loads[2].wait()
    convolve(act_two_b, w_out, hid_three)
    center_three, scale_three, _ = norm_stats(2, hid_three[...])
    normed_three = (hid_three[...] - center_three) * scale_three
    summed = (
        jnp.where(live, normed_three * gain_ref[2:3, :] + bias_ref[2:3, :], 0.0) + act_one[...]
    )
    sigma = sigmoid(summed)
    features_ref[...] = jnp.where(live, summed * sigma, 0.0).astype(jnp.bfloat16)

    slope = sigma * (1.0 + summed * (1.0 - sigma))
    act_one[...] = jnp.where(live, cotangent_ref[...].astype(jnp.float32) * slope, 0.0)
    grad_hidden[...] = norm_grad(3, 2, act_one[...], normed_three, scale_three, total)
    start_rows(2, grad_hidden[...])
    grad_act[...] = jnp.zeros_like(grad_act)
    steps = units // PAIR

    def receive(source_at, hidden_at):
        swap_rows(source_at).wait()
        pair_source_t[...] = swap_in[source_at].astype(jnp.bfloat16).T
        swap_rows(hidden_at).wait()
        pair_hidden[...] = swap_in[hidden_at].astype(jnp.bfloat16)

    def slots_from(at):
        return (lambda: slot(at), lambda: slot(at + 1))

    source_t[...] = act_two_b[...].T
    convolve_back(w_out, grad_act, 0, no_slot, no_slot)
    if reduce_here:
        swap_neighbours.wait()
        receive(1, 2)
        convolve_pair(0, slot)
    normed, pre = pre_two()
    incoming = jnp.where(live, grad_act[...] * silu_slope(pre), 0.0)
    grad_hidden[...] = norm_grad(
        4, 1, incoming, normed, scale_two, total, slots_from(steps)
    )
    start_rows(3, grad_hidden[...])
    grad_act[...] = act_one[...]
    source_t[...] = act_one_b[...].T
    done = steps + 2
    convolve_back(
        w_mid,
        grad_act,
        units,
        lambda at: slot_when(lax.rem(at, 3) == 0, done + at // 3),
        lambda at: slot_when(lax.rem(at, 4) == 0, done + 3 + at // 4),
    )
    done = units
    if reduce_here:
        receive(0, 3)
        convolve_pair(units, lambda at: slot(done + at))
    done = units + steps
    normed, pre = pre_one()
    incoming = jnp.where(live, grad_act[...] * silu_slope(pre), 0.0)
    grad_hidden[...] = norm_grad(5, 0, incoming, normed, scale_one, total, slots_from(done))
    down_rows = down_offsets * in_width
    if reduce_here:
        down_all[...] = dot(cols_down[...].T, grad_hidden[...])
        kept = down_rows // 2
        swap_down = swap(
            5, down_all.at[pl.ds(pl.multiple_of(kept * (1 - pair), kept), kept), :], down_got
        )
        swap_down.start()
    else:
        grads[2 * units * width :, :] = dot(cols_down[...].T, grad_hidden[...])
    slot(done + 2)
    for child in range(children):
        total_child = jnp.zeros((rows, in_width), jnp.float32)
        for k in range(child, down_offsets, children):
            there = side_cols[:, offsets + k : offsets + k + 1] < fine_rows
            total_child += jnp.where(there, dot_last(grad_hidden[...], w_down[k]), 0.0)
        spread_fine[pl.ds(child, rows, stride=children), :] = total_child
    fine_grad_ref[...] = spread_fine[...].astype(jnp.bfloat16)

    if reduce_here:

        def rest(at, carry):
            slot(at)
            return carry

        lax.fori_loop(done + 3, 2 * units, rest, 0)
        swap_down.wait()
        grads[2 * units * width :, :] = (
            down_all[pl.ds(pl.multiple_of(kept * pair, kept), kept), :] + down_got[...]
        )
        lax.fori_loop(2 * units, chunks + STAGES, rest, 0)

        def finish(c, carry):
            store_of(c).wait()
            return carry

        lax.fori_loop(0, chunks, finish, 0)
    else:
        store = pltpu.make_async_copy(grads, grads_hbm, store_sem.at[0])
        store.start()
        store.wait()


def place_kernel(
    features_ref,
    fine_grad_ref,
    grads_ref,
    gain_ref,
    bias_ref,
    features_out,
    fine_grad_out,
    grad_down_out,
    grad_mid_out,
    grad_out_out,
    gain_out,
    bias_out,
    held,
    load_sem,
    store_sem,
):
    offsets, width = grad_mid_out.shape[:2]
    units = (offsets + 1) // 2
    piece = (units + 1) // 2
    moves = []
    for pair in range(2):
        for at, target in enumerate((grad_out_out, grad_mid_out)):
            for first in range(0, units, piece):
                count = min(piece, offsets - units * pair - first, units - first)
                here = (pair, pl.ds(at * units + first, count))
                moves.append((here, target.at[pl.ds(units * pair + first, count)]))
        down_units = grad_down_out.shape[0] // 2
        here = (pair, pl.ds(2 * units, down_units))
        moves.append((here, grad_down_out.at[pl.ds(pair * down_units, down_units)]))
    loads = [
        pltpu.make_async_copy(grads_ref.at[here], held.at[here], load_sem.at[at])
        for at, (here, _) in enumerate(moves)
    ]
    stores = [
        pltpu.make_async_copy(held.at[here], target, store_sem.at[at])
        for at, (here, target) in enumerate(moves)
    ]
    for load in loads:
        load.start()
    features_out[...] = features_ref[...]
    fine_grad_out[...] = fine_grad_ref[...]
    gain_out[...] = gain_ref[...]
    bias_out[...] = bias_ref[...]
    for load, store in zip(loads, stores):
        load.wait()
        store.start()
    for store in stores:
        store.wait()


def per_device(
    dp_size,
    group_size,
    fine_features,
    down_map,
    neighbours,
    voxel_counts,
    down_weight,
    mid_weight,
    out_weight,
    norm_gain,
    norm_bias,
    cotangent,
):
    rows, width = cotangent.shape
    fine_rows, in_width = fine_features.shape
    offsets = neighbours.shape[1]
    down_offsets = down_map.shape[1]
    f32, bf16, i32 = jnp.float32, jnp.bfloat16, jnp.int32
    vmem = pl.BlockSpec(memory_space=pltpu.VMEM)
    smem = pl.BlockSpec(memory_space=pltpu.SMEM)
    hbm = pl.BlockSpec(memory_space=pl.ANY)
    shape = jax.ShapeDtypeStruct
    reduce_here = dp_size == 8 and group_size == 4
    share = 2 if reduce_here else 1
    units = (offsets + 1) // 2 * 2 // share
    chunks = 2 * units + down_offsets * in_width // (share * width)
    grad_rows = chunks * width
    padded = (offsets + 1) // 2 * 2
    features, fine_grad, grads, gain_grad, bias_grad = pl.pallas_call(
        functools.partial(kernel, dp_size, group_size, reduce_here),
        out_shape=(
            shape((rows, width), bf16),
            shape((fine_rows, in_width), bf16),
            shape((share, chunks, width, width) if reduce_here else (grad_rows, width), f32),
            shape(norm_gain.shape, f32),
            shape(norm_bias.shape, f32),
        ),
        in_specs=[vmem, vmem, vmem, smem, hbm, hbm, hbm, vmem, vmem, vmem],
        out_specs=(vmem, vmem, hbm, vmem, vmem),
        scratch_shapes=[
            pltpu.VMEM(down_weight.shape, bf16),
            pltpu.VMEM((padded, width, width), bf16),
            pltpu.VMEM((padded, width, width), bf16),
            pltpu.VMEM((fine_rows, in_width), f32),
            pltpu.VMEM((rows, down_offsets * in_width), bf16),
            pltpu.VMEM((rows // BLOCK, offsets, rows, 128), bf16),
            pltpu.VMEM((rows, GROUP * width), bf16),
            pltpu.VMEM((rows, width), f32),
            pltpu.VMEM((rows, width), bf16),
            pltpu.VMEM((rows, width), bf16),
            pltpu.VMEM((rows, width), f32),
            pltpu.VMEM((rows, width), f32),
            pltpu.VMEM((rows, width), f32),
            pltpu.VMEM((rows, width), bf16),
            pltpu.VMEM((rows, width), bf16),
            pltpu.VMEM((width, rows), bf16),
            pltpu.VMEM((width, rows), bf16),
            pltpu.VMEM((rows, width), f32),
            pltpu.VMEM((128, rows), i32),
            pltpu.VMEM((rows, 128), i32),
            pltpu.VMEM((padded, rows), i32),
            pltpu.VMEM((padded, rows), i32),
            pltpu.VMEM((4, rows, width), f32),
            pltpu.VMEM((4, rows, width), f32),
            pltpu.VMEM((down_offsets * in_width, width), f32),
            pltpu.VMEM((down_offsets * in_width // 2, width), f32),
            pltpu.VMEM((grad_rows, width), f32),
            pltpu.VMEM((2, chunks if reduce_here else 1, width, width), f32),
            pltpu.VMEM((RING * width // 2, width), f32),
            pltpu.VMEM((chunks * width // 8, width), f32),
            pltpu.VMEM((chunks * width // 8, width), f32),
            pltpu.VMEM((chunks * width // 16, width), f32),
            pltpu.VMEM((chunks * width // 16, width), f32),
            pltpu.VMEM((chunks * width // 32, width), f32),
            pltpu.VMEM((chunks * width // 32, width), f32),
            pltpu.VMEM((6, group_size, 8, width), f32),
            pltpu.VMEM((6, dp_size, 8, width), f32),
            pltpu.SemaphoreType.DMA((3,)),
            pltpu.SemaphoreType.DMA((chunks,)),
            pltpu.SemaphoreType.DMA((RING, COPIES)),
            pltpu.SemaphoreType.DMA((RING, COPIES)),
            pltpu.SemaphoreType.DMA((6,)),
            pltpu.SemaphoreType.DMA((6,)),
            pltpu.SemaphoreType.DMA((6, group_size - 1)),
            pltpu.SemaphoreType.DMA((6, group_size - 1)),
            pltpu.SemaphoreType.DMA((6, dp_size - 1)),
            pltpu.SemaphoreType.DMA((6, dp_size - 1)),
        ],
        compiler_params=pltpu.CompilerParams(
            collective_id=0, has_side_effects=True, vmem_limit_bytes=60 * 1024 * 1024
        ),
    )(
        fine_features,
        down_map.T,
        neighbours.T,
        voxel_counts,
        down_weight,
        mid_weight,
        out_weight,
        norm_gain,
        norm_bias,
        cotangent,
    )
    if not reduce_here:
        grads = lax.psum(grads, ("dp", "group"))
        middle, end = offsets * width, 2 * padded * width
        grad_out = grads[:middle].reshape(out_weight.shape)
        grad_mid = grads[padded * width : padded * width + middle].reshape(mid_weight.shape)
        grad_down = grads[end:].reshape(down_weight.shape)
        return (features, fine_grad, grad_down, grad_mid, grad_out, gain_grad, bias_grad)
    features, fine_grad, grad_down, grad_mid, grad_out, gain_grad, bias_grad = pl.pallas_call(
        place_kernel,
        out_shape=(
            shape(features.shape, bf16),
            shape(fine_grad.shape, bf16),
            shape((down_offsets * in_width // width, width, width), f32),
            shape(mid_weight.shape, f32),
            shape(out_weight.shape, f32),
            shape(norm_gain.shape, f32),
            shape(norm_bias.shape, f32),
        ),
        in_specs=[vmem, vmem, hbm, vmem, vmem],
        out_specs=(vmem, vmem, hbm, hbm, hbm, vmem, vmem),
        scratch_shapes=[
            pltpu.VMEM(grads.shape, f32),
            pltpu.SemaphoreType.DMA((10,)),
            pltpu.SemaphoreType.DMA((10,)),
        ],
        compiler_params=pltpu.CompilerParams(vmem_limit_bytes=32 * 1024 * 1024),
    )(features, fine_grad, grads, gain_grad, bias_grad)
    grad_down = grad_down.reshape(down_weight.shape)
    return (features, fine_grad, grad_down, grad_mid, grad_out, gain_grad, bias_grad)


def solution(mesh):
    in_specs = (
        P(("dp", "group"), None),
        P(("dp", "group"), None),
        P(("dp", "group"), None),
        P(("dp", "group")),
        P(),
        P(),
        P(),
        P(),
        P(),
        P(("dp", "group"), None),
    )
    out_specs = (P(("dp", "group"), None), P(("dp", "group"), None), P(), P(), P(), P(), P())
    return jax.shard_map(
        functools.partial(per_device, mesh.shape["dp"], mesh.shape["group"]),
        mesh=mesh,
        in_specs=in_specs,
        out_specs=out_specs,
        check_vma=False,
    )
```

```python
import functools

import jax
import jax.numpy as jnp
from jax import lax
from jax.experimental import pallas as pl
from jax.experimental.pallas import tpu as pltpu
from jax.sharding import PartitionSpec as P

eps_norm = 1e-05
MESH = pl.DeviceIdType.MESH
GROUP = 3
BLOCK = 256
PAIR = 2
COPIES = 18
STAGES = 8
RING = 8


def sigmoid(value):
    return 1.0 / (1.0 + jnp.exp(-value))


def silu_slope(value):
    sigma = sigmoid(value)
    return sigma * (1.0 + value * (1.0 - sigma))


def dot(left, right):
    return jnp.dot(left, right, preferred_element_type=jnp.float32)


def dot_last(left, right):
    return lax.dot_general(
        left, right, (((1,), (1,)), ((), ())), preferred_element_type=jnp.float32
    )


def kernel(
    dp_size,
    group_size,
    reduce_here,
    fine_ref,
    down_rows_ref,
    nb_rows,
    count_ref,
    down_hbm,
    mid_hbm,
    out_hbm,
    gain_ref,
    bias_ref,
    cotangent_ref,
    features_ref,
    fine_grad_ref,
    grads_hbm,
    gain_grad_ref,
    bias_grad_ref,
    w_down,
    w_mid,
    w_out,
    spread_fine,
    cols_down,
    nb_cols,
    pickers,
    columns,
    act_one,
    act_one_b,
    act_two_b,
    hid_one,
    hid_two,
    hid_three,
    held,
    grad_hidden,
    source_t,
    pair_source_t,
    grad_act,
    side,
    side_cols,
    nb_own,
    nb_pair,
    swap_out,
    swap_in,
    down_all,
    down_got,
    grads,
    results,
    from_core,
    from_first_a,
    from_first_b,
    from_second_a,
    from_second_b,
    from_line_a,
    from_line_b,
    near,
    far,
    load_sem,
    store_sem,
    sum_send,
    sum_recv,
    swap_send,
    swap_recv,
    near_send,
    near_recv,
    far_send,
    far_recv,
):
    rows, width = cotangent_ref.shape
    offsets = nb_rows.shape[0]
    fine_rows, in_width = fine_ref.shape
    children = fine_rows // rows
    down_offsets = down_rows_ref.shape[0]
    units = (offsets + 1) // 2 * (1 if reduce_here else 2)
    chunks = 2 * units + down_offsets * in_width // (2 * width)
    dp_me = lax.axis_index("dp")
    group_me = lax.axis_index("group")

    loads = [
        pltpu.make_async_copy(source, target, load_sem.at[at])
        for at, (source, target) in enumerate(
            (
                (down_hbm, w_down),
                (mid_hbm, w_mid.at[pl.ds(0, offsets)]),
                (out_hbm, w_out.at[pl.ds(0, offsets)]),
            )
        )
    ]
    for load in loads:
        load.start()

    barrier = pltpu.get_barrier_semaphore()
    for step in range(1, group_size):
        pl.semaphore_signal(
            barrier,
            inc=1,
            device_id={"group": lax.rem(group_me + step, group_size)},
            device_id_type=MESH,
        )
    for step in range(1, dp_size):
        pl.semaphore_signal(
            barrier,
            inc=1,
            device_id={"dp": lax.rem(dp_me + step, dp_size)},
            device_id_type=MESH,
        )
    pl.semaphore_wait(barrier, group_size + dp_size - 2)

    def share(at, axis, me, size, slots, send, recv):
        copies = []
        for step in range(1, size):
            copies.append(
                pltpu.make_async_remote_copy(
                    src_ref=slots.at[at, me],
                    dst_ref=slots.at[at, me],
                    send_sem=send.at[at, step - 1],
                    recv_sem=recv.at[at, step - 1],
                    device_id={axis: lax.rem(me + step, size)},
                    device_id_type=MESH,
                )
            )
        for copy in copies:
            copy.start()
        return copies

    def exchange(at, block, combine, meanwhile=(None, None)):
        near[at, group_me] = block
        copies = share(at, "group", group_me, group_size, near, near_send, near_recv)
        if meanwhile[0] is not None:
            meanwhile[0]()
        for copy in copies:
            copy.wait()
        far[at, dp_me] = combine([near[at, slot] for slot in range(group_size)])
        copies = share(at, "dp", dp_me, dp_size, far, far_send, far_recv)
        if meanwhile[1] is not None:
            meanwhile[1]()
        for copy in copies:
            copy.wait()
        return combine([far[at, slot] for slot in range(dp_size)])

    lanes = width // 2

    def stack(first, second, third):
        filler = jnp.zeros((2, lanes), jnp.float32)
        return jnp.concatenate([first, second, third, filler], axis=0)

    def fold(value):
        return jnp.concatenate([value[:, :lanes], value[:, lanes:]], axis=0)

    def unfold(value):
        return jnp.concatenate([value[0:1], value[1:2]], axis=1)

    def add_all(blocks):
        total = blocks[0]
        for block in blocks[1:]:
            total = total + block
        return total

    def merge_all(blocks):
        count = add_all([block[4:6] for block in blocks])
        center = add_all([block[4:6] * block[0:2] for block in blocks]) / count
        squares = add_all(
            [
                block[2:4] + block[4:6] * (block[0:2] - center) * (block[0:2] - center)
                for block in blocks
            ]
        )
        return stack(center, squares, count)

    count = count_ref[0]
    own_count = jnp.full((1, width), count.astype(jnp.float32))
    live = lax.broadcasted_iota(jnp.int32, (rows, width), 0) < count

    def norm_stats(at, hidden, meanwhile=(None, None)):
        center = jnp.sum(hidden, axis=0, keepdims=True) / own_count
        centered = jnp.where(live, hidden - center, 0.0)
        squares = jnp.sum(centered * centered, axis=0, keepdims=True)
        merged = exchange(
            at, stack(fold(center), fold(squares), fold(own_count)), merge_all, meanwhile
        )
        total = unfold(merged[4:6])
        scale = lax.rsqrt(unfold(merged[2:4]) / total + eps_norm)
        return unfold(merged[0:2]), scale, total

    def norm_grad(at, norm, incoming, normed, scale, total, meanwhile=(None, None)):
        shift_sum = fold(jnp.sum(incoming, axis=0, keepdims=True))
        scale_sum = fold(jnp.sum(incoming * normed, axis=0, keepdims=True))
        summed = exchange(
            at, stack(shift_sum, scale_sum, jnp.zeros_like(shift_sum)), add_all, meanwhile
        )
        shift_sum, scale_sum = unfold(summed[0:2]), unfold(summed[2:4])
        bias_grad_ref[norm : norm + 1, :] = shift_sum
        gain_grad_ref[norm : norm + 1, :] = scale_sum
        hidden_grad = (
            scale
            * gain_ref[norm : norm + 1, :]
            * (incoming - shift_sum / total - normed * (scale_sum / total))
        )
        return jnp.where(live, hidden_grad, 0.0).astype(jnp.bfloat16)

    def pick(mask):
        return jnp.where(mask, jnp.bfloat16(1), jnp.bfloat16(0))

    def counting(shape, axis):
        return lax.broadcasted_iota(jnp.int32, shape, axis).astype(jnp.float32).astype(jnp.bfloat16)

    def place_columns(count):
        picked = dot(pickers[: count * rows, :], held[...]).astype(jnp.bfloat16)
        for part in range(count):
            columns[:, part * width : (part + 1) * width] = picked[part * rows : (part + 1) * rows]

    def convolve(weight, hidden):
        places = counting((rows, BLOCK), 1)
        hidden[...] = jnp.zeros_like(hidden)

        def step(at, carry):
            for part in range(GROUP):
                for block in range(rows // BLOCK):
                    wanted = jnp.concatenate(
                        [nb_cols[block, at * GROUP + part]] * (BLOCK // 128), axis=1
                    )
                    pickers[
                        part * rows : (part + 1) * rows, block * BLOCK : (block + 1) * BLOCK
                    ] = pick(wanted == places)
            place_columns(GROUP)
            weights = weight[pl.ds(at * GROUP, GROUP)].reshape(GROUP * width, width)
            hidden[...] += dot(columns[...], weights)
            return carry

        lax.fori_loop(0, offsets // GROUP, step, 0)

    def spread_rows(neighbours, first_offset):
        places = counting((BLOCK, rows), 0)
        for part in range(PAIR):
            wanted = neighbours[pl.ds(first_offset + part, 1), :].astype(jnp.float32)
            for first in range(0, rows, BLOCK):
                here = jnp.broadcast_to(wanted - first, (16, rows)).astype(jnp.bfloat16)
                pickers[part * rows + first : part * rows + first + BLOCK, :] = pick(
                    jnp.concatenate([here] * (BLOCK // 16), axis=0) == places
                )
        place_columns(PAIR)
        return columns[:, : PAIR * width]

    def unit_rows(unit):
        return pl.ds(pl.multiple_of(unit * width, width), width)

    def convolve_back(weight, act_grad, first_unit, own_slot, other_slot):
        def step(first_offset, at, weigh):
            spread = spread_rows(nb_own, first_offset)
            weights = jnp.concatenate(
                [weight[first_offset + part] for part in range(PAIR)], axis=1
            )
            act_grad[...] += dot_last(spread, weights)
            if weigh:
                product = dot(source_t[...], spread)
                for part in range(PAIR):
                    grads[unit_rows(first_unit + PAIR * at + part), :] = product[
                        :, part * width : (part + 1) * width
                    ]

        def own(at, carry):
            step(own_offset + PAIR * at, at, True)
            own_slot(at)
            return carry

        def other(at, carry):
            step(other_offset + PAIR * at, at, False)
            other_slot(at)
            return carry

        lax.fori_loop(0, units // PAIR, own, 0)
        if reduce_here:
            lax.fori_loop(0, units // PAIR, other, 0)

    def convolve_pair(first_unit, at_slot):
        def step(at, carry):
            spread = spread_rows(nb_pair, own_offset + PAIR * at)
            product = dot(pair_source_t[...], spread)
            for part in range(PAIR):
                here = unit_rows(first_unit + PAIR * at + part)
                grads[here, :] = grads[here, :] + product[:, part * width : (part + 1) * width]
            at_slot(at)
            return carry

        lax.fori_loop(0, units // PAIR, step, 0)

    core, row = lax.rem(group_me, 2), group_me // 2
    column, plane = lax.rem(dp_me, 2), dp_me // 2
    pair, high = lax.rem(plane, 2), plane // 2
    planes = 4
    core_peer = {"group": group_me + 1 - 2 * core}
    row_peer = {"group": group_me + 2 - 4 * row}
    column_peer = {"dp": dp_me + 1 - 2 * column}
    pair_peer = {"dp": dp_me + 2 - 4 * pair}
    cross_peer = {"dp": dp_me + 4 - 8 * high}
    own_offset = units * pair if reduce_here else 0
    other_offset = units * (1 - pair)
    half, fourth, eighth, piece = width // 2, width // 8, width // 16, width // 32

    def keep_rows():
        own = half * core
        a, b = own + fourth * column, own + 2 * fourth + fourth * row
        aa, bb = a + eighth * row, b + eighth * column
        return own, (a, b), (aa, bb), (aa + piece * high, bb + piece * high)

    def give_rows():
        _, (a, b), (aa, bb), _ = keep_rows()
        return (
            half * (1 - core),
            (a + fourth * (1 - 2 * column), b + fourth * (1 - 2 * row)),
            (aa + eighth * (1 - 2 * row), bb + eighth * (1 - 2 * column)),
            (aa + piece * (1 - high), bb + piece * (1 - high)),
        )

    def at_rows(ref, c, first, count):
        start = pl.multiple_of(c * width + first, count)
        return ref.at[pl.ds(start, count), :]

    def landing(ref, c, count):
        return ref.at[pl.ds(pl.multiple_of(c * count, count), count), :]

    def place_of(c, first, count):
        return results.at[:, c, pl.ds(pl.multiple_of(first, count), count), :]

    def send(c, number, source, target, peer):
        turn = lax.rem(c, RING)
        return pltpu.make_async_remote_copy(
            src_ref=source,
            dst_ref=target,
            send_sem=sum_send.at[turn, number],
            recv_sem=sum_recv.at[turn, number],
            device_id=peer,
            device_id_type=MESH,
        )

    def own_place(c, lane):
        first = keep_rows()[3][lane]
        return (
            at_rows(grads, c, first, piece),
            results.at[pair, c, pl.ds(pl.multiple_of(first, piece), piece), :],
        )

    def copies_of(c, stage):
        keep, give = keep_rows(), give_rows()
        if stage == 0:
            target = landing(from_core, lax.rem(c, RING), half)
            return [send(c, 0, at_rows(grads, c, give[0], half), target, core_peer)]
        if stage < 4:
            count = (fourth, eighth, piece)[stage - 1]
            targets = (
                (from_first_a, from_first_b),
                (from_second_a, from_second_b),
                (from_line_a, from_line_b),
            )[stage - 1]
            peers = (
                (column_peer, row_peer),
                (row_peer, column_peer),
                (cross_peer, cross_peer),
            )[stage - 1]
            return [
                send(
                    c,
                    2 * stage - 1 + lane,
                    at_rows(grads, c, give[stage][lane], count),
                    landing(targets[lane], c, count),
                    peers[lane],
                )
                for lane in range(2)
            ]
        if stage == 4:
            return [
                send(
                    c,
                    7 + (planes - 1) * lane + step - 1,
                    *own_place(c, lane),
                    {"dp": 2 * lax.rem(plane + step, planes) + column},
                )
                for lane in range(2)
                for step in range(1, planes)
            ]
        first = 7 + 2 * (planes - 1)
        if stage < 7:
            level, count = ((2, eighth), (1, fourth))[stage - 5]
            peers = ((row_peer, column_peer), (column_peer, row_peer))[stage - 5]
            blocks = [place_of(c, keep[level][lane], count) for lane in range(2)]
            return [
                send(c, first + 2 * (stage - 5) + lane, blocks[lane], blocks[lane], peers[lane])
                for lane in range(2)
            ]
        block = place_of(c, keep[0], half)
        return [send(c, first + 4, block, block, core_peer)]

    def store_of(c):
        return pltpu.make_async_copy(results.at[:, c], grads_hbm.at[:, c], store_sem.at[c])

    def stage_of(c, stage):
        if stage > 0:
            for copy in copies_of(c, stage - 1):
                copy.wait()
        keep = keep_rows()
        if 1 <= stage <= 4:
            count = (half, fourth, eighth, piece)[stage - 1]
            firsts = ((keep[0],), *keep[1:])[stage - 1]
            landings = (
                (from_core,),
                (from_first_a, from_first_b),
                (from_second_a, from_second_b),
                (from_line_a, from_line_b),
            )[stage - 1]
            turn = lax.rem(c, RING) if stage == 1 else c
            for first, landed in zip(firsts, landings):
                here = pl.ds(pl.multiple_of(c * width + first, count), count)
                there = pl.ds(pl.multiple_of(turn * count, count), count)
                grads[here, :] = grads[here, :] + landed[there, :]
        if stage == 4:
            for lane in range(2):
                first = pl.ds(pl.multiple_of(keep[3][lane], piece), piece)
                here = pl.ds(pl.multiple_of(c * width + keep[3][lane], piece), piece)
                results[pair, c, first, :] = grads[here, :]
        if stage == STAGES:
            store_of(c).start()
        else:
            for copy in copies_of(c, stage):
                copy.start()

    def slot(at):
        if not reduce_here:
            return
        for stage in range(STAGES + 1):
            c = at - stage

            @pl.when((c >= 0) & (c < chunks))
            def _():
                stage_of(c, stage)

    def slot_when(condition, at):
        @pl.when(condition)
        def _():
            slot(at)

    def no_slot(at):
        pass

    def swap(at, source, target):
        return pltpu.make_async_remote_copy(
            src_ref=source,
            dst_ref=target,
            send_sem=swap_send.at[at],
            recv_sem=swap_recv.at[at],
            device_id=pair_peer,
            device_id_type=MESH,
        )

    def swap_rows(at):
        return swap(at, swap_out.at[at], swap_in.at[at])

    def start_rows(at, value):
        if reduce_here:
            swap_out[at] = value.astype(jnp.float32)
            swap_rows(at).start()

    side[...] = jnp.zeros_like(side)
    side[:offsets, :] = nb_rows[...]
    side[offsets : offsets + down_offsets, :] = down_rows_ref[...]
    side_cols[...] = side[...].T
    nb_own[...] = jnp.full_like(nb_own, rows)
    nb_own[:offsets, :] = nb_rows[...]
    swap_neighbours = swap(4, nb_own, nb_pair)
    if reduce_here:
        swap_neighbours.start()
    for weight in (w_mid, w_out):
        weight[offsets:] = jnp.zeros_like(weight[offsets:])

    spread_fine[...] = fine_ref[...].astype(jnp.float32)
    for k in range(down_offsets):
        child = spread_fine[pl.ds(k % children, rows, stride=children), :]
        there = side_cols[:, offsets + k : offsets + k + 1] < fine_rows
        cols_down[:, k * in_width : (k + 1) * in_width] = jnp.where(there, child, 0.0).astype(
            jnp.bfloat16
        )
    loads[0].wait()
    hid_one[...] = dot(cols_down[...], w_down[...].reshape(down_offsets * in_width, width))

    def spread_neighbours():
        for k in range(offsets):
            wanted = jnp.broadcast_to(side_cols[:, k : k + 1], (rows, 128)).astype(jnp.float32)
            for block in range(rows // BLOCK):
                nb_cols[block, k] = (wanted - block * BLOCK).astype(jnp.bfloat16)

    center_one, scale_one, total = norm_stats(0, hid_one[...], (spread_neighbours, None))

    def pre_one():
        normed = (hid_one[...] - center_one) * scale_one
        return normed, normed * gain_ref[0:1, :] + bias_ref[0:1, :]

    _, pre = pre_one()
    act_one[...] = jnp.where(live, pre * sigmoid(pre), 0.0)
    act_one_b[...] = act_one[...].astype(jnp.bfloat16)
    start_rows(0, act_one_b[...])
    loads[1].wait()
    held[...] = act_one_b[...]
    convolve(w_mid, hid_two)
    center_two, scale_two, _ = norm_stats(1, hid_two[...])

    def pre_two():
        normed = (hid_two[...] - center_two) * scale_two
        return normed, normed * gain_ref[1:2, :] + bias_ref[1:2, :]

    _, pre = pre_two()
    act_two_b[...] = jnp.where(live, pre * sigmoid(pre), 0.0).astype(jnp.bfloat16)
    start_rows(1, act_two_b[...])
    loads[2].wait()
    held[...] = act_two_b[...]
    convolve(w_out, hid_three)
    center_three, scale_three, _ = norm_stats(2, hid_three[...])
    normed_three = (hid_three[...] - center_three) * scale_three
    summed = (
        jnp.where(live, normed_three * gain_ref[2:3, :] + bias_ref[2:3, :], 0.0) + act_one[...]
    )
    sigma = sigmoid(summed)
    features_ref[...] = jnp.where(live, summed * sigma, 0.0).astype(jnp.bfloat16)

    slope = sigma * (1.0 + summed * (1.0 - sigma))
    act_one[...] = jnp.where(live, cotangent_ref[...].astype(jnp.float32) * slope, 0.0)
    grad_hidden[...] = norm_grad(3, 2, act_one[...], normed_three, scale_three, total)
    start_rows(2, grad_hidden[...])
    held[...] = grad_hidden[...]
    grad_act[...] = jnp.zeros_like(grad_act)
    steps = units // PAIR

    def receive(source_at, hidden_at):
        swap_rows(source_at).wait()
        pair_source_t[...] = swap_in[source_at].astype(jnp.bfloat16).T
        swap_rows(hidden_at).wait()
        held[...] = swap_in[hidden_at].astype(jnp.bfloat16)

    def slots_from(at):
        return (lambda: slot(at), lambda: slot(at + 1))

    source_t[...] = act_two_b[...].T
    convolve_back(w_out, grad_act, 0, no_slot, no_slot)
    if reduce_here:
        swap_neighbours.wait()
        receive(1, 2)
        convolve_pair(0, slot)
    normed, pre = pre_two()
    incoming = jnp.where(live, grad_act[...] * silu_slope(pre), 0.0)
    grad_hidden[...] = norm_grad(
        4, 1, incoming, normed, scale_two, total, slots_from(steps)
    )
    start_rows(3, grad_hidden[...])
    held[...] = grad_hidden[...]
    grad_act[...] = act_one[...]
    source_t[...] = act_one_b[...].T
    done = steps + 2
    convolve_back(
        w_mid,
        grad_act,
        units,
        lambda at: slot_when(lax.rem(at, 3) == 0, done + at // 3),
        lambda at: slot_when(lax.rem(at, 4) == 0, done + 3 + at // 4),
    )
    done = units
    if reduce_here:
        receive(0, 3)
        convolve_pair(units, lambda at: slot(done + at))
    done = units + steps
    normed, pre = pre_one()
    incoming = jnp.where(live, grad_act[...] * silu_slope(pre), 0.0)
    grad_hidden[...] = norm_grad(5, 0, incoming, normed, scale_one, total, slots_from(done))
    down_rows = down_offsets * in_width
    if reduce_here:
        down_all[...] = dot(cols_down[...].T, grad_hidden[...])
        kept = down_rows // 2
        swap_down = swap(
            5, down_all.at[pl.ds(pl.multiple_of(kept * (1 - pair), kept), kept), :], down_got
        )
        swap_down.start()
    else:
        grads[2 * units * width :, :] = dot(cols_down[...].T, grad_hidden[...])
    slot(done + 2)
    for child in range(children):
        total_child = jnp.zeros((rows, in_width), jnp.float32)
        for k in range(child, down_offsets, children):
            there = side_cols[:, offsets + k : offsets + k + 1] < fine_rows
            total_child += jnp.where(there, dot_last(grad_hidden[...], w_down[k]), 0.0)
        spread_fine[pl.ds(child, rows, stride=children), :] = total_child
    fine_grad_ref[...] = spread_fine[...].astype(jnp.bfloat16)

    if reduce_here:

        def rest(at, carry):
            slot(at)
            return carry

        lax.fori_loop(done + 3, 2 * units, rest, 0)
        swap_down.wait()
        grads[2 * units * width :, :] = (
            down_all[pl.ds(pl.multiple_of(kept * pair, kept), kept), :] + down_got[...]
        )
        lax.fori_loop(2 * units, chunks + STAGES, rest, 0)

        def finish(c, carry):
            store_of(c).wait()
            return carry

        lax.fori_loop(0, chunks, finish, 0)
    else:
        store = pltpu.make_async_copy(grads, grads_hbm, store_sem.at[0])
        store.start()
        store.wait()


def place_kernel(
    features_ref,
    fine_grad_ref,
    grads_ref,
    gain_ref,
    bias_ref,
    features_out,
    fine_grad_out,
    grad_down_out,
    grad_mid_out,
    grad_out_out,
    gain_out,
    bias_out,
    held,
    load_sem,
    store_sem,
):
    offsets, width = grad_mid_out.shape[:2]
    units = (offsets + 1) // 2
    piece = (units + 1) // 2
    moves = []
    for pair in range(2):
        for at, target in enumerate((grad_out_out, grad_mid_out)):
            for first in range(0, units, piece):
                count = min(piece, offsets - units * pair - first, units - first)
                here = (pair, pl.ds(at * units + first, count))
                moves.append((here, target.at[pl.ds(units * pair + first, count)]))
        down_units = grad_down_out.shape[0] // 2
        here = (pair, pl.ds(2 * units, down_units))
        moves.append((here, grad_down_out.at[pl.ds(pair * down_units, down_units)]))
    loads = [
        pltpu.make_async_copy(grads_ref.at[here], held.at[here], load_sem.at[at])
        for at, (here, _) in enumerate(moves)
    ]
    stores = [
        pltpu.make_async_copy(held.at[here], target, store_sem.at[at])
        for at, (here, target) in enumerate(moves)
    ]
    for load in loads:
        load.start()
    features_out[...] = features_ref[...]
    fine_grad_out[...] = fine_grad_ref[...]
    gain_out[...] = gain_ref[...]
    bias_out[...] = bias_ref[...]
    for load, store in zip(loads, stores):
        load.wait()
        store.start()
    for store in stores:
        store.wait()


def per_device(
    dp_size,
    group_size,
    fine_features,
    down_map,
    neighbours,
    voxel_counts,
    down_weight,
    mid_weight,
    out_weight,
    norm_gain,
    norm_bias,
    cotangent,
):
    rows, width = cotangent.shape
    fine_rows, in_width = fine_features.shape
    offsets = neighbours.shape[1]
    down_offsets = down_map.shape[1]
    f32, bf16, i32 = jnp.float32, jnp.bfloat16, jnp.int32
    vmem = pl.BlockSpec(memory_space=pltpu.VMEM)
    smem = pl.BlockSpec(memory_space=pltpu.SMEM)
    hbm = pl.BlockSpec(memory_space=pl.ANY)
    shape = jax.ShapeDtypeStruct
    reduce_here = dp_size == 8 and group_size == 4
    share = 2 if reduce_here else 1
    units = (offsets + 1) // 2 * 2 // share
    chunks = 2 * units + down_offsets * in_width // (share * width)
    grad_rows = chunks * width
    padded = (offsets + 1) // 2 * 2
    features, fine_grad, grads, gain_grad, bias_grad = pl.pallas_call(
        functools.partial(kernel, dp_size, group_size, reduce_here),
        out_shape=(
            shape((rows, width), bf16),
            shape((fine_rows, in_width), bf16),
            shape((share, chunks, width, width) if reduce_here else (grad_rows, width), f32),
            shape(norm_gain.shape, f32),
            shape(norm_bias.shape, f32),
        ),
        in_specs=[vmem, vmem, vmem, smem, hbm, hbm, hbm, vmem, vmem, vmem],
        out_specs=(vmem, vmem, hbm, vmem, vmem),
        scratch_shapes=[
            pltpu.VMEM(down_weight.shape, bf16),
            pltpu.VMEM((padded, width, width), bf16),
            pltpu.VMEM((padded, width, width), bf16),
            pltpu.VMEM((fine_rows, in_width), f32),
            pltpu.VMEM((rows, down_offsets * in_width), bf16),
            pltpu.VMEM((rows // BLOCK, offsets, rows, 128), bf16),
            pltpu.VMEM((GROUP * rows, rows), bf16),
            pltpu.VMEM((rows, GROUP * width), bf16),
            pltpu.VMEM((rows, width), f32),
            pltpu.VMEM((rows, width), bf16),
            pltpu.VMEM((rows, width), bf16),
            pltpu.VMEM((rows, width), f32),
            pltpu.VMEM((rows, width), f32),
            pltpu.VMEM((rows, width), f32),
            pltpu.VMEM((rows, width), bf16),
            pltpu.VMEM((rows, width), bf16),
            pltpu.VMEM((width, rows), bf16),
            pltpu.VMEM((width, rows), bf16),
            pltpu.VMEM((rows, width), f32),
            pltpu.VMEM((128, rows), i32),
            pltpu.VMEM((rows, 128), i32),
            pltpu.VMEM((padded, rows), i32),
            pltpu.VMEM((padded, rows), i32),
            pltpu.VMEM((4, rows, width), f32),
            pltpu.VMEM((4, rows, width), f32),
            pltpu.VMEM((down_offsets * in_width, width), f32),
            pltpu.VMEM((down_offsets * in_width // 2, width), f32),
            pltpu.VMEM((grad_rows, width), f32),
            pltpu.VMEM((2, chunks if reduce_here else 1, width, width), f32),
            pltpu.VMEM((RING * width // 2, width), f32),
            pltpu.VMEM((chunks * width // 8, width), f32),
            pltpu.VMEM((chunks * width // 8, width), f32),
            pltpu.VMEM((chunks * width // 16, width), f32),
            pltpu.VMEM((chunks * width // 16, width), f32),
            pltpu.VMEM((chunks * width // 32, width), f32),
            pltpu.VMEM((chunks * width // 32, width), f32),
            pltpu.VMEM((6, group_size, 8, width // 2), f32),
            pltpu.VMEM((6, dp_size, 8, width // 2), f32),
            pltpu.SemaphoreType.DMA((3,)),
            pltpu.SemaphoreType.DMA((chunks,)),
            pltpu.SemaphoreType.DMA((RING, COPIES)),
            pltpu.SemaphoreType.DMA((RING, COPIES)),
            pltpu.SemaphoreType.DMA((6,)),
            pltpu.SemaphoreType.DMA((6,)),
            pltpu.SemaphoreType.DMA((6, group_size - 1)),
            pltpu.SemaphoreType.DMA((6, group_size - 1)),
            pltpu.SemaphoreType.DMA((6, dp_size - 1)),
            pltpu.SemaphoreType.DMA((6, dp_size - 1)),
        ],
        compiler_params=pltpu.CompilerParams(
            collective_id=0, has_side_effects=True, vmem_limit_bytes=60 * 1024 * 1024
        ),
    )(
        fine_features,
        down_map.T,
        neighbours.T,
        voxel_counts,
        down_weight,
        mid_weight,
        out_weight,
        norm_gain,
        norm_bias,
        cotangent,
    )
    if not reduce_here:
        grads = lax.psum(grads, ("dp", "group"))
        middle, end = offsets * width, 2 * padded * width
        grad_out = grads[:middle].reshape(out_weight.shape)
        grad_mid = grads[padded * width : padded * width + middle].reshape(mid_weight.shape)
        grad_down = grads[end:].reshape(down_weight.shape)
        return (features, fine_grad, grad_down, grad_mid, grad_out, gain_grad, bias_grad)
    features, fine_grad, grad_down, grad_mid, grad_out, gain_grad, bias_grad = pl.pallas_call(
        place_kernel,
        out_shape=(
            shape(features.shape, bf16),
            shape(fine_grad.shape, bf16),
            shape((down_offsets * in_width // width, width, width), f32),
            shape(mid_weight.shape, f32),
            shape(out_weight.shape, f32),
            shape(norm_gain.shape, f32),
            shape(norm_bias.shape, f32),
        ),
        in_specs=[vmem, vmem, hbm, vmem, vmem],
        out_specs=(vmem, vmem, hbm, hbm, hbm, vmem, vmem),
        scratch_shapes=[
            pltpu.VMEM(grads.shape, f32),
            pltpu.SemaphoreType.DMA((10,)),
            pltpu.SemaphoreType.DMA((10,)),
        ],
        compiler_params=pltpu.CompilerParams(vmem_limit_bytes=32 * 1024 * 1024),
    )(features, fine_grad, grads, gain_grad, bias_grad)
    grad_down = grad_down.reshape(down_weight.shape)
    return (features, fine_grad, grad_down, grad_mid, grad_out, gain_grad, bias_grad)


def solution(mesh):
    in_specs = (
        P(("dp", "group"), None),
        P(("dp", "group"), None),
        P(("dp", "group"), None),
        P(("dp", "group")),
        P(),
        P(),
        P(),
        P(),
        P(),
        P(("dp", "group"), None),
    )
    out_specs = (P(("dp", "group"), None), P(("dp", "group"), None), P(), P(), P(), P(), P())
    return jax.shard_map(
        functools.partial(per_device, mesh.shape["dp"], mesh.shape["group"]),
        mesh=mesh,
        in_specs=in_specs,
        out_specs=out_specs,
        check_vma=False,
    )
```

```python
import functools

import jax
import jax.numpy as jnp
from jax import lax
from jax.experimental import pallas as pl
from jax.experimental.pallas import tpu as pltpu
from jax.sharding import PartitionSpec as P

eps_norm = 1e-05
MESH = pl.DeviceIdType.MESH
GROUP = 3
BLOCK = 256
PAIR = 2
COPIES = 18
STAGES = 8
LAG = 2
RING = 8


def sigmoid(value):
    return 1.0 / (1.0 + jnp.exp(-value))


def silu_slope(value):
    sigma = sigmoid(value)
    return sigma * (1.0 + value * (1.0 - sigma))


def dot(left, right):
    return jnp.dot(left, right, preferred_element_type=jnp.float32)


def dot_last(left, right):
    return lax.dot_general(
        left, right, (((1,), (1,)), ((), ())), preferred_element_type=jnp.float32
    )


def kernel(
    dp_size,
    group_size,
    reduce_here,
    fine_ref,
    down_rows_ref,
    nb_rows,
    count_ref,
    down_hbm,
    mid_hbm,
    out_hbm,
    gain_ref,
    bias_ref,
    cotangent_ref,
    features_ref,
    fine_grad_ref,
    grads_hbm,
    gain_grad_ref,
    bias_grad_ref,
    w_down,
    w_mid,
    w_out,
    spread_fine,
    cols_down,
    nb_cols,
    pickers,
    columns,
    act_one,
    act_one_b,
    act_two_b,
    hid_one,
    hid_two,
    hid_three,
    held,
    grad_hidden,
    source_t,
    pair_source_t,
    grad_act,
    side,
    side_cols,
    nb_own,
    nb_pair,
    swap_out,
    swap_in,
    down_all,
    down_got,
    grads,
    results,
    from_core,
    from_first_a,
    from_first_b,
    from_second_a,
    from_second_b,
    from_line_a,
    from_line_b,
    near,
    far,
    load_sem,
    store_sem,
    sum_send,
    sum_recv,
    swap_send,
    swap_recv,
    near_send,
    near_recv,
    far_send,
    far_recv,
):
    rows, width = cotangent_ref.shape
    offsets = nb_rows.shape[0]
    fine_rows, in_width = fine_ref.shape
    children = fine_rows // rows
    down_offsets = down_rows_ref.shape[0]
    units = (offsets + 1) // 2 * (1 if reduce_here else 2)
    chunks = 2 * units + down_offsets * in_width // (2 * width)
    dp_me = lax.axis_index("dp")
    group_me = lax.axis_index("group")

    loads = [
        pltpu.make_async_copy(source, target, load_sem.at[at])
        for at, (source, target) in enumerate(
            (
                (down_hbm, w_down),
                (mid_hbm, w_mid.at[pl.ds(0, offsets)]),
                (out_hbm, w_out.at[pl.ds(0, offsets)]),
            )
        )
    ]
    for load in loads:
        load.start()

    barrier = pltpu.get_barrier_semaphore()
    for step in range(1, group_size):
        pl.semaphore_signal(
            barrier,
            inc=1,
            device_id={"group": lax.rem(group_me + step, group_size)},
            device_id_type=MESH,
        )
    for step in range(1, dp_size):
        pl.semaphore_signal(
            barrier,
            inc=1,
            device_id={"dp": lax.rem(dp_me + step, dp_size)},
            device_id_type=MESH,
        )
    pl.semaphore_wait(barrier, group_size + dp_size - 2)

    def share(at, axis, me, size, slots, send, recv):
        copies = []
        for step in range(1, size):
            copies.append(
                pltpu.make_async_remote_copy(
                    src_ref=slots.at[at, me],
                    dst_ref=slots.at[at, me],
                    send_sem=send.at[at, step - 1],
                    recv_sem=recv.at[at, step - 1],
                    device_id={axis: lax.rem(me + step, size)},
                    device_id_type=MESH,
                )
            )
        for copy in copies:
            copy.start()
        return copies

    def exchange(at, block, combine, meanwhile=(None, None)):
        near[at, group_me] = block
        copies = share(at, "group", group_me, group_size, near, near_send, near_recv)
        if meanwhile[0] is not None:
            meanwhile[0]()
        for copy in copies:
            copy.wait()
        far[at, dp_me] = combine([near[at, slot] for slot in range(group_size)])
        copies = share(at, "dp", dp_me, dp_size, far, far_send, far_recv)
        if meanwhile[1] is not None:
            meanwhile[1]()
        for copy in copies:
            copy.wait()
        return combine([far[at, slot] for slot in range(dp_size)])

    lanes = width // 2

    def stack(first, second, third):
        filler = jnp.zeros((2, lanes), jnp.float32)
        return jnp.concatenate([first, second, third, filler], axis=0)

    def fold(value):
        return jnp.concatenate([value[:, :lanes], value[:, lanes:]], axis=0)

    def unfold(value):
        return jnp.concatenate([value[0:1], value[1:2]], axis=1)

    def add_all(blocks):
        total = blocks[0]
        for block in blocks[1:]:
            total = total + block
        return total

    def merge_all(blocks):
        count = add_all([block[4:6] for block in blocks])
        center = add_all([block[4:6] * block[0:2] for block in blocks]) / count
        squares = add_all(
            [
                block[2:4] + block[4:6] * (block[0:2] - center) * (block[0:2] - center)
                for block in blocks
            ]
        )
        return stack(center, squares, count)

    count = count_ref[0]
    own_count = jnp.full((1, width), count.astype(jnp.float32))
    live = lax.broadcasted_iota(jnp.int32, (rows, width), 0) < count

    def norm_stats(at, hidden, meanwhile=(None, None)):
        center = jnp.sum(hidden, axis=0, keepdims=True) / own_count
        centered = jnp.where(live, hidden - center, 0.0)
        squares = jnp.sum(centered * centered, axis=0, keepdims=True)
        merged = exchange(
            at, stack(fold(center), fold(squares), fold(own_count)), merge_all, meanwhile
        )
        total = unfold(merged[4:6])
        scale = lax.rsqrt(unfold(merged[2:4]) / total + eps_norm)
        return unfold(merged[0:2]), scale, total

    def norm_grad(at, norm, incoming, normed, scale, total, meanwhile=(None, None)):
        shift_sum = fold(jnp.sum(incoming, axis=0, keepdims=True))
        scale_sum = fold(jnp.sum(incoming * normed, axis=0, keepdims=True))
        summed = exchange(
            at, stack(shift_sum, scale_sum, jnp.zeros_like(shift_sum)), add_all, meanwhile
        )
        shift_sum, scale_sum = unfold(summed[0:2]), unfold(summed[2:4])
        bias_grad_ref[norm : norm + 1, :] = shift_sum
        gain_grad_ref[norm : norm + 1, :] = scale_sum
        hidden_grad = (
            scale
            * gain_ref[norm : norm + 1, :]
            * (incoming - shift_sum / total - normed * (scale_sum / total))
        )
        return jnp.where(live, hidden_grad, 0.0).astype(jnp.bfloat16)

    def pick(mask):
        return jnp.where(mask, jnp.bfloat16(1), jnp.bfloat16(0))

    def counting(shape, axis):
        return lax.broadcasted_iota(jnp.int32, shape, axis).astype(jnp.float32).astype(jnp.bfloat16)

    def place_columns(count):
        picked = dot(pickers[: count * rows, :], held[...]).astype(jnp.bfloat16)
        for part in range(count):
            columns[:, part * width : (part + 1) * width] = picked[part * rows : (part + 1) * rows]

    def convolve(weight, hidden):
        places = counting((rows, BLOCK), 1)
        hidden[...] = jnp.zeros_like(hidden)

        def step(at, carry):
            for part in range(GROUP):
                for block in range(rows // BLOCK):
                    wanted = jnp.concatenate(
                        [nb_cols[block, at * GROUP + part]] * (BLOCK // 128), axis=1
                    )
                    pickers[
                        part * rows : (part + 1) * rows, block * BLOCK : (block + 1) * BLOCK
                    ] = pick(wanted == places)
            place_columns(GROUP)
            weights = weight[pl.ds(at * GROUP, GROUP)].reshape(GROUP * width, width)
            hidden[...] += dot(columns[...], weights)
            return carry

        lax.fori_loop(0, offsets // GROUP, step, 0)

    def spread_rows(neighbours, first_offset):
        places = counting((BLOCK, rows), 0)
        for part in range(PAIR):
            wanted = neighbours[pl.ds(first_offset + part, 1), :].astype(jnp.float32)
            for first in range(0, rows, BLOCK):
                here = jnp.broadcast_to(wanted - first, (16, rows)).astype(jnp.bfloat16)
                pickers[part * rows + first : part * rows + first + BLOCK, :] = pick(
                    jnp.concatenate([here] * (BLOCK // 16), axis=0) == places
                )
        place_columns(PAIR)
        return columns[:, : PAIR * width]

    def unit_rows(unit):
        return pl.ds(pl.multiple_of(unit * width, width), width)

    def convolve_back(weight, act_grad, first_unit, own_slot, other_slot):
        def step(first_offset, at, weigh):
            spread = spread_rows(nb_own, first_offset)
            weights = jnp.concatenate(
                [weight[first_offset + part] for part in range(PAIR)], axis=1
            )
            act_grad[...] += dot_last(spread, weights)
            if weigh:
                product = dot(source_t[...], spread)
                for part in range(PAIR):
                    grads[unit_rows(first_unit + PAIR * at + part), :] = product[
                        :, part * width : (part + 1) * width
                    ]

        def own(at, carry):
            step(own_offset + PAIR * at, at, True)
            own_slot(at)
            return carry

        def other(at, carry):
            step(other_offset + PAIR * at, at, False)
            other_slot(at)
            return carry

        lax.fori_loop(0, units // PAIR, own, 0)
        if reduce_here:
            lax.fori_loop(0, units // PAIR, other, 0)

    def convolve_pair(first_unit, at_slot):
        def step(at, carry):
            spread = spread_rows(nb_pair, own_offset + PAIR * at)
            product = dot(pair_source_t[...], spread)
            for part in range(PAIR):
                here = unit_rows(first_unit + PAIR * at + part)
                grads[here, :] = grads[here, :] + product[:, part * width : (part + 1) * width]
            at_slot(at)
            return carry

        lax.fori_loop(0, units // PAIR, step, 0)

    core, row = lax.rem(group_me, 2), group_me // 2
    column, plane = lax.rem(dp_me, 2), dp_me // 2
    pair, high = lax.rem(plane, 2), plane // 2
    planes = 4
    core_peer = {"group": group_me + 1 - 2 * core}
    row_peer = {"group": group_me + 2 - 4 * row}
    column_peer = {"dp": dp_me + 1 - 2 * column}
    pair_peer = {"dp": dp_me + 2 - 4 * pair}
    cross_peer = {"dp": dp_me + 4 - 8 * high}
    own_offset = units * pair if reduce_here else 0
    other_offset = units * (1 - pair)
    half, fourth, eighth, piece = width // 2, width // 8, width // 16, width // 32

    def keep_rows():
        own = half * core
        a, b = own + fourth * column, own + 2 * fourth + fourth * row
        aa, bb = a + eighth * row, b + eighth * column
        return own, (a, b), (aa, bb), (aa + piece * high, bb + piece * high)

    def give_rows():
        _, (a, b), (aa, bb), _ = keep_rows()
        return (
            half * (1 - core),
            (a + fourth * (1 - 2 * column), b + fourth * (1 - 2 * row)),
            (aa + eighth * (1 - 2 * row), bb + eighth * (1 - 2 * column)),
            (aa + piece * (1 - high), bb + piece * (1 - high)),
        )

    def at_rows(ref, c, first, count):
        start = pl.multiple_of(c * width + first, count)
        return ref.at[pl.ds(start, count), :]

    def landing(ref, c, count):
        return ref.at[pl.ds(pl.multiple_of(c * count, count), count), :]

    def place_of(c, first, count):
        return results.at[:, c, pl.ds(pl.multiple_of(first, count), count), :]

    def send(c, number, source, target, peer):
        turn = lax.rem(c, RING)
        return pltpu.make_async_remote_copy(
            src_ref=source,
            dst_ref=target,
            send_sem=sum_send.at[turn, number],
            recv_sem=sum_recv.at[turn, number],
            device_id=peer,
            device_id_type=MESH,
        )

    def own_place(c, lane):
        first = keep_rows()[3][lane]
        return (
            at_rows(grads, c, first, piece),
            results.at[pair, c, pl.ds(pl.multiple_of(first, piece), piece), :],
        )

    def copies_of(c, stage):
        keep, give = keep_rows(), give_rows()
        if stage == 0:
            target = landing(from_core, lax.rem(c, RING), half)
            return [send(c, 0, at_rows(grads, c, give[0], half), target, core_peer)]
        if stage < 4:
            count = (fourth, eighth, piece)[stage - 1]
            targets = (
                (from_first_a, from_first_b),
                (from_second_a, from_second_b),
                (from_line_a, from_line_b),
            )[stage - 1]
            peers = (
                (column_peer, row_peer),
                (row_peer, column_peer),
                (cross_peer, cross_peer),
            )[stage - 1]
            return [
                send(
                    c,
                    2 * stage - 1 + lane,
                    at_rows(grads, c, give[stage][lane], count),
                    landing(targets[lane], c, count),
                    peers[lane],
                )
                for lane in range(2)
            ]
        if stage == 4:
            return [
                send(
                    c,
                    7 + (planes - 1) * lane + step - 1,
                    *own_place(c, lane),
                    {"dp": 2 * lax.rem(plane + step, planes) + column},
                )
                for lane in range(2)
                for step in range(1, planes)
            ]
        first = 7 + 2 * (planes - 1)
        if stage < 7:
            level, count = ((2, eighth), (1, fourth))[stage - 5]
            peers = ((row_peer, column_peer), (column_peer, row_peer))[stage - 5]
            blocks = [place_of(c, keep[level][lane], count) for lane in range(2)]
            return [
                send(c, first + 2 * (stage - 5) + lane, blocks[lane], blocks[lane], peers[lane])
                for lane in range(2)
            ]
        block = place_of(c, keep[0], half)
        return [send(c, first + 4, block, block, core_peer)]

    def store_of(c):
        return pltpu.make_async_copy(results.at[:, c], grads_hbm.at[:, c], store_sem.at[c])

    def stage_of(c, stage):
        if stage > 0:
            for copy in copies_of(c, stage - 1):
                copy.wait()
        keep = keep_rows()
        if 1 <= stage <= 4:
            count = (half, fourth, eighth, piece)[stage - 1]
            firsts = ((keep[0],), *keep[1:])[stage - 1]
            landings = (
                (from_core,),
                (from_first_a, from_first_b),
                (from_second_a, from_second_b),
                (from_line_a, from_line_b),
            )[stage - 1]
            turn = lax.rem(c, RING) if stage == 1 else c
            for first, landed in zip(firsts, landings):
                here = pl.ds(pl.multiple_of(c * width + first, count), count)
                there = pl.ds(pl.multiple_of(turn * count, count), count)
                grads[here, :] = grads[here, :] + landed[there, :]
        if stage == 4:
            for lane in range(2):
                first = pl.ds(pl.multiple_of(keep[3][lane], piece), piece)
                here = pl.ds(pl.multiple_of(c * width + keep[3][lane], piece), piece)
                results[pair, c, first, :] = grads[here, :]
        if stage == STAGES:
            store_of(c).start()
        else:
            for copy in copies_of(c, stage):
                copy.start()

    def slot(at):
        if not reduce_here:
            return
        for stage in range(STAGES + 1):
            c = at - LAG * stage

            @pl.when((c >= 0) & (c < chunks))
            def _():
                stage_of(c, stage)

    def slot_when(condition, at):
        @pl.when(condition)
        def _():
            slot(at)

    def no_slot(at):
        pass

    def swap(at, source, target):
        return pltpu.make_async_remote_copy(
            src_ref=source,
            dst_ref=target,
            send_sem=swap_send.at[at],
            recv_sem=swap_recv.at[at],
            device_id=pair_peer,
            device_id_type=MESH,
        )

    def swap_rows(at):
        return swap(at, swap_out.at[at], swap_in.at[at])

    def start_rows(at, value):
        if reduce_here:
            swap_out[at] = value.astype(jnp.float32)
            swap_rows(at).start()

    side[...] = jnp.zeros_like(side)
    side[:offsets, :] = nb_rows[...]
    side[offsets : offsets + down_offsets, :] = down_rows_ref[...]
    side_cols[...] = side[...].T
    nb_own[...] = jnp.full_like(nb_own, rows)
    nb_own[:offsets, :] = nb_rows[...]
    swap_neighbours = swap(4, nb_own, nb_pair)
    if reduce_here:
        swap_neighbours.start()
    for weight in (w_mid, w_out):
        weight[offsets:] = jnp.zeros_like(weight[offsets:])

    spread_fine[...] = fine_ref[...].astype(jnp.float32)
    for k in range(down_offsets):
        child = spread_fine[pl.ds(k % children, rows, stride=children), :]
        there = side_cols[:, offsets + k : offsets + k + 1] < fine_rows
        cols_down[:, k * in_width : (k + 1) * in_width] = jnp.where(there, child, 0.0).astype(
            jnp.bfloat16
        )
    loads[0].wait()
    hid_one[...] = dot(cols_down[...], w_down[...].reshape(down_offsets * in_width, width))

    def spread_neighbours():
        for k in range(offsets):
            wanted = jnp.broadcast_to(side_cols[:, k : k + 1], (rows, 128)).astype(jnp.float32)
            for block in range(rows // BLOCK):
                nb_cols[block, k] = (wanted - block * BLOCK).astype(jnp.bfloat16)

    center_one, scale_one, total = norm_stats(0, hid_one[...], (spread_neighbours, None))

    def pre_one():
        normed = (hid_one[...] - center_one) * scale_one
        return normed, normed * gain_ref[0:1, :] + bias_ref[0:1, :]

    _, pre = pre_one()
    act_one[...] = jnp.where(live, pre * sigmoid(pre), 0.0)
    act_one_b[...] = act_one[...].astype(jnp.bfloat16)
    start_rows(0, act_one_b[...])
    loads[1].wait()
    held[...] = act_one_b[...]
    convolve(w_mid, hid_two)
    center_two, scale_two, _ = norm_stats(1, hid_two[...])

    def pre_two():
        normed = (hid_two[...] - center_two) * scale_two
        return normed, normed * gain_ref[1:2, :] + bias_ref[1:2, :]

    _, pre = pre_two()
    act_two_b[...] = jnp.where(live, pre * sigmoid(pre), 0.0).astype(jnp.bfloat16)
    start_rows(1, act_two_b[...])
    loads[2].wait()
    held[...] = act_two_b[...]
    convolve(w_out, hid_three)
    center_three, scale_three, _ = norm_stats(2, hid_three[...])
    normed_three = (hid_three[...] - center_three) * scale_three
    summed = (
        jnp.where(live, normed_three * gain_ref[2:3, :] + bias_ref[2:3, :], 0.0) + act_one[...]
    )
    sigma = sigmoid(summed)
    features_ref[...] = jnp.where(live, summed * sigma, 0.0).astype(jnp.bfloat16)

    slope = sigma * (1.0 + summed * (1.0 - sigma))
    act_one[...] = jnp.where(live, cotangent_ref[...].astype(jnp.float32) * slope, 0.0)
    grad_hidden[...] = norm_grad(3, 2, act_one[...], normed_three, scale_three, total)
    start_rows(2, grad_hidden[...])
    held[...] = grad_hidden[...]
    grad_act[...] = jnp.zeros_like(grad_act)
    steps = units // PAIR

    def receive(source_at, hidden_at):
        swap_rows(source_at).wait()
        pair_source_t[...] = swap_in[source_at].astype(jnp.bfloat16).T
        swap_rows(hidden_at).wait()
        held[...] = swap_in[hidden_at].astype(jnp.bfloat16)

    def slots_from(at):
        return (lambda: slot(at), lambda: slot(at + 1))

    source_t[...] = act_two_b[...].T
    convolve_back(w_out, grad_act, 0, no_slot, no_slot)
    if reduce_here:
        swap_neighbours.wait()
        receive(1, 2)
        convolve_pair(0, slot)
    normed, pre = pre_two()
    incoming = jnp.where(live, grad_act[...] * silu_slope(pre), 0.0)
    grad_hidden[...] = norm_grad(
        4, 1, incoming, normed, scale_two, total, slots_from(steps)
    )
    start_rows(3, grad_hidden[...])
    held[...] = grad_hidden[...]
    grad_act[...] = act_one[...]
    source_t[...] = act_one_b[...].T
    done = steps + 2
    convolve_back(
        w_mid,
        grad_act,
        units,
        lambda at: slot_when(lax.rem(at, 3) == 0, done + at // 3),
        lambda at: slot_when(lax.rem(at, 4) == 0, done + 3 + at // 4),
    )
    done = units
    if reduce_here:
        receive(0, 3)
        convolve_pair(units, lambda at: slot(done + at))
    done = units + steps
    normed, pre = pre_one()
    incoming = jnp.where(live, grad_act[...] * silu_slope(pre), 0.0)
    grad_hidden[...] = norm_grad(5, 0, incoming, normed, scale_one, total, slots_from(done))
    down_rows = down_offsets * in_width
    if reduce_here:
        down_all[...] = dot(cols_down[...].T, grad_hidden[...])
        kept = down_rows // 2
        swap_down = swap(
            5, down_all.at[pl.ds(pl.multiple_of(kept * (1 - pair), kept), kept), :], down_got
        )
        swap_down.start()
    else:
        grads[2 * units * width :, :] = dot(cols_down[...].T, grad_hidden[...])
    slot(done + 2)
    for child in range(children):
        total_child = jnp.zeros((rows, in_width), jnp.float32)
        for k in range(child, down_offsets, children):
            there = side_cols[:, offsets + k : offsets + k + 1] < fine_rows
            total_child += jnp.where(there, dot_last(grad_hidden[...], w_down[k]), 0.0)
        spread_fine[pl.ds(child, rows, stride=children), :] = total_child
    fine_grad_ref[...] = spread_fine[...].astype(jnp.bfloat16)

    if reduce_here:

        def rest(at, carry):
            slot(at)
            return carry

        lax.fori_loop(done + 3, 2 * units, rest, 0)
        swap_down.wait()
        grads[2 * units * width :, :] = (
            down_all[pl.ds(pl.multiple_of(kept * pair, kept), kept), :] + down_got[...]
        )
        lax.fori_loop(2 * units, chunks + LAG * STAGES, rest, 0)

        def finish(c, carry):
            store_of(c).wait()
            return carry

        lax.fori_loop(0, chunks, finish, 0)
    else:
        store = pltpu.make_async_copy(grads, grads_hbm, store_sem.at[0])
        store.start()
        store.wait()


def place_kernel(
    features_ref,
    fine_grad_ref,
    grads_ref,
    gain_ref,
    bias_ref,
    features_out,
    fine_grad_out,
    grad_down_out,
    grad_mid_out,
    grad_out_out,
    gain_out,
    bias_out,
    held,
    load_sem,
    store_sem,
):
    offsets, width = grad_mid_out.shape[:2]
    units = (offsets + 1) // 2
    piece = (units + 1) // 2
    moves = []
    for pair in range(2):
        for at, target in enumerate((grad_out_out, grad_mid_out)):
            for first in range(0, units, piece):
                count = min(piece, offsets - units * pair - first, units - first)
                here = (pair, pl.ds(at * units + first, count))
                moves.append((here, target.at[pl.ds(units * pair + first, count)]))
        down_units = grad_down_out.shape[0] // 2
        here = (pair, pl.ds(2 * units, down_units))
        moves.append((here, grad_down_out.at[pl.ds(pair * down_units, down_units)]))
    loads = [
        pltpu.make_async_copy(grads_ref.at[here], held.at[here], load_sem.at[at])
        for at, (here, _) in enumerate(moves)
    ]
    stores = [
        pltpu.make_async_copy(held.at[here], target, store_sem.at[at])
        for at, (here, target) in enumerate(moves)
    ]
    for load in loads:
        load.start()
    features_out[...] = features_ref[...]
    fine_grad_out[...] = fine_grad_ref[...]
    gain_out[...] = gain_ref[...]
    bias_out[...] = bias_ref[...]
    for load, store in zip(loads, stores):
        load.wait()
        store.start()
    for store in stores:
        store.wait()


def per_device(
    dp_size,
    group_size,
    fine_features,
    down_map,
    neighbours,
    voxel_counts,
    down_weight,
    mid_weight,
    out_weight,
    norm_gain,
    norm_bias,
    cotangent,
):
    rows, width = cotangent.shape
    fine_rows, in_width = fine_features.shape
    offsets = neighbours.shape[1]
    down_offsets = down_map.shape[1]
    f32, bf16, i32 = jnp.float32, jnp.bfloat16, jnp.int32
    vmem = pl.BlockSpec(memory_space=pltpu.VMEM)
    smem = pl.BlockSpec(memory_space=pltpu.SMEM)
    hbm = pl.BlockSpec(memory_space=pl.ANY)
    shape = jax.ShapeDtypeStruct
    reduce_here = dp_size == 8 and group_size == 4
    share = 2 if reduce_here else 1
    units = (offsets + 1) // 2 * 2 // share
    chunks = 2 * units + down_offsets * in_width // (share * width)
    grad_rows = chunks * width
    padded = (offsets + 1) // 2 * 2
    features, fine_grad, grads, gain_grad, bias_grad = pl.pallas_call(
        functools.partial(kernel, dp_size, group_size, reduce_here),
        out_shape=(
            shape((rows, width), bf16),
            shape((fine_rows, in_width), bf16),
            shape((share, chunks, width, width) if reduce_here else (grad_rows, width), f32),
            shape(norm_gain.shape, f32),
            shape(norm_bias.shape, f32),
        ),
        in_specs=[vmem, vmem, vmem, smem, hbm, hbm, hbm, vmem, vmem, vmem],
        out_specs=(vmem, vmem, hbm, vmem, vmem),
        scratch_shapes=[
            pltpu.VMEM(down_weight.shape, bf16),
            pltpu.VMEM((padded, width, width), bf16),
            pltpu.VMEM((padded, width, width), bf16),
            pltpu.VMEM((fine_rows, in_width), f32),
            pltpu.VMEM((rows, down_offsets * in_width), bf16),
            pltpu.VMEM((rows // BLOCK, offsets, rows, 128), bf16),
            pltpu.VMEM((GROUP * rows, rows), bf16),
            pltpu.VMEM((rows, GROUP * width), bf16),
            pltpu.VMEM((rows, width), f32),
            pltpu.VMEM((rows, width), bf16),
            pltpu.VMEM((rows, width), bf16),
            pltpu.VMEM((rows, width), f32),
            pltpu.VMEM((rows, width), f32),
            pltpu.VMEM((rows, width), f32),
            pltpu.VMEM((rows, width), bf16),
            pltpu.VMEM((rows, width), bf16),
            pltpu.VMEM((width, rows), bf16),
            pltpu.VMEM((width, rows), bf16),
            pltpu.VMEM((rows, width), f32),
            pltpu.VMEM((128, rows), i32),
            pltpu.VMEM((rows, 128), i32),
            pltpu.VMEM((padded, rows), i32),
            pltpu.VMEM((padded, rows), i32),
            pltpu.VMEM((4, rows, width), f32),
            pltpu.VMEM((4, rows, width), f32),
            pltpu.VMEM((down_offsets * in_width, width), f32),
            pltpu.VMEM((down_offsets * in_width // 2, width), f32),
            pltpu.VMEM((grad_rows, width), f32),
            pltpu.VMEM((2, chunks if reduce_here else 1, width, width), f32),
            pltpu.VMEM((RING * width // 2, width), f32),
            pltpu.VMEM((chunks * width // 8, width), f32),
            pltpu.VMEM((chunks * width // 8, width), f32),
            pltpu.VMEM((chunks * width // 16, width), f32),
            pltpu.VMEM((chunks * width // 16, width), f32),
            pltpu.VMEM((chunks * width // 32, width), f32),
            pltpu.VMEM((chunks * width // 32, width), f32),
            pltpu.VMEM((6, group_size, 8, width // 2), f32),
            pltpu.VMEM((6, dp_size, 8, width // 2), f32),
            pltpu.SemaphoreType.DMA((3,)),
            pltpu.SemaphoreType.DMA((chunks,)),
            pltpu.SemaphoreType.DMA((RING, COPIES)),
            pltpu.SemaphoreType.DMA((RING, COPIES)),
            pltpu.SemaphoreType.DMA((6,)),
            pltpu.SemaphoreType.DMA((6,)),
            pltpu.SemaphoreType.DMA((6, group_size - 1)),
            pltpu.SemaphoreType.DMA((6, group_size - 1)),
            pltpu.SemaphoreType.DMA((6, dp_size - 1)),
            pltpu.SemaphoreType.DMA((6, dp_size - 1)),
        ],
        compiler_params=pltpu.CompilerParams(
            collective_id=0, has_side_effects=True, vmem_limit_bytes=60 * 1024 * 1024
        ),
    )(
        fine_features,
        down_map.T,
        neighbours.T,
        voxel_counts,
        down_weight,
        mid_weight,
        out_weight,
        norm_gain,
        norm_bias,
        cotangent,
    )
    if not reduce_here:
        grads = lax.psum(grads, ("dp", "group"))
        middle, end = offsets * width, 2 * padded * width
        grad_out = grads[:middle].reshape(out_weight.shape)
        grad_mid = grads[padded * width : padded * width + middle].reshape(mid_weight.shape)
        grad_down = grads[end:].reshape(down_weight.shape)
        return (features, fine_grad, grad_down, grad_mid, grad_out, gain_grad, bias_grad)
    features, fine_grad, grad_down, grad_mid, grad_out, gain_grad, bias_grad = pl.pallas_call(
        place_kernel,
        out_shape=(
            shape(features.shape, bf16),
            shape(fine_grad.shape, bf16),
            shape((down_offsets * in_width // width, width, width), f32),
            shape(mid_weight.shape, f32),
            shape(out_weight.shape, f32),
            shape(norm_gain.shape, f32),
            shape(norm_bias.shape, f32),
        ),
        in_specs=[vmem, vmem, hbm, vmem, vmem],
        out_specs=(vmem, vmem, hbm, hbm, hbm, vmem, vmem),
        scratch_shapes=[
            pltpu.VMEM(grads.shape, f32),
            pltpu.SemaphoreType.DMA((10,)),
            pltpu.SemaphoreType.DMA((10,)),
        ],
        compiler_params=pltpu.CompilerParams(vmem_limit_bytes=32 * 1024 * 1024),
    )(features, fine_grad, grads, gain_grad, bias_grad)
    grad_down = grad_down.reshape(down_weight.shape)
    return (features, fine_grad, grad_down, grad_mid, grad_out, gain_grad, bias_grad)


def solution(mesh):
    in_specs = (
        P(("dp", "group"), None),
        P(("dp", "group"), None),
        P(("dp", "group"), None),
        P(("dp", "group")),
        P(),
        P(),
        P(),
        P(),
        P(),
        P(("dp", "group"), None),
    )
    out_specs = (P(("dp", "group"), None), P(("dp", "group"), None), P(), P(), P(), P(), P())
    return jax.shard_map(
        functools.partial(per_device, mesh.shape["dp"], mesh.shape["group"]),
        mesh=mesh,
        in_specs=in_specs,
        out_specs=out_specs,
        check_vma=False,
    )
```

```python
import functools

import jax
import jax.numpy as jnp
from jax import lax
from jax.experimental import pallas as pl
from jax.experimental.pallas import tpu as pltpu
from jax.sharding import PartitionSpec as P

eps_norm = 1e-05
MESH = pl.DeviceIdType.MESH
GROUP = 3
BLOCK = 256
PAIR = 2
COPIES = 14
STAGES = 8
GROUPS = (4, 2, 4)
GAP = 4
DOWN_GAP = 3
LAG = 2
RING = 8


def sigmoid(value):
    return 1.0 / (1.0 + jnp.exp(-value))


def silu_slope(value):
    sigma = sigmoid(value)
    return sigma * (1.0 + value * (1.0 - sigma))


def dot(left, right):
    return jnp.dot(left, right, preferred_element_type=jnp.float32)


def dot_last(left, right):
    return lax.dot_general(
        left, right, (((1,), (1,)), ((), ())), preferred_element_type=jnp.float32
    )


def kernel(
    dp_size,
    group_size,
    reduce_here,
    fine_ref,
    down_rows_ref,
    nb_rows,
    count_ref,
    down_hbm,
    mid_hbm,
    out_hbm,
    gain_ref,
    bias_ref,
    cotangent_ref,
    features_ref,
    fine_grad_ref,
    grads_hbm,
    gain_grad_ref,
    bias_grad_ref,
    w_down,
    w_mid,
    w_out,
    spread_fine,
    cols_down,
    nb_cols,
    pickers,
    columns,
    act_one,
    act_one_b,
    act_two_b,
    hid_one,
    hid_two,
    hid_three,
    held,
    grad_hidden,
    source_t,
    pair_source_t,
    grad_act,
    side,
    side_cols,
    nb_own,
    nb_pair,
    swap_out,
    swap_in,
    down_all,
    down_got,
    grads,
    results,
    from_core,
    from_first_a,
    from_first_b,
    from_second_a,
    from_second_b,
    from_line,
    near,
    far,
    load_sem,
    store_sem,
    sum_send,
    sum_recv,
    swap_send,
    swap_recv,
    near_send,
    near_recv,
    far_send,
    far_recv,
):
    rows, width = cotangent_ref.shape
    offsets = nb_rows.shape[0]
    fine_rows, in_width = fine_ref.shape
    children = fine_rows // rows
    down_offsets = down_rows_ref.shape[0]
    units = (offsets + 1) // 2 * (1 if reduce_here else 2)
    chunks = grads.shape[0]
    dp_me = lax.axis_index("dp")
    group_me = lax.axis_index("group")

    loads = [
        pltpu.make_async_copy(source, target, load_sem.at[at])
        for at, (source, target) in enumerate(
            (
                (down_hbm, w_down),
                (mid_hbm, w_mid.at[pl.ds(0, offsets)]),
                (out_hbm, w_out.at[pl.ds(0, offsets)]),
            )
        )
    ]
    for load in loads:
        load.start()

    barrier = pltpu.get_barrier_semaphore()
    for step in range(1, group_size):
        pl.semaphore_signal(
            barrier,
            inc=1,
            device_id={"group": lax.rem(group_me + step, group_size)},
            device_id_type=MESH,
        )
    for step in range(1, dp_size):
        pl.semaphore_signal(
            barrier,
            inc=1,
            device_id={"dp": lax.rem(dp_me + step, dp_size)},
            device_id_type=MESH,
        )
    pl.semaphore_wait(barrier, group_size + dp_size - 2)

    def share(at, axis, me, size, slots, send, recv):
        copies = []
        for step in range(1, size):
            copies.append(
                pltpu.make_async_remote_copy(
                    src_ref=slots.at[at, me],
                    dst_ref=slots.at[at, me],
                    send_sem=send.at[at, step - 1],
                    recv_sem=recv.at[at, step - 1],
                    device_id={axis: lax.rem(me + step, size)},
                    device_id_type=MESH,
                )
            )
        for copy in copies:
            copy.start()
        return copies

    def exchange(at, block, combine, meanwhile=(None, None)):
        near[at, group_me] = block
        copies = share(at, "group", group_me, group_size, near, near_send, near_recv)
        if meanwhile[0] is not None:
            meanwhile[0]()
        for copy in copies:
            copy.wait()
        far[at, dp_me] = combine([near[at, slot] for slot in range(group_size)])
        copies = share(at, "dp", dp_me, dp_size, far, far_send, far_recv)
        if meanwhile[1] is not None:
            meanwhile[1]()
        for copy in copies:
            copy.wait()
        return combine([far[at, slot] for slot in range(dp_size)])

    lanes = width // 2

    def stack(first, second, third):
        filler = jnp.zeros((2, lanes), jnp.float32)
        return jnp.concatenate([first, second, third, filler], axis=0)

    def fold(value):
        return jnp.concatenate([value[:, :lanes], value[:, lanes:]], axis=0)

    def unfold(value):
        return jnp.concatenate([value[0:1], value[1:2]], axis=1)

    def add_all(blocks):
        total = blocks[0]
        for block in blocks[1:]:
            total = total + block
        return total

    def merge_all(blocks):
        count = add_all([block[4:6] for block in blocks])
        center = add_all([block[4:6] * block[0:2] for block in blocks]) / count
        squares = add_all(
            [
                block[2:4] + block[4:6] * (block[0:2] - center) * (block[0:2] - center)
                for block in blocks
            ]
        )
        return stack(center, squares, count)

    count = count_ref[0]
    own_count = jnp.full((1, width), count.astype(jnp.float32))
    live = lax.broadcasted_iota(jnp.int32, (rows, width), 0) < count

    def norm_stats(at, hidden, meanwhile=(None, None)):
        center = jnp.sum(hidden, axis=0, keepdims=True) / own_count
        centered = jnp.where(live, hidden - center, 0.0)
        squares = jnp.sum(centered * centered, axis=0, keepdims=True)
        merged = exchange(
            at, stack(fold(center), fold(squares), fold(own_count)), merge_all, meanwhile
        )
        total = unfold(merged[4:6])
        scale = lax.rsqrt(unfold(merged[2:4]) / total + eps_norm)
        return unfold(merged[0:2]), scale, total

    def norm_grad(at, norm, incoming, normed, scale, total, meanwhile=(None, None)):
        shift_sum = fold(jnp.sum(incoming, axis=0, keepdims=True))
        scale_sum = fold(jnp.sum(incoming * normed, axis=0, keepdims=True))
        summed = exchange(
            at, stack(shift_sum, scale_sum, jnp.zeros_like(shift_sum)), add_all, meanwhile
        )
        shift_sum, scale_sum = unfold(summed[0:2]), unfold(summed[2:4])
        bias_grad_ref[norm : norm + 1, :] = shift_sum
        gain_grad_ref[norm : norm + 1, :] = scale_sum
        hidden_grad = (
            scale
            * gain_ref[norm : norm + 1, :]
            * (incoming - shift_sum / total - normed * (scale_sum / total))
        )
        return jnp.where(live, hidden_grad, 0.0).astype(jnp.bfloat16)

    def pick(mask):
        return jnp.where(mask, jnp.bfloat16(1), jnp.bfloat16(0))

    def counting(shape, axis):
        return lax.broadcasted_iota(jnp.int32, shape, axis).astype(jnp.float32).astype(jnp.bfloat16)

    def place_columns(count):
        picked = dot(pickers[: count * rows, :], held[...]).astype(jnp.bfloat16)
        for part in range(count):
            columns[:, part * width : (part + 1) * width] = picked[part * rows : (part + 1) * rows]

    def convolve(weight, hidden):
        places = counting((rows, BLOCK), 1)
        places = (places, -1 - places)
        hidden[...] = jnp.zeros_like(hidden)

        def step(at, carry):
            for part in range(GROUP):
                wanted = jnp.concatenate([nb_cols[at * GROUP + part]] * (BLOCK // 128), axis=1)
                for block in range(2):
                    pickers[
                        part * rows : (part + 1) * rows, block * BLOCK : (block + 1) * BLOCK
                    ] = pick(wanted == places[block])
            place_columns(GROUP)
            weights = weight[pl.ds(at * GROUP, GROUP)].reshape(GROUP * width, width)
            hidden[...] += dot(columns[...], weights)
            return carry

        lax.fori_loop(0, offsets // GROUP, step, 0)

    def spread_rows(neighbours, first_offset):
        places = counting((BLOCK, rows), 0)
        for part in range(PAIR):
            wanted = neighbours[pl.ds(first_offset + part, 1), :].astype(jnp.float32)
            for first in range(0, rows, BLOCK):
                here = jnp.broadcast_to(wanted - first, (16, rows)).astype(jnp.bfloat16)
                pickers[part * rows + first : part * rows + first + BLOCK, :] = pick(
                    jnp.concatenate([here] * (BLOCK // 16), axis=0) == places
                )
        place_columns(PAIR)
        return columns[:, : PAIR * width]

    def put(first_unit, at, product, more):
        for part in range(PAIR):
            value = product[:, part * width : (part + 1) * width]
            if reduce_here:
                c = first_unit // PAIR + at
                value = value.reshape(grads.shape[1:4] + (8, width))
                here_rows = slice(8 * part, 8 * part + 8)
                if more:
                    value = value + grads[c, :, :, :, here_rows]
                grads[c, :, :, :, here_rows] = value
            else:
                unit = pl.multiple_of((first_unit + PAIR * at + part) * width, width)
                grads[pl.ds(unit, width), :] = value

    def convolve_back(weight, act_grad, first_unit, own_slot, other_slot):
        def step(first_offset, at, weigh):
            spread = spread_rows(nb_own, first_offset)
            weights = jnp.concatenate(
                [weight[first_offset + part] for part in range(PAIR)], axis=1
            )
            act_grad[...] += dot_last(spread, weights)
            if weigh:
                put(first_unit, at, dot(source_t[...], spread), False)

        def own_offsets(at, carry):
            step(own_offset + PAIR * at, at, True)
            own_slot(at)
            return carry

        def other_offsets(at, carry):
            step(other_offset + PAIR * at, at, False)
            other_slot(at)
            return carry

        lax.fori_loop(0, units // PAIR, own_offsets, 0)
        if reduce_here:
            lax.fori_loop(0, units // PAIR, other_offsets, 0)

    def convolve_pair(first_unit, first_step, last_step, first_slot):
        def step(at, carry):
            spread = spread_rows(nb_pair, own_offset + PAIR * at)
            put(first_unit, at, dot(pair_source_t[...], spread), True)
            slot(first_slot + at)
            return carry

        lax.fori_loop(first_step, last_step, step, 0)

    core, row = lax.rem(group_me, 2), group_me // 2
    column, plane = lax.rem(dp_me, 2), dp_me // 2
    pair, high = lax.rem(plane, 2), plane // 2
    planes = 4
    core_peer = {"group": group_me + 1 - 2 * core}
    row_peer = {"group": group_me + 2 - 4 * row}
    column_peer = {"dp": dp_me + 1 - 2 * column}
    pair_peer = {"dp": dp_me + 2 - 4 * pair}
    cross_peer = {"dp": dp_me + 4 - 8 * high}
    own_offset = units * pair if reduce_here else 0
    other_offset = units * (1 - pair)
    own = pl.ds(2 * core, 2)
    lane_a, lane_b = 2 * core, 2 * core + 1
    kept_row, given_row = pl.ds(2 * row, 2), pl.ds(2 * (1 - row), 2)

    def send(c, number, source, target, peer):
        turn = lax.rem(c, RING)
        return pltpu.make_async_remote_copy(
            src_ref=source,
            dst_ref=target,
            send_sem=sum_send.at[turn, number],
            recv_sem=sum_recv.at[turn, number],
            device_id=peer,
            device_id_type=MESH,
        )

    def copies_of(c, stage):
        part = grads.at[c]
        if stage == 0:
            given = part.at[pl.ds(2 * (1 - core), 2)]
            return [send(c, 0, given, from_core.at[lax.rem(c, RING)], core_peer)]
        if stage == 1:
            return [
                send(c, 1, part.at[lane_a, 1 - column], from_first_a.at[c], column_peer),
                send(c, 2, part.at[lane_b, :, given_row], from_first_b.at[c], row_peer),
            ]
        if stage == 2:
            return [
                send(c, 3, part.at[lane_a, column, given_row], from_second_a.at[c], row_peer),
                send(c, 4, part.at[lane_b, 1 - column, kept_row], from_second_b.at[c], column_peer),
            ]
        if stage == 3:
            given = part.at[own, column, 2 * row + 1 - high]
            return [send(c, 5, given, from_line.at[c], cross_peer)]
        if stage == 4:
            source = part.at[own, column, 2 * row + high]
            target = results.at[pair, c, own, column, 2 * row + high]
            return [
                send(
                    c,
                    5 + step,
                    source,
                    target,
                    {"dp": 2 * lax.rem(plane + step, planes) + column},
                )
                for step in range(1, planes)
            ]
        if stage == 5:
            block_a = results.at[:, c, lane_a, column, kept_row]
            block_b = results.at[:, c, lane_b, column, kept_row]
            return [
                send(c, 9, block_a, block_a, row_peer),
                send(c, 10, block_b, block_b, column_peer),
            ]
        if stage == 6:
            block_a = results.at[:, c, lane_a, column]
            block_b = results.at[:, c, lane_b, :, kept_row]
            return [
                send(c, 11, block_a, block_a, column_peer),
                send(c, 12, block_b, block_b, row_peer),
            ]
        block = results.at[:, c, own]
        return [send(c, 13, block, block, core_peer)]

    def stores_of(c):
        return [
            pltpu.make_async_copy(
                results.at[:, c, :, :, :, pl.ds(8 * unit, 8)],
                grads_hbm.at[:, PAIR * c + unit],
                store_sem.at[c, unit],
            )
            for unit in range(PAIR)
        ]

    def stage_of(c, stage):
        if stage > 0:
            for copy in copies_of(c, stage - 1):
                copy.wait()
        if stage == 1:
            grads[c, own] = grads[c, own] + from_core[lax.rem(c, RING)]
        if stage == 2:
            grads[c, lane_a, column] = grads[c, lane_a, column] + from_first_a[c]
            grads[c, lane_b, :, kept_row] = grads[c, lane_b, :, kept_row] + from_first_b[c]
        if stage == 3:
            grads[c, lane_a, column, kept_row] = grads[c, lane_a, column, kept_row] + from_second_a[c]
            grads[c, lane_b, column, kept_row] = grads[c, lane_b, column, kept_row] + from_second_b[c]
        if stage == 4:
            mine = 2 * row + high
            grads[c, own, column, mine] = grads[c, own, column, mine] + from_line[c]
            results[pair, c, own, column, mine] = grads[c, own, column, mine]
        copies = stores_of(c) if stage == STAGES else copies_of(c, stage)
        for copy in copies:
            copy.start()

    per_weight = units // PAIR
    entries = 2 * per_weight + GAP + DOWN_GAP + 1

    def slot(at):
        if not reduce_here:
            return
        for stage in range(STAGES + 1):
            entry = at - LAG * stage
            second = entry >= per_weight + GAP
            third = entry >= entries - 1
            there_is = (
                ((entry >= 0) & (entry < per_weight))
                | (second & (entry < 2 * per_weight + GAP))
                | (third & (entry < entries))
            )
            if isinstance(at, int):
                if there_is:
                    stage_of(entry - GAP * second - DOWN_GAP * third, stage)
                continue
            c = entry - GAP * second.astype(jnp.int32) - DOWN_GAP * third.astype(jnp.int32)

            @pl.when(there_is)
            def _():
                stage_of(c, stage)

    def slot_when(condition, at):
        @pl.when(condition)
        def _():
            slot(at)

    def no_slot(at):
        pass

    def swap(at, source, target):
        return pltpu.make_async_remote_copy(
            src_ref=source,
            dst_ref=target,
            send_sem=swap_send.at[at],
            recv_sem=swap_recv.at[at],
            device_id=pair_peer,
            device_id_type=MESH,
        )

    def swap_rows(at):
        return swap(at, swap_out.at[at % 2], swap_in.at[at])

    def start_rows(at, value):
        if reduce_here:
            if at >= 2:
                swap_rows(at - 2).wait_send()
            swap_out[at % 2] = value.astype(jnp.float32)
            swap_rows(at).start()

    side[...] = jnp.zeros_like(side)
    side[:offsets, :] = nb_rows[...]
    side[offsets : offsets + down_offsets, :] = down_rows_ref[...]
    side_cols[...] = side[...].T
    nb_own[...] = jnp.full_like(nb_own, rows)
    nb_own[:offsets, :] = nb_rows[...]
    swap_neighbours = swap(4, nb_own, nb_pair)
    if reduce_here:
        swap_neighbours.start()
    for weight in (w_mid, w_out):
        weight[offsets:] = jnp.zeros_like(weight[offsets:])

    spread_fine[...] = fine_ref[...].astype(jnp.float32)
    for k in range(down_offsets):
        child = spread_fine[pl.ds(k % children, rows, stride=children), :]
        there = side_cols[:, offsets + k : offsets + k + 1] < fine_rows
        cols_down[:, k * in_width : (k + 1) * in_width] = jnp.where(there, child, 0.0).astype(
            jnp.bfloat16
        )
    loads[0].wait()
    hid_one[...] = dot(cols_down[...], w_down[...].reshape(down_offsets * in_width, width))

    def spread_neighbours():
        for k in range(offsets):
            wanted = side_cols[:, k : k + 1]
            code = jnp.where(
                wanted < BLOCK, wanted, jnp.where(wanted < rows, BLOCK - 1 - wanted, 4 * BLOCK)
            )
            nb_cols[k] = jnp.broadcast_to(code, (rows, 128)).astype(jnp.float32).astype(jnp.bfloat16)

    center_one, scale_one, total = norm_stats(0, hid_one[...], (spread_neighbours, None))

    def pre_one():
        normed = (hid_one[...] - center_one) * scale_one
        return normed, normed * gain_ref[0:1, :] + bias_ref[0:1, :]

    _, pre = pre_one()
    act_one[...] = jnp.where(live, pre * sigmoid(pre), 0.0)
    act_one_b[...] = act_one[...].astype(jnp.bfloat16)
    start_rows(0, act_one_b[...])
    loads[1].wait()
    held[...] = act_one_b[...]
    convolve(w_mid, hid_two)
    center_two, scale_two, _ = norm_stats(1, hid_two[...])

    def pre_two():
        normed = (hid_two[...] - center_two) * scale_two
        return normed, normed * gain_ref[1:2, :] + bias_ref[1:2, :]

    _, pre = pre_two()
    act_two_b[...] = jnp.where(live, pre * sigmoid(pre), 0.0).astype(jnp.bfloat16)
    start_rows(1, act_two_b[...])
    loads[2].wait()
    held[...] = act_two_b[...]
    convolve(w_out, hid_three)
    center_three, scale_three, _ = norm_stats(2, hid_three[...])
    normed_three = (hid_three[...] - center_three) * scale_three
    summed = (
        jnp.where(live, normed_three * gain_ref[2:3, :] + bias_ref[2:3, :], 0.0) + act_one[...]
    )
    sigma = sigmoid(summed)
    features_ref[...] = jnp.where(live, summed * sigma, 0.0).astype(jnp.bfloat16)

    slope = sigma * (1.0 + summed * (1.0 - sigma))
    act_one[...] = jnp.where(live, cotangent_ref[...].astype(jnp.float32) * slope, 0.0)
    grad_hidden[...] = norm_grad(3, 2, act_one[...], normed_three, scale_three, total)
    start_rows(2, grad_hidden[...])
    held[...] = grad_hidden[...]
    grad_act[...] = jnp.zeros_like(grad_act)
    steps = units // PAIR

    def receive(source_at, hidden_at):
        swap_rows(source_at).wait_recv()
        pair_source_t[...] = swap_in[source_at].astype(jnp.bfloat16).T
        swap_rows(hidden_at).wait_recv()
        held[...] = swap_in[hidden_at].astype(jnp.bfloat16)

    def pair_halves(first_unit, first_slot):
        middle = (steps + 1) // 2
        return (
            lambda: convolve_pair(first_unit, 0, middle, first_slot),
            lambda: convolve_pair(first_unit, middle, steps, first_slot),
        )

    nothing = (None, None)
    source_t[...] = act_two_b[...].T
    convolve_back(w_out, grad_act, 0, no_slot, no_slot)
    normed, pre = pre_two()
    incoming = jnp.where(live, grad_act[...] * silu_slope(pre), 0.0)
    if reduce_here:
        swap_neighbours.wait()
        receive(1, 2)
    beside = pair_halves(0, 0) if reduce_here else nothing
    grad_hidden[...] = norm_grad(4, 1, incoming, normed, scale_two, total, beside)
    start_rows(3, grad_hidden[...])
    held[...] = grad_hidden[...]
    grad_act[...] = act_one[...]
    source_t[...] = act_one_b[...].T
    early = (GAP + 1) // 2
    convolve_back(
        w_mid,
        grad_act,
        units,
        lambda at: slot_when((at >= 1) & (at < 1 + early), steps + at - 1),
        lambda at: slot_when((at >= 1) & (at < 1 + GAP - early), steps + early + at - 1),
    )
    normed, pre = pre_one()
    incoming = jnp.where(live, grad_act[...] * silu_slope(pre), 0.0)
    if reduce_here:
        receive(0, 3)
    beside = pair_halves(units, steps + GAP) if reduce_here else nothing
    grad_hidden[...] = norm_grad(5, 0, incoming, normed, scale_one, total, beside)
    done = 2 * steps + GAP
    down_rows = down_offsets * in_width
    if reduce_here:
        down_all[...] = dot(cols_down[...].T, grad_hidden[...])
        kept = down_rows // 2
        swap_down = swap(
            5, down_all.at[pl.ds(pl.multiple_of(kept * (1 - pair), kept), kept), :], down_got
        )
        swap_down.start()
    else:
        grads[2 * units * width :, :] = dot(cols_down[...].T, grad_hidden[...])
    slot(done)
    for child in range(children):
        total_child = jnp.zeros((rows, in_width), jnp.float32)
        for k in range(child, down_offsets, children):
            there = side_cols[:, offsets + k : offsets + k + 1] < fine_rows
            total_child += jnp.where(there, dot_last(grad_hidden[...], w_down[k]), 0.0)
        spread_fine[pl.ds(child, rows, stride=children), :] = total_child
    fine_grad_ref[...] = spread_fine[...].astype(jnp.bfloat16)

    if reduce_here:

        def rest(at, carry):
            slot(at)
            return carry

        lax.fori_loop(done + 1, done + DOWN_GAP, rest, 0)
        swap_down.wait()
        for at in (2, 3):
            swap_rows(at).wait_send()
        for part in range(PAIR):
            total_down = (
                down_all[pl.ds(pl.multiple_of(kept * pair + part * width, width), width), :]
                + down_got[part * width : (part + 1) * width, :]
            )
            grads[chunks - 1, :, :, :, 8 * part : 8 * part + 8] = total_down.reshape(
                grads.shape[1:4] + (8, width)
            )
        lax.fori_loop(done + DOWN_GAP, entries + LAG * STAGES, rest, 0)

        def finish(c, carry):
            for store in stores_of(c):
                store.wait()
            return carry

        lax.fori_loop(0, chunks, finish, 0)
    else:
        store = pltpu.make_async_copy(grads, grads_hbm, store_sem.at[0, 0])
        store.start()
        store.wait()


def place_kernel(
    features_ref,
    fine_grad_ref,
    grads_ref,
    gain_ref,
    bias_ref,
    features_out,
    fine_grad_out,
    grad_down_out,
    grad_mid_out,
    grad_out_out,
    gain_out,
    bias_out,
    held,
    load_sem,
    store_sem,
):
    offsets, width = grad_mid_out.shape[:2]
    units = (offsets + 1) // 2
    piece = (units + 1) // 2
    moves = []
    for pair in range(2):
        for at, target in enumerate((grad_out_out, grad_mid_out)):
            for first in range(0, units, piece):
                count = min(piece, offsets - units * pair - first, units - first)
                here = (pair, pl.ds(at * units + first, count))
                moves.append((here, target.at[pl.ds(units * pair + first, count)]))
        down_units = grad_down_out.shape[0] // 2
        here = (pair, pl.ds(2 * units, down_units))
        moves.append((here, grad_down_out.at[pl.ds(pair * down_units, down_units)]))
    loads = [
        pltpu.make_async_copy(grads_ref.at[here], held.at[here], load_sem.at[at])
        for at, (here, _) in enumerate(moves)
    ]
    stores = [
        pltpu.make_async_copy(held.at[here], target, store_sem.at[at])
        for at, (here, target) in enumerate(moves)
    ]
    for load in loads:
        load.start()
    features_out[...] = features_ref[...]
    fine_grad_out[...] = fine_grad_ref[...]
    gain_out[...] = gain_ref[...]
    bias_out[...] = bias_ref[...]
    for load, store in zip(loads, stores):
        load.wait()
        store.start()
    for store in stores:
        store.wait()


def per_device(
    dp_size,
    group_size,
    fine_features,
    down_map,
    neighbours,
    voxel_counts,
    down_weight,
    mid_weight,
    out_weight,
    norm_gain,
    norm_bias,
    cotangent,
):
    rows, width = cotangent.shape
    fine_rows, in_width = fine_features.shape
    offsets = neighbours.shape[1]
    down_offsets = down_map.shape[1]
    f32, bf16, i32 = jnp.float32, jnp.bfloat16, jnp.int32
    vmem = pl.BlockSpec(memory_space=pltpu.VMEM)
    smem = pl.BlockSpec(memory_space=pltpu.SMEM)
    hbm = pl.BlockSpec(memory_space=pl.ANY)
    shape = jax.ShapeDtypeStruct
    reduce_here = dp_size == 8 and group_size == 4
    share = 2 if reduce_here else 1
    units = (offsets + 1) // 2 * 2 // share
    all_units = 2 * units + down_offsets * in_width // (share * width)
    grad_rows = all_units * width
    chunks = all_units // PAIR
    padded = (offsets + 1) // 2 * 2
    features, fine_grad, grads, gain_grad, bias_grad = pl.pallas_call(
        functools.partial(kernel, dp_size, group_size, reduce_here),
        out_shape=(
            shape((rows, width), bf16),
            shape((fine_rows, in_width), bf16),
            shape((2, all_units, *GROUPS, 8, width) if reduce_here else (grad_rows, width), f32),
            shape(norm_gain.shape, f32),
            shape(norm_bias.shape, f32),
        ),
        in_specs=[vmem, vmem, vmem, smem, hbm, hbm, hbm, vmem, vmem, vmem],
        out_specs=(vmem, vmem, hbm, vmem, vmem),
        scratch_shapes=[
            pltpu.VMEM(down_weight.shape, bf16),
            pltpu.VMEM((padded, width, width), bf16),
            pltpu.VMEM((padded, width, width), bf16),
            pltpu.VMEM((fine_rows, in_width), f32),
            pltpu.VMEM((rows, down_offsets * in_width), bf16),
            pltpu.VMEM((offsets, rows, 128), bf16),
            pltpu.VMEM((GROUP * rows, rows), bf16),
            pltpu.VMEM((rows, GROUP * width), bf16),
            pltpu.VMEM((rows, width), f32),
            pltpu.VMEM((rows, width), bf16),
            pltpu.VMEM((rows, width), bf16),
            pltpu.VMEM((rows, width), f32),
            pltpu.VMEM((rows, width), f32),
            pltpu.VMEM((rows, width), f32),
            pltpu.VMEM((rows, width), bf16),
            pltpu.VMEM((rows, width), bf16),
            pltpu.VMEM((width, rows), bf16),
            pltpu.VMEM((width, rows), bf16),
            pltpu.VMEM((rows, width), f32),
            pltpu.VMEM((128, rows), i32),
            pltpu.VMEM((rows, 128), i32),
            pltpu.VMEM((padded, rows), i32),
            pltpu.VMEM((padded, rows), i32),
            pltpu.VMEM((2, rows, width), f32),
            pltpu.VMEM((4, rows, width), f32),
            pltpu.VMEM((down_offsets * in_width, width), f32),
            pltpu.VMEM((down_offsets * in_width // 2, width), f32),
            pltpu.VMEM(
                (chunks, *GROUPS, 8 * PAIR, width) if reduce_here else (grad_rows, width), f32
            ),
            pltpu.VMEM((2, chunks if reduce_here else 1, *GROUPS, 8 * PAIR, width), f32),
            pltpu.VMEM((RING, 2, *GROUPS[1:], 8 * PAIR, width), f32),
            pltpu.VMEM((chunks, GROUPS[2], 8 * PAIR, width), f32),
            pltpu.VMEM((chunks, GROUPS[1], 2, 8 * PAIR, width), f32),
            pltpu.VMEM((chunks, 2, 8 * PAIR, width), f32),
            pltpu.VMEM((chunks, 2, 8 * PAIR, width), f32),
            pltpu.VMEM((chunks, 2, 8 * PAIR, width), f32),
            pltpu.VMEM((6, group_size, 8, width // 2), f32),
            pltpu.VMEM((6, dp_size, 8, width // 2), f32),
            pltpu.SemaphoreType.DMA((3,)),
            pltpu.SemaphoreType.DMA((chunks, PAIR)),
            pltpu.SemaphoreType.DMA((RING, COPIES)),
            pltpu.SemaphoreType.DMA((RING, COPIES)),
            pltpu.SemaphoreType.DMA((6,)),
            pltpu.SemaphoreType.DMA((6,)),
            pltpu.SemaphoreType.DMA((6, group_size - 1)),
            pltpu.SemaphoreType.DMA((6, group_size - 1)),
            pltpu.SemaphoreType.DMA((6, dp_size - 1)),
            pltpu.SemaphoreType.DMA((6, dp_size - 1)),
        ],
        compiler_params=pltpu.CompilerParams(
            collective_id=0, has_side_effects=True, vmem_limit_bytes=60 * 1024 * 1024
        ),
    )(
        fine_features,
        down_map.T,
        neighbours.T,
        voxel_counts,
        down_weight,
        mid_weight,
        out_weight,
        norm_gain,
        norm_bias,
        cotangent,
    )
    if not reduce_here:
        grads = lax.psum(grads, ("dp", "group"))
        middle, end = offsets * width, 2 * padded * width
        grad_out = grads[:middle].reshape(out_weight.shape)
        grad_mid = grads[padded * width : padded * width + middle].reshape(mid_weight.shape)
        grad_down = grads[end:].reshape(down_weight.shape)
        return (features, fine_grad, grad_down, grad_mid, grad_out, gain_grad, bias_grad)
    grads = grads.reshape(2, all_units, width, width)
    features, fine_grad, grad_down, grad_mid, grad_out, gain_grad, bias_grad = pl.pallas_call(
        place_kernel,
        out_shape=(
            shape(features.shape, bf16),
            shape(fine_grad.shape, bf16),
            shape((down_offsets * in_width // width, width, width), f32),
            shape(mid_weight.shape, f32),
            shape(out_weight.shape, f32),
            shape(norm_gain.shape, f32),
            shape(norm_bias.shape, f32),
        ),
        in_specs=[vmem, vmem, hbm, vmem, vmem],
        out_specs=(vmem, vmem, hbm, hbm, hbm, vmem, vmem),
        scratch_shapes=[
            pltpu.VMEM(grads.shape, f32),
            pltpu.SemaphoreType.DMA((10,)),
            pltpu.SemaphoreType.DMA((10,)),
        ],
        compiler_params=pltpu.CompilerParams(vmem_limit_bytes=32 * 1024 * 1024),
    )(features, fine_grad, grads, gain_grad, bias_grad)
    grad_down = grad_down.reshape(down_weight.shape)
    return (features, fine_grad, grad_down, grad_mid, grad_out, gain_grad, bias_grad)


def solution(mesh):
    in_specs = (
        P(("dp", "group"), None),
        P(("dp", "group"), None),
        P(("dp", "group"), None),
        P(("dp", "group")),
        P(),
        P(),
        P(),
        P(),
        P(),
        P(("dp", "group"), None),
    )
    out_specs = (P(("dp", "group"), None), P(("dp", "group"), None), P(), P(), P(), P(), P())
    return jax.shard_map(
        functools.partial(per_device, mesh.shape["dp"], mesh.shape["group"]),
        mesh=mesh,
        in_specs=in_specs,
        out_specs=out_specs,
        check_vma=False,
    )
```

```python
import functools

import jax
import jax.numpy as jnp
from jax import lax
from jax.experimental import pallas as pl
from jax.experimental.pallas import tpu as pltpu
from jax.sharding import PartitionSpec as P

eps_norm = 1e-05
MESH = pl.DeviceIdType.MESH
GROUP = 3
BLOCK = 256
PAIR = 2
COPIES = 14
STAGES = 8
GROUPS = (4, 2, 4)
LAG = 2
RING = 8


def sigmoid(value):
    return 1.0 / (1.0 + jnp.exp(-value))


def silu_slope(value):
    sigma = sigmoid(value)
    return sigma * (1.0 + value * (1.0 - sigma))


def dot(left, right):
    return jnp.dot(left, right, preferred_element_type=jnp.float32)


def dot_last(left, right):
    return lax.dot_general(
        left, right, (((1,), (1,)), ((), ())), preferred_element_type=jnp.float32
    )


def kernel(
    dp_size,
    group_size,
    reduce_here,
    fine_ref,
    down_rows_ref,
    nb_rows,
    count_ref,
    down_hbm,
    mid_hbm,
    out_hbm,
    gain_ref,
    bias_ref,
    cotangent_ref,
    features_ref,
    fine_grad_ref,
    grads_hbm,
    gain_grad_ref,
    bias_grad_ref,
    w_down,
    w_mid,
    w_out,
    spread_fine,
    cols_down,
    nb_cols,
    pickers,
    columns,
    act_one,
    act_one_b,
    act_two_b,
    hid_one,
    hid_two,
    hid_three,
    held,
    grad_hidden,
    source_t,
    pair_source_t,
    grad_act,
    side,
    side_cols,
    nb_own,
    nb_pair,
    swap_out,
    swap_in,
    down_all,
    down_got,
    grads,
    results,
    from_core,
    from_first_a,
    from_first_b,
    from_second_a,
    from_second_b,
    from_line,
    near,
    far,
    load_sem,
    store_sem,
    sum_send,
    sum_recv,
    swap_send,
    swap_recv,
    near_send,
    near_recv,
    far_send,
    far_recv,
):
    rows, width = cotangent_ref.shape
    offsets = nb_rows.shape[0]
    fine_rows, in_width = fine_ref.shape
    children = fine_rows // rows
    down_offsets = down_rows_ref.shape[0]
    units = (offsets + 1) // 2 * (1 if reduce_here else 2)
    chunks = grads.shape[0]
    dp_me = lax.axis_index("dp")
    group_me = lax.axis_index("group")

    loads = [
        pltpu.make_async_copy(source, target, load_sem.at[at])
        for at, (source, target) in enumerate(
            (
                (down_hbm, w_down),
                (mid_hbm, w_mid.at[pl.ds(0, offsets)]),
                (out_hbm, w_out.at[pl.ds(0, offsets)]),
            )
        )
    ]
    for load in loads:
        load.start()

    barrier = pltpu.get_barrier_semaphore()
    for step in range(1, group_size):
        pl.semaphore_signal(
            barrier,
            inc=1,
            device_id={"group": lax.rem(group_me + step, group_size)},
            device_id_type=MESH,
        )
    for step in range(1, dp_size):
        pl.semaphore_signal(
            barrier,
            inc=1,
            device_id={"dp": lax.rem(dp_me + step, dp_size)},
            device_id_type=MESH,
        )
    pl.semaphore_wait(barrier, group_size + dp_size - 2)

    def share(at, axis, me, size, slots, send, recv):
        copies = []
        for step in range(1, size):
            copies.append(
                pltpu.make_async_remote_copy(
                    src_ref=slots.at[at, me],
                    dst_ref=slots.at[at, me],
                    send_sem=send.at[at, step - 1],
                    recv_sem=recv.at[at, step - 1],
                    device_id={axis: lax.rem(me + step, size)},
                    device_id_type=MESH,
                )
            )
        for copy in copies:
            copy.start()
        return copies

    def exchange(at, block, combine, meanwhile=(None, None)):
        near[at, group_me] = block
        copies = share(at, "group", group_me, group_size, near, near_send, near_recv)
        if meanwhile[0] is not None:
            meanwhile[0]()
        for copy in copies:
            copy.wait()
        far[at, dp_me] = combine([near[at, slot] for slot in range(group_size)])
        copies = share(at, "dp", dp_me, dp_size, far, far_send, far_recv)
        if meanwhile[1] is not None:
            meanwhile[1]()
        for copy in copies:
            copy.wait()
        return combine([far[at, slot] for slot in range(dp_size)])

    lanes = width // 2

    def stack(first, second, third):
        filler = jnp.zeros((2, lanes), jnp.float32)
        return jnp.concatenate([first, second, third, filler], axis=0)

    def fold(value):
        return jnp.concatenate([value[:, :lanes], value[:, lanes:]], axis=0)

    def unfold(value):
        return jnp.concatenate([value[0:1], value[1:2]], axis=1)

    def add_all(blocks):
        total = blocks[0]
        for block in blocks[1:]:
            total = total + block
        return total

    def merge_all(blocks):
        count = add_all([block[4:6] for block in blocks])
        center = add_all([block[4:6] * block[0:2] for block in blocks]) / count
        squares = add_all(
            [
                block[2:4] + block[4:6] * (block[0:2] - center) * (block[0:2] - center)
                for block in blocks
            ]
        )
        return stack(center, squares, count)

    count = count_ref[0]
    own_count = jnp.full((1, width), count.astype(jnp.float32))
    live = lax.broadcasted_iota(jnp.int32, (rows, width), 0) < count

    def norm_stats(at, hidden, meanwhile=(None, None)):
        center = jnp.sum(hidden, axis=0, keepdims=True) / own_count
        centered = jnp.where(live, hidden - center, 0.0)
        squares = jnp.sum(centered * centered, axis=0, keepdims=True)
        merged = exchange(
            at, stack(fold(center), fold(squares), fold(own_count)), merge_all, meanwhile
        )
        total = unfold(merged[4:6])
        scale = lax.rsqrt(unfold(merged[2:4]) / total + eps_norm)
        return unfold(merged[0:2]), scale, total

    def norm_grad(at, norm, incoming, normed, scale, total, meanwhile=(None, None)):
        shift_sum = fold(jnp.sum(incoming, axis=0, keepdims=True))
        scale_sum = fold(jnp.sum(incoming * normed, axis=0, keepdims=True))
        summed = exchange(
            at, stack(shift_sum, scale_sum, jnp.zeros_like(shift_sum)), add_all, meanwhile
        )
        shift_sum, scale_sum = unfold(summed[0:2]), unfold(summed[2:4])
        bias_grad_ref[norm : norm + 1, :] = shift_sum
        gain_grad_ref[norm : norm + 1, :] = scale_sum
        hidden_grad = (
            scale
            * gain_ref[norm : norm + 1, :]
            * (incoming - shift_sum / total - normed * (scale_sum / total))
        )
        return jnp.where(live, hidden_grad, 0.0).astype(jnp.bfloat16)

    def pick(mask):
        return jnp.where(mask, jnp.bfloat16(1), jnp.bfloat16(0))

    def counting(shape, axis):
        return lax.broadcasted_iota(jnp.int32, shape, axis).astype(jnp.float32).astype(jnp.bfloat16)

    def place_columns(count):
        picked = dot(pickers[: count * rows, :], held[...]).astype(jnp.bfloat16)
        for part in range(count):
            columns[:, part * width : (part + 1) * width] = picked[part * rows : (part + 1) * rows]

    def convolve(weight, hidden):
        places = counting((rows, BLOCK), 1)
        places = (places, -1 - places)
        hidden[...] = jnp.zeros_like(hidden)

        def step(at, carry):
            for part in range(GROUP):
                wanted = jnp.concatenate([nb_cols[at * GROUP + part]] * (BLOCK // 128), axis=1)
                for block in range(2):
                    pickers[
                        part * rows : (part + 1) * rows, block * BLOCK : (block + 1) * BLOCK
                    ] = pick(wanted == places[block])
            place_columns(GROUP)
            weights = weight[pl.ds(at * GROUP, GROUP)].reshape(GROUP * width, width)
            hidden[...] += dot(columns[...], weights)
            return carry

        lax.fori_loop(0, offsets // GROUP, step, 0)

    def spread_rows(neighbours, first_offset):
        places = counting((BLOCK, rows), 0)
        for part in range(PAIR):
            wanted = neighbours[pl.ds(first_offset + part, 1), :].astype(jnp.float32)
            for first in range(0, rows, BLOCK):
                here = jnp.broadcast_to(wanted - first, (16, rows)).astype(jnp.bfloat16)
                pickers[part * rows + first : part * rows + first + BLOCK, :] = pick(
                    jnp.concatenate([here] * (BLOCK // 16), axis=0) == places
                )
        place_columns(PAIR)
        return columns[:, : PAIR * width]

    def put(first_unit, at, product, more):
        for part in range(PAIR):
            value = product[:, part * width : (part + 1) * width]
            if reduce_here:
                c = first_unit // PAIR + at
                value = value.reshape(grads.shape[1:4] + (8, width))
                here_rows = slice(8 * part, 8 * part + 8)
                if more:
                    value = value + grads[c, :, :, :, here_rows]
                grads[c, :, :, :, here_rows] = value
            else:
                unit = pl.multiple_of((first_unit + PAIR * at + part) * width, width)
                grads[pl.ds(unit, width), :] = value

    def convolve_back(weight, act_grad, first_unit, own_slot, other_slot):
        def step(first_offset, at, weigh):
            spread = spread_rows(nb_own, first_offset)
            weights = jnp.concatenate(
                [weight[first_offset + part] for part in range(PAIR)], axis=1
            )
            act_grad[...] += dot_last(spread, weights)
            if weigh:
                put(first_unit, at, dot(source_t[...], spread), False)

        def own_offsets(at, carry):
            step(own_offset + PAIR * at, at, True)
            own_slot(at)
            return carry

        def other_offsets(at, carry):
            step(other_offset + PAIR * at, at, False)
            other_slot(at)
            return carry

        lax.fori_loop(0, units // PAIR, own_offsets, 0)
        if reduce_here:
            lax.fori_loop(0, units // PAIR, other_offsets, 0)

    def convolve_pair(first_unit, first_step, last_step, first_slot):
        def step(at, carry):
            spread = spread_rows(nb_pair, own_offset + PAIR * at)
            put(first_unit, at, dot(pair_source_t[...], spread), True)
            slot_when(lax.rem(at, 3) == 0, first_slot + at // 3)
            return carry

        lax.fori_loop(first_step, last_step, step, 0)

    core, row = lax.rem(group_me, 2), group_me // 2
    column, plane = lax.rem(dp_me, 2), dp_me // 2
    pair, high = lax.rem(plane, 2), plane // 2
    planes = 4
    core_peer = {"group": group_me + 1 - 2 * core}
    row_peer = {"group": group_me + 2 - 4 * row}
    column_peer = {"dp": dp_me + 1 - 2 * column}
    pair_peer = {"dp": dp_me + 2 - 4 * pair}
    cross_peer = {"dp": dp_me + 4 - 8 * high}
    own_offset = units * pair if reduce_here else 0
    other_offset = units * (1 - pair)
    own = pl.ds(2 * core, 2)
    lane_a, lane_b = 2 * core, 2 * core + 1
    kept_row, given_row = pl.ds(2 * row, 2), pl.ds(2 * (1 - row), 2)

    def send(c, number, source, target, peer):
        turn = lax.rem(c, RING)
        return pltpu.make_async_remote_copy(
            src_ref=source,
            dst_ref=target,
            send_sem=sum_send.at[turn, number],
            recv_sem=sum_recv.at[turn, number],
            device_id=peer,
            device_id_type=MESH,
        )

    def copies_of(c, stage):
        part = grads.at[c]
        if stage == 0:
            given = part.at[pl.ds(2 * (1 - core), 2)]
            return [send(c, 0, given, from_core.at[lax.rem(c, RING)], core_peer)]
        if stage == 1:
            return [
                send(c, 1, part.at[lane_a, 1 - column], from_first_a.at[c], column_peer),
                send(c, 2, part.at[lane_b, :, given_row], from_first_b.at[c], row_peer),
            ]
        if stage == 2:
            return [
                send(c, 3, part.at[lane_a, column, given_row], from_second_a.at[c], row_peer),
                send(c, 4, part.at[lane_b, 1 - column, kept_row], from_second_b.at[c], column_peer),
            ]
        if stage == 3:
            given = part.at[own, column, 2 * row + 1 - high]
            return [send(c, 5, given, from_line.at[c], cross_peer)]
        if stage == 4:
            source = part.at[own, column, 2 * row + high]
            target = results.at[pair, c, own, column, 2 * row + high]
            return [
                send(
                    c,
                    5 + step,
                    source,
                    target,
                    {"dp": 2 * lax.rem(plane + step, planes) + column},
                )
                for step in range(1, planes)
            ]
        if stage == 5:
            block_a = results.at[:, c, lane_a, column, kept_row]
            block_b = results.at[:, c, lane_b, column, kept_row]
            return [
                send(c, 9, block_a, block_a, row_peer),
                send(c, 10, block_b, block_b, column_peer),
            ]
        if stage == 6:
            block_a = results.at[:, c, lane_a, column]
            block_b = results.at[:, c, lane_b, :, kept_row]
            return [
                send(c, 11, block_a, block_a, column_peer),
                send(c, 12, block_b, block_b, row_peer),
            ]
        block = results.at[:, c, own]
        return [send(c, 13, block, block, core_peer)]

    def stores_of(c):
        return [
            pltpu.make_async_copy(
                results.at[:, c, :, :, :, pl.ds(8 * unit, 8)],
                grads_hbm.at[:, PAIR * c + unit],
                store_sem.at[c, unit],
            )
            for unit in range(PAIR)
        ]

    def stage_of(c, stage):
        if stage > 0:
            for copy in copies_of(c, stage - 1):
                copy.wait()
        if stage == 1:
            grads[c, own] = grads[c, own] + from_core[lax.rem(c, RING)]
        if stage == 2:
            grads[c, lane_a, column] = grads[c, lane_a, column] + from_first_a[c]
            grads[c, lane_b, :, kept_row] = grads[c, lane_b, :, kept_row] + from_first_b[c]
        if stage == 3:
            grads[c, lane_a, column, kept_row] = grads[c, lane_a, column, kept_row] + from_second_a[c]
            grads[c, lane_b, column, kept_row] = grads[c, lane_b, column, kept_row] + from_second_b[c]
        if stage == 4:
            mine = 2 * row + high
            grads[c, own, column, mine] = grads[c, own, column, mine] + from_line[c]
            results[pair, c, own, column, mine] = grads[c, own, column, mine]
        copies = stores_of(c) if stage == STAGES else copies_of(c, stage)
        for copy in copies:
            copy.start()

    def slot(at):
        if not reduce_here:
            return
        for stage in range(STAGES + 1):
            c = at - LAG * stage
            if isinstance(at, int):
                if 0 <= c < chunks:
                    stage_of(c, stage)
                continue

            @pl.when((c >= 0) & (c < chunks))
            def _():
                stage_of(c, stage)

    def slot_when(condition, at):
        @pl.when(condition)
        def _():
            slot(at)

    def no_slot(at):
        pass

    def swap(at, source, target):
        return pltpu.make_async_remote_copy(
            src_ref=source,
            dst_ref=target,
            send_sem=swap_send.at[at],
            recv_sem=swap_recv.at[at],
            device_id=pair_peer,
            device_id_type=MESH,
        )

    def swap_rows(at):
        return swap(at, swap_out.at[at % 2], swap_in.at[at])

    def start_rows(at, value):
        if reduce_here:
            if at >= 2:
                swap_rows(at - 2).wait_send()
            swap_out[at % 2] = value.astype(jnp.float32)
            swap_rows(at).start()

    side[...] = jnp.zeros_like(side)
    side[:offsets, :] = nb_rows[...]
    side[offsets : offsets + down_offsets, :] = down_rows_ref[...]
    side_cols[...] = side[...].T
    nb_own[...] = jnp.full_like(nb_own, rows)
    nb_own[:offsets, :] = nb_rows[...]
    swap_neighbours = swap(4, nb_own, nb_pair)
    if reduce_here:
        swap_neighbours.start()
    for weight in (w_mid, w_out):
        weight[offsets:] = jnp.zeros_like(weight[offsets:])

    spread_fine[...] = fine_ref[...].astype(jnp.float32)
    for k in range(down_offsets):
        child = spread_fine[pl.ds(k % children, rows, stride=children), :]
        there = side_cols[:, offsets + k : offsets + k + 1] < fine_rows
        cols_down[:, k * in_width : (k + 1) * in_width] = jnp.where(there, child, 0.0).astype(
            jnp.bfloat16
        )
    loads[0].wait()
    hid_one[...] = dot(cols_down[...], w_down[...].reshape(down_offsets * in_width, width))

    def spread_neighbours():
        for k in range(offsets):
            wanted = side_cols[:, k : k + 1]
            code = jnp.where(
                wanted < BLOCK, wanted, jnp.where(wanted < rows, BLOCK - 1 - wanted, 4 * BLOCK)
            )
            nb_cols[k] = jnp.broadcast_to(code, (rows, 128)).astype(jnp.float32).astype(jnp.bfloat16)

    center_one, scale_one, total = norm_stats(0, hid_one[...], (spread_neighbours, None))

    def pre_one():
        normed = (hid_one[...] - center_one) * scale_one
        return normed, normed * gain_ref[0:1, :] + bias_ref[0:1, :]

    _, pre = pre_one()
    act_one[...] = jnp.where(live, pre * sigmoid(pre), 0.0)
    act_one_b[...] = act_one[...].astype(jnp.bfloat16)
    start_rows(0, act_one_b[...])
    loads[1].wait()
    held[...] = act_one_b[...]
    convolve(w_mid, hid_two)
    center_two, scale_two, _ = norm_stats(1, hid_two[...])

    def pre_two():
        normed = (hid_two[...] - center_two) * scale_two
        return normed, normed * gain_ref[1:2, :] + bias_ref[1:2, :]

    _, pre = pre_two()
    act_two_b[...] = jnp.where(live, pre * sigmoid(pre), 0.0).astype(jnp.bfloat16)
    start_rows(1, act_two_b[...])
    loads[2].wait()
    held[...] = act_two_b[...]
    convolve(w_out, hid_three)
    center_three, scale_three, _ = norm_stats(2, hid_three[...])
    normed_three = (hid_three[...] - center_three) * scale_three
    summed = (
        jnp.where(live, normed_three * gain_ref[2:3, :] + bias_ref[2:3, :], 0.0) + act_one[...]
    )
    sigma = sigmoid(summed)
    features_ref[...] = jnp.where(live, summed * sigma, 0.0).astype(jnp.bfloat16)

    slope = sigma * (1.0 + summed * (1.0 - sigma))
    act_one[...] = jnp.where(live, cotangent_ref[...].astype(jnp.float32) * slope, 0.0)
    grad_hidden[...] = norm_grad(3, 2, act_one[...], normed_three, scale_three, total)
    start_rows(2, grad_hidden[...])
    held[...] = grad_hidden[...]
    grad_act[...] = jnp.zeros_like(grad_act)
    steps = units // PAIR

    def receive(source_at, hidden_at):
        swap_rows(source_at).wait_recv()
        pair_source_t[...] = swap_in[source_at].astype(jnp.bfloat16).T
        swap_rows(hidden_at).wait_recv()
        held[...] = swap_in[hidden_at].astype(jnp.bfloat16)

    def pair_halves(first_unit, first_slot):
        middle = (steps + 1) // 2
        return (
            lambda: convolve_pair(first_unit, 0, middle, first_slot),
            lambda: convolve_pair(first_unit, middle, steps, first_slot),
        )

    nothing = (None, None)
    source_t[...] = act_two_b[...].T
    convolve_back(w_out, grad_act, 0, no_slot, no_slot)
    normed, pre = pre_two()
    incoming = jnp.where(live, grad_act[...] * silu_slope(pre), 0.0)
    if reduce_here:
        swap_neighbours.wait()
        receive(1, 2)
    beside = pair_halves(0, 0) if reduce_here else nothing
    grad_hidden[...] = norm_grad(4, 1, incoming, normed, scale_two, total, beside)
    start_rows(3, grad_hidden[...])
    held[...] = grad_hidden[...]
    grad_act[...] = act_one[...]
    source_t[...] = act_one_b[...].T
    convolve_back(
        w_mid,
        grad_act,
        units,
        lambda at: slot_when(at == 3, 3),
        lambda at: slot_when(at == 2, 4),
    )
    normed, pre = pre_one()
    incoming = jnp.where(live, grad_act[...] * silu_slope(pre), 0.0)
    if reduce_here:
        receive(0, 3)
    beside = pair_halves(units, 5) if reduce_here else nothing
    grad_hidden[...] = norm_grad(5, 0, incoming, normed, scale_one, total, beside)
    done = 8
    down_rows = down_offsets * in_width
    if reduce_here:
        down_all[...] = dot(cols_down[...].T, grad_hidden[...])
        kept = down_rows // 2
        swap_down = swap(
            5, down_all.at[pl.ds(pl.multiple_of(kept * (1 - pair), kept), kept), :], down_got
        )
        swap_down.start()
    else:
        grads[2 * units * width :, :] = dot(cols_down[...].T, grad_hidden[...])
    slot(done)
    for child in range(children):
        total_child = jnp.zeros((rows, in_width), jnp.float32)
        for k in range(child, down_offsets, children):
            there = side_cols[:, offsets + k : offsets + k + 1] < fine_rows
            total_child += jnp.where(there, dot_last(grad_hidden[...], w_down[k]), 0.0)
        spread_fine[pl.ds(child, rows, stride=children), :] = total_child
    fine_grad_ref[...] = spread_fine[...].astype(jnp.bfloat16)

    if reduce_here:

        def rest(at, carry):
            slot(at)
            return carry

        lax.fori_loop(done + 1, chunks - 1, rest, 0)
        swap_down.wait()
        for at in (2, 3):
            swap_rows(at).wait_send()
        for part in range(PAIR):
            total_down = (
                down_all[pl.ds(pl.multiple_of(kept * pair + part * width, width), width), :]
                + down_got[part * width : (part + 1) * width, :]
            )
            grads[chunks - 1, :, :, :, 8 * part : 8 * part + 8] = total_down.reshape(
                grads.shape[1:4] + (8, width)
            )
        lax.fori_loop(chunks - 1, chunks + LAG * STAGES, rest, 0)

        def finish(c, carry):
            for store in stores_of(c):
                store.wait()
            return carry

        lax.fori_loop(0, chunks, finish, 0)
    else:
        store = pltpu.make_async_copy(grads, grads_hbm, store_sem.at[0, 0])
        store.start()
        store.wait()


def place_kernel(
    features_ref,
    fine_grad_ref,
    grads_ref,
    gain_ref,
    bias_ref,
    features_out,
    fine_grad_out,
    grad_down_out,
    grad_mid_out,
    grad_out_out,
    gain_out,
    bias_out,
    held,
    load_sem,
    store_sem,
):
    offsets, width = grad_mid_out.shape[:2]
    units = (offsets + 1) // 2
    piece = (units + 1) // 2
    moves = []
    for pair in range(2):
        for at, target in enumerate((grad_out_out, grad_mid_out)):
            for first in range(0, units, piece):
                count = min(piece, offsets - units * pair - first, units - first)
                here = (pair, pl.ds(at * units + first, count))
                moves.append((here, target.at[pl.ds(units * pair + first, count)]))
        down_units = grad_down_out.shape[0] // 2
        here = (pair, pl.ds(2 * units, down_units))
        moves.append((here, grad_down_out.at[pl.ds(pair * down_units, down_units)]))
    loads = [
        pltpu.make_async_copy(grads_ref.at[here], held.at[here], load_sem.at[at])
        for at, (here, _) in enumerate(moves)
    ]
    stores = [
        pltpu.make_async_copy(held.at[here], target, store_sem.at[at])
        for at, (here, target) in enumerate(moves)
    ]
    for load in loads:
        load.start()
    features_out[...] = features_ref[...]
    fine_grad_out[...] = fine_grad_ref[...]
    gain_out[...] = gain_ref[...]
    bias_out[...] = bias_ref[...]
    for load, store in zip(loads, stores):
        load.wait()
        store.start()
    for store in stores:
        store.wait()


def per_device(
    dp_size,
    group_size,
    fine_features,
    down_map,
    neighbours,
    voxel_counts,
    down_weight,
    mid_weight,
    out_weight,
    norm_gain,
    norm_bias,
    cotangent,
):
    rows, width = cotangent.shape
    fine_rows, in_width = fine_features.shape
    offsets = neighbours.shape[1]
    down_offsets = down_map.shape[1]
    f32, bf16, i32 = jnp.float32, jnp.bfloat16, jnp.int32
    vmem = pl.BlockSpec(memory_space=pltpu.VMEM)
    smem = pl.BlockSpec(memory_space=pltpu.SMEM)
    hbm = pl.BlockSpec(memory_space=pl.ANY)
    shape = jax.ShapeDtypeStruct
    reduce_here = dp_size == 8 and group_size == 4
    share = 2 if reduce_here else 1
    units = (offsets + 1) // 2 * 2 // share
    all_units = 2 * units + down_offsets * in_width // (share * width)
    grad_rows = all_units * width
    chunks = all_units // PAIR
    padded = (offsets + 1) // 2 * 2
    features, fine_grad, grads, gain_grad, bias_grad = pl.pallas_call(
        functools.partial(kernel, dp_size, group_size, reduce_here),
        out_shape=(
            shape((rows, width), bf16),
            shape((fine_rows, in_width), bf16),
            shape((2, all_units, *GROUPS, 8, width) if reduce_here else (grad_rows, width), f32),
            shape(norm_gain.shape, f32),
            shape(norm_bias.shape, f32),
        ),
        in_specs=[vmem, vmem, vmem, smem, hbm, hbm, hbm, vmem, vmem, vmem],
        out_specs=(vmem, vmem, hbm, vmem, vmem),
        scratch_shapes=[
            pltpu.VMEM(down_weight.shape, bf16),
            pltpu.VMEM((padded, width, width), bf16),
            pltpu.VMEM((padded, width, width), bf16),
            pltpu.VMEM((fine_rows, in_width), f32),
            pltpu.VMEM((rows, down_offsets * in_width), bf16),
            pltpu.VMEM((offsets, rows, 128), bf16),
            pltpu.VMEM((GROUP * rows, rows), bf16),
            pltpu.VMEM((rows, GROUP * width), bf16),
            pltpu.VMEM((rows, width), f32),
            pltpu.VMEM((rows, width), bf16),
            pltpu.VMEM((rows, width), bf16),
            pltpu.VMEM((rows, width), f32),
            pltpu.VMEM((rows, width), f32),
            pltpu.VMEM((rows, width), f32),
            pltpu.VMEM((rows, width), bf16),
            pltpu.VMEM((rows, width), bf16),
            pltpu.VMEM((width, rows), bf16),
            pltpu.VMEM((width, rows), bf16),
            pltpu.VMEM((rows, width), f32),
            pltpu.VMEM((128, rows), i32),
            pltpu.VMEM((rows, 128), i32),
            pltpu.VMEM((padded, rows), i32),
            pltpu.VMEM((padded, rows), i32),
            pltpu.VMEM((2, rows, width), f32),
            pltpu.VMEM((4, rows, width), f32),
            pltpu.VMEM((down_offsets * in_width, width), f32),
            pltpu.VMEM((down_offsets * in_width // 2, width), f32),
            pltpu.VMEM(
                (chunks, *GROUPS, 8 * PAIR, width) if reduce_here else (grad_rows, width), f32
            ),
            pltpu.VMEM((2, chunks if reduce_here else 1, *GROUPS, 8 * PAIR, width), f32),
            pltpu.VMEM((RING, 2, *GROUPS[1:], 8 * PAIR, width), f32),
            pltpu.VMEM((chunks, GROUPS[2], 8 * PAIR, width), f32),
            pltpu.VMEM((chunks, GROUPS[1], 2, 8 * PAIR, width), f32),
            pltpu.VMEM((chunks, 2, 8 * PAIR, width), f32),
            pltpu.VMEM((chunks, 2, 8 * PAIR, width), f32),
            pltpu.VMEM((chunks, 2, 8 * PAIR, width), f32),
            pltpu.VMEM((6, group_size, 8, width // 2), f32),
            pltpu.VMEM((6, dp_size, 8, width // 2), f32),
            pltpu.SemaphoreType.DMA((3,)),
            pltpu.SemaphoreType.DMA((chunks, PAIR)),
            pltpu.SemaphoreType.DMA((RING, COPIES)),
            pltpu.SemaphoreType.DMA((RING, COPIES)),
            pltpu.SemaphoreType.DMA((6,)),
            pltpu.SemaphoreType.DMA((6,)),
            pltpu.SemaphoreType.DMA((6, group_size - 1)),
            pltpu.SemaphoreType.DMA((6, group_size - 1)),
            pltpu.SemaphoreType.DMA((6, dp_size - 1)),
            pltpu.SemaphoreType.DMA((6, dp_size - 1)),
        ],
        compiler_params=pltpu.CompilerParams(
            collective_id=0, has_side_effects=True, vmem_limit_bytes=60 * 1024 * 1024
        ),
    )(
        fine_features,
        down_map.T,
        neighbours.T,
        voxel_counts,
        down_weight,
        mid_weight,
        out_weight,
        norm_gain,
        norm_bias,
        cotangent,
    )
    if not reduce_here:
        grads = lax.psum(grads, ("dp", "group"))
        middle, end = offsets * width, 2 * padded * width
        grad_out = grads[:middle].reshape(out_weight.shape)
        grad_mid = grads[padded * width : padded * width + middle].reshape(mid_weight.shape)
        grad_down = grads[end:].reshape(down_weight.shape)
        return (features, fine_grad, grad_down, grad_mid, grad_out, gain_grad, bias_grad)
    grads = grads.reshape(2, all_units, width, width)
    features, fine_grad, grad_down, grad_mid, grad_out, gain_grad, bias_grad = pl.pallas_call(
        place_kernel,
        out_shape=(
            shape(features.shape, bf16),
            shape(fine_grad.shape, bf16),
            shape((down_offsets * in_width // width, width, width), f32),
            shape(mid_weight.shape, f32),
            shape(out_weight.shape, f32),
            shape(norm_gain.shape, f32),
            shape(norm_bias.shape, f32),
        ),
        in_specs=[vmem, vmem, hbm, vmem, vmem],
        out_specs=(vmem, vmem, hbm, hbm, hbm, vmem, vmem),
        scratch_shapes=[
            pltpu.VMEM(grads.shape, f32),
            pltpu.SemaphoreType.DMA((10,)),
            pltpu.SemaphoreType.DMA((10,)),
        ],
        compiler_params=pltpu.CompilerParams(vmem_limit_bytes=60 * 1024 * 1024),
    )(features, fine_grad, grads, gain_grad, bias_grad)
    grad_down = grad_down.reshape(down_weight.shape)
    return (features, fine_grad, grad_down, grad_mid, grad_out, gain_grad, bias_grad)


def solution(mesh):
    in_specs = (
        P(("dp", "group"), None),
        P(("dp", "group"), None),
        P(("dp", "group"), None),
        P(("dp", "group")),
        P(),
        P(),
        P(),
        P(),
        P(),
        P(("dp", "group"), None),
    )
    out_specs = (P(("dp", "group"), None), P(("dp", "group"), None), P(), P(), P(), P(), P())
    return jax.shard_map(
        functools.partial(per_device, mesh.shape["dp"], mesh.shape["group"]),
        mesh=mesh,
        in_specs=in_specs,
        out_specs=out_specs,
        check_vma=False,
    )
```

```python
import functools

import jax
import jax.numpy as jnp
from jax import lax
from jax.experimental import pallas as pl
from jax.experimental.pallas import tpu as pltpu
from jax.sharding import PartitionSpec as P

eps_norm = 1e-05
MESH = pl.DeviceIdType.MESH
GROUP = 3
BLOCK = 256
PAIR = 2
COPIES = 14
STAGES = 8
GROUPS = (4, 2, 4)
GAP = 4
DOWN_GAP = 3
LAG = 2
RING = 8


def sigmoid(value):
    return 1.0 / (1.0 + jnp.exp(-value))


def silu_slope(value):
    sigma = sigmoid(value)
    return sigma * (1.0 + value * (1.0 - sigma))


def dot(left, right):
    return jnp.dot(left, right, preferred_element_type=jnp.float32)


def dot_last(left, right):
    return lax.dot_general(
        left, right, (((1,), (1,)), ((), ())), preferred_element_type=jnp.float32
    )


def kernel(
    dp_size,
    group_size,
    reduce_here,
    fine_ref,
    down_rows_ref,
    nb_rows,
    count_ref,
    down_hbm,
    mid_hbm,
    out_hbm,
    gain_ref,
    bias_ref,
    cotangent_ref,
    features_ref,
    fine_grad_ref,
    results,
    gain_grad_ref,
    bias_grad_ref,
    w_down,
    w_mid,
    w_out,
    spread_fine,
    cols_down,
    nb_cols,
    pickers,
    columns,
    act_one,
    act_one_b,
    act_two_b,
    hid_one,
    hid_two,
    hid_three,
    held,
    grad_hidden,
    source_t,
    pair_source_t,
    grad_act,
    side,
    side_cols,
    nb_own,
    nb_pair,
    swap_out,
    swap_in,
    down_all,
    down_got,
    grads,
    from_core,
    from_first_a,
    from_first_b,
    from_second_a,
    from_second_b,
    from_line,
    near,
    far,
    load_sem,
    sum_send,
    sum_recv,
    swap_send,
    swap_recv,
    near_send,
    near_recv,
    far_send,
    far_recv,
):
    rows, width = cotangent_ref.shape
    offsets = nb_rows.shape[0]
    fine_rows, in_width = fine_ref.shape
    children = fine_rows // rows
    down_offsets = down_rows_ref.shape[0]
    units = (offsets + 1) // 2 * (1 if reduce_here else 2)
    chunks = grads.shape[0]
    dp_me = lax.axis_index("dp")
    group_me = lax.axis_index("group")

    loads = [
        pltpu.make_async_copy(source, target, load_sem.at[at])
        for at, (source, target) in enumerate(
            (
                (down_hbm, w_down),
                (mid_hbm, w_mid.at[pl.ds(0, offsets)]),
                (out_hbm, w_out.at[pl.ds(0, offsets)]),
            )
        )
    ]
    for load in loads:
        load.start()

    barrier = pltpu.get_barrier_semaphore()
    for step in range(1, group_size):
        pl.semaphore_signal(
            barrier,
            inc=1,
            device_id={"group": lax.rem(group_me + step, group_size)},
            device_id_type=MESH,
        )
    for step in range(1, dp_size):
        pl.semaphore_signal(
            barrier,
            inc=1,
            device_id={"dp": lax.rem(dp_me + step, dp_size)},
            device_id_type=MESH,
        )

    def share(at, axis, me, size, slots, send, recv):
        copies = []
        for step in range(1, size):
            copies.append(
                pltpu.make_async_remote_copy(
                    src_ref=slots.at[at, me],
                    dst_ref=slots.at[at, me],
                    send_sem=send.at[at, step - 1],
                    recv_sem=recv.at[at, step - 1],
                    device_id={axis: lax.rem(me + step, size)},
                    device_id_type=MESH,
                )
            )
        for copy in copies:
            copy.start()
        return copies

    def exchange(at, block, combine, meanwhile=(None, None)):
        near[at, group_me] = block
        copies = share(at, "group", group_me, group_size, near, near_send, near_recv)
        if meanwhile[0] is not None:
            meanwhile[0]()
        for copy in copies:
            copy.wait()
        far[at, dp_me] = combine([near[at, slot] for slot in range(group_size)])
        copies = share(at, "dp", dp_me, dp_size, far, far_send, far_recv)
        if meanwhile[1] is not None:
            meanwhile[1]()
        for copy in copies:
            copy.wait()
        return combine([far[at, slot] for slot in range(dp_size)])

    lanes = width // 2

    def stack(first, second, third):
        filler = jnp.zeros((2, lanes), jnp.float32)
        return jnp.concatenate([first, second, third, filler], axis=0)

    def fold(value):
        return jnp.concatenate([value[:, :lanes], value[:, lanes:]], axis=0)

    def unfold(value):
        return jnp.concatenate([value[0:1], value[1:2]], axis=1)

    def add_all(blocks):
        total = blocks[0]
        for block in blocks[1:]:
            total = total + block
        return total

    def merge_all(blocks):
        count = add_all([block[4:6] for block in blocks])
        center = add_all([block[4:6] * block[0:2] for block in blocks]) / count
        squares = add_all(
            [
                block[2:4] + block[4:6] * (block[0:2] - center) * (block[0:2] - center)
                for block in blocks
            ]
        )
        return stack(center, squares, count)

    count = count_ref[0]
    own_count = jnp.full((1, width), count.astype(jnp.float32))
    live = lax.broadcasted_iota(jnp.int32, (rows, width), 0) < count

    def norm_stats(at, hidden, meanwhile=(None, None)):
        center = jnp.sum(hidden, axis=0, keepdims=True) / own_count
        centered = jnp.where(live, hidden - center, 0.0)
        squares = jnp.sum(centered * centered, axis=0, keepdims=True)
        merged = exchange(
            at, stack(fold(center), fold(squares), fold(own_count)), merge_all, meanwhile
        )
        total = unfold(merged[4:6])
        scale = lax.rsqrt(unfold(merged[2:4]) / total + eps_norm)
        return unfold(merged[0:2]), scale, total

    def norm_grad(at, norm, incoming, normed, scale, total, meanwhile=(None, None)):
        shift_sum = fold(jnp.sum(incoming, axis=0, keepdims=True))
        scale_sum = fold(jnp.sum(incoming * normed, axis=0, keepdims=True))
        summed = exchange(
            at, stack(shift_sum, scale_sum, jnp.zeros_like(shift_sum)), add_all, meanwhile
        )
        shift_sum, scale_sum = unfold(summed[0:2]), unfold(summed[2:4])
        bias_grad_ref[norm : norm + 1, :] = shift_sum
        gain_grad_ref[norm : norm + 1, :] = scale_sum
        hidden_grad = (
            scale
            * gain_ref[norm : norm + 1, :]
            * (incoming - shift_sum / total - normed * (scale_sum / total))
        )
        return jnp.where(live, hidden_grad, 0.0).astype(jnp.bfloat16)

    def pick(mask):
        return jnp.where(mask, jnp.bfloat16(1), jnp.bfloat16(0))

    def counting(shape, axis):
        return lax.broadcasted_iota(jnp.int32, shape, axis).astype(jnp.float32).astype(jnp.bfloat16)

    def place_columns(count):
        picked = dot(pickers[: count * rows, :], held[...]).astype(jnp.bfloat16)
        for part in range(count):
            columns[:, part * width : (part + 1) * width] = picked[part * rows : (part + 1) * rows]

    def convolve(weight, hidden):
        places = counting((rows, BLOCK), 1)
        places = (places, -1 - places)
        hidden[...] = jnp.zeros_like(hidden)

        def step(at, carry):
            for part in range(GROUP):
                wanted = jnp.concatenate([nb_cols[at * GROUP + part]] * (BLOCK // 128), axis=1)
                for block in range(2):
                    pickers[
                        part * rows : (part + 1) * rows, block * BLOCK : (block + 1) * BLOCK
                    ] = pick(wanted == places[block])
            place_columns(GROUP)
            weights = weight[pl.ds(at * GROUP, GROUP)].reshape(GROUP * width, width)
            hidden[...] += dot(columns[...], weights)
            return carry

        lax.fori_loop(0, offsets // GROUP, step, 0)

    def spread_rows(neighbours, first_offset):
        places = counting((BLOCK, rows), 0)
        for part in range(PAIR):
            wanted = neighbours[pl.ds(first_offset + part, 1), :].astype(jnp.float32)
            for first in range(0, rows, BLOCK):
                here = jnp.broadcast_to(wanted - first, (16, rows)).astype(jnp.bfloat16)
                pickers[part * rows + first : part * rows + first + BLOCK, :] = pick(
                    jnp.concatenate([here] * (BLOCK // 16), axis=0) == places
                )
        place_columns(PAIR)
        return columns[:, : PAIR * width]

    def put(first_unit, at, product, more):
        for part in range(PAIR):
            value = product[:, part * width : (part + 1) * width]
            if reduce_here:
                c = first_unit // PAIR + at
                value = value.reshape(grads.shape[1:4] + (8, width))
                here_rows = slice(8 * part, 8 * part + 8)
                if more:
                    value = value + grads[c, :, :, :, here_rows]
                grads[c, :, :, :, here_rows] = value
            else:
                unit = pl.multiple_of((first_unit + PAIR * at + part) * width, width)
                grads[pl.ds(unit, width), :] = value

    def convolve_back(weight, act_grad, first_unit, own_slot, other_slot):
        def step(first_offset, at, weigh):
            spread = spread_rows(nb_own, first_offset)
            weights = jnp.concatenate(
                [weight[first_offset + part] for part in range(PAIR)], axis=1
            )
            act_grad[...] += dot_last(spread, weights)
            if weigh:
                put(first_unit, at, dot(source_t[...], spread), False)

        def own_offsets(at, carry):
            step(own_offset + PAIR * at, at, True)
            own_slot(at)
            return carry

        def other_offsets(at, carry):
            step(other_offset + PAIR * at, at, False)
            other_slot(at)
            return carry

        lax.fori_loop(0, units // PAIR, own_offsets, 0)
        if reduce_here:
            lax.fori_loop(0, units // PAIR, other_offsets, 0)

    def convolve_pair(first_unit, first_step, last_step, first_slot):
        def step(at, carry):
            spread = spread_rows(nb_pair, own_offset + PAIR * at)
            put(first_unit, at, dot(pair_source_t[...], spread), True)
            slot(first_slot + at)
            return carry

        lax.fori_loop(first_step, last_step, step, 0)

    core, row = lax.rem(group_me, 2), group_me // 2
    column, plane = lax.rem(dp_me, 2), dp_me // 2
    pair, high = lax.rem(plane, 2), plane // 2
    planes = 4
    core_peer = {"group": group_me + 1 - 2 * core}
    row_peer = {"group": group_me + 2 - 4 * row}
    column_peer = {"dp": dp_me + 1 - 2 * column}
    pair_peer = {"dp": dp_me + 2 - 4 * pair}
    cross_peer = {"dp": dp_me + 4 - 8 * high}
    own_offset = units * pair if reduce_here else 0
    other_offset = units * (1 - pair)
    own = pl.ds(2 * core, 2)
    lane_a, lane_b = 2 * core, 2 * core + 1
    kept_row, given_row = pl.ds(2 * row, 2), pl.ds(2 * (1 - row), 2)

    def send(c, number, source, target, peer):
        turn = lax.rem(c, RING)
        return pltpu.make_async_remote_copy(
            src_ref=source,
            dst_ref=target,
            send_sem=sum_send.at[turn, number],
            recv_sem=sum_recv.at[turn, number],
            device_id=peer,
            device_id_type=MESH,
        )

    def copies_of(c, stage):
        part, both = grads.at[c], pl.ds(PAIR * c, PAIR)
        if stage == 0:
            given = part.at[pl.ds(2 * (1 - core), 2)]
            return [send(c, 0, given, from_core.at[lax.rem(c, RING)], core_peer)]
        if stage == 1:
            return [
                send(c, 1, part.at[lane_a, 1 - column], from_first_a.at[c], column_peer),
                send(c, 2, part.at[lane_b, :, given_row], from_first_b.at[c], row_peer),
            ]
        if stage == 2:
            return [
                send(c, 3, part.at[lane_a, column, given_row], from_second_a.at[c], row_peer),
                send(c, 4, part.at[lane_b, 1 - column, kept_row], from_second_b.at[c], column_peer),
            ]
        if stage == 3:
            given = part.at[own, column, 2 * row + 1 - high]
            return [send(c, 5, given, from_line.at[c], cross_peer)]
        if stage == 4:
            block = results.at[pair, both, own, column, 2 * row + high]
            return [
                send(
                    c,
                    5 + step,
                    block,
                    block,
                    {"dp": 2 * lax.rem(plane + step, planes) + column},
                )
                for step in range(1, planes)
            ]
        if stage == 5:
            block_a = results.at[:, both, lane_a, column, kept_row]
            block_b = results.at[:, both, lane_b, column, kept_row]
            return [
                send(c, 9, block_a, block_a, row_peer),
                send(c, 10, block_b, block_b, column_peer),
            ]
        if stage == 6:
            block_a = results.at[:, both, lane_a, column]
            block_b = results.at[:, both, lane_b, :, kept_row]
            return [
                send(c, 11, block_a, block_a, column_peer),
                send(c, 12, block_b, block_b, row_peer),
            ]
        block = results.at[:, both, own]
        return [send(c, 13, block, block, core_peer)]

    def stage_of(c, stage):
        if stage > 0:
            for copy in copies_of(c, stage - 1):
                copy.wait()
        if stage == 1:
            grads[c, own] = grads[c, own] + from_core[lax.rem(c, RING)]
        if stage == 2:
            grads[c, lane_a, column] = grads[c, lane_a, column] + from_first_a[c]
            grads[c, lane_b, :, kept_row] = grads[c, lane_b, :, kept_row] + from_first_b[c]
        if stage == 3:
            grads[c, lane_a, column, kept_row] = grads[c, lane_a, column, kept_row] + from_second_a[c]
            grads[c, lane_b, column, kept_row] = grads[c, lane_b, column, kept_row] + from_second_b[c]
        if stage == 4:
            mine = 2 * row + high
            grads[c, own, column, mine] = grads[c, own, column, mine] + from_line[c]
            for unit in range(PAIR):
                results[pair, PAIR * c + unit, own, column, mine] = grads[
                    c, own, column, mine, 8 * unit : 8 * unit + 8
                ]
        if stage < STAGES:
            for copy in copies_of(c, stage):
                copy.start()

    per_weight = units // PAIR
    entries = 2 * per_weight + GAP + DOWN_GAP + 1

    def slot(at):
        if not reduce_here:
            return
        for stage in range(STAGES + 1):
            entry = at - LAG * stage
            second = entry >= per_weight + GAP
            third = entry >= entries - 1
            there_is = (
                ((entry >= 0) & (entry < per_weight))
                | (second & (entry < 2 * per_weight + GAP))
                | (third & (entry < entries))
            )
            if isinstance(at, int):
                if there_is:
                    stage_of(entry - GAP * second - DOWN_GAP * third, stage)
                continue
            c = entry - GAP * second.astype(jnp.int32) - DOWN_GAP * third.astype(jnp.int32)

            @pl.when(there_is)
            def _():
                stage_of(c, stage)

    def slot_when(condition, at):
        @pl.when(condition)
        def _():
            slot(at)

    def no_slot(at):
        pass

    def swap(at, source, target):
        return pltpu.make_async_remote_copy(
            src_ref=source,
            dst_ref=target,
            send_sem=swap_send.at[at],
            recv_sem=swap_recv.at[at],
            device_id=pair_peer,
            device_id_type=MESH,
        )

    def swap_rows(at):
        return swap(at, swap_out.at[at % 2], swap_in.at[at])

    def start_rows(at, value):
        if reduce_here:
            swap_out[at % 2] = value.astype(jnp.float32)
            swap_rows(at).start()

    side[...] = jnp.zeros_like(side)
    side[:offsets, :] = nb_rows[...]
    side[offsets : offsets + down_offsets, :] = down_rows_ref[...]
    side_cols[...] = side[...].T
    nb_own[...] = jnp.full_like(nb_own, rows)
    nb_own[:offsets, :] = nb_rows[...]
    swap_neighbours = swap(4, nb_own, nb_pair)
    for weight in (w_mid, w_out):
        weight[offsets:] = jnp.zeros_like(weight[offsets:])

    spread_fine[...] = fine_ref[...].astype(jnp.float32)
    for k in range(down_offsets):
        child = spread_fine[pl.ds(k % children, rows, stride=children), :]
        there = side_cols[:, offsets + k : offsets + k + 1] < fine_rows
        cols_down[:, k * in_width : (k + 1) * in_width] = jnp.where(there, child, 0.0).astype(
            jnp.bfloat16
        )
    loads[0].wait()
    hid_one[...] = dot(cols_down[...], w_down[...].reshape(down_offsets * in_width, width))

    def spread_neighbours():
        for k in range(offsets):
            wanted = side_cols[:, k : k + 1]
            code = jnp.where(
                wanted < BLOCK, wanted, jnp.where(wanted < rows, BLOCK - 1 - wanted, 4 * BLOCK)
            )
            nb_cols[k] = jnp.broadcast_to(code, (rows, 128)).astype(jnp.float32).astype(jnp.bfloat16)

    pl.semaphore_wait(barrier, group_size + dp_size - 2)

    swap_one = swap(0, hid_one, swap_in.at[0])
    swap_two = swap(1, hid_two, swap_in.at[1])

    def start_one():
        swap_neighbours.start()
        swap_one.start()

    def start_two():
        swap_two.start()

    beside = (spread_neighbours, start_one if reduce_here else None)
    center_one, scale_one, total = norm_stats(0, hid_one[...], beside)

    def pre_one(hidden=hid_one):
        normed = (hidden[...] - center_one) * scale_one
        return normed, normed * gain_ref[0:1, :] + bias_ref[0:1, :]

    _, pre = pre_one()
    act_one[...] = jnp.where(live, pre * sigmoid(pre), 0.0)
    act_one_b[...] = act_one[...].astype(jnp.bfloat16)
    loads[1].wait()
    held[...] = act_one_b[...]
    convolve(w_mid, hid_two)
    center_two, scale_two, _ = norm_stats(
        1, hid_two[...], (None, start_two if reduce_here else None)
    )

    def pre_two(hidden=hid_two):
        normed = (hidden[...] - center_two) * scale_two
        return normed, normed * gain_ref[1:2, :] + bias_ref[1:2, :]

    _, pre = pre_two()
    act_two_b[...] = jnp.where(live, pre * sigmoid(pre), 0.0).astype(jnp.bfloat16)
    loads[2].wait()
    held[...] = act_two_b[...]
    convolve(w_out, hid_three)
    center_three, scale_three, _ = norm_stats(2, hid_three[...])
    normed_three = (hid_three[...] - center_three) * scale_three
    summed = (
        jnp.where(live, normed_three * gain_ref[2:3, :] + bias_ref[2:3, :], 0.0) + act_one[...]
    )
    sigma = sigmoid(summed)
    features_ref[...] = jnp.where(live, summed * sigma, 0.0).astype(jnp.bfloat16)

    slope = sigma * (1.0 + summed * (1.0 - sigma))
    act_one[...] = jnp.where(live, cotangent_ref[...].astype(jnp.float32) * slope, 0.0)
    grad_hidden[...] = norm_grad(3, 2, act_one[...], normed_three, scale_three, total)
    start_rows(2, grad_hidden[...])
    held[...] = grad_hidden[...]
    grad_act[...] = jnp.zeros_like(grad_act)
    steps = units // PAIR

    def receive(swapped, pre_of, source_at, hidden_at):
        swapped.wait()
        _, pre = pre_of(swap_in.at[source_at])
        pair_source_t[...] = (pre * sigmoid(pre)).astype(jnp.bfloat16).T
        swap_rows(hidden_at).wait()
        held[...] = swap_in[hidden_at].astype(jnp.bfloat16)

    def pair_halves(first_unit, first_slot):
        middle = (steps + 1) // 2
        return (
            lambda: convolve_pair(first_unit, 0, middle, first_slot),
            lambda: convolve_pair(first_unit, middle, steps, first_slot),
        )

    nothing = (None, None)
    source_t[...] = act_two_b[...].T
    convolve_back(w_out, grad_act, 0, no_slot, no_slot)
    normed, pre = pre_two()
    incoming = jnp.where(live, grad_act[...] * silu_slope(pre), 0.0)
    if reduce_here:
        swap_neighbours.wait()
        receive(swap_two, pre_two, 1, 2)
    beside = pair_halves(0, 0) if reduce_here else nothing
    grad_hidden[...] = norm_grad(4, 1, incoming, normed, scale_two, total, beside)
    start_rows(3, grad_hidden[...])
    held[...] = grad_hidden[...]
    grad_act[...] = act_one[...]
    source_t[...] = act_one_b[...].T
    early = (GAP + 1) // 2
    convolve_back(
        w_mid,
        grad_act,
        units,
        lambda at: slot_when((at >= 1) & (at < 1 + early), steps + at - 1),
        lambda at: slot_when((at >= 1) & (at < 1 + GAP - early), steps + early + at - 1),
    )
    normed, pre = pre_one()
    incoming = jnp.where(live, grad_act[...] * silu_slope(pre), 0.0)
    if reduce_here:
        receive(swap_one, pre_one, 0, 3)
    beside = pair_halves(units, steps + GAP) if reduce_here else nothing
    grad_hidden[...] = norm_grad(5, 0, incoming, normed, scale_one, total, beside)
    done = 2 * steps + GAP
    down_rows = down_offsets * in_width
    if reduce_here:
        down_all[...] = dot(cols_down[...].T, grad_hidden[...])
        kept = down_rows // 2
        swap_down = swap(
            5, down_all.at[pl.ds(pl.multiple_of(kept * (1 - pair), kept), kept), :], down_got
        )
        swap_down.start()
    else:
        grads[2 * units * width :, :] = dot(cols_down[...].T, grad_hidden[...])
    slot(done)
    for child in range(children):
        total_child = jnp.zeros((rows, in_width), jnp.float32)
        for k in range(child, down_offsets, children):
            there = side_cols[:, offsets + k : offsets + k + 1] < fine_rows
            total_child += jnp.where(there, dot_last(grad_hidden[...], w_down[k]), 0.0)
        spread_fine[pl.ds(child, rows, stride=children), :] = total_child
    fine_grad_ref[...] = spread_fine[...].astype(jnp.bfloat16)

    if reduce_here:

        def rest(at, carry):
            slot(at)
            return carry

        lax.fori_loop(done + 1, done + DOWN_GAP, rest, 0)
        swap_down.wait()
        for part in range(PAIR):
            total_down = (
                down_all[pl.ds(pl.multiple_of(kept * pair + part * width, width), width), :]
                + down_got[part * width : (part + 1) * width, :]
            )
            grads[chunks - 1, :, :, :, 8 * part : 8 * part + 8] = total_down.reshape(
                grads.shape[1:4] + (8, width)
            )
        lax.fori_loop(done + DOWN_GAP, entries + LAG * STAGES, rest, 0)
    else:
        store = pltpu.make_async_copy(grads, results, load_sem.at[0])
        store.start()
        store.wait()


def place_kernel(
    features_ref,
    fine_grad_ref,
    grads_ref,
    gain_ref,
    bias_ref,
    features_out,
    fine_grad_out,
    grad_down_out,
    grad_mid_out,
    grad_out_out,
    gain_out,
    bias_out,
    sem,
):
    offsets = grad_mid_out.shape[0]
    units = (offsets + 1) // 2
    piece = (units + 1) // 2
    moves = []
    for pair in range(2):
        for at, target in enumerate((grad_out_out, grad_mid_out)):
            for first in range(0, units, piece):
                count = min(piece, offsets - units * pair - first, units - first)
                here = grads_ref.at[pair, pl.ds(at * units + first, count)]
                moves.append((here, target.at[pl.ds(units * pair + first, count)]))
        down_units = grad_down_out.shape[0] // 2
        here = grads_ref.at[pair, pl.ds(2 * units, down_units)]
        moves.append((here, grad_down_out.at[pl.ds(pair * down_units, down_units)]))
    copies = [
        pltpu.make_async_copy(source, target, sem.at[at])
        for at, (source, target) in enumerate(moves)
    ]
    for copy in copies:
        copy.start()
    features_out[...] = features_ref[...]
    fine_grad_out[...] = fine_grad_ref[...]
    gain_out[...] = gain_ref[...]
    bias_out[...] = bias_ref[...]
    for copy in copies:
        copy.wait()


def per_device(
    dp_size,
    group_size,
    fine_features,
    down_map,
    neighbours,
    voxel_counts,
    down_weight,
    mid_weight,
    out_weight,
    norm_gain,
    norm_bias,
    cotangent,
):
    rows, width = cotangent.shape
    fine_rows, in_width = fine_features.shape
    offsets = neighbours.shape[1]
    down_offsets = down_map.shape[1]
    f32, bf16, i32 = jnp.float32, jnp.bfloat16, jnp.int32
    vmem = pl.BlockSpec(memory_space=pltpu.VMEM)
    smem = pl.BlockSpec(memory_space=pltpu.SMEM)
    hbm = pl.BlockSpec(memory_space=pl.ANY)
    shape = jax.ShapeDtypeStruct
    reduce_here = dp_size == 8 and group_size == 4
    share = 2 if reduce_here else 1
    units = (offsets + 1) // 2 * 2 // share
    all_units = 2 * units + down_offsets * in_width // (share * width)
    grad_rows = all_units * width
    chunks = all_units // PAIR
    padded = (offsets + 1) // 2 * 2
    features, fine_grad, grads, gain_grad, bias_grad = pl.pallas_call(
        functools.partial(kernel, dp_size, group_size, reduce_here),
        out_shape=(
            shape((rows, width), bf16),
            shape((fine_rows, in_width), bf16),
            pltpu.VMEM((2, all_units, *GROUPS, 8, width), f32)
            if reduce_here
            else shape((grad_rows, width), f32),
            shape(norm_gain.shape, f32),
            shape(norm_bias.shape, f32),
        ),
        in_specs=[vmem, vmem, vmem, smem, hbm, hbm, hbm, vmem, vmem, vmem],
        out_specs=(vmem, vmem, vmem if reduce_here else hbm, vmem, vmem),
        scratch_shapes=[
            pltpu.VMEM(down_weight.shape, bf16),
            pltpu.VMEM((padded, width, width), bf16),
            pltpu.VMEM((padded, width, width), bf16),
            pltpu.VMEM((fine_rows, in_width), f32),
            pltpu.VMEM((rows, down_offsets * in_width), bf16),
            pltpu.VMEM((offsets, rows, 128), bf16),
            pltpu.VMEM((GROUP * rows, rows), bf16),
            pltpu.VMEM((rows, GROUP * width), bf16),
            pltpu.VMEM((rows, width), f32),
            pltpu.VMEM((rows, width), bf16),
            pltpu.VMEM((rows, width), bf16),
            pltpu.VMEM((rows, width), f32),
            pltpu.VMEM((rows, width), f32),
            pltpu.VMEM((rows, width), f32),
            pltpu.VMEM((rows, width), bf16),
            pltpu.VMEM((rows, width), bf16),
            pltpu.VMEM((width, rows), bf16),
            pltpu.VMEM((width, rows), bf16),
            pltpu.VMEM((rows, width), f32),
            pltpu.VMEM((128, rows), i32),
            pltpu.VMEM((rows, 128), i32),
            pltpu.VMEM((padded, rows), i32),
            pltpu.VMEM((padded, rows), i32),
            pltpu.VMEM((2, rows, width), f32),
            pltpu.VMEM((4, rows, width), f32),
            pltpu.VMEM((down_offsets * in_width, width), f32),
            pltpu.VMEM((down_offsets * in_width // 2, width), f32),
            pltpu.VMEM(
                (chunks, *GROUPS, 8 * PAIR, width) if reduce_here else (grad_rows, width), f32
            ),
            pltpu.VMEM((RING, 2, *GROUPS[1:], 8 * PAIR, width), f32),
            pltpu.VMEM((chunks, GROUPS[2], 8 * PAIR, width), f32),
            pltpu.VMEM((chunks, GROUPS[1], 2, 8 * PAIR, width), f32),
            pltpu.VMEM((chunks, 2, 8 * PAIR, width), f32),
            pltpu.VMEM((chunks, 2, 8 * PAIR, width), f32),
            pltpu.VMEM((chunks, 2, 8 * PAIR, width), f32),
            pltpu.VMEM((6, group_size, 8, width // 2), f32),
            pltpu.VMEM((6, dp_size, 8, width // 2), f32),
            pltpu.SemaphoreType.DMA((3,)),
            pltpu.SemaphoreType.DMA((RING, COPIES)),
            pltpu.SemaphoreType.DMA((RING, COPIES)),
            pltpu.SemaphoreType.DMA((6,)),
            pltpu.SemaphoreType.DMA((6,)),
            pltpu.SemaphoreType.DMA((6, group_size - 1)),
            pltpu.SemaphoreType.DMA((6, group_size - 1)),
            pltpu.SemaphoreType.DMA((6, dp_size - 1)),
            pltpu.SemaphoreType.DMA((6, dp_size - 1)),
        ],
        compiler_params=pltpu.CompilerParams(
            collective_id=0, has_side_effects=True, vmem_limit_bytes=(46 if reduce_here else 60) * 1024 * 1024
        ),
    )(
        fine_features,
        down_map.T,
        neighbours.T,
        voxel_counts,
        down_weight,
        mid_weight,
        out_weight,
        norm_gain,
        norm_bias,
        cotangent,
    )
    if not reduce_here:
        grads = lax.psum(grads, ("dp", "group"))
        middle, end = offsets * width, 2 * padded * width
        grad_out = grads[:middle].reshape(out_weight.shape)
        grad_mid = grads[padded * width : padded * width + middle].reshape(mid_weight.shape)
        grad_down = grads[end:].reshape(down_weight.shape)
        return (features, fine_grad, grad_down, grad_mid, grad_out, gain_grad, bias_grad)
    grads = pltpu.with_memory_space_constraint(grads, pltpu.VMEM)
    features, fine_grad, grad_down, grad_mid, grad_out, gain_grad, bias_grad = pl.pallas_call(
        place_kernel,
        out_shape=(
            shape(features.shape, bf16),
            shape(fine_grad.shape, bf16),
            shape((down_offsets * in_width // width, *GROUPS, 8, width), f32),
            shape((offsets, *GROUPS, 8, width), f32),
            shape((offsets, *GROUPS, 8, width), f32),
            shape(norm_gain.shape, f32),
            shape(norm_bias.shape, f32),
        ),
        in_specs=[vmem] * 5,
        out_specs=(vmem, vmem, hbm, hbm, hbm, vmem, vmem),
        scratch_shapes=[pltpu.SemaphoreType.DMA((10,))],
        compiler_params=pltpu.CompilerParams(vmem_limit_bytes=8 * 1024 * 1024),
    )(features, fine_grad, grads, gain_grad, bias_grad)
    grad_down = grad_down.reshape(down_weight.shape)
    grad_mid = grad_mid.reshape(mid_weight.shape)
    grad_out = grad_out.reshape(out_weight.shape)
    return (features, fine_grad, grad_down, grad_mid, grad_out, gain_grad, bias_grad)


def solution(mesh):
    in_specs = (
        P(("dp", "group"), None),
        P(("dp", "group"), None),
        P(("dp", "group"), None),
        P(("dp", "group")),
        P(),
        P(),
        P(),
        P(),
        P(),
        P(("dp", "group"), None),
    )
    out_specs = (P(("dp", "group"), None), P(("dp", "group"), None), P(), P(), P(), P(), P())
    return jax.shard_map(
        functools.partial(per_device, mesh.shape["dp"], mesh.shape["group"]),
        mesh=mesh,
        in_specs=in_specs,
        out_specs=out_specs,
        check_vma=False,
    )
```

```python
import functools

import jax
import jax.numpy as jnp
from jax import lax
from jax.experimental import pallas as pl
from jax.experimental.pallas import tpu as pltpu
from jax.sharding import PartitionSpec as P

eps_norm = 1e-05
MESH = pl.DeviceIdType.MESH
GROUP = 3
BLOCK = 256
PAIR = 2
COPIES = 14
GROUPS = (4, 2, 4)
GAP = 1
LAGS = (0, 1, 2, 3, 5, 7, 8, 9, 10)
RING = 8


def sigmoid(value):
    return 1.0 / (1.0 + jnp.exp(-value))


def silu_slope(value):
    sigma = sigmoid(value)
    return sigma * (1.0 + value * (1.0 - sigma))


def dot(left, right):
    return jnp.dot(left, right, preferred_element_type=jnp.float32)


def dot_last(left, right):
    return lax.dot_general(
        left, right, (((1,), (1,)), ((), ())), preferred_element_type=jnp.float32
    )


def kernel(
    dp_size,
    group_size,
    reduce_here,
    fine_ref,
    down_rows_ref,
    nb_rows,
    count_ref,
    down_hbm,
    mid_hbm,
    out_hbm,
    gain_ref,
    bias_ref,
    cotangent_ref,
    features_ref,
    fine_grad_ref,
    results,
    gain_grad_ref,
    bias_grad_ref,
    w_down,
    w_mid,
    w_out,
    spread_fine,
    cols_down,
    nb_cols,
    pickers,
    columns,
    act_one,
    act_one_b,
    act_two_b,
    hid_one,
    hid_two,
    hid_three,
    held,
    grad_hidden,
    source_t,
    pair_source_t,
    grad_act,
    side,
    side_cols,
    nb_own,
    nb_pair,
    swap_out,
    swap_in,
    down_all,
    down_got,
    grads,
    from_core,
    from_first_a,
    from_first_b,
    from_second_a,
    from_second_b,
    from_line,
    near,
    far,
    load_sem,
    sum_send,
    sum_recv,
    swap_send,
    swap_recv,
    near_send,
    near_recv,
    far_send,
    far_recv,
):
    rows, width = cotangent_ref.shape
    offsets = nb_rows.shape[0]
    fine_rows, in_width = fine_ref.shape
    children = fine_rows // rows
    down_offsets = down_rows_ref.shape[0]
    units = (offsets + 1) // 2 * (1 if reduce_here else 2)
    chunks = grads.shape[0]
    dp_me = lax.axis_index("dp")
    group_me = lax.axis_index("group")

    loads = [
        pltpu.make_async_copy(source, target, load_sem.at[at])
        for at, (source, target) in enumerate(
            (
                (down_hbm, w_down),
                (mid_hbm, w_mid.at[pl.ds(0, offsets)]),
                (out_hbm, w_out.at[pl.ds(0, offsets)]),
            )
        )
    ]
    for load in loads:
        load.start()

    barrier = pltpu.get_barrier_semaphore()
    for step in range(1, group_size):
        pl.semaphore_signal(
            barrier,
            inc=1,
            device_id={"group": lax.rem(group_me + step, group_size)},
            device_id_type=MESH,
        )
    for step in range(1, dp_size):
        pl.semaphore_signal(
            barrier,
            inc=1,
            device_id={"dp": lax.rem(dp_me + step, dp_size)},
            device_id_type=MESH,
        )

    def share(at, axis, me, size, slots, send, recv):
        copies = []
        for step in range(1, size):
            copies.append(
                pltpu.make_async_remote_copy(
                    src_ref=slots.at[at, me],
                    dst_ref=slots.at[at, me],
                    send_sem=send.at[at, step - 1],
                    recv_sem=recv.at[at, step - 1],
                    device_id={axis: lax.rem(me + step, size)},
                    device_id_type=MESH,
                )
            )
        for copy in copies:
            copy.start()
        return copies

    def exchange(at, block, combine, meanwhile=(None, None)):
        near[at, group_me] = block
        copies = share(at, "group", group_me, group_size, near, near_send, near_recv)
        if meanwhile[0] is not None:
            meanwhile[0]()
        for copy in copies:
            copy.wait()
        far[at, dp_me] = combine([near[at, slot] for slot in range(group_size)])
        copies = share(at, "dp", dp_me, dp_size, far, far_send, far_recv)
        if meanwhile[1] is not None:
            meanwhile[1]()
        for copy in copies:
            copy.wait()
        return combine([far[at, slot] for slot in range(dp_size)])

    lanes = width // 2

    def stack(first, second, third):
        filler = jnp.zeros((2, lanes), jnp.float32)
        return jnp.concatenate([first, second, third, filler], axis=0)

    def fold(value):
        return jnp.concatenate([value[:, :lanes], value[:, lanes:]], axis=0)

    def unfold(value):
        return jnp.concatenate([value[0:1], value[1:2]], axis=1)

    def add_all(blocks):
        total = blocks[0]
        for block in blocks[1:]:
            total = total + block
        return total

    def merge_all(blocks):
        count = add_all([block[4:6] for block in blocks])
        center = add_all([block[4:6] * block[0:2] for block in blocks]) / count
        squares = add_all(
            [
                block[2:4] + block[4:6] * (block[0:2] - center) * (block[0:2] - center)
                for block in blocks
            ]
        )
        return stack(center, squares, count)

    count = count_ref[0]
    own_count = jnp.full((1, width), count.astype(jnp.float32))
    live = lax.broadcasted_iota(jnp.int32, (rows, width), 0) < count

    def norm_stats(at, hidden, meanwhile=(None, None)):
        center = jnp.sum(hidden, axis=0, keepdims=True) / own_count
        centered = jnp.where(live, hidden - center, 0.0)
        squares = jnp.sum(centered * centered, axis=0, keepdims=True)
        merged = exchange(
            at, stack(fold(center), fold(squares), fold(own_count)), merge_all, meanwhile
        )
        total = unfold(merged[4:6])
        scale = lax.rsqrt(unfold(merged[2:4]) / total + eps_norm)
        return unfold(merged[0:2]), scale, total

    def norm_grad(at, norm, incoming, normed, scale, total, meanwhile=(None, None)):
        shift_sum = fold(jnp.sum(incoming, axis=0, keepdims=True))
        scale_sum = fold(jnp.sum(incoming * normed, axis=0, keepdims=True))
        summed = exchange(
            at, stack(shift_sum, scale_sum, jnp.zeros_like(shift_sum)), add_all, meanwhile
        )
        shift_sum, scale_sum = unfold(summed[0:2]), unfold(summed[2:4])
        bias_grad_ref[norm : norm + 1, :] = shift_sum
        gain_grad_ref[norm : norm + 1, :] = scale_sum
        hidden_grad = (
            scale
            * gain_ref[norm : norm + 1, :]
            * (incoming - shift_sum / total - normed * (scale_sum / total))
        )
        return jnp.where(live, hidden_grad, 0.0).astype(jnp.bfloat16)

    def pick(mask):
        return jnp.where(mask, jnp.bfloat16(1), jnp.bfloat16(0))

    def counting(shape, axis):
        return lax.broadcasted_iota(jnp.int32, shape, axis).astype(jnp.float32).astype(jnp.bfloat16)

    def place_columns(count):
        picked = dot(pickers[: count * rows, :], held[...]).astype(jnp.bfloat16)
        for part in range(count):
            columns[:, part * width : (part + 1) * width] = picked[part * rows : (part + 1) * rows]

    def convolve(weight, hidden):
        places = counting((rows, BLOCK), 1)
        places = (places, -1 - places)
        hidden[...] = jnp.zeros_like(hidden)

        def step(at, carry):
            for part in range(GROUP):
                wanted = jnp.concatenate([nb_cols[at * GROUP + part]] * (BLOCK // 128), axis=1)
                for block in range(2):
                    pickers[
                        part * rows : (part + 1) * rows, block * BLOCK : (block + 1) * BLOCK
                    ] = pick(wanted == places[block])
            place_columns(GROUP)
            weights = weight[pl.ds(at * GROUP, GROUP)].reshape(GROUP * width, width)
            hidden[...] += dot(columns[...], weights)
            return carry

        lax.fori_loop(0, offsets // GROUP, step, 0)

    def spread_rows(neighbours, first_offset):
        places = counting((BLOCK, rows), 0)
        for part in range(PAIR):
            wanted = neighbours[pl.ds(first_offset + part, 1), :].astype(jnp.float32)
            for first in range(0, rows, BLOCK):
                here = jnp.broadcast_to(wanted - first, (16, rows)).astype(jnp.bfloat16)
                pickers[part * rows + first : part * rows + first + BLOCK, :] = pick(
                    jnp.concatenate([here] * (BLOCK // 16), axis=0) == places
                )
        place_columns(PAIR)
        return columns[:, : PAIR * width]

    def put(first_unit, at, product, more):
        for part in range(PAIR):
            value = product[:, part * width : (part + 1) * width]
            if reduce_here:
                c = first_unit // PAIR + at
                value = value.reshape(grads.shape[1:4] + (8, width))
                here_rows = slice(8 * part, 8 * part + 8)
                if more:
                    value = value + grads[c, :, :, :, here_rows]
                grads[c, :, :, :, here_rows] = value
            else:
                unit = pl.multiple_of((first_unit + PAIR * at + part) * width, width)
                grads[pl.ds(unit, width), :] = value

    def convolve_back(weight, act_grad, first_unit, own_slot, other_slot):
        def step(first_offset, at, weigh):
            spread = spread_rows(nb_own, first_offset)
            weights = jnp.concatenate(
                [weight[first_offset + part] for part in range(PAIR)], axis=1
            )
            act_grad[...] += dot_last(spread, weights)
            if weigh:
                put(first_unit, at, dot(source_t[...], spread), False)

        def own_offsets(at, carry):
            step(own_offset + PAIR * at, at, True)
            own_slot(at)
            return carry

        def other_offsets(at, carry):
            step(other_offset + PAIR * at, at, False)
            other_slot(at)
            return carry

        lax.fori_loop(0, units // PAIR, own_offsets, 0)
        if reduce_here:
            lax.fori_loop(0, units // PAIR, other_offsets, 0)

    def convolve_pair(first_unit, first_step, last_step, at_slot):
        def step(at, carry):
            spread = spread_rows(nb_pair, own_offset + PAIR * at)
            put(first_unit, at, dot(pair_source_t[...], spread), True)
            at_slot(at)
            return carry

        lax.fori_loop(first_step, last_step, step, 0)

    core, row = lax.rem(group_me, 2), group_me // 2
    column, plane = lax.rem(dp_me, 2), dp_me // 2
    pair, high = lax.rem(plane, 2), plane // 2
    planes = 4
    core_peer = {"group": group_me + 1 - 2 * core}
    row_peer = {"group": group_me + 2 - 4 * row}
    column_peer = {"dp": dp_me + 1 - 2 * column}
    pair_peer = {"dp": dp_me + 2 - 4 * pair}
    cross_peer = {"dp": dp_me + 4 - 8 * high}
    own_offset = units * pair if reduce_here else 0
    other_offset = units * (1 - pair)
    own = pl.ds(2 * core, 2)
    lane_a, lane_b = 2 * core, 2 * core + 1
    kept_row, given_row = pl.ds(2 * row, 2), pl.ds(2 * (1 - row), 2)

    def send(c, number, source, target, peer):
        turn = lax.rem(c, RING)
        return pltpu.make_async_remote_copy(
            src_ref=source,
            dst_ref=target,
            send_sem=sum_send.at[turn, number],
            recv_sem=sum_recv.at[turn, number],
            device_id=peer,
            device_id_type=MESH,
        )

    def copies_of(c, stage):
        part, both = grads.at[c], pl.ds(PAIR * c, PAIR)
        if stage == 0:
            given = part.at[pl.ds(2 * (1 - core), 2)]
            return [send(c, 0, given, from_core.at[lax.rem(c, RING)], core_peer)]
        if stage == 1:
            return [
                send(c, 1, part.at[lane_a, 1 - column], from_first_a.at[c], column_peer),
                send(c, 2, part.at[lane_b, :, given_row], from_first_b.at[c], row_peer),
            ]
        if stage == 2:
            return [
                send(c, 3, part.at[lane_a, column, given_row], from_second_a.at[c], row_peer),
                send(c, 4, part.at[lane_b, 1 - column, kept_row], from_second_b.at[c], column_peer),
            ]
        if stage == 3:
            given = part.at[own, column, 2 * row + 1 - high]
            return [send(c, 5, given, from_line.at[c], cross_peer)]
        if stage == 4:
            block = results.at[pair, both, own, column, 2 * row + high]
            return [
                send(
                    c,
                    5 + step,
                    block,
                    block,
                    {"dp": 2 * lax.rem(plane + step, planes) + column},
                )
                for step in range(1, planes)
            ]
        if stage == 5:
            block_a = results.at[:, both, lane_a, column, kept_row]
            block_b = results.at[:, both, lane_b, column, kept_row]
            return [
                send(c, 9, block_a, block_a, row_peer),
                send(c, 10, block_b, block_b, column_peer),
            ]
        if stage == 6:
            block_a = results.at[:, both, lane_a, column]
            block_b = results.at[:, both, lane_b, :, kept_row]
            return [
                send(c, 11, block_a, block_a, column_peer),
                send(c, 12, block_b, block_b, row_peer),
            ]
        block = results.at[:, both, own]
        return [send(c, 13, block, block, core_peer)]

    def stage_of(c, stage):
        if stage > 0:
            for copy in copies_of(c, stage - 1):
                copy.wait()
        if stage == 1:
            grads[c, own] = grads[c, own] + from_core[lax.rem(c, RING)]
        if stage == 2:
            grads[c, lane_a, column] = grads[c, lane_a, column] + from_first_a[c]
            grads[c, lane_b, :, kept_row] = grads[c, lane_b, :, kept_row] + from_first_b[c]
        if stage == 3:
            grads[c, lane_a, column, kept_row] = grads[c, lane_a, column, kept_row] + from_second_a[c]
            grads[c, lane_b, column, kept_row] = grads[c, lane_b, column, kept_row] + from_second_b[c]
        if stage == 4:
            mine = 2 * row + high
            grads[c, own, column, mine] = grads[c, own, column, mine] + from_line[c]
            for unit in range(PAIR):
                results[pair, PAIR * c + unit, own, column, mine] = grads[
                    c, own, column, mine, 8 * unit : 8 * unit + 8
                ]
        if stage < len(LAGS) - 1:
            for copy in copies_of(c, stage):
                copy.start()

    per_weight = units // PAIR

    def slot(at):
        if not reduce_here:
            return
        for stage, lag in enumerate(LAGS):
            entry = at - lag
            if isinstance(at, int):
                c = entry if entry < per_weight else max(entry - GAP, per_weight - 1)
                if 0 <= entry < chunks + GAP and (c == entry or entry >= per_weight + GAP):
                    stage_of(c, stage)
                continue
            second = entry >= per_weight + GAP

            @pl.when(
                ((entry >= 0) & (entry < per_weight)) | (second & (entry < chunks + GAP))
            )
            def _():
                stage_of(entry - GAP * second.astype(jnp.int32), stage)

    def slot_after(at, steps_with, first_slot):
        wanted, number = False, first_slot
        for step in steps_with:
            wanted = wanted | (at == step)
            number = number + (at > step).astype(jnp.int32)

        @pl.when(wanted)
        def _():
            slot(number)

    def no_slot(at):
        pass

    def swap(at, source, target):
        return pltpu.make_async_remote_copy(
            src_ref=source,
            dst_ref=target,
            send_sem=swap_send.at[at],
            recv_sem=swap_recv.at[at],
            device_id=pair_peer,
            device_id_type=MESH,
        )

    def swap_rows(at):
        return swap(at, swap_out.at[at % 2], swap_in.at[at])

    def start_rows(at, value):
        if reduce_here:
            swap_out[at % 2] = value.astype(jnp.float32)
            swap_rows(at).start()

    side[...] = jnp.zeros_like(side)
    side[:offsets, :] = nb_rows[...]
    side[offsets : offsets + down_offsets, :] = down_rows_ref[...]
    side_cols[...] = side[...].T
    nb_own[...] = jnp.full_like(nb_own, rows)
    nb_own[:offsets, :] = nb_rows[...]
    swap_neighbours = swap(4, nb_own, nb_pair)
    for weight in (w_mid, w_out):
        weight[offsets:] = jnp.zeros_like(weight[offsets:])

    spread_fine[...] = fine_ref[...].astype(jnp.float32)
    for k in range(down_offsets):
        child = spread_fine[pl.ds(k % children, rows, stride=children), :]
        there = side_cols[:, offsets + k : offsets + k + 1] < fine_rows
        cols_down[:, k * in_width : (k + 1) * in_width] = jnp.where(there, child, 0.0).astype(
            jnp.bfloat16
        )
    loads[0].wait()
    hid_one[...] = dot(cols_down[...], w_down[...].reshape(down_offsets * in_width, width))

    def spread_neighbours():
        for k in range(offsets):
            wanted = side_cols[:, k : k + 1]
            code = jnp.where(
                wanted < BLOCK, wanted, jnp.where(wanted < rows, BLOCK - 1 - wanted, 4 * BLOCK)
            )
            nb_cols[k] = jnp.broadcast_to(code, (rows, 128)).astype(jnp.float32).astype(jnp.bfloat16)

    pl.semaphore_wait(barrier, group_size + dp_size - 2)

    swap_one = swap(0, hid_one, swap_in.at[0])
    swap_two = swap(1, hid_two, swap_in.at[1])

    def start_one():
        swap_neighbours.start()
        swap_one.start()

    def start_two():
        swap_two.start()

    beside = (spread_neighbours, start_one if reduce_here else None)
    center_one, scale_one, total = norm_stats(0, hid_one[...], beside)

    def pre_one(hidden=hid_one):
        normed = (hidden[...] - center_one) * scale_one
        return normed, normed * gain_ref[0:1, :] + bias_ref[0:1, :]

    _, pre = pre_one()
    act_one[...] = jnp.where(live, pre * sigmoid(pre), 0.0)
    act_one_b[...] = act_one[...].astype(jnp.bfloat16)
    loads[1].wait()
    held[...] = act_one_b[...]
    convolve(w_mid, hid_two)
    center_two, scale_two, _ = norm_stats(
        1, hid_two[...], (None, start_two if reduce_here else None)
    )

    def pre_two(hidden=hid_two):
        normed = (hidden[...] - center_two) * scale_two
        return normed, normed * gain_ref[1:2, :] + bias_ref[1:2, :]

    _, pre = pre_two()
    act_two_b[...] = jnp.where(live, pre * sigmoid(pre), 0.0).astype(jnp.bfloat16)
    loads[2].wait()
    held[...] = act_two_b[...]
    convolve(w_out, hid_three)
    center_three, scale_three, _ = norm_stats(2, hid_three[...])
    normed_three = (hid_three[...] - center_three) * scale_three
    summed = (
        jnp.where(live, normed_three * gain_ref[2:3, :] + bias_ref[2:3, :], 0.0) + act_one[...]
    )
    sigma = sigmoid(summed)
    features_ref[...] = jnp.where(live, summed * sigma, 0.0).astype(jnp.bfloat16)

    slope = sigma * (1.0 + summed * (1.0 - sigma))
    act_one[...] = jnp.where(live, cotangent_ref[...].astype(jnp.float32) * slope, 0.0)
    grad_hidden[...] = norm_grad(3, 2, act_one[...], normed_three, scale_three, total)
    start_rows(2, grad_hidden[...])
    held[...] = grad_hidden[...]
    grad_act[...] = jnp.zeros_like(grad_act)
    steps = units // PAIR

    def receive(swapped, pre_of, source_at, hidden_at):
        swapped.wait()
        _, pre = pre_of(swap_in.at[source_at])
        pair_source_t[...] = (pre * sigmoid(pre)).astype(jnp.bfloat16).T
        swap_rows(hidden_at).wait()
        held[...] = swap_in[hidden_at].astype(jnp.bfloat16)

    def pair_halves(first_unit, at_slot):
        middle = (steps + 1) // 2
        return (
            lambda: convolve_pair(first_unit, 0, middle, at_slot),
            lambda: convolve_pair(first_unit, middle, steps, at_slot),
        )

    nothing = (None, None)
    source_t[...] = act_two_b[...].T
    convolve_back(w_out, grad_act, 0, no_slot, no_slot)
    normed, pre = pre_two()
    incoming = jnp.where(live, grad_act[...] * silu_slope(pre), 0.0)
    if reduce_here:
        swap_neighbours.wait()
        receive(swap_two, pre_two, 1, 2)
    after = lambda at: slot_after(at, (1, 3, 4, 6), 0)
    beside = pair_halves(0, after) if reduce_here else nothing
    grad_hidden[...] = norm_grad(4, 1, incoming, normed, scale_two, total, beside)
    start_rows(3, grad_hidden[...])
    held[...] = grad_hidden[...]
    grad_act[...] = act_one[...]
    source_t[...] = act_one_b[...].T
    convolve_back(
        w_mid, grad_act, units, no_slot, lambda at: slot_after(at, (1, 3, 5), 4)
    )
    normed, pre = pre_one()
    incoming = jnp.where(live, grad_act[...] * silu_slope(pre), 0.0)
    if reduce_here:
        receive(swap_one, pre_one, 0, 3)
    after = lambda at: slot_after(at, (0, 1, 3, 4, 5), 7)
    beside = pair_halves(units, after) if reduce_here else nothing
    grad_hidden[...] = norm_grad(5, 0, incoming, normed, scale_one, total, beside)
    down_rows = down_offsets * in_width
    if reduce_here:
        down_all[...] = dot(cols_down[...].T, grad_hidden[...])
        kept = down_rows // 2
        swap_down = swap(
            5, down_all.at[pl.ds(pl.multiple_of(kept * (1 - pair), kept), kept), :], down_got
        )
        swap_down.start()
    else:
        grads[2 * units * width :, :] = dot(cols_down[...].T, grad_hidden[...])
    slot(12)
    slot(13)
    for child in range(children):
        total_child = jnp.zeros((rows, in_width), jnp.float32)
        for k in range(child, down_offsets, children):
            there = side_cols[:, offsets + k : offsets + k + 1] < fine_rows
            total_child += jnp.where(there, dot_last(grad_hidden[...], w_down[k]), 0.0)
        spread_fine[pl.ds(child, rows, stride=children), :] = total_child
    fine_grad_ref[...] = spread_fine[...].astype(jnp.bfloat16)
    slot(14)

    if reduce_here:

        def rest(at, carry):
            slot(at)
            return carry

        lax.fori_loop(15, chunks - 1 + GAP, rest, 0)
        swap_down.wait()
        for part in range(PAIR):
            total_down = (
                down_all[pl.ds(pl.multiple_of(kept * pair + part * width, width), width), :]
                + down_got[part * width : (part + 1) * width, :]
            )
            grads[chunks - 1, :, :, :, 8 * part : 8 * part + 8] = total_down.reshape(
                grads.shape[1:4] + (8, width)
            )
        lax.fori_loop(chunks - 1 + GAP, chunks + GAP + LAGS[-1], rest, 0)
    else:
        store = pltpu.make_async_copy(grads, results, load_sem.at[0])
        store.start()
        store.wait()


def place_kernel(
    features_ref,
    fine_grad_ref,
    grads_ref,
    gain_ref,
    bias_ref,
    features_out,
    fine_grad_out,
    grad_down_out,
    grad_mid_out,
    grad_out_out,
    gain_out,
    bias_out,
    sem,
):
    offsets = grad_mid_out.shape[0]
    units = (offsets + 1) // 2
    piece = (units + 1) // 2
    moves = []
    for pair in range(2):
        for at, target in enumerate((grad_out_out, grad_mid_out)):
            for first in range(0, units, piece):
                count = min(piece, offsets - units * pair - first, units - first)
                here = grads_ref.at[pair, pl.ds(at * units + first, count)]
                moves.append((here, target.at[pl.ds(units * pair + first, count)]))
        down_units = grad_down_out.shape[0] // 2
        here = grads_ref.at[pair, pl.ds(2 * units, down_units)]
        moves.append((here, grad_down_out.at[pl.ds(pair * down_units, down_units)]))
    copies = [
        pltpu.make_async_copy(source, target, sem.at[at])
        for at, (source, target) in enumerate(moves)
    ]
    for copy in copies:
        copy.start()
    features_out[...] = features_ref[...]
    fine_grad_out[...] = fine_grad_ref[...]
    gain_out[...] = gain_ref[...]
    bias_out[...] = bias_ref[...]
    for copy in copies:
        copy.wait()


def per_device(
    dp_size,
    group_size,
    fine_features,
    down_map,
    neighbours,
    voxel_counts,
    down_weight,
    mid_weight,
    out_weight,
    norm_gain,
    norm_bias,
    cotangent,
):
    rows, width = cotangent.shape
    fine_rows, in_width = fine_features.shape
    offsets = neighbours.shape[1]
    down_offsets = down_map.shape[1]
    f32, bf16, i32 = jnp.float32, jnp.bfloat16, jnp.int32
    vmem = pl.BlockSpec(memory_space=pltpu.VMEM)
    smem = pl.BlockSpec(memory_space=pltpu.SMEM)
    hbm = pl.BlockSpec(memory_space=pl.ANY)
    shape = jax.ShapeDtypeStruct
    reduce_here = dp_size == 8 and group_size == 4
    result = pltpu.VMEM if reduce_here else shape
    share = 2 if reduce_here else 1
    units = (offsets + 1) // 2 * 2 // share
    all_units = 2 * units + down_offsets * in_width // (share * width)
    grad_rows = all_units * width
    chunks = all_units // PAIR
    padded = (offsets + 1) // 2 * 2
    features, fine_grad, grads, gain_grad, bias_grad = pl.pallas_call(
        functools.partial(kernel, dp_size, group_size, reduce_here),
        out_shape=(
            result((rows, width), bf16),
            result((fine_rows, in_width), bf16),
            pltpu.VMEM((2, all_units, *GROUPS, 8, width), f32)
            if reduce_here
            else shape((grad_rows, width), f32),
            result(norm_gain.shape, f32),
            result(norm_bias.shape, f32),
        ),
        in_specs=[vmem, vmem, vmem, smem, hbm, hbm, hbm, vmem, vmem, vmem],
        out_specs=(vmem, vmem, vmem if reduce_here else hbm, vmem, vmem),
        scratch_shapes=[
            pltpu.VMEM(down_weight.shape, bf16),
            pltpu.VMEM((padded, width, width), bf16),
            pltpu.VMEM((padded, width, width), bf16),
            pltpu.VMEM((fine_rows, in_width), f32),
            pltpu.VMEM((rows, down_offsets * in_width), bf16),
            pltpu.VMEM((offsets, rows, 128), bf16),
            pltpu.VMEM((GROUP * rows, rows), bf16),
            pltpu.VMEM((rows, GROUP * width), bf16),
            pltpu.VMEM((rows, width), f32),
            pltpu.VMEM((rows, width), bf16),
            pltpu.VMEM((rows, width), bf16),
            pltpu.VMEM((rows, width), f32),
            pltpu.VMEM((rows, width), f32),
            pltpu.VMEM((rows, width), f32),
            pltpu.VMEM((rows, width), bf16),
            pltpu.VMEM((rows, width), bf16),
            pltpu.VMEM((width, rows), bf16),
            pltpu.VMEM((width, rows), bf16),
            pltpu.VMEM((rows, width), f32),
            pltpu.VMEM((128, rows), i32),
            pltpu.VMEM((rows, 128), i32),
            pltpu.VMEM((padded, rows), i32),
            pltpu.VMEM((padded, rows), i32),
            pltpu.VMEM((2, rows, width), f32),
            pltpu.VMEM((4, rows, width), f32),
            pltpu.VMEM((down_offsets * in_width, width), f32),
            pltpu.VMEM((down_offsets * in_width // 2, width), f32),
            pltpu.VMEM(
                (chunks, *GROUPS, 8 * PAIR, width) if reduce_here else (grad_rows, width), f32
            ),
            pltpu.VMEM((RING, 2, *GROUPS[1:], 8 * PAIR, width), f32),
            pltpu.VMEM((chunks, GROUPS[2], 8 * PAIR, width), f32),
            pltpu.VMEM((chunks, GROUPS[1], 2, 8 * PAIR, width), f32),
            pltpu.VMEM((chunks, 2, 8 * PAIR, width), f32),
            pltpu.VMEM((chunks, 2, 8 * PAIR, width), f32),
            pltpu.VMEM((chunks, 2, 8 * PAIR, width), f32),
            pltpu.VMEM((6, group_size, 8, width // 2), f32),
            pltpu.VMEM((6, dp_size, 8, width // 2), f32),
            pltpu.SemaphoreType.DMA((3,)),
            pltpu.SemaphoreType.DMA((RING, COPIES)),
            pltpu.SemaphoreType.DMA((RING, COPIES)),
            pltpu.SemaphoreType.DMA((6,)),
            pltpu.SemaphoreType.DMA((6,)),
            pltpu.SemaphoreType.DMA((6, group_size - 1)),
            pltpu.SemaphoreType.DMA((6, group_size - 1)),
            pltpu.SemaphoreType.DMA((6, dp_size - 1)),
            pltpu.SemaphoreType.DMA((6, dp_size - 1)),
        ],
        compiler_params=pltpu.CompilerParams(
            collective_id=0, has_side_effects=True, vmem_limit_bytes=(46 if reduce_here else 60) * 1024 * 1024
        ),
    )(
        fine_features,
        down_map.T,
        neighbours.T,
        voxel_counts,
        down_weight,
        mid_weight,
        out_weight,
        norm_gain,
        norm_bias,
        cotangent,
    )
    if not reduce_here:
        grads = lax.psum(grads, ("dp", "group"))
        middle, end = offsets * width, 2 * padded * width
        grad_out = grads[:middle].reshape(out_weight.shape)
        grad_mid = grads[padded * width : padded * width + middle].reshape(mid_weight.shape)
        grad_down = grads[end:].reshape(down_weight.shape)
        return (features, fine_grad, grad_down, grad_mid, grad_out, gain_grad, bias_grad)
    held = [
        pltpu.with_memory_space_constraint(value, pltpu.VMEM)
        for value in (features, fine_grad, grads, gain_grad, bias_grad)
    ]
    features, fine_grad, grad_down, grad_mid, grad_out, gain_grad, bias_grad = pl.pallas_call(
        place_kernel,
        out_shape=(
            shape(features.shape, bf16),
            shape(fine_grad.shape, bf16),
            shape((down_offsets * in_width // width, *GROUPS, 8, width), f32),
            shape((offsets, *GROUPS, 8, width), f32),
            shape((offsets, *GROUPS, 8, width), f32),
            shape(norm_gain.shape, f32),
            shape(norm_bias.shape, f32),
        ),
        in_specs=[vmem] * 5,
        out_specs=(vmem, vmem, hbm, hbm, hbm, vmem, vmem),
        scratch_shapes=[pltpu.SemaphoreType.DMA((10,))],
        compiler_params=pltpu.CompilerParams(vmem_limit_bytes=8 * 1024 * 1024),
    )(*held)
    grad_down = grad_down.reshape(down_weight.shape)
    grad_mid = grad_mid.reshape(mid_weight.shape)
    grad_out = grad_out.reshape(out_weight.shape)
    return (features, fine_grad, grad_down, grad_mid, grad_out, gain_grad, bias_grad)


def solution(mesh):
    in_specs = (
        P(("dp", "group"), None),
        P(("dp", "group"), None),
        P(("dp", "group"), None),
        P(("dp", "group")),
        P(),
        P(),
        P(),
        P(),
        P(),
        P(("dp", "group"), None),
    )
    out_specs = (P(("dp", "group"), None), P(("dp", "group"), None), P(), P(), P(), P(), P())
    return jax.shard_map(
        functools.partial(per_device, mesh.shape["dp"], mesh.shape["group"]),
        mesh=mesh,
        in_specs=in_specs,
        out_specs=out_specs,
        check_vma=False,
    )
```

```python
import functools

import jax
import jax.numpy as jnp
from jax import lax
from jax.experimental import pallas as pl
from jax.experimental.pallas import tpu as pltpu
from jax.sharding import PartitionSpec as P

eps_norm = 1e-05
MESH = pl.DeviceIdType.MESH
GROUP = 3
BLOCK = 256
PAIR = 2
COPIES = 14
GROUPS = (4, 2, 4)
GAP = 1
LAGS = (0, 1, 2, 3, 5, 7, 8, 9, 10)
RING = 8


def sigmoid(value):
    return 1.0 / (1.0 + jnp.exp(-value))


def silu_slope(value):
    sigma = sigmoid(value)
    return sigma * (1.0 + value * (1.0 - sigma))


def dot(left, right):
    return jnp.dot(left, right, preferred_element_type=jnp.float32)


def dot_last(left, right):
    return lax.dot_general(
        left, right, (((1,), (1,)), ((), ())), preferred_element_type=jnp.float32
    )


def kernel(
    dp_size,
    group_size,
    reduce_here,
    fine_ref,
    down_rows_ref,
    nb_rows,
    count_ref,
    down_hbm,
    mid_hbm,
    out_hbm,
    gain_ref,
    bias_ref,
    cotangent_ref,
    features_ref,
    fine_grad_ref,
    results,
    gain_grad_ref,
    bias_grad_ref,
    w_down,
    w_mid,
    w_out,
    spread_fine,
    cols_down,
    nb_cols,
    pickers,
    columns,
    act_one,
    act_one_b,
    act_two_b,
    hid_one,
    hid_two,
    hid_three,
    held,
    grad_hidden,
    source_t,
    pair_source_t,
    grad_act,
    side,
    side_cols,
    nb_own,
    nb_pair,
    swap_out,
    swap_in,
    down_all,
    down_got,
    grads,
    from_core,
    from_first_a,
    from_first_b,
    from_second_a,
    from_second_b,
    from_line,
    near,
    far,
    load_sem,
    sum_send,
    sum_recv,
    swap_send,
    swap_recv,
    near_send,
    near_recv,
    far_send,
    far_recv,
):
    rows, width = cotangent_ref.shape
    offsets = nb_rows.shape[0]
    fine_rows, in_width = fine_ref.shape
    children = fine_rows // rows
    down_offsets = down_rows_ref.shape[0]
    units = (offsets + 1) // 2 * (1 if reduce_here else 2)
    chunks = grads.shape[0]
    dp_me = lax.axis_index("dp")
    group_me = lax.axis_index("group")

    loads = [
        pltpu.make_async_copy(source, target, load_sem.at[at])
        for at, (source, target) in enumerate(
            (
                (down_hbm, w_down),
                (mid_hbm, w_mid.at[pl.ds(0, offsets)]),
                (out_hbm, w_out.at[pl.ds(0, offsets)]),
            )
        )
    ]
    for load in loads:
        load.start()

    barrier = pltpu.get_barrier_semaphore()
    for step in range(1, group_size):
        pl.semaphore_signal(
            barrier,
            inc=1,
            device_id={"group": lax.rem(group_me + step, group_size)},
            device_id_type=MESH,
        )
    for step in range(1, dp_size):
        pl.semaphore_signal(
            barrier,
            inc=1,
            device_id={"dp": lax.rem(dp_me + step, dp_size)},
            device_id_type=MESH,
        )

    def share(at, axis, me, size, slots, send, recv):
        copies = []
        for step in range(1, size):
            copies.append(
                pltpu.make_async_remote_copy(
                    src_ref=slots.at[at, me],
                    dst_ref=slots.at[at, me],
                    send_sem=send.at[at, step - 1],
                    recv_sem=recv.at[at, step - 1],
                    device_id={axis: lax.rem(me + step, size)},
                    device_id_type=MESH,
                )
            )
        for copy in copies:
            copy.start()
        return copies

    def exchange(at, block, combine, meanwhile=(None, None)):
        near[at, group_me] = block
        copies = share(at, "group", group_me, group_size, near, near_send, near_recv)
        if meanwhile[0] is not None:
            meanwhile[0]()
        for copy in copies:
            copy.wait()
        far[at, dp_me] = combine([near[at, slot] for slot in range(group_size)])
        copies = share(at, "dp", dp_me, dp_size, far, far_send, far_recv)
        if meanwhile[1] is not None:
            meanwhile[1]()
        for copy in copies:
            copy.wait()
        return combine([far[at, slot] for slot in range(dp_size)])

    lanes = width // 2

    def stack(first, second, third):
        filler = jnp.zeros((2, lanes), jnp.float32)
        return jnp.concatenate([first, second, third, filler], axis=0)

    def fold(value):
        return jnp.concatenate([value[:, :lanes], value[:, lanes:]], axis=0)

    def unfold(value):
        return jnp.concatenate([value[0:1], value[1:2]], axis=1)

    def add_all(blocks):
        total = blocks[0]
        for block in blocks[1:]:
            total = total + block
        return total

    def merge_all(blocks):
        count = add_all([block[4:6] for block in blocks])
        center = add_all([block[4:6] * block[0:2] for block in blocks]) / count
        squares = add_all(
            [
                block[2:4] + block[4:6] * (block[0:2] - center) * (block[0:2] - center)
                for block in blocks
            ]
        )
        return stack(center, squares, count)

    count = count_ref[0]
    own_count = jnp.full((1, width), count.astype(jnp.float32))
    live = lax.broadcasted_iota(jnp.int32, (rows, width), 0) < count

    def norm_stats(at, hidden, meanwhile=(None, None)):
        center = jnp.sum(hidden, axis=0, keepdims=True) / own_count
        centered = jnp.where(live, hidden - center, 0.0)
        squares = jnp.sum(centered * centered, axis=0, keepdims=True)
        merged = exchange(
            at, stack(fold(center), fold(squares), fold(own_count)), merge_all, meanwhile
        )
        total = unfold(merged[4:6])
        scale = lax.rsqrt(unfold(merged[2:4]) / total + eps_norm)
        return unfold(merged[0:2]), scale, total

    def norm_grad(at, norm, incoming, normed, scale, total, meanwhile=(None, None)):
        shift_sum = fold(jnp.sum(incoming, axis=0, keepdims=True))
        scale_sum = fold(jnp.sum(incoming * normed, axis=0, keepdims=True))
        summed = exchange(
            at, stack(shift_sum, scale_sum, jnp.zeros_like(shift_sum)), add_all, meanwhile
        )
        shift_sum, scale_sum = unfold(summed[0:2]), unfold(summed[2:4])
        bias_grad_ref[norm : norm + 1, :] = shift_sum
        gain_grad_ref[norm : norm + 1, :] = scale_sum
        hidden_grad = (
            scale
            * gain_ref[norm : norm + 1, :]
            * (incoming - shift_sum / total - normed * (scale_sum / total))
        )
        return jnp.where(live, hidden_grad, 0.0).astype(jnp.bfloat16)

    def pick(mask):
        return jnp.where(mask, jnp.bfloat16(1), jnp.bfloat16(0))

    def counting(shape, axis):
        return lax.broadcasted_iota(jnp.int32, shape, axis).astype(jnp.float32).astype(jnp.bfloat16)

    def place_columns(turn, count):
        picked = dot(pickers[turn, : count * rows, :], held[...]).astype(jnp.bfloat16)
        for part in range(count):
            columns[turn, :, part * width : (part + 1) * width] = picked[
                part * rows : (part + 1) * rows
            ]

    def run_steps(first, last, count, build, use, after):
        build(first % 2, first)

        def one(turn, step, more):
            place_columns(turn, count)
            if more:
                build(1 - turn, step + 1)
            use(turn, step)

        bodies = (last - first - 1) // 2

        def body(at, carry):
            for turn in range(2):
                one((first + turn) % 2, first + 2 * at + turn, True)
            for turn in range(2):
                after(first + 2 * at + turn)
            return carry

        lax.fori_loop(0, bodies, body, 0)
        for step in range(first + 2 * bodies, last):
            one(step % 2, step, step + 1 < last)
            after(step)

    def convolve(weight, hidden):
        places = counting((rows, BLOCK), 1)
        places = (places, -1 - places)
        hidden[...] = jnp.zeros_like(hidden)

        def build(turn, step):
            for part in range(GROUP):
                wanted = jnp.concatenate([nb_cols[step * GROUP + part]] * (BLOCK // 128), axis=1)
                for block in range(2):
                    pickers[
                        turn,
                        part * rows : (part + 1) * rows,
                        block * BLOCK : (block + 1) * BLOCK,
                    ] = pick(wanted == places[block])

        def use(turn, step):
            weights = weight[pl.ds(step * GROUP, GROUP)].reshape(GROUP * width, width)
            hidden[...] += dot(columns[turn], weights)

        run_steps(0, offsets // GROUP, GROUP, build, use, no_slot)

    def build_spread(neighbours, first_offset):
        places = counting((BLOCK, rows), 0)

        def build(turn, step):
            for part in range(PAIR):
                wanted = neighbours[pl.ds(first_offset + PAIR * step + part, 1), :]
                wanted = wanted.astype(jnp.float32)
                for first in range(0, rows, BLOCK):
                    here = jnp.broadcast_to(wanted - first, (16, rows)).astype(jnp.bfloat16)
                    pickers[turn, part * rows + first : part * rows + first + BLOCK, :] = pick(
                        jnp.concatenate([here] * (BLOCK // 16), axis=0) == places
                    )

        return build

    def no_slot(at):
        pass

    def put(first_unit, at, product, more):
        for part in range(PAIR):
            value = product[:, part * width : (part + 1) * width]
            if reduce_here:
                c = first_unit // PAIR + at
                value = value.reshape(grads.shape[1:4] + (8, width))
                here_rows = slice(8 * part, 8 * part + 8)
                if more:
                    value = value + grads[c, :, :, :, here_rows]
                grads[c, :, :, :, here_rows] = value
            else:
                unit = pl.multiple_of((first_unit + PAIR * at + part) * width, width)
                grads[pl.ds(unit, width), :] = value

    def convolve_back(weight, act_grad, first_unit, own_slot, other_slot):
        def use_of(first_offset, weigh):
            def use(turn, step):
                spread = columns[turn, :, : PAIR * width]
                k = first_offset + PAIR * step
                weights = jnp.concatenate([weight[k + part] for part in range(PAIR)], axis=1)
                act_grad[...] += dot_last(spread, weights)
                if weigh:
                    put(first_unit, step, dot(source_t[...], spread), False)

            return use

        steps = units // PAIR
        build = build_spread(nb_own, own_offset)
        run_steps(0, steps, PAIR, build, use_of(own_offset, True), own_slot)
        if reduce_here:
            build = build_spread(nb_own, other_offset)
            run_steps(0, steps, PAIR, build, use_of(other_offset, False), other_slot)

    def convolve_pair(first_unit, first_step, last_step, at_slot):
        def use(turn, step):
            spread = columns[turn, :, : PAIR * width]
            put(first_unit, step, dot(pair_source_t[...], spread), True)

        build = build_spread(nb_pair, own_offset)
        run_steps(first_step, last_step, PAIR, build, use, at_slot)

    core, row = lax.rem(group_me, 2), group_me // 2
    column, plane = lax.rem(dp_me, 2), dp_me // 2
    pair, high = lax.rem(plane, 2), plane // 2
    planes = 4
    core_peer = {"group": group_me + 1 - 2 * core}
    row_peer = {"group": group_me + 2 - 4 * row}
    column_peer = {"dp": dp_me + 1 - 2 * column}
    pair_peer = {"dp": dp_me + 2 - 4 * pair}
    cross_peer = {"dp": dp_me + 4 - 8 * high}
    own_offset = units * pair if reduce_here else 0
    other_offset = units * (1 - pair)
    own = pl.ds(2 * core, 2)
    lane_a, lane_b = 2 * core, 2 * core + 1
    kept_row, given_row = pl.ds(2 * row, 2), pl.ds(2 * (1 - row), 2)

    def send(c, number, source, target, peer):
        turn = lax.rem(c, RING)
        return pltpu.make_async_remote_copy(
            src_ref=source,
            dst_ref=target,
            send_sem=sum_send.at[turn, number],
            recv_sem=sum_recv.at[turn, number],
            device_id=peer,
            device_id_type=MESH,
        )

    def copies_of(c, stage):
        part, both = grads.at[c], pl.ds(PAIR * c, PAIR)
        if stage == 0:
            given = part.at[pl.ds(2 * (1 - core), 2)]
            return [send(c, 0, given, from_core.at[lax.rem(c, RING)], core_peer)]
        if stage == 1:
            return [
                send(c, 1, part.at[lane_a, 1 - column], from_first_a.at[c], column_peer),
                send(c, 2, part.at[lane_b, :, given_row], from_first_b.at[c], row_peer),
            ]
        if stage == 2:
            return [
                send(c, 3, part.at[lane_a, column, given_row], from_second_a.at[c], row_peer),
                send(c, 4, part.at[lane_b, 1 - column, kept_row], from_second_b.at[c], column_peer),
            ]
        if stage == 3:
            given = part.at[own, column, 2 * row + 1 - high]
            return [send(c, 5, given, from_line.at[c], cross_peer)]
        if stage == 4:
            block = results.at[pair, both, own, column, 2 * row + high]
            return [
                send(
                    c,
                    5 + step,
                    block,
                    block,
                    {"dp": 2 * lax.rem(plane + step, planes) + column},
                )
                for step in range(1, planes)
            ]
        if stage == 5:
            block_a = results.at[:, both, lane_a, column, kept_row]
            block_b = results.at[:, both, lane_b, column, kept_row]
            return [
                send(c, 9, block_a, block_a, row_peer),
                send(c, 10, block_b, block_b, column_peer),
            ]
        if stage == 6:
            block_a = results.at[:, both, lane_a, column]
            block_b = results.at[:, both, lane_b, :, kept_row]
            return [
                send(c, 11, block_a, block_a, column_peer),
                send(c, 12, block_b, block_b, row_peer),
            ]
        block = results.at[:, both, own]
        return [send(c, 13, block, block, core_peer)]

    def stage_of(c, stage):
        if stage > 0:
            for copy in copies_of(c, stage - 1):
                copy.wait()
        if stage == 1:
            grads[c, own] = grads[c, own] + from_core[lax.rem(c, RING)]
        if stage == 2:
            grads[c, lane_a, column] = grads[c, lane_a, column] + from_first_a[c]
            grads[c, lane_b, :, kept_row] = grads[c, lane_b, :, kept_row] + from_first_b[c]
        if stage == 3:
            grads[c, lane_a, column, kept_row] = grads[c, lane_a, column, kept_row] + from_second_a[c]
            grads[c, lane_b, column, kept_row] = grads[c, lane_b, column, kept_row] + from_second_b[c]
        if stage == 4:
            mine = 2 * row + high
            grads[c, own, column, mine] = grads[c, own, column, mine] + from_line[c]
            for unit in range(PAIR):
                results[pair, PAIR * c + unit, own, column, mine] = grads[
                    c, own, column, mine, 8 * unit : 8 * unit + 8
                ]
        if stage < len(LAGS) - 1:
            for copy in copies_of(c, stage):
                copy.start()

    per_weight = units // PAIR

    def slot(at):
        if not reduce_here:
            return
        for stage, lag in enumerate(LAGS):
            entry = at - lag
            if isinstance(at, int):
                c = entry if entry < per_weight else max(entry - GAP, per_weight - 1)
                if 0 <= entry < chunks + GAP and (c == entry or entry >= per_weight + GAP):
                    stage_of(c, stage)
                continue
            second = entry >= per_weight + GAP

            @pl.when(
                ((entry >= 0) & (entry < per_weight)) | (second & (entry < chunks + GAP))
            )
            def _():
                stage_of(entry - GAP * second.astype(jnp.int32), stage)

    def slot_after(at, steps_with, first_slot):
        if isinstance(at, int):
            if at in steps_with:
                slot(first_slot + steps_with.index(at))
            return
        wanted, number = False, first_slot
        for step in steps_with:
            wanted = wanted | (at == step)
            number = number + (at > step).astype(jnp.int32)

        @pl.when(wanted)
        def _():
            slot(number)

    def swap(at, source, target):
        return pltpu.make_async_remote_copy(
            src_ref=source,
            dst_ref=target,
            send_sem=swap_send.at[at],
            recv_sem=swap_recv.at[at],
            device_id=pair_peer,
            device_id_type=MESH,
        )

    def swap_rows(at):
        return swap(at, swap_out.at[at % 2], swap_in.at[at])

    def start_rows(at, value):
        if reduce_here:
            swap_out[at % 2] = value.astype(jnp.float32)
            swap_rows(at).start()

    side[...] = jnp.zeros_like(side)
    side[:offsets, :] = nb_rows[...]
    side[offsets : offsets + down_offsets, :] = down_rows_ref[...]
    side_cols[...] = side[...].T
    nb_own[...] = jnp.full_like(nb_own, rows)
    nb_own[:offsets, :] = nb_rows[...]
    swap_neighbours = swap(4, nb_own, nb_pair)
    for weight in (w_mid, w_out):
        weight[offsets:] = jnp.zeros_like(weight[offsets:])

    spread_fine[...] = fine_ref[...].astype(jnp.float32)
    for k in range(down_offsets):
        child = spread_fine[pl.ds(k % children, rows, stride=children), :]
        there = side_cols[:, offsets + k : offsets + k + 1] < fine_rows
        cols_down[:, k * in_width : (k + 1) * in_width] = jnp.where(there, child, 0.0).astype(
            jnp.bfloat16
        )
    loads[0].wait()
    hid_one[...] = dot(cols_down[...], w_down[...].reshape(down_offsets * in_width, width))

    def spread_neighbours():
        for k in range(offsets):
            wanted = side_cols[:, k : k + 1]
            code = jnp.where(
                wanted < BLOCK, wanted, jnp.where(wanted < rows, BLOCK - 1 - wanted, 4 * BLOCK)
            )
            nb_cols[k] = jnp.broadcast_to(code, (rows, 128)).astype(jnp.float32).astype(jnp.bfloat16)

    pl.semaphore_wait(barrier, group_size + dp_size - 2)

    swap_one = swap(0, hid_one, swap_in.at[0])
    swap_two = swap(1, hid_two, swap_in.at[1])

    def start_one():
        swap_neighbours.start()
        swap_one.start()

    def start_two():
        swap_two.start()

    beside = (spread_neighbours, start_one if reduce_here else None)
    center_one, scale_one, total = norm_stats(0, hid_one[...], beside)

    def pre_one(hidden=hid_one):
        normed = (hidden[...] - center_one) * scale_one
        return normed, normed * gain_ref[0:1, :] + bias_ref[0:1, :]

    _, pre = pre_one()
    act_one[...] = jnp.where(live, pre * sigmoid(pre), 0.0)
    act_one_b[...] = act_one[...].astype(jnp.bfloat16)
    loads[1].wait()
    held[...] = act_one_b[...]
    convolve(w_mid, hid_two)
    center_two, scale_two, _ = norm_stats(
        1, hid_two[...], (None, start_two if reduce_here else None)
    )

    def pre_two(hidden=hid_two):
        normed = (hidden[...] - center_two) * scale_two
        return normed, normed * gain_ref[1:2, :] + bias_ref[1:2, :]

    _, pre = pre_two()
    act_two_b[...] = jnp.where(live, pre * sigmoid(pre), 0.0).astype(jnp.bfloat16)
    loads[2].wait()
    held[...] = act_two_b[...]
    convolve(w_out, hid_three)
    center_three, scale_three, _ = norm_stats(2, hid_three[...])
    normed_three = (hid_three[...] - center_three) * scale_three
    summed = (
        jnp.where(live, normed_three * gain_ref[2:3, :] + bias_ref[2:3, :], 0.0) + act_one[...]
    )
    sigma = sigmoid(summed)
    features_ref[...] = jnp.where(live, summed * sigma, 0.0).astype(jnp.bfloat16)

    slope = sigma * (1.0 + summed * (1.0 - sigma))
    act_one[...] = jnp.where(live, cotangent_ref[...].astype(jnp.float32) * slope, 0.0)
    grad_hidden[...] = norm_grad(3, 2, act_one[...], normed_three, scale_three, total)
    start_rows(2, grad_hidden[...])
    held[...] = grad_hidden[...]
    grad_act[...] = jnp.zeros_like(grad_act)
    steps = units // PAIR

    def receive(swapped, pre_of, source_at, hidden_at):
        swapped.wait()
        _, pre = pre_of(swap_in.at[source_at])
        pair_source_t[...] = (pre * sigmoid(pre)).astype(jnp.bfloat16).T
        swap_rows(hidden_at).wait()
        held[...] = swap_in[hidden_at].astype(jnp.bfloat16)

    def pair_halves(first_unit, at_slot):
        middle = (steps + 1) // 2
        return (
            lambda: convolve_pair(first_unit, 0, middle, at_slot),
            lambda: convolve_pair(first_unit, middle, steps, at_slot),
        )

    nothing = (None, None)
    source_t[...] = act_two_b[...].T
    convolve_back(w_out, grad_act, 0, no_slot, no_slot)
    normed, pre = pre_two()
    incoming = jnp.where(live, grad_act[...] * silu_slope(pre), 0.0)
    if reduce_here:
        swap_neighbours.wait()
        receive(swap_two, pre_two, 1, 2)
    after = lambda at: slot_after(at, (1, 3, 4, 6), 0)
    beside = pair_halves(0, after) if reduce_here else nothing
    grad_hidden[...] = norm_grad(4, 1, incoming, normed, scale_two, total, beside)
    start_rows(3, grad_hidden[...])
    held[...] = grad_hidden[...]
    grad_act[...] = act_one[...]
    source_t[...] = act_one_b[...].T
    convolve_back(
        w_mid, grad_act, units, no_slot, lambda at: slot_after(at, (1, 3, 5), 4)
    )
    normed, pre = pre_one()
    incoming = jnp.where(live, grad_act[...] * silu_slope(pre), 0.0)
    if reduce_here:
        receive(swap_one, pre_one, 0, 3)
    after = lambda at: slot_after(at, (0, 1, 3, 4, 5), 7)
    beside = pair_halves(units, after) if reduce_here else nothing
    grad_hidden[...] = norm_grad(5, 0, incoming, normed, scale_one, total, beside)
    down_rows = down_offsets * in_width
    if reduce_here:
        down_all[...] = dot(cols_down[...].T, grad_hidden[...])
        kept = down_rows // 2
        swap_down = swap(
            5, down_all.at[pl.ds(pl.multiple_of(kept * (1 - pair), kept), kept), :], down_got
        )
        swap_down.start()
    else:
        grads[2 * units * width :, :] = dot(cols_down[...].T, grad_hidden[...])
    slot(12)
    slot(13)
    for child in range(children):
        total_child = jnp.zeros((rows, in_width), jnp.float32)
        for k in range(child, down_offsets, children):
            there = side_cols[:, offsets + k : offsets + k + 1] < fine_rows
            total_child += jnp.where(there, dot_last(grad_hidden[...], w_down[k]), 0.0)
        spread_fine[pl.ds(child, rows, stride=children), :] = total_child
    fine_grad_ref[...] = spread_fine[...].astype(jnp.bfloat16)
    slot(14)

    if reduce_here:

        def rest(at, carry):
            slot(at)
            return carry

        lax.fori_loop(15, chunks - 1 + GAP, rest, 0)
        swap_down.wait()
        for part in range(PAIR):
            total_down = (
                down_all[pl.ds(pl.multiple_of(kept * pair + part * width, width), width), :]
                + down_got[part * width : (part + 1) * width, :]
            )
            grads[chunks - 1, :, :, :, 8 * part : 8 * part + 8] = total_down.reshape(
                grads.shape[1:4] + (8, width)
            )
        lax.fori_loop(chunks - 1 + GAP, chunks + GAP + LAGS[-1], rest, 0)
    else:
        store = pltpu.make_async_copy(grads, results, load_sem.at[0])
        store.start()
        store.wait()


def place_kernel(
    features_ref,
    fine_grad_ref,
    grads_ref,
    gain_ref,
    bias_ref,
    features_out,
    fine_grad_out,
    grad_down_out,
    grad_mid_out,
    grad_out_out,
    gain_out,
    bias_out,
    sem,
):
    offsets = grad_mid_out.shape[0]
    units = (offsets + 1) // 2
    piece = (units + 1) // 2
    moves = []
    for pair in range(2):
        for at, target in enumerate((grad_out_out, grad_mid_out)):
            for first in range(0, units, piece):
                count = min(piece, offsets - units * pair - first, units - first)
                here = grads_ref.at[pair, pl.ds(at * units + first, count)]
                moves.append((here, target.at[pl.ds(units * pair + first, count)]))
        down_units = grad_down_out.shape[0] // 2
        here = grads_ref.at[pair, pl.ds(2 * units, down_units)]
        moves.append((here, grad_down_out.at[pl.ds(pair * down_units, down_units)]))
    copies = [
        pltpu.make_async_copy(source, target, sem.at[at])
        for at, (source, target) in enumerate(moves)
    ]
    for copy in copies:
        copy.start()
    features_out[...] = features_ref[...]
    fine_grad_out[...] = fine_grad_ref[...]
    gain_out[...] = gain_ref[...]
    bias_out[...] = bias_ref[...]
    for copy in copies:
        copy.wait()


def per_device(
    dp_size,
    group_size,
    fine_features,
    down_map,
    neighbours,
    voxel_counts,
    down_weight,
    mid_weight,
    out_weight,
    norm_gain,
    norm_bias,
    cotangent,
):
    rows, width = cotangent.shape
    fine_rows, in_width = fine_features.shape
    offsets = neighbours.shape[1]
    down_offsets = down_map.shape[1]
    f32, bf16, i32 = jnp.float32, jnp.bfloat16, jnp.int32
    vmem = pl.BlockSpec(memory_space=pltpu.VMEM)
    smem = pl.BlockSpec(memory_space=pltpu.SMEM)
    hbm = pl.BlockSpec(memory_space=pl.ANY)
    shape = jax.ShapeDtypeStruct
    reduce_here = dp_size == 8 and group_size == 4
    result = pltpu.VMEM if reduce_here else shape
    share = 2 if reduce_here else 1
    units = (offsets + 1) // 2 * 2 // share
    all_units = 2 * units + down_offsets * in_width // (share * width)
    grad_rows = all_units * width
    chunks = all_units // PAIR
    padded = (offsets + 1) // 2 * 2
    features, fine_grad, grads, gain_grad, bias_grad = pl.pallas_call(
        functools.partial(kernel, dp_size, group_size, reduce_here),
        out_shape=(
            result((rows, width), bf16),
            result((fine_rows, in_width), bf16),
            pltpu.VMEM((2, all_units, *GROUPS, 8, width), f32)
            if reduce_here
            else shape((grad_rows, width), f32),
            result(norm_gain.shape, f32),
            result(norm_bias.shape, f32),
        ),
        in_specs=[vmem, vmem, vmem, smem, hbm, hbm, hbm, vmem, vmem, vmem],
        out_specs=(vmem, vmem, vmem if reduce_here else hbm, vmem, vmem),
        scratch_shapes=[
            pltpu.VMEM(down_weight.shape, bf16),
            pltpu.VMEM((padded, width, width), bf16),
            pltpu.VMEM((padded, width, width), bf16),
            pltpu.VMEM((fine_rows, in_width), f32),
            pltpu.VMEM((rows, down_offsets * in_width), bf16),
            pltpu.VMEM((offsets, rows, 128), bf16),
            pltpu.VMEM((2, GROUP * rows, rows), bf16),
            pltpu.VMEM((2, rows, GROUP * width), bf16),
            pltpu.VMEM((rows, width), f32),
            pltpu.VMEM((rows, width), bf16),
            pltpu.VMEM((rows, width), bf16),
            pltpu.VMEM((rows, width), f32),
            pltpu.VMEM((rows, width), f32),
            pltpu.VMEM((rows, width), f32),
            pltpu.VMEM((rows, width), bf16),
            pltpu.VMEM((rows, width), bf16),
            pltpu.VMEM((width, rows), bf16),
            pltpu.VMEM((width, rows), bf16),
            pltpu.VMEM((rows, width), f32),
            pltpu.VMEM((128, rows), i32),
            pltpu.VMEM((rows, 128), i32),
            pltpu.VMEM((padded, rows), i32),
            pltpu.VMEM((padded, rows), i32),
            pltpu.VMEM((2, rows, width), f32),
            pltpu.VMEM((4, rows, width), f32),
            pltpu.VMEM((down_offsets * in_width, width), f32),
            pltpu.VMEM((down_offsets * in_width // 2, width), f32),
            pltpu.VMEM(
                (chunks, *GROUPS, 8 * PAIR, width) if reduce_here else (grad_rows, width), f32
            ),
            pltpu.VMEM((RING, 2, *GROUPS[1:], 8 * PAIR, width), f32),
            pltpu.VMEM((chunks, GROUPS[2], 8 * PAIR, width), f32),
            pltpu.VMEM((chunks, GROUPS[1], 2, 8 * PAIR, width), f32),
            pltpu.VMEM((chunks, 2, 8 * PAIR, width), f32),
            pltpu.VMEM((chunks, 2, 8 * PAIR, width), f32),
            pltpu.VMEM((chunks, 2, 8 * PAIR, width), f32),
            pltpu.VMEM((6, group_size, 8, width // 2), f32),
            pltpu.VMEM((6, dp_size, 8, width // 2), f32),
            pltpu.SemaphoreType.DMA((3,)),
            pltpu.SemaphoreType.DMA((RING, COPIES)),
            pltpu.SemaphoreType.DMA((RING, COPIES)),
            pltpu.SemaphoreType.DMA((6,)),
            pltpu.SemaphoreType.DMA((6,)),
            pltpu.SemaphoreType.DMA((6, group_size - 1)),
            pltpu.SemaphoreType.DMA((6, group_size - 1)),
            pltpu.SemaphoreType.DMA((6, dp_size - 1)),
            pltpu.SemaphoreType.DMA((6, dp_size - 1)),
        ],
        compiler_params=pltpu.CompilerParams(
            collective_id=0, has_side_effects=True, vmem_limit_bytes=(46 if reduce_here else 60) * 1024 * 1024
        ),
    )(
        fine_features,
        down_map.T,
        neighbours.T,
        voxel_counts,
        down_weight,
        mid_weight,
        out_weight,
        norm_gain,
        norm_bias,
        cotangent,
    )
    if not reduce_here:
        grads = lax.psum(grads, ("dp", "group"))
        middle, end = offsets * width, 2 * padded * width
        grad_out = grads[:middle].reshape(out_weight.shape)
        grad_mid = grads[padded * width : padded * width + middle].reshape(mid_weight.shape)
        grad_down = grads[end:].reshape(down_weight.shape)
        return (features, fine_grad, grad_down, grad_mid, grad_out, gain_grad, bias_grad)
    held = [
        pltpu.with_memory_space_constraint(value, pltpu.VMEM)
        for value in (features, fine_grad, grads, gain_grad, bias_grad)
    ]
    features, fine_grad, grad_down, grad_mid, grad_out, gain_grad, bias_grad = pl.pallas_call(
        place_kernel,
        out_shape=(
            shape(features.shape, bf16),
            shape(fine_grad.shape, bf16),
            shape((down_offsets * in_width // width, *GROUPS, 8, width), f32),
            shape((offsets, *GROUPS, 8, width), f32),
            shape((offsets, *GROUPS, 8, width), f32),
            shape(norm_gain.shape, f32),
            shape(norm_bias.shape, f32),
        ),
        in_specs=[vmem] * 5,
        out_specs=(vmem, vmem, hbm, hbm, hbm, vmem, vmem),
        scratch_shapes=[pltpu.SemaphoreType.DMA((10,))],
        compiler_params=pltpu.CompilerParams(vmem_limit_bytes=8 * 1024 * 1024),
    )(*held)
    grad_down = grad_down.reshape(down_weight.shape)
    grad_mid = grad_mid.reshape(mid_weight.shape)
    grad_out = grad_out.reshape(out_weight.shape)
    return (features, fine_grad, grad_down, grad_mid, grad_out, gain_grad, bias_grad)


def solution(mesh):
    in_specs = (
        P(("dp", "group"), None),
        P(("dp", "group"), None),
        P(("dp", "group"), None),
        P(("dp", "group")),
        P(),
        P(),
        P(),
        P(),
        P(),
        P(("dp", "group"), None),
    )
    out_specs = (P(("dp", "group"), None), P(("dp", "group"), None), P(), P(), P(), P(), P())
    return jax.shard_map(
        functools.partial(per_device, mesh.shape["dp"], mesh.shape["group"]),
        mesh=mesh,
        in_specs=in_specs,
        out_specs=out_specs,
        check_vma=False,
    )
```

```python
import functools

import jax
import jax.numpy as jnp
from jax import lax
from jax.experimental import pallas as pl
from jax.experimental.pallas import tpu as pltpu
from jax.sharding import PartitionSpec as P

eps_norm = 1e-05
MESH = pl.DeviceIdType.MESH
GROUP = 3
BLOCK = 256
PAIR = 2
COPIES = 14
GROUPS = (4, 2, 4)
GAP = 1
LAGS = (0, 1, 2, 3, 5, 7, 8, 9, 10)
RING = 8


def sigmoid(value):
    return 1.0 / (1.0 + jnp.exp(-value))


def silu_slope(value):
    sigma = sigmoid(value)
    return sigma * (1.0 + value * (1.0 - sigma))


def dot(left, right):
    return jnp.dot(left, right, preferred_element_type=jnp.float32)


def dot_last(left, right):
    return lax.dot_general(
        left, right, (((1,), (1,)), ((), ())), preferred_element_type=jnp.float32
    )


def kernel(
    dp_size,
    group_size,
    reduce_here,
    fine_ref,
    down_rows_ref,
    nb_rows,
    count_ref,
    down_hbm,
    mid_hbm,
    out_hbm,
    gain_ref,
    bias_ref,
    cotangent_ref,
    features_ref,
    fine_grad_ref,
    results,
    gain_grad_ref,
    bias_grad_ref,
    w_down,
    w_mid,
    w_out,
    spread_fine,
    cols_down,
    nb_cols,
    pickers,
    columns,
    side_by_side,
    act_one,
    act_one_b,
    act_two_b,
    hid_one,
    hid_two,
    hid_three,
    held,
    grad_hidden,
    source_t,
    pair_source_t,
    grad_act,
    side,
    side_cols,
    nb_own,
    nb_pair,
    swap_out,
    swap_in,
    down_all,
    down_got,
    grads,
    from_core,
    from_first_a,
    from_first_b,
    from_second_a,
    from_second_b,
    from_line,
    near,
    far,
    load_sem,
    sum_send,
    sum_recv,
    swap_send,
    swap_recv,
    near_send,
    near_recv,
    far_send,
    far_recv,
):
    rows, width = cotangent_ref.shape
    offsets = nb_rows.shape[0]
    fine_rows, in_width = fine_ref.shape
    children = fine_rows // rows
    down_offsets = down_rows_ref.shape[0]
    units = (offsets + 1) // 2 * (1 if reduce_here else 2)
    chunks = grads.shape[0]
    dp_me = lax.axis_index("dp")
    group_me = lax.axis_index("group")

    loads = [
        pltpu.make_async_copy(source, target, load_sem.at[at])
        for at, (source, target) in enumerate(
            (
                (down_hbm, w_down),
                (mid_hbm, w_mid.at[pl.ds(0, offsets)]),
                (out_hbm, w_out.at[pl.ds(0, offsets)]),
            )
        )
    ]
    for load in loads:
        load.start()

    barrier = pltpu.get_barrier_semaphore()
    for step in range(1, group_size):
        pl.semaphore_signal(
            barrier,
            inc=1,
            device_id={"group": lax.rem(group_me + step, group_size)},
            device_id_type=MESH,
        )
    for step in range(1, dp_size):
        pl.semaphore_signal(
            barrier,
            inc=1,
            device_id={"dp": lax.rem(dp_me + step, dp_size)},
            device_id_type=MESH,
        )

    def share(at, axis, me, size, slots, send, recv):
        copies = []
        for step in range(1, size):
            copies.append(
                pltpu.make_async_remote_copy(
                    src_ref=slots.at[at, me],
                    dst_ref=slots.at[at, me],
                    send_sem=send.at[at, step - 1],
                    recv_sem=recv.at[at, step - 1],
                    device_id={axis: lax.rem(me + step, size)},
                    device_id_type=MESH,
                )
            )
        for copy in copies:
            copy.start()
        return copies

    def exchange(at, block, combine, meanwhile=(None, None)):
        near[at, group_me] = block
        copies = share(at, "group", group_me, group_size, near, near_send, near_recv)
        if meanwhile[0] is not None:
            meanwhile[0]()
        for copy in copies:
            copy.wait()
        far[at, dp_me] = combine([near[at, slot] for slot in range(group_size)])
        copies = share(at, "dp", dp_me, dp_size, far, far_send, far_recv)
        if meanwhile[1] is not None:
            meanwhile[1]()
        for copy in copies:
            copy.wait()
        return combine([far[at, slot] for slot in range(dp_size)])

    lanes = width // 2

    def stack(first, second, third):
        filler = jnp.zeros((2, lanes), jnp.float32)
        return jnp.concatenate([first, second, third, filler], axis=0)

    def fold(value):
        return jnp.concatenate([value[:, :lanes], value[:, lanes:]], axis=0)

    def unfold(value):
        return jnp.concatenate([value[0:1], value[1:2]], axis=1)

    def add_all(blocks):
        total = blocks[0]
        for block in blocks[1:]:
            total = total + block
        return total

    def merge_all(blocks):
        count = add_all([block[4:6] for block in blocks])
        center = add_all([block[4:6] * block[0:2] for block in blocks]) / count
        squares = add_all(
            [
                block[2:4] + block[4:6] * (block[0:2] - center) * (block[0:2] - center)
                for block in blocks
            ]
        )
        return stack(center, squares, count)

    count = count_ref[0]
    own_count = jnp.full((1, width), count.astype(jnp.float32))
    live = lax.broadcasted_iota(jnp.int32, (rows, width), 0) < count

    def norm_stats(at, hidden, meanwhile=(None, None)):
        center = jnp.sum(hidden, axis=0, keepdims=True) / own_count
        centered = jnp.where(live, hidden - center, 0.0)
        squares = jnp.sum(centered * centered, axis=0, keepdims=True)
        merged = exchange(
            at, stack(fold(center), fold(squares), fold(own_count)), merge_all, meanwhile
        )
        total = unfold(merged[4:6])
        scale = lax.rsqrt(unfold(merged[2:4]) / total + eps_norm)
        return unfold(merged[0:2]), scale, total

    def norm_grad(at, norm, incoming, normed, scale, total, meanwhile=(None, None)):
        shift_sum = fold(jnp.sum(incoming, axis=0, keepdims=True))
        scale_sum = fold(jnp.sum(incoming * normed, axis=0, keepdims=True))
        summed = exchange(
            at, stack(shift_sum, scale_sum, jnp.zeros_like(shift_sum)), add_all, meanwhile
        )
        shift_sum, scale_sum = unfold(summed[0:2]), unfold(summed[2:4])
        bias_grad_ref[norm : norm + 1, :] = shift_sum
        gain_grad_ref[norm : norm + 1, :] = scale_sum
        hidden_grad = (
            scale
            * gain_ref[norm : norm + 1, :]
            * (incoming - shift_sum / total - normed * (scale_sum / total))
        )
        return jnp.where(live, hidden_grad, 0.0).astype(jnp.bfloat16)

    def pick(mask):
        return jnp.where(mask, jnp.bfloat16(1), jnp.bfloat16(0))

    def counting(shape, axis):
        return lax.broadcasted_iota(jnp.int32, shape, axis).astype(jnp.float32).astype(jnp.bfloat16)

    def place_spread(turn, step):
        picked = dot(pickers[turn, : PAIR * rows, :], held[...]).astype(jnp.bfloat16)
        for part in range(PAIR):
            columns[turn, :, part * width : (part + 1) * width] = picked[
                part * rows : (part + 1) * rows
            ]

    def run_steps(first, last, build, place, use, after):
        build(first % 2, first)

        def one(turn, step, more):
            place(turn, step)
            if more:
                build(1 - turn, step + 1)
            use(turn, step)

        bodies = (last - first - 1) // 2

        def body(at, carry):
            for turn in range(2):
                one((first + turn) % 2, first + 2 * at + turn, True)
            for turn in range(2):
                after(first + 2 * at + turn)
            return carry

        lax.fori_loop(0, bodies, body, 0)
        for step in range(first + 2 * bodies, last):
            one(step % 2, step, step + 1 < last)
            after(step)

    def convolve(source, weight, hidden):
        places = counting((rows, BLOCK), 1)
        hidden[...] = jnp.zeros_like(hidden)
        for block in range(2):
            side_by_side[:, block * width : (block + 1) * width] = source[
                block * BLOCK : (block + 1) * BLOCK, :
            ]

        def build(turn, step):
            for part in range(GROUP):
                code = nb_cols[step * GROUP + part]
                wanted = jnp.concatenate([jnp.maximum(code, -1 - code)] * (BLOCK // 128), axis=1)
                pickers[turn, part * rows : (part + 1) * rows, :BLOCK] = pick(wanted == places)

        def use(turn, step):
            weights = weight[pl.ds(step * GROUP, GROUP)].reshape(GROUP * width, width)
            hidden[...] += dot(columns[turn], weights)

        def place(turn, step):
            for part in range(GROUP):
                found = dot(
                    pickers[turn, part * rows : (part + 1) * rows, :BLOCK], side_by_side[...]
                )
                code = nb_cols[step * GROUP + part].astype(jnp.float32)
                second = jnp.concatenate([code] * (width // 128), axis=1) < 0
                columns[turn, :, part * width : (part + 1) * width] = jnp.where(
                    second, found[:, width:], found[:, :width]
                ).astype(jnp.bfloat16)

        run_steps(0, offsets // GROUP, build, place, use, no_slot)

    def build_spread(neighbours, first_offset):
        places = counting((BLOCK, rows), 0)

        def build(turn, step):
            for part in range(PAIR):
                wanted = neighbours[pl.ds(first_offset + PAIR * step + part, 1), :]
                wanted = wanted.astype(jnp.float32)
                for first in range(0, rows, BLOCK):
                    here = jnp.broadcast_to(wanted - first, (16, rows)).astype(jnp.bfloat16)
                    pickers[turn, part * rows + first : part * rows + first + BLOCK, :] = pick(
                        jnp.concatenate([here] * (BLOCK // 16), axis=0) == places
                    )

        return build

    def no_slot(at):
        pass

    def put(first_unit, at, product, more):
        for part in range(PAIR):
            value = product[:, part * width : (part + 1) * width]
            if reduce_here:
                c = first_unit // PAIR + at
                value = value.reshape(grads.shape[1:4] + (8, width))
                here_rows = slice(8 * part, 8 * part + 8)
                if more:
                    value = value + grads[c, :, :, :, here_rows]
                grads[c, :, :, :, here_rows] = value
            else:
                unit = pl.multiple_of((first_unit + PAIR * at + part) * width, width)
                grads[pl.ds(unit, width), :] = value

    def convolve_back(weight, act_grad, first_unit, own_slot, other_slot):
        def use_of(first_offset, weigh):
            def use(turn, step):
                spread = columns[turn, :, : PAIR * width]
                k = first_offset + PAIR * step
                weights = jnp.concatenate([weight[k + part] for part in range(PAIR)], axis=1)
                act_grad[...] += dot_last(spread, weights)
                if weigh:
                    put(first_unit, step, dot(source_t[...], spread), False)

            return use

        steps = units // PAIR
        build = build_spread(nb_own, own_offset)
        run_steps(0, steps, build, place_spread, use_of(own_offset, True), own_slot)
        if reduce_here:
            build = build_spread(nb_own, other_offset)
            run_steps(0, steps, build, place_spread, use_of(other_offset, False), other_slot)

    def convolve_pair(first_unit, first_step, last_step, at_slot):
        def use(turn, step):
            spread = columns[turn, :, : PAIR * width]
            put(first_unit, step, dot(pair_source_t[...], spread), True)

        build = build_spread(nb_pair, own_offset)
        run_steps(first_step, last_step, build, place_spread, use, at_slot)

    core, row = lax.rem(group_me, 2), group_me // 2
    column, plane = lax.rem(dp_me, 2), dp_me // 2
    pair, high = lax.rem(plane, 2), plane // 2
    planes = 4
    core_peer = {"group": group_me + 1 - 2 * core}
    row_peer = {"group": group_me + 2 - 4 * row}
    column_peer = {"dp": dp_me + 1 - 2 * column}
    pair_peer = {"dp": dp_me + 2 - 4 * pair}
    cross_peer = {"dp": dp_me + 4 - 8 * high}
    own_offset = units * pair if reduce_here else 0
    other_offset = units * (1 - pair)
    own = pl.ds(2 * core, 2)
    lane_a, lane_b = 2 * core, 2 * core + 1
    kept_row, given_row = pl.ds(2 * row, 2), pl.ds(2 * (1 - row), 2)

    def send(c, number, source, target, peer):
        turn = lax.rem(c, RING)
        return pltpu.make_async_remote_copy(
            src_ref=source,
            dst_ref=target,
            send_sem=sum_send.at[turn, number],
            recv_sem=sum_recv.at[turn, number],
            device_id=peer,
            device_id_type=MESH,
        )

    def copies_of(c, stage):
        part, both = grads.at[c], pl.ds(PAIR * c, PAIR)
        if stage == 0:
            given = part.at[pl.ds(2 * (1 - core), 2)]
            return [send(c, 0, given, from_core.at[lax.rem(c, RING)], core_peer)]
        if stage == 1:
            return [
                send(c, 1, part.at[lane_a, 1 - column], from_first_a.at[c], column_peer),
                send(c, 2, part.at[lane_b, :, given_row], from_first_b.at[c], row_peer),
            ]
        if stage == 2:
            return [
                send(c, 3, part.at[lane_a, column, given_row], from_second_a.at[c], row_peer),
                send(c, 4, part.at[lane_b, 1 - column, kept_row], from_second_b.at[c], column_peer),
            ]
        if stage == 3:
            given = part.at[own, column, 2 * row + 1 - high]
            return [send(c, 5, given, from_line.at[c], cross_peer)]
        if stage == 4:
            block = results.at[pair, both, own, column, 2 * row + high]
            return [
                send(
                    c,
                    5 + step,
                    block,
                    block,
                    {"dp": 2 * lax.rem(plane + step, planes) + column},
                )
                for step in range(1, planes)
            ]
        if stage == 5:
            block_a = results.at[:, both, lane_a, column, kept_row]
            block_b = results.at[:, both, lane_b, column, kept_row]
            return [
                send(c, 9, block_a, block_a, row_peer),
                send(c, 10, block_b, block_b, column_peer),
            ]
        if stage == 6:
            block_a = results.at[:, both, lane_a, column]
            block_b = results.at[:, both, lane_b, :, kept_row]
            return [
                send(c, 11, block_a, block_a, column_peer),
                send(c, 12, block_b, block_b, row_peer),
            ]
        block = results.at[:, both, own]
        return [send(c, 13, block, block, core_peer)]

    def stage_of(c, stage):
        if stage > 0:
            for copy in copies_of(c, stage - 1):
                copy.wait()
        if stage == 1:
            grads[c, own] = grads[c, own] + from_core[lax.rem(c, RING)]
        if stage == 2:
            grads[c, lane_a, column] = grads[c, lane_a, column] + from_first_a[c]
            grads[c, lane_b, :, kept_row] = grads[c, lane_b, :, kept_row] + from_first_b[c]
        if stage == 3:
            grads[c, lane_a, column, kept_row] = grads[c, lane_a, column, kept_row] + from_second_a[c]
            grads[c, lane_b, column, kept_row] = grads[c, lane_b, column, kept_row] + from_second_b[c]
        if stage == 4:
            mine = 2 * row + high
            grads[c, own, column, mine] = grads[c, own, column, mine] + from_line[c]
            for unit in range(PAIR):
                results[pair, PAIR * c + unit, own, column, mine] = grads[
                    c, own, column, mine, 8 * unit : 8 * unit + 8
                ]
        if stage < len(LAGS) - 1:
            for copy in copies_of(c, stage):
                copy.start()

    per_weight = units // PAIR

    def slot(at):
        if not reduce_here:
            return
        for stage, lag in enumerate(LAGS):
            entry = at - lag
            if isinstance(at, int):
                c = entry if entry < per_weight else max(entry - GAP, per_weight - 1)
                if 0 <= entry < chunks + GAP and (c == entry or entry >= per_weight + GAP):
                    stage_of(c, stage)
                continue
            second = entry >= per_weight + GAP

            @pl.when(
                ((entry >= 0) & (entry < per_weight)) | (second & (entry < chunks + GAP))
            )
            def _():
                stage_of(entry - GAP * second.astype(jnp.int32), stage)

    def slot_after(at, steps_with, first_slot):
        if isinstance(at, int):
            if at in steps_with:
                slot(first_slot + steps_with.index(at))
            return
        wanted, number = False, first_slot
        for step in steps_with:
            wanted = wanted | (at == step)
            number = number + (at > step).astype(jnp.int32)

        @pl.when(wanted)
        def _():
            slot(number)

    def swap(at, source, target):
        return pltpu.make_async_remote_copy(
            src_ref=source,
            dst_ref=target,
            send_sem=swap_send.at[at],
            recv_sem=swap_recv.at[at],
            device_id=pair_peer,
            device_id_type=MESH,
        )

    def swap_rows(at):
        return swap(at, swap_out.at[at % 2], swap_in.at[at])

    def start_rows(at, value):
        if reduce_here:
            swap_out[at % 2] = value.astype(jnp.float32)
            swap_rows(at).start()

    places = nb_rows[...]
    codes = jnp.where(places < BLOCK, places, jnp.where(places < rows, BLOCK - 1 - places, 4 * BLOCK))
    side[...] = jnp.zeros_like(side)
    side[:offsets, :] = codes.astype(jnp.float32)
    side[offsets : offsets + down_offsets, :] = down_rows_ref[...].astype(jnp.float32)
    side_cols[...] = side[...].T
    nb_own[...] = jnp.full_like(nb_own, rows)
    nb_own[:offsets, :] = nb_rows[...]
    swap_neighbours = swap(4, nb_own, nb_pair)
    for weight in (w_mid, w_out):
        weight[offsets:] = jnp.zeros_like(weight[offsets:])

    spread_fine[...] = fine_ref[...].astype(jnp.float32)
    for k in range(down_offsets):
        child = spread_fine[pl.ds(k % children, rows, stride=children), :]
        there = side_cols[:, offsets + k : offsets + k + 1] < fine_rows
        cols_down[:, k * in_width : (k + 1) * in_width] = jnp.where(there, child, 0.0).astype(
            jnp.bfloat16
        )
    loads[0].wait()
    hid_one[...] = dot(cols_down[...], w_down[...].reshape(down_offsets * in_width, width))

    def spread_neighbours():
        for k in range(offsets):
            nb_cols[k] = jnp.broadcast_to(side_cols[:, k : k + 1], (rows, 128)).astype(jnp.bfloat16)

    pl.semaphore_wait(barrier, group_size + dp_size - 2)

    swap_one = swap(0, hid_one, swap_in.at[0])
    swap_two = swap(1, hid_two, swap_in.at[1])

    def start_one():
        swap_neighbours.start()
        swap_one.start()

    def start_two():
        swap_two.start()

    beside = (spread_neighbours, start_one if reduce_here else None)
    center_one, scale_one, total = norm_stats(0, hid_one[...], beside)

    def pre_one(hidden=hid_one):
        normed = (hidden[...] - center_one) * scale_one
        return normed, normed * gain_ref[0:1, :] + bias_ref[0:1, :]

    _, pre = pre_one()
    act_one[...] = jnp.where(live, pre * sigmoid(pre), 0.0)
    act_one_b[...] = act_one[...].astype(jnp.bfloat16)
    loads[1].wait()
    convolve(act_one_b, w_mid, hid_two)
    center_two, scale_two, _ = norm_stats(
        1, hid_two[...], (None, start_two if reduce_here else None)
    )

    def pre_two(hidden=hid_two):
        normed = (hidden[...] - center_two) * scale_two
        return normed, normed * gain_ref[1:2, :] + bias_ref[1:2, :]

    _, pre = pre_two()
    act_two_b[...] = jnp.where(live, pre * sigmoid(pre), 0.0).astype(jnp.bfloat16)
    loads[2].wait()
    convolve(act_two_b, w_out, hid_three)
    center_three, scale_three, _ = norm_stats(2, hid_three[...])
    normed_three = (hid_three[...] - center_three) * scale_three
    summed = (
        jnp.where(live, normed_three * gain_ref[2:3, :] + bias_ref[2:3, :], 0.0) + act_one[...]
    )
    sigma = sigmoid(summed)
    features_ref[...] = jnp.where(live, summed * sigma, 0.0).astype(jnp.bfloat16)

    slope = sigma * (1.0 + summed * (1.0 - sigma))
    act_one[...] = jnp.where(live, cotangent_ref[...].astype(jnp.float32) * slope, 0.0)
    grad_hidden[...] = norm_grad(3, 2, act_one[...], normed_three, scale_three, total)
    start_rows(2, grad_hidden[...])
    held[...] = grad_hidden[...]
    grad_act[...] = jnp.zeros_like(grad_act)
    steps = units // PAIR

    def receive(swapped, pre_of, source_at, hidden_at):
        swapped.wait()
        _, pre = pre_of(swap_in.at[source_at])
        pair_source_t[...] = (pre * sigmoid(pre)).astype(jnp.bfloat16).T
        swap_rows(hidden_at).wait()
        held[...] = swap_in[hidden_at].astype(jnp.bfloat16)

    def pair_halves(first_unit, at_slot):
        middle = (steps + 1) // 2
        return (
            lambda: convolve_pair(first_unit, 0, middle, at_slot),
            lambda: convolve_pair(first_unit, middle, steps, at_slot),
        )

    nothing = (None, None)
    source_t[...] = act_two_b[...].T
    convolve_back(w_out, grad_act, 0, no_slot, no_slot)
    normed, pre = pre_two()
    incoming = jnp.where(live, grad_act[...] * silu_slope(pre), 0.0)
    if reduce_here:
        swap_neighbours.wait()
        receive(swap_two, pre_two, 1, 2)
    after = lambda at: slot_after(at, (1, 3, 4, 6), 0)
    beside = pair_halves(0, after) if reduce_here else nothing
    grad_hidden[...] = norm_grad(4, 1, incoming, normed, scale_two, total, beside)
    start_rows(3, grad_hidden[...])
    held[...] = grad_hidden[...]
    grad_act[...] = act_one[...]
    source_t[...] = act_one_b[...].T
    convolve_back(
        w_mid, grad_act, units, no_slot, lambda at: slot_after(at, (1, 3, 5), 4)
    )
    normed, pre = pre_one()
    incoming = jnp.where(live, grad_act[...] * silu_slope(pre), 0.0)
    if reduce_here:
        receive(swap_one, pre_one, 0, 3)
    after = lambda at: slot_after(at, (0, 1, 3, 4, 5), 7)
    beside = pair_halves(units, after) if reduce_here else nothing
    grad_hidden[...] = norm_grad(5, 0, incoming, normed, scale_one, total, beside)
    down_rows = down_offsets * in_width
    if reduce_here:
        down_all[...] = dot(cols_down[...].T, grad_hidden[...])
        kept = down_rows // 2
        swap_down = swap(
            5, down_all.at[pl.ds(pl.multiple_of(kept * (1 - pair), kept), kept), :], down_got
        )
        swap_down.start()
    else:
        grads[2 * units * width :, :] = dot(cols_down[...].T, grad_hidden[...])
    slot(12)
    slot(13)
    for child in range(children):
        total_child = jnp.zeros((rows, in_width), jnp.float32)
        for k in range(child, down_offsets, children):
            there = side_cols[:, offsets + k : offsets + k + 1] < fine_rows
            total_child += jnp.where(there, dot_last(grad_hidden[...], w_down[k]), 0.0)
        spread_fine[pl.ds(child, rows, stride=children), :] = total_child
    fine_grad_ref[...] = spread_fine[...].astype(jnp.bfloat16)
    slot(14)

    if reduce_here:

        def rest(at, carry):
            slot(at)
            return carry

        lax.fori_loop(15, chunks - 1 + GAP, rest, 0)
        swap_down.wait()
        for part in range(PAIR):
            total_down = (
                down_all[pl.ds(pl.multiple_of(kept * pair + part * width, width), width), :]
                + down_got[part * width : (part + 1) * width, :]
            )
            grads[chunks - 1, :, :, :, 8 * part : 8 * part + 8] = total_down.reshape(
                grads.shape[1:4] + (8, width)
            )
        lax.fori_loop(chunks - 1 + GAP, chunks + GAP + LAGS[-1], rest, 0)
    else:
        store = pltpu.make_async_copy(grads, results, load_sem.at[0])
        store.start()
        store.wait()


def place_kernel(
    features_ref,
    fine_grad_ref,
    grads_ref,
    gain_ref,
    bias_ref,
    features_out,
    fine_grad_out,
    grad_down_out,
    grad_mid_out,
    grad_out_out,
    gain_out,
    bias_out,
    sem,
):
    offsets = grad_mid_out.shape[0]
    units = (offsets + 1) // 2
    piece = (units + 1) // 2
    moves = []
    for pair in range(2):
        for at, target in enumerate((grad_out_out, grad_mid_out)):
            for first in range(0, units, piece):
                count = min(piece, offsets - units * pair - first, units - first)
                here = grads_ref.at[pair, pl.ds(at * units + first, count)]
                moves.append((here, target.at[pl.ds(units * pair + first, count)]))
        down_units = grad_down_out.shape[0] // 2
        here = grads_ref.at[pair, pl.ds(2 * units, down_units)]
        moves.append((here, grad_down_out.at[pl.ds(pair * down_units, down_units)]))
    copies = [
        pltpu.make_async_copy(source, target, sem.at[at])
        for at, (source, target) in enumerate(moves)
    ]
    for copy in copies:
        copy.start()
    features_out[...] = features_ref[...]
    fine_grad_out[...] = fine_grad_ref[...]
    gain_out[...] = gain_ref[...]
    bias_out[...] = bias_ref[...]
    for copy in copies:
        copy.wait()


def per_device(
    dp_size,
    group_size,
    fine_features,
    down_map,
    neighbours,
    voxel_counts,
    down_weight,
    mid_weight,
    out_weight,
    norm_gain,
    norm_bias,
    cotangent,
):
    rows, width = cotangent.shape
    fine_rows, in_width = fine_features.shape
    offsets = neighbours.shape[1]
    down_offsets = down_map.shape[1]
    f32, bf16, i32 = jnp.float32, jnp.bfloat16, jnp.int32
    vmem = pl.BlockSpec(memory_space=pltpu.VMEM)
    smem = pl.BlockSpec(memory_space=pltpu.SMEM)
    hbm = pl.BlockSpec(memory_space=pl.ANY)
    shape = jax.ShapeDtypeStruct
    reduce_here = dp_size == 8 and group_size == 4
    result = pltpu.VMEM if reduce_here else shape
    share = 2 if reduce_here else 1
    units = (offsets + 1) // 2 * 2 // share
    all_units = 2 * units + down_offsets * in_width // (share * width)
    grad_rows = all_units * width
    chunks = all_units // PAIR
    padded = (offsets + 1) // 2 * 2
    features, fine_grad, grads, gain_grad, bias_grad = pl.pallas_call(
        functools.partial(kernel, dp_size, group_size, reduce_here),
        out_shape=(
            result((rows, width), bf16),
            result((fine_rows, in_width), bf16),
            pltpu.VMEM((2, all_units, *GROUPS, 8, width), f32)
            if reduce_here
            else shape((grad_rows, width), f32),
            result(norm_gain.shape, f32),
            result(norm_bias.shape, f32),
        ),
        in_specs=[vmem, vmem, vmem, smem, hbm, hbm, hbm, vmem, vmem, vmem],
        out_specs=(vmem, vmem, vmem if reduce_here else hbm, vmem, vmem),
        scratch_shapes=[
            pltpu.VMEM(down_weight.shape, bf16),
            pltpu.VMEM((padded, width, width), bf16),
            pltpu.VMEM((padded, width, width), bf16),
            pltpu.VMEM((fine_rows, in_width), f32),
            pltpu.VMEM((rows, down_offsets * in_width), bf16),
            pltpu.VMEM((offsets, rows, 128), bf16),
            pltpu.VMEM((2, GROUP * rows, rows), bf16),
            pltpu.VMEM((2, rows, GROUP * width), bf16),
            pltpu.VMEM((BLOCK, 2 * width), bf16),
            pltpu.VMEM((rows, width), f32),
            pltpu.VMEM((rows, width), bf16),
            pltpu.VMEM((rows, width), bf16),
            pltpu.VMEM((rows, width), f32),
            pltpu.VMEM((rows, width), f32),
            pltpu.VMEM((rows, width), f32),
            pltpu.VMEM((rows, width), bf16),
            pltpu.VMEM((rows, width), bf16),
            pltpu.VMEM((width, rows), bf16),
            pltpu.VMEM((width, rows), bf16),
            pltpu.VMEM((rows, width), f32),
            pltpu.VMEM((128, rows), f32),
            pltpu.VMEM((rows, 128), f32),
            pltpu.VMEM((padded, rows), i32),
            pltpu.VMEM((padded, rows), i32),
            pltpu.VMEM((2, rows, width), f32),
            pltpu.VMEM((4, rows, width), f32),
            pltpu.VMEM((down_offsets * in_width, width), f32),
            pltpu.VMEM((down_offsets * in_width // 2, width), f32),
            pltpu.VMEM(
                (chunks, *GROUPS, 8 * PAIR, width) if reduce_here else (grad_rows, width), f32
            ),
            pltpu.VMEM((RING, 2, *GROUPS[1:], 8 * PAIR, width), f32),
            pltpu.VMEM((chunks, GROUPS[2], 8 * PAIR, width), f32),
            pltpu.VMEM((chunks, GROUPS[1], 2, 8 * PAIR, width), f32),
            pltpu.VMEM((chunks, 2, 8 * PAIR, width), f32),
            pltpu.VMEM((chunks, 2, 8 * PAIR, width), f32),
            pltpu.VMEM((chunks, 2, 8 * PAIR, width), f32),
            pltpu.VMEM((6, group_size, 8, width // 2), f32),
            pltpu.VMEM((6, dp_size, 8, width // 2), f32),
            pltpu.SemaphoreType.DMA((3,)),
            pltpu.SemaphoreType.DMA((RING, COPIES)),
            pltpu.SemaphoreType.DMA((RING, COPIES)),
            pltpu.SemaphoreType.DMA((6,)),
            pltpu.SemaphoreType.DMA((6,)),
            pltpu.SemaphoreType.DMA((6, group_size - 1)),
            pltpu.SemaphoreType.DMA((6, group_size - 1)),
            pltpu.SemaphoreType.DMA((6, dp_size - 1)),
            pltpu.SemaphoreType.DMA((6, dp_size - 1)),
        ],
        compiler_params=pltpu.CompilerParams(
            collective_id=0, has_side_effects=True, vmem_limit_bytes=(46 if reduce_here else 60) * 1024 * 1024
        ),
    )(
        fine_features,
        down_map.T,
        neighbours.T,
        voxel_counts,
        down_weight,
        mid_weight,
        out_weight,
        norm_gain,
        norm_bias,
        cotangent,
    )
    if not reduce_here:
        grads = lax.psum(grads, ("dp", "group"))
        middle, end = offsets * width, 2 * padded * width
        grad_out = grads[:middle].reshape(out_weight.shape)
        grad_mid = grads[padded * width : padded * width + middle].reshape(mid_weight.shape)
        grad_down = grads[end:].reshape(down_weight.shape)
        return (features, fine_grad, grad_down, grad_mid, grad_out, gain_grad, bias_grad)
    held = [
        pltpu.with_memory_space_constraint(value, pltpu.VMEM)
        for value in (features, fine_grad, grads, gain_grad, bias_grad)
    ]
    features, fine_grad, grad_down, grad_mid, grad_out, gain_grad, bias_grad = pl.pallas_call(
        place_kernel,
        out_shape=(
            shape(features.shape, bf16),
            shape(fine_grad.shape, bf16),
            shape((down_offsets * in_width // width, *GROUPS, 8, width), f32),
            shape((offsets, *GROUPS, 8, width), f32),
            shape((offsets, *GROUPS, 8, width), f32),
            shape(norm_gain.shape, f32),
            shape(norm_bias.shape, f32),
        ),
        in_specs=[vmem] * 5,
        out_specs=(vmem, vmem, hbm, hbm, hbm, vmem, vmem),
        scratch_shapes=[pltpu.SemaphoreType.DMA((10,))],
        compiler_params=pltpu.CompilerParams(vmem_limit_bytes=8 * 1024 * 1024),
    )(*held)
    grad_down = grad_down.reshape(down_weight.shape)
    grad_mid = grad_mid.reshape(mid_weight.shape)
    grad_out = grad_out.reshape(out_weight.shape)
    return (features, fine_grad, grad_down, grad_mid, grad_out, gain_grad, bias_grad)


def solution(mesh):
    in_specs = (
        P(("dp", "group"), None),
        P(("dp", "group"), None),
        P(("dp", "group"), None),
        P(("dp", "group")),
        P(),
        P(),
        P(),
        P(),
        P(),
        P(("dp", "group"), None),
    )
    out_specs = (P(("dp", "group"), None), P(("dp", "group"), None), P(), P(), P(), P(), P())
    return jax.shard_map(
        functools.partial(per_device, mesh.shape["dp"], mesh.shape["group"]),
        mesh=mesh,
        in_specs=in_specs,
        out_specs=out_specs,
        check_vma=False,
    )
```

```python
import functools

import jax
import jax.numpy as jnp
from jax import lax
from jax.experimental import pallas as pl
from jax.experimental.pallas import tpu as pltpu
from jax.sharding import PartitionSpec as P

eps_norm = 1e-05
MESH = pl.DeviceIdType.MESH
GROUP = 3
BLOCK = 256
PAIR = 2
COPIES = 14
GROUPS = (4, 2, 4)
GAP = 2
LAGS = (0, 1, 2, 3, 5, 7, 8, 11, 12)
RING = 8


def sigmoid(value):
    return 1.0 / (1.0 + jnp.exp(-value))


def silu_slope(value):
    sigma = sigmoid(value)
    return sigma * (1.0 + value * (1.0 - sigma))


def dot(left, right):
    return jnp.dot(left, right, preferred_element_type=jnp.float32)


def dot_last(left, right):
    return lax.dot_general(
        left, right, (((1,), (1,)), ((), ())), preferred_element_type=jnp.float32
    )


def kernel(
    dp_size,
    group_size,
    reduce_here,
    fine_ref,
    down_rows_ref,
    nb_rows,
    count_ref,
    down_hbm,
    mid_hbm,
    out_hbm,
    gain_ref,
    bias_ref,
    cotangent_ref,
    features_ref,
    fine_grad_ref,
    results,
    gain_grad_ref,
    bias_grad_ref,
    w_down,
    w_mid,
    w_out,
    spread_fine,
    cols_down,
    nb_cols,
    pickers,
    columns,
    side_by_side,
    act_one,
    act_one_b,
    act_two_b,
    hid_one,
    hid_two,
    hid_three,
    held,
    grad_hidden,
    source_t,
    pair_source_t,
    grad_act,
    side,
    side_cols,
    nb_own,
    nb_pair,
    swap_out,
    swap_in,
    down_all,
    down_got,
    grads,
    from_core,
    from_first_a,
    from_first_b,
    from_second_a,
    from_second_b,
    from_line,
    near,
    far,
    load_sem,
    sum_send,
    sum_recv,
    swap_send,
    swap_recv,
    near_send,
    near_recv,
    far_send,
    far_recv,
):
    rows, width = cotangent_ref.shape
    offsets = nb_rows.shape[0]
    fine_rows, in_width = fine_ref.shape
    children = fine_rows // rows
    down_offsets = down_rows_ref.shape[0]
    units = (offsets + 1) // 2 * (1 if reduce_here else 2)
    chunks = grads.shape[0]
    dp_me = lax.axis_index("dp")
    group_me = lax.axis_index("group")

    loads = [
        pltpu.make_async_copy(source, target, load_sem.at[at])
        for at, (source, target) in enumerate(
            (
                (down_hbm, w_down),
                (mid_hbm, w_mid.at[pl.ds(0, offsets)]),
                (out_hbm, w_out.at[pl.ds(0, offsets)]),
            )
        )
    ]
    for load in loads:
        load.start()

    direct = reduce_here
    peers = [
        {
            "dp": lax.rem(dp_me + dp_step, dp_size),
            "group": lax.rem(group_me + group_step, group_size),
        }
        for dp_step in reversed(range(dp_size))
        for group_step in reversed(range(group_size))
        if (dp_step or group_step) and (direct or not dp_step or not group_step)
    ]
    barrier = pltpu.get_barrier_semaphore()
    for peer in peers:
        pl.semaphore_signal(barrier, inc=1, device_id=peer, device_id_type=MESH)

    def share(at, axis, me, size, slots, send, recv):
        copies = []
        for step in range(1, size):
            copies.append(
                pltpu.make_async_remote_copy(
                    src_ref=slots.at[at, me],
                    dst_ref=slots.at[at, me],
                    send_sem=send.at[at, step - 1],
                    recv_sem=recv.at[at, step - 1],
                    device_id={axis: lax.rem(me + step, size)},
                    device_id_type=MESH,
                )
            )
        for copy in copies:
            copy.start()
        return copies

    def exchange_direct(at, block, combine, meanwhile):
        me = dp_me * group_size + group_me
        near[at, me] = block
        for peer in peers:
            pltpu.make_async_remote_copy(
                src_ref=near.at[at, me],
                dst_ref=near.at[at, me],
                send_sem=near_send.at[at, 0],
                recv_sem=near_recv.at[at, 0],
                device_id=peer,
                device_id_type=MESH,
            ).start()
        for work in meanwhile:
            if work is not None:
                work()
        others = near.at[at, pl.ds(0, len(peers))]
        for sem in (near_recv, near_send):
            pltpu.make_async_copy(others, others, sem.at[at, 0]).wait()
        return combine([near[at, slot] for slot in range(len(peers) + 1)])

    def exchange(at, block, combine, meanwhile=(None, None)):
        if direct:
            return exchange_direct(at, block, combine, meanwhile)
        near[at, group_me] = block
        copies = share(at, "group", group_me, group_size, near, near_send, near_recv)
        if meanwhile[0] is not None:
            meanwhile[0]()
        for copy in copies:
            copy.wait()
        far[at, dp_me] = combine([near[at, slot] for slot in range(group_size)])
        copies = share(at, "dp", dp_me, dp_size, far, far_send, far_recv)
        if meanwhile[1] is not None:
            meanwhile[1]()
        for copy in copies:
            copy.wait()
        return combine([far[at, slot] for slot in range(dp_size)])

    lanes = width // 2

    def stack(first, second, third):
        filler = jnp.zeros((2, lanes), jnp.float32)
        return jnp.concatenate([first, second, third, filler], axis=0)

    def fold(value):
        return jnp.concatenate([value[:, :lanes], value[:, lanes:]], axis=0)

    def unfold(value):
        return jnp.concatenate([value[0:1], value[1:2]], axis=1)

    def add_all(blocks):
        total = blocks[0]
        for block in blocks[1:]:
            total = total + block
        return total

    def merge_all(blocks):
        count = add_all([block[4:6] for block in blocks])
        center = add_all([block[4:6] * block[0:2] for block in blocks]) / count
        squares = add_all(
            [
                block[2:4] + block[4:6] * (block[0:2] - center) * (block[0:2] - center)
                for block in blocks
            ]
        )
        return stack(center, squares, count)

    count = count_ref[...]
    own_count = jnp.broadcast_to(count.astype(jnp.float32), (1, width))
    live = lax.broadcasted_iota(jnp.int32, (rows, width), 0) < count

    def norm_stats(at, hidden, meanwhile=(None, None)):
        center = jnp.sum(hidden, axis=0, keepdims=True) / own_count
        centered = jnp.where(live, hidden - center, 0.0)
        squares = jnp.sum(centered * centered, axis=0, keepdims=True)
        merged = exchange(
            at, stack(fold(center), fold(squares), fold(own_count)), merge_all, meanwhile
        )
        total = unfold(merged[4:6])
        scale = lax.rsqrt(unfold(merged[2:4]) / total + eps_norm)
        return unfold(merged[0:2]), scale, total

    def norm_grad(at, norm, incoming, normed, scale, total, meanwhile=(None, None)):
        shift_sum = fold(jnp.sum(incoming, axis=0, keepdims=True))
        scale_sum = fold(jnp.sum(incoming * normed, axis=0, keepdims=True))
        summed = exchange(
            at, stack(shift_sum, scale_sum, jnp.zeros_like(shift_sum)), add_all, meanwhile
        )
        shift_sum, scale_sum = unfold(summed[0:2]), unfold(summed[2:4])
        bias_grad_ref[norm : norm + 1, :] = shift_sum
        gain_grad_ref[norm : norm + 1, :] = scale_sum
        hidden_grad = (
            scale
            * gain_ref[norm : norm + 1, :]
            * (incoming - shift_sum / total - normed * (scale_sum / total))
        )
        return jnp.where(live, hidden_grad, 0.0).astype(jnp.bfloat16)

    def pick(mask):
        return jnp.where(mask, jnp.bfloat16(1), jnp.bfloat16(0))

    def counting(shape, axis):
        return lax.broadcasted_iota(jnp.int32, shape, axis).astype(jnp.float32).astype(jnp.bfloat16)

    def place_spread(turn, step):
        picked = dot(pickers[turn, : PAIR * rows, :], held[...]).astype(jnp.bfloat16)
        for part in range(PAIR):
            columns[turn, :, part * width : (part + 1) * width] = picked[
                part * rows : (part + 1) * rows
            ]

    def run_steps(first, last, build, place, use, after):
        build(first % 2, first)

        def one(turn, step, more):
            place(turn, step)
            if more:
                build(1 - turn, step + 1)
            use(turn, step)

        bodies = (last - first - 1) // 2

        def body(at, carry):
            for turn in range(2):
                one((first + turn) % 2, first + 2 * at + turn, True)
            for turn in range(2):
                after(first + 2 * at + turn)
            return carry

        lax.fori_loop(0, bodies, body, 0)
        for step in range(first + 2 * bodies, last):
            one(step % 2, step, step + 1 < last)
            after(step)

    def convolve(source, weight, hidden):
        places = counting((rows, BLOCK), 1)
        hidden[...] = jnp.zeros_like(hidden)
        for block in range(2):
            side_by_side[:, block * width : (block + 1) * width] = source[
                block * BLOCK : (block + 1) * BLOCK, :
            ]

        def build(turn, step):
            for part in range(GROUP):
                code = nb_cols[step * GROUP + part]
                wanted = jnp.concatenate([jnp.maximum(code, -1 - code)] * (BLOCK // 128), axis=1)
                pickers[turn, part * rows : (part + 1) * rows, :BLOCK] = pick(wanted == places)

        def use(turn, step):
            weights = weight[pl.ds(step * GROUP, GROUP)].reshape(GROUP * width, width)
            hidden[...] += dot(columns[turn], weights)

        def place(turn, step):
            for part in range(GROUP):
                found = dot(
                    pickers[turn, part * rows : (part + 1) * rows, :BLOCK], side_by_side[...]
                )
                code = nb_cols[step * GROUP + part].astype(jnp.float32)
                second = jnp.concatenate([code] * (width // 128), axis=1) < 0
                columns[turn, :, part * width : (part + 1) * width] = jnp.where(
                    second, found[:, width:], found[:, :width]
                ).astype(jnp.bfloat16)

        run_steps(0, offsets // GROUP, build, place, use, no_slot)

    def build_spread(neighbours, first_offset):
        places = counting((BLOCK, rows), 0)

        def build(turn, step):
            for part in range(PAIR):
                wanted = neighbours[pl.ds(first_offset + PAIR * step + part, 1), :]
                wanted = wanted.astype(jnp.float32)
                for first in range(0, rows, BLOCK):
                    here = jnp.broadcast_to(wanted - first, (16, rows)).astype(jnp.bfloat16)
                    pickers[turn, part * rows + first : part * rows + first + BLOCK, :] = pick(
                        jnp.concatenate([here] * (BLOCK // 16), axis=0) == places
                    )

        return build

    def no_slot(at):
        pass

    def put(first_unit, at, product, more):
        for part in range(PAIR):
            value = product[:, part * width : (part + 1) * width]
            if reduce_here:
                c = first_unit // PAIR + at
                value = value.reshape(grads.shape[1:4] + (8, width))
                here_rows = slice(8 * part, 8 * part + 8)
                if more:
                    value = value + grads[c, :, :, :, here_rows]
                grads[c, :, :, :, here_rows] = value
            else:
                unit = pl.multiple_of((first_unit + PAIR * at + part) * width, width)
                grads[pl.ds(unit, width), :] = value

    def convolve_back(weight, act_grad, first_unit, own_slot, other_slot):
        def use_of(first_offset, weigh):
            def use(turn, step):
                spread = columns[turn, :, : PAIR * width]
                k = first_offset + PAIR * step
                weights = jnp.concatenate([weight[k + part] for part in range(PAIR)], axis=1)
                act_grad[...] += dot_last(spread, weights)
                if weigh:
                    put(first_unit, step, dot(source_t[...], spread), False)

            return use

        steps = units // PAIR
        build = build_spread(nb_own, own_offset)
        run_steps(0, steps, build, place_spread, use_of(own_offset, True), own_slot)
        if reduce_here:
            build = build_spread(nb_own, other_offset)
            run_steps(0, steps, build, place_spread, use_of(other_offset, False), other_slot)

    def convolve_pair(first_unit, first_step, last_step, at_slot):
        def use(turn, step):
            spread = columns[turn, :, : PAIR * width]
            put(first_unit, step, dot(pair_source_t[...], spread), True)

        build = build_spread(nb_pair, own_offset)
        run_steps(first_step, last_step, build, place_spread, use, at_slot)

    core, row = lax.rem(group_me, 2), group_me // 2
    column, plane = lax.rem(dp_me, 2), dp_me // 2
    pair, high = lax.rem(plane, 2), plane // 2
    planes = 4
    core_peer = {"group": group_me + 1 - 2 * core}
    row_peer = {"group": group_me + 2 - 4 * row}
    column_peer = {"dp": dp_me + 1 - 2 * column}
    pair_peer = {"dp": dp_me + 2 - 4 * pair}
    cross_peer = {"dp": dp_me + 4 - 8 * high}
    own_offset = units * pair if reduce_here else 0
    other_offset = units * (1 - pair)
    own = pl.ds(2 * core, 2)
    lane_a, lane_b = 2 * core, 2 * core + 1
    kept_row, given_row = pl.ds(2 * row, 2), pl.ds(2 * (1 - row), 2)

    def send(c, number, source, target, peer):
        turn = lax.rem(c, RING)
        return pltpu.make_async_remote_copy(
            src_ref=source,
            dst_ref=target,
            send_sem=sum_send.at[turn, number],
            recv_sem=sum_recv.at[turn, number],
            device_id=peer,
            device_id_type=MESH,
        )

    def copies_of(c, stage):
        part, both = grads.at[c], pl.ds(PAIR * c, PAIR)
        if stage == 0:
            given = part.at[pl.ds(2 * (1 - core), 2)]
            return [send(c, 0, given, from_core.at[lax.rem(c, RING)], core_peer)]
        if stage == 1:
            return [
                send(c, 1, part.at[lane_a, 1 - column], from_first_a.at[c], column_peer),
                send(c, 2, part.at[lane_b, :, given_row], from_first_b.at[c], row_peer),
            ]
        if stage == 2:
            return [
                send(c, 3, part.at[lane_a, column, given_row], from_second_a.at[c], row_peer),
                send(c, 4, part.at[lane_b, 1 - column, kept_row], from_second_b.at[c], column_peer),
            ]
        if stage == 3:
            given = part.at[own, column, 2 * row + 1 - high]
            return [send(c, 5, given, from_line.at[c], cross_peer)]
        if stage == 4:
            block = results.at[pair, both, own, column, 2 * row + high]
            return [
                send(
                    c,
                    5 + step,
                    block,
                    block,
                    {"dp": 2 * lax.rem(plane + step, planes) + column},
                )
                for step in range(1, planes)
            ]
        if stage == 5:
            block_a = results.at[:, both, lane_a, column, kept_row]
            block_b = results.at[:, both, lane_b, column, kept_row]
            return [
                send(c, 9, block_a, block_a, row_peer),
                send(c, 10, block_b, block_b, column_peer),
            ]
        if stage == 6:
            block_a = results.at[:, both, lane_a, column]
            block_b = results.at[:, both, lane_b, :, kept_row]
            return [
                send(c, 11, block_a, block_a, column_peer),
                send(c, 12, block_b, block_b, row_peer),
            ]
        block = results.at[:, both, own]
        return [send(c, 13, block, block, core_peer)]

    def stage_of(c, stage):
        if stage > 0:
            for copy in copies_of(c, stage - 1):
                copy.wait()
        if stage == 1:
            grads[c, own] = grads[c, own] + from_core[lax.rem(c, RING)]
        if stage == 2:
            grads[c, lane_a, column] = grads[c, lane_a, column] + from_first_a[c]
            grads[c, lane_b, :, kept_row] = grads[c, lane_b, :, kept_row] + from_first_b[c]
        if stage == 3:
            grads[c, lane_a, column, kept_row] = grads[c, lane_a, column, kept_row] + from_second_a[c]
            grads[c, lane_b, column, kept_row] = grads[c, lane_b, column, kept_row] + from_second_b[c]
        if stage == 4:
            mine = 2 * row + high
            grads[c, own, column, mine] = grads[c, own, column, mine] + from_line[c]
            for unit in range(PAIR):
                results[pair, PAIR * c + unit, own, column, mine] = grads[
                    c, own, column, mine, 8 * unit : 8 * unit + 8
                ]
        if stage < len(LAGS) - 1:
            for copy in copies_of(c, stage):
                copy.start()

    per_weight = units // PAIR

    def slot(at):
        if not reduce_here:
            return
        for stage, lag in enumerate(LAGS):
            entry = at - lag
            if isinstance(at, int):
                c = entry if entry < per_weight else max(entry - GAP, per_weight - 1)
                if 0 <= entry < chunks + GAP and (c == entry or entry >= per_weight + GAP):
                    stage_of(c, stage)
                continue
            second = entry >= per_weight + GAP

            @pl.when(
                ((entry >= 0) & (entry < per_weight)) | (second & (entry < chunks + GAP))
            )
            def _():
                stage_of(entry - GAP * second.astype(jnp.int32), stage)

    def slot_after(at, steps_with, first_slot):
        if isinstance(at, int):
            if at in steps_with:
                slot(first_slot + steps_with.index(at))
            return
        wanted, number = False, first_slot
        for step in steps_with:
            wanted = wanted | (at == step)
            number = number + (at > step).astype(jnp.int32)

        @pl.when(wanted)
        def _():
            slot(number)

    def swap(at, source, target):
        return pltpu.make_async_remote_copy(
            src_ref=source,
            dst_ref=target,
            send_sem=swap_send.at[at],
            recv_sem=swap_recv.at[at],
            device_id=pair_peer,
            device_id_type=MESH,
        )

    def swap_rows(at):
        return swap(at, swap_out.at[at % 2], swap_in.at[at])

    def start_rows(at, value):
        if reduce_here:
            swap_out[at % 2] = value.astype(jnp.float32)
            swap_rows(at).start()

    places = nb_rows[...]
    codes = jnp.where(places < BLOCK, places, jnp.where(places < rows, BLOCK - 1 - places, 4 * BLOCK))
    side[...] = jnp.zeros_like(side)
    side[:offsets, :] = codes.astype(jnp.float32)
    side[offsets : offsets + down_offsets, :] = down_rows_ref[...].astype(jnp.float32)
    side_cols[...] = side[...].T
    nb_own[...] = jnp.full_like(nb_own, rows)
    nb_own[:offsets, :] = nb_rows[...]
    swap_neighbours = swap(4, nb_own, nb_pair)
    for weight in (w_mid, w_out):
        weight[offsets:] = jnp.zeros_like(weight[offsets:])

    spread_fine[...] = fine_ref[...].astype(jnp.float32)
    for k in range(down_offsets):
        child = spread_fine[pl.ds(k % children, rows, stride=children), :]
        there = side_cols[:, offsets + k : offsets + k + 1] < fine_rows
        cols_down[:, k * in_width : (k + 1) * in_width] = jnp.where(there, child, 0.0).astype(
            jnp.bfloat16
        )
    loads[0].wait()
    hid_one[...] = dot(cols_down[...], w_down[...].reshape(down_offsets * in_width, width))

    def spread_neighbours():
        for k in range(offsets):
            nb_cols[k] = jnp.broadcast_to(side_cols[:, k : k + 1], (rows, 128)).astype(jnp.bfloat16)

    pl.semaphore_wait(barrier, len(peers))

    swap_one = swap(0, hid_one, swap_in.at[0])
    swap_two = swap(1, hid_two, swap_in.at[1])

    def start_one():
        swap_neighbours.start()
        swap_one.start()

    def start_two():
        swap_two.start()

    beside = (spread_neighbours, start_one if reduce_here else None)
    center_one, scale_one, total = norm_stats(0, hid_one[...], beside)

    def pre_one(hidden=hid_one):
        normed = (hidden[...] - center_one) * scale_one
        return normed, normed * gain_ref[0:1, :] + bias_ref[0:1, :]

    _, pre = pre_one()
    act_one[...] = jnp.where(live, pre * sigmoid(pre), 0.0)
    act_one_b[...] = act_one[...].astype(jnp.bfloat16)
    loads[1].wait()
    convolve(act_one_b, w_mid, hid_two)
    center_two, scale_two, _ = norm_stats(
        1, hid_two[...], (None, start_two if reduce_here else None)
    )

    def pre_two(hidden=hid_two):
        normed = (hidden[...] - center_two) * scale_two
        return normed, normed * gain_ref[1:2, :] + bias_ref[1:2, :]

    _, pre = pre_two()
    act_two_b[...] = jnp.where(live, pre * sigmoid(pre), 0.0).astype(jnp.bfloat16)
    loads[2].wait()
    convolve(act_two_b, w_out, hid_three)
    center_three, scale_three, _ = norm_stats(2, hid_three[...])
    normed_three = (hid_three[...] - center_three) * scale_three
    summed = (
        jnp.where(live, normed_three * gain_ref[2:3, :] + bias_ref[2:3, :], 0.0) + act_one[...]
    )
    sigma = sigmoid(summed)
    features_ref[...] = jnp.where(live, summed * sigma, 0.0).astype(jnp.bfloat16)

    slope = sigma * (1.0 + summed * (1.0 - sigma))
    act_one[...] = jnp.where(live, cotangent_ref[...].astype(jnp.float32) * slope, 0.0)
    grad_hidden[...] = norm_grad(3, 2, act_one[...], normed_three, scale_three, total)
    start_rows(2, grad_hidden[...])
    held[...] = grad_hidden[...]
    grad_act[...] = jnp.zeros_like(grad_act)
    steps = units // PAIR

    def receive(swapped, pre_of, source_at, hidden_at):
        swapped.wait()
        _, pre = pre_of(swap_in.at[source_at])
        pair_source_t[...] = (pre * sigmoid(pre)).astype(jnp.bfloat16).T
        swap_rows(hidden_at).wait()
        held[...] = swap_in[hidden_at].astype(jnp.bfloat16)

    def pair_halves(first_unit, at_slot):
        middle = (steps + 1) // 2
        return (
            lambda: convolve_pair(first_unit, 0, middle, at_slot),
            lambda: convolve_pair(first_unit, middle, steps, at_slot),
        )

    nothing = (None, None)
    source_t[...] = act_two_b[...].T
    convolve_back(w_out, grad_act, 0, no_slot, no_slot)
    normed, pre = pre_two()
    incoming = jnp.where(live, grad_act[...] * silu_slope(pre), 0.0)
    if reduce_here:
        swap_neighbours.wait()
        receive(swap_two, pre_two, 1, 2)
    after = lambda at: slot_after(at, (1, 3, 4, 6), 0)
    beside = pair_halves(0, after) if reduce_here else nothing
    grad_hidden[...] = norm_grad(4, 1, incoming, normed, scale_two, total, beside)
    start_rows(3, grad_hidden[...])
    held[...] = grad_hidden[...]
    grad_act[...] = act_one[...]
    source_t[...] = act_one_b[...].T
    convolve_back(
        w_mid,
        grad_act,
        units,
        lambda at: slot_after(at, (0, 5), 4),
        lambda at: slot_after(at, (1, 3, 5), 6),
    )
    normed, pre = pre_one()
    incoming = jnp.where(live, grad_act[...] * silu_slope(pre), 0.0)
    if reduce_here:
        receive(swap_one, pre_one, 0, 3)
    after = lambda at: slot_after(at, (0, 3, 5, 6), 9)
    beside = pair_halves(units, after) if reduce_here else nothing
    grad_hidden[...] = norm_grad(5, 0, incoming, normed, scale_one, total, beside)
    down_rows = down_offsets * in_width
    if reduce_here:
        down_all[...] = dot(cols_down[...].T, grad_hidden[...])
        kept = down_rows // 2
        swap_down = swap(
            5, down_all.at[pl.ds(pl.multiple_of(kept * (1 - pair), kept), kept), :], down_got
        )
        swap_down.start()
    else:
        grads[2 * units * width :, :] = dot(cols_down[...].T, grad_hidden[...])
    for child in range(children):
        total_child = jnp.zeros((rows, in_width), jnp.float32)
        for k in range(child, down_offsets, children):
            there = side_cols[:, offsets + k : offsets + k + 1] < fine_rows
            total_child += jnp.where(there, dot_last(grad_hidden[...], w_down[k]), 0.0)
        spread_fine[pl.ds(child, rows, stride=children), :] = total_child
    fine_grad_ref[...] = spread_fine[...].astype(jnp.bfloat16)

    if reduce_here:

        def rest(at, carry):
            slot(at)
            return carry

        lax.fori_loop(13, chunks - 1 + GAP, rest, 0)
        swap_down.wait()
        for part in range(PAIR):
            total_down = (
                down_all[pl.ds(pl.multiple_of(kept * pair + part * width, width), width), :]
                + down_got[part * width : (part + 1) * width, :]
            )
            grads[chunks - 1, :, :, :, 8 * part : 8 * part + 8] = total_down.reshape(
                grads.shape[1:4] + (8, width)
            )
        lax.fori_loop(chunks - 1 + GAP, chunks + GAP + LAGS[-1], rest, 0)
    else:
        store = pltpu.make_async_copy(grads, results, load_sem.at[0])
        store.start()
        store.wait()


def place_kernel(
    features_ref,
    fine_grad_ref,
    grads_ref,
    gain_ref,
    bias_ref,
    features_out,
    fine_grad_out,
    grad_down_out,
    grad_mid_out,
    grad_out_out,
    gain_out,
    bias_out,
    sem,
):
    offsets = grad_mid_out.shape[0]
    units = (offsets + 1) // 2
    piece = (units + 1) // 2
    moves = []
    for pair in range(2):
        for at, target in enumerate((grad_out_out, grad_mid_out)):
            for first in range(0, units, piece):
                count = min(piece, offsets - units * pair - first, units - first)
                here = grads_ref.at[pair, pl.ds(at * units + first, count)]
                moves.append((here, target.at[pl.ds(units * pair + first, count)]))
        down_units = grad_down_out.shape[0] // 2
        here = grads_ref.at[pair, pl.ds(2 * units, down_units)]
        moves.append((here, grad_down_out.at[pl.ds(pair * down_units, down_units)]))
    copies = [
        pltpu.make_async_copy(source, target, sem.at[at])
        for at, (source, target) in enumerate(moves)
    ]
    for copy in copies:
        copy.start()
    features_out[...] = features_ref[...]
    fine_grad_out[...] = fine_grad_ref[...]
    gain_out[...] = gain_ref[...]
    bias_out[...] = bias_ref[...]
    for copy in copies:
        copy.wait()


def per_device(
    dp_size,
    group_size,
    fine_features,
    down_map,
    neighbours,
    voxel_counts,
    down_weight,
    mid_weight,
    out_weight,
    norm_gain,
    norm_bias,
    cotangent,
):
    rows, width = cotangent.shape
    fine_rows, in_width = fine_features.shape
    offsets = neighbours.shape[1]
    down_offsets = down_map.shape[1]
    f32, bf16, i32 = jnp.float32, jnp.bfloat16, jnp.int32
    vmem = pl.BlockSpec(memory_space=pltpu.VMEM)
    hbm = pl.BlockSpec(memory_space=pl.ANY)
    shape = jax.ShapeDtypeStruct
    reduce_here = dp_size == 8 and group_size == 4
    result = pltpu.VMEM if reduce_here else shape
    near_size, far_size = (dp_size * group_size, 1) if reduce_here else (group_size, dp_size)
    share = 2 if reduce_here else 1
    units = (offsets + 1) // 2 * 2 // share
    all_units = 2 * units + down_offsets * in_width // (share * width)
    grad_rows = all_units * width
    chunks = all_units // PAIR
    padded = (offsets + 1) // 2 * 2
    features, fine_grad, grads, gain_grad, bias_grad = pl.pallas_call(
        functools.partial(kernel, dp_size, group_size, reduce_here),
        out_shape=(
            result((rows, width), bf16),
            result((fine_rows, in_width), bf16),
            pltpu.VMEM((2, all_units, *GROUPS, 8, width), f32)
            if reduce_here
            else shape((grad_rows, width), f32),
            result(norm_gain.shape, f32),
            result(norm_bias.shape, f32),
        ),
        in_specs=[vmem, vmem, vmem, vmem, hbm, hbm, hbm, vmem, vmem, vmem],
        out_specs=(vmem, vmem, vmem if reduce_here else hbm, vmem, vmem),
        scratch_shapes=[
            pltpu.VMEM(down_weight.shape, bf16),
            pltpu.VMEM((padded, width, width), bf16),
            pltpu.VMEM((padded, width, width), bf16),
            pltpu.VMEM((fine_rows, in_width), f32),
            pltpu.VMEM((rows, down_offsets * in_width), bf16),
            pltpu.VMEM((offsets, rows, 128), bf16),
            pltpu.VMEM((2, GROUP * rows, rows), bf16),
            pltpu.VMEM((2, rows, GROUP * width), bf16),
            pltpu.VMEM((BLOCK, 2 * width), bf16),
            pltpu.VMEM((rows, width), f32),
            pltpu.VMEM((rows, width), bf16),
            pltpu.VMEM((rows, width), bf16),
            pltpu.VMEM((rows, width), f32),
            pltpu.VMEM((rows, width), f32),
            pltpu.VMEM((rows, width), f32),
            pltpu.VMEM((rows, width), bf16),
            pltpu.VMEM((rows, width), bf16),
            pltpu.VMEM((width, rows), bf16),
            pltpu.VMEM((width, rows), bf16),
            pltpu.VMEM((rows, width), f32),
            pltpu.VMEM((128, rows), f32),
            pltpu.VMEM((rows, 128), f32),
            pltpu.VMEM((padded, rows), i32),
            pltpu.VMEM((padded, rows), i32),
            pltpu.VMEM((2, rows, width), f32),
            pltpu.VMEM((4, rows, width), f32),
            pltpu.VMEM((down_offsets * in_width, width), f32),
            pltpu.VMEM((down_offsets * in_width // 2, width), f32),
            pltpu.VMEM(
                (chunks, *GROUPS, 8 * PAIR, width) if reduce_here else (grad_rows, width), f32
            ),
            pltpu.VMEM((RING, 2, *GROUPS[1:], 8 * PAIR, width), f32),
            pltpu.VMEM((chunks, GROUPS[2], 8 * PAIR, width), f32),
            pltpu.VMEM((chunks, GROUPS[1], 2, 8 * PAIR, width), f32),
            pltpu.VMEM((chunks, 2, 8 * PAIR, width), f32),
            pltpu.VMEM((chunks, 2, 8 * PAIR, width), f32),
            pltpu.VMEM((chunks, 2, 8 * PAIR, width), f32),
            pltpu.VMEM((6, near_size, 8, width // 2), f32),
            pltpu.VMEM((6, far_size, 8, width // 2), f32),
            pltpu.SemaphoreType.DMA((3,)),
            pltpu.SemaphoreType.DMA((RING, COPIES)),
            pltpu.SemaphoreType.DMA((RING, COPIES)),
            pltpu.SemaphoreType.DMA((6,)),
            pltpu.SemaphoreType.DMA((6,)),
            pltpu.SemaphoreType.DMA((6, group_size - 1)),
            pltpu.SemaphoreType.DMA((6, group_size - 1)),
            pltpu.SemaphoreType.DMA((6, far_size)),
            pltpu.SemaphoreType.DMA((6, far_size)),
        ],
        compiler_params=pltpu.CompilerParams(
            collective_id=0, has_side_effects=True, vmem_limit_bytes=(46 if reduce_here else 60) * 1024 * 1024
        ),
    )(
        fine_features,
        down_map.T,
        neighbours.T,
        voxel_counts.reshape(1, 1),
        down_weight,
        mid_weight,
        out_weight,
        norm_gain,
        norm_bias,
        cotangent,
    )
    if not reduce_here:
        grads = lax.psum(grads, ("dp", "group"))
        middle, end = offsets * width, 2 * padded * width
        grad_out = grads[:middle].reshape(out_weight.shape)
        grad_mid = grads[padded * width : padded * width + middle].reshape(mid_weight.shape)
        grad_down = grads[end:].reshape(down_weight.shape)
        return (features, fine_grad, grad_down, grad_mid, grad_out, gain_grad, bias_grad)
    held = [
        pltpu.with_memory_space_constraint(value, pltpu.VMEM)
        for value in (features, fine_grad, grads, gain_grad, bias_grad)
    ]
    features, fine_grad, grad_down, grad_mid, grad_out, gain_grad, bias_grad = pl.pallas_call(
        place_kernel,
        out_shape=(
            shape(features.shape, bf16),
            shape(fine_grad.shape, bf16),
            shape((down_offsets * in_width // width, *GROUPS, 8, width), f32),
            shape((offsets, *GROUPS, 8, width), f32),
            shape((offsets, *GROUPS, 8, width), f32),
            shape(norm_gain.shape, f32),
            shape(norm_bias.shape, f32),
        ),
        in_specs=[vmem] * 5,
        out_specs=(vmem, vmem, hbm, hbm, hbm, vmem, vmem),
        scratch_shapes=[pltpu.SemaphoreType.DMA((10,))],
        compiler_params=pltpu.CompilerParams(vmem_limit_bytes=8 * 1024 * 1024),
    )(*held)
    grad_down = grad_down.reshape(down_weight.shape)
    grad_mid = grad_mid.reshape(mid_weight.shape)
    grad_out = grad_out.reshape(out_weight.shape)
    return (features, fine_grad, grad_down, grad_mid, grad_out, gain_grad, bias_grad)


def solution(mesh):
    in_specs = (
        P(("dp", "group"), None),
        P(("dp", "group"), None),
        P(("dp", "group"), None),
        P(("dp", "group")),
        P(),
        P(),
        P(),
        P(),
        P(),
        P(("dp", "group"), None),
    )
    out_specs = (P(("dp", "group"), None), P(("dp", "group"), None), P(), P(), P(), P(), P())
    return jax.shard_map(
        functools.partial(per_device, mesh.shape["dp"], mesh.shape["group"]),
        mesh=mesh,
        in_specs=in_specs,
        out_specs=out_specs,
        check_vma=False,
    )
```

```python
import functools

import jax
import jax.numpy as jnp
from jax import lax
from jax.experimental import pallas as pl
from jax.experimental.pallas import tpu as pltpu
from jax.sharding import PartitionSpec as P

eps_norm = 1e-05
MESH = pl.DeviceIdType.MESH
GROUP = 3
BLOCK = 256
PAIR = 2
COPIES = 14
GROUPS = (4, 2, 4)
GAP = 2
LAGS = (0, 1, 2, 3, 5, 7, 8, 11, 12)
RING = 8


def sigmoid(value):
    return 1.0 / (1.0 + jnp.exp(-value))


def silu_slope(value):
    sigma = sigmoid(value)
    return sigma * (1.0 + value * (1.0 - sigma))


def dot(left, right):
    return jnp.dot(left, right, preferred_element_type=jnp.float32)


def dot_last(left, right):
    return lax.dot_general(
        left, right, (((1,), (1,)), ((), ())), preferred_element_type=jnp.float32
    )


def kernel(
    dp_size,
    group_size,
    reduce_here,
    fine_ref,
    down_rows_ref,
    nb_rows,
    count_ref,
    down_hbm,
    mid_hbm,
    out_hbm,
    gain_ref,
    bias_ref,
    cotangent_ref,
    features_ref,
    fine_grad_ref,
    results,
    gain_grad_ref,
    bias_grad_ref,
    w_down,
    w_mid,
    w_out,
    spread_fine,
    cols_down,
    nb_cols,
    pickers,
    columns,
    side_by_side,
    act_one,
    act_one_b,
    act_two_b,
    hid_one,
    hid_two,
    hid_three,
    held,
    grad_hidden,
    source_t,
    pair_source_t,
    grad_act,
    side,
    side_cols,
    nb_own,
    nb_pair,
    swap_out,
    swap_in,
    down_all,
    down_got,
    grads,
    from_core,
    from_first_a,
    from_first_b,
    from_second_a,
    from_second_b,
    from_line,
    near,
    far,
    load_sem,
    sum_send,
    sum_recv,
    swap_send,
    swap_recv,
    near_send,
    near_recv,
    far_send,
    far_recv,
):
    rows, width = cotangent_ref.shape
    offsets = nb_rows.shape[0]
    fine_rows, in_width = fine_ref.shape
    children = fine_rows // rows
    down_offsets = down_rows_ref.shape[0]
    units = (offsets + 1) // 2 * (1 if reduce_here else 2)
    chunks = grads.shape[0]
    dp_me = lax.axis_index("dp")
    group_me = lax.axis_index("group")

    loads = [
        pltpu.make_async_copy(source, target, load_sem.at[at])
        for at, (source, target) in enumerate(
            (
                (down_hbm, w_down),
                (mid_hbm, w_mid.at[pl.ds(0, offsets)]),
                (out_hbm, w_out.at[pl.ds(0, offsets)]),
            )
        )
    ]
    for load in loads:
        load.start()

    direct = reduce_here
    peers = [
        {
            "dp": lax.rem(dp_me + dp_step, dp_size),
            "group": lax.rem(group_me + group_step, group_size),
        }
        for dp_step in reversed(range(dp_size))
        for group_step in reversed(range(group_size))
        if (dp_step or group_step) and (direct or not dp_step or not group_step)
    ]
    barrier = pltpu.get_barrier_semaphore()
    for peer in peers:
        pl.semaphore_signal(barrier, inc=1, device_id=peer, device_id_type=MESH)

    def share(at, axis, me, size, slots, send, recv):
        copies = []
        for step in range(1, size):
            copies.append(
                pltpu.make_async_remote_copy(
                    src_ref=slots.at[at, me],
                    dst_ref=slots.at[at, me],
                    send_sem=send.at[at, step - 1],
                    recv_sem=recv.at[at, step - 1],
                    device_id={axis: lax.rem(me + step, size)},
                    device_id_type=MESH,
                )
            )
        for copy in copies:
            copy.start()
        return copies

    def exchange_direct(at, block, combine, meanwhile):
        me = dp_me * group_size + group_me
        near[at, me] = block
        for peer in peers:
            pltpu.make_async_remote_copy(
                src_ref=near.at[at, me],
                dst_ref=near.at[at, me],
                send_sem=near_send.at[at, 0],
                recv_sem=near_recv.at[at, 0],
                device_id=peer,
                device_id_type=MESH,
            ).start()
        for work in meanwhile:
            if work is not None:
                work()
        others = near.at[at, pl.ds(0, len(peers))]
        for sem in (near_recv, near_send):
            pltpu.make_async_copy(others, others, sem.at[at, 0]).wait()
        return combine([near[at, slot] for slot in range(len(peers) + 1)])

    def exchange(at, block, combine, meanwhile=(None, None)):
        if direct:
            return exchange_direct(at, block, combine, meanwhile)
        near[at, group_me] = block
        copies = share(at, "group", group_me, group_size, near, near_send, near_recv)
        if meanwhile[0] is not None:
            meanwhile[0]()
        for copy in copies:
            copy.wait()
        far[at, dp_me] = combine([near[at, slot] for slot in range(group_size)])
        copies = share(at, "dp", dp_me, dp_size, far, far_send, far_recv)
        if meanwhile[1] is not None:
            meanwhile[1]()
        for copy in copies:
            copy.wait()
        return combine([far[at, slot] for slot in range(dp_size)])

    lanes = width // 2

    def stack(first, second, third):
        filler = jnp.zeros((2, lanes), jnp.float32)
        return jnp.concatenate([first, second, third, filler], axis=0)

    def fold(value):
        return jnp.concatenate([value[:, :lanes], value[:, lanes:]], axis=0)

    def unfold(value):
        return jnp.concatenate([value[0:1], value[1:2]], axis=1)

    def add_all(blocks):
        total = blocks[0]
        for block in blocks[1:]:
            total = total + block
        return total

    def merge_all(blocks):
        count = add_all([block[4:6] for block in blocks])
        center = add_all([block[4:6] * block[0:2] for block in blocks]) / count
        squares = add_all(
            [
                block[2:4] + block[4:6] * (block[0:2] - center) * (block[0:2] - center)
                for block in blocks
            ]
        )
        return stack(center, squares, count)

    count = count_ref[...]
    own_count = jnp.broadcast_to(count.astype(jnp.float32), (1, width))

    def over_rows(body, start=0, tile=64, all_rows=rows):
        def step(at, carry):
            first = pl.multiple_of(at * tile, tile)
            return body(pl.ds(first, tile), first, carry)

        return lax.fori_loop(0, all_rows // tile, step, start)

    def live_rows(first, tile=64):
        return lax.broadcasted_iota(jnp.int32, (tile, width), 0) + first < count

    no_sum = jnp.zeros((8, width), jnp.float32)

    def add_to(total, value):
        return total + jnp.sum(value.reshape(-1, 8, width), axis=0)

    def sum_of(total):
        return jnp.sum(total, axis=0, keepdims=True)

    def norm_stats(at, hidden, meanwhile=(None, None)):
        center = sum_of(
            over_rows(lambda here, first, total: add_to(total, hidden[here, :]), no_sum)
        )
        center = center / own_count

        def square(here, first, total):
            centered = jnp.where(live_rows(first), hidden[here, :] - center, 0.0)
            return add_to(total, centered * centered)

        squares = sum_of(over_rows(square, no_sum))
        merged = exchange(
            at, stack(fold(center), fold(squares), fold(own_count)), merge_all, meanwhile
        )
        total = unfold(merged[4:6])
        scale = lax.rsqrt(unfold(merged[2:4]) / total + eps_norm)
        return unfold(merged[0:2]), scale, total

    def norm_grad(at, norm, sums, incoming, normed_of, scale, total, reset, meanwhile):
        shift_sum, scale_sum = (fold(sum_of(value)) for value in sums)
        summed = exchange(
            at, stack(shift_sum, scale_sum, jnp.zeros_like(shift_sum)), add_all, meanwhile
        )
        shift_sum, scale_sum = unfold(summed[0:2]), unfold(summed[2:4])
        bias_grad_ref[norm : norm + 1, :] = shift_sum
        gain_grad_ref[norm : norm + 1, :] = scale_sum
        factor = scale * gain_ref[norm : norm + 1, :]
        shift_mean, scale_mean = shift_sum / total, scale_sum / total

        def grad(here, first, carry):
            value = factor * (incoming[here, :] - shift_mean - normed_of(here) * scale_mean)
            value = jnp.where(live_rows(first), value, 0.0).astype(jnp.bfloat16)
            grad_hidden[here, :] = value
            held[here, :] = value
            if at < 5:
                grad_act[here, :] = reset(here)
                if reduce_here:
                    swap_out[at % 2, here, :] = value.astype(jnp.float32)
            return carry

        over_rows(grad)

    def pick(mask):
        return jnp.where(mask, jnp.bfloat16(1), jnp.bfloat16(0))

    def counting(shape, axis):
        return lax.broadcasted_iota(jnp.int32, shape, axis).astype(jnp.float32).astype(jnp.bfloat16)

    def place_spread(turn, step):
        picked = dot(pickers[turn, : PAIR * rows, :], held[...]).astype(jnp.bfloat16)
        for part in range(PAIR):
            columns[turn, :, part * width : (part + 1) * width] = picked[
                part * rows : (part + 1) * rows
            ]

    def run_steps(first, last, build, place, use, after):
        build(first % 2, first)

        def one(turn, step, more):
            place(turn, step)
            if more:
                build(1 - turn, step + 1)
            use(turn, step)

        bodies = (last - first - 1) // 2

        def body(at, carry):
            for turn in range(2):
                one((first + turn) % 2, first + 2 * at + turn, True)
            for turn in range(2):
                after(first + 2 * at + turn)
            return carry

        lax.fori_loop(0, bodies, body, 0)
        for step in range(first + 2 * bodies, last):
            one(step % 2, step, step + 1 < last)
            after(step)

    def convolve(source, weight, hidden):
        places = counting((rows, BLOCK), 1)
        hidden[...] = jnp.zeros_like(hidden)
        for block in range(2):
            side_by_side[:, block * width : (block + 1) * width] = source[
                block * BLOCK : (block + 1) * BLOCK, :
            ]

        def build(turn, step):
            for part in range(GROUP):
                code = nb_cols[step * GROUP + part]
                wanted = jnp.concatenate([jnp.maximum(code, -1 - code)] * (BLOCK // 128), axis=1)
                pickers[turn, part * rows : (part + 1) * rows, :BLOCK] = pick(wanted == places)

        def use(turn, step):
            weights = weight[pl.ds(step * GROUP, GROUP)].reshape(GROUP * width, width)
            hidden[...] += dot(columns[turn], weights)

        def place(turn, step):
            for part in range(GROUP):
                found = dot(
                    pickers[turn, part * rows : (part + 1) * rows, :BLOCK], side_by_side[...]
                )
                code = nb_cols[step * GROUP + part].astype(jnp.float32)
                second = jnp.concatenate([code] * (width // 128), axis=1) < 0
                columns[turn, :, part * width : (part + 1) * width] = jnp.where(
                    second, found[:, width:], found[:, :width]
                ).astype(jnp.bfloat16)

        run_steps(0, offsets // GROUP, build, place, use, no_slot)

    def build_spread(neighbours, first_offset):
        places = counting((BLOCK, rows), 0)

        def build(turn, step):
            for part in range(PAIR):
                wanted = neighbours[pl.ds(first_offset + PAIR * step + part, 1), :]
                wanted = wanted.astype(jnp.float32)
                for first in range(0, rows, BLOCK):
                    here = jnp.broadcast_to(wanted - first, (16, rows)).astype(jnp.bfloat16)
                    pickers[turn, part * rows + first : part * rows + first + BLOCK, :] = pick(
                        jnp.concatenate([here] * (BLOCK // 16), axis=0) == places
                    )

        return build

    def no_slot(at):
        pass

    def put(first_unit, at, product, more):
        for part in range(PAIR):
            value = product[:, part * width : (part + 1) * width]
            if reduce_here:
                c = first_unit // PAIR + at
                value = value.reshape(grads.shape[1:4] + (8, width))
                here_rows = slice(8 * part, 8 * part + 8)
                if more:
                    value = value + grads[c, :, :, :, here_rows]
                grads[c, :, :, :, here_rows] = value
            else:
                unit = pl.multiple_of((first_unit + PAIR * at + part) * width, width)
                grads[pl.ds(unit, width), :] = value

    def convolve_back(weight, act_grad, first_unit, own_slot, other_slot):
        def use_of(first_offset, weigh):
            def use(turn, step):
                spread = columns[turn, :, : PAIR * width]
                k = first_offset + PAIR * step
                weights = jnp.concatenate([weight[k + part] for part in range(PAIR)], axis=1)
                act_grad[...] += dot_last(spread, weights)
                if weigh:
                    put(first_unit, step, dot(source_t[...], spread), False)

            return use

        steps = units // PAIR
        build = build_spread(nb_own, own_offset)
        run_steps(0, steps, build, place_spread, use_of(own_offset, True), own_slot)
        if reduce_here:
            build = build_spread(nb_own, other_offset)
            run_steps(0, steps, build, place_spread, use_of(other_offset, False), other_slot)

    def convolve_pair(first_unit, first_step, last_step, at_slot):
        def use(turn, step):
            spread = columns[turn, :, : PAIR * width]
            put(first_unit, step, dot(pair_source_t[...], spread), True)

        build = build_spread(nb_pair, own_offset)
        run_steps(first_step, last_step, build, place_spread, use, at_slot)

    core, row = lax.rem(group_me, 2), group_me // 2
    column, plane = lax.rem(dp_me, 2), dp_me // 2
    pair, high = lax.rem(plane, 2), plane // 2
    planes = 4
    core_peer = {"group": group_me + 1 - 2 * core}
    row_peer = {"group": group_me + 2 - 4 * row}
    column_peer = {"dp": dp_me + 1 - 2 * column}
    pair_peer = {"dp": dp_me + 2 - 4 * pair}
    cross_peer = {"dp": dp_me + 4 - 8 * high}
    own_offset = units * pair if reduce_here else 0
    other_offset = units * (1 - pair)
    own = pl.ds(2 * core, 2)
    lane_a, lane_b = 2 * core, 2 * core + 1
    kept_row, given_row = pl.ds(2 * row, 2), pl.ds(2 * (1 - row), 2)

    def send(c, number, source, target, peer):
        turn = lax.rem(c, RING)
        return pltpu.make_async_remote_copy(
            src_ref=source,
            dst_ref=target,
            send_sem=sum_send.at[turn, number],
            recv_sem=sum_recv.at[turn, number],
            device_id=peer,
            device_id_type=MESH,
        )

    def copies_of(c, stage):
        part, both = grads.at[c], pl.ds(PAIR * c, PAIR)
        if stage == 0:
            given = part.at[pl.ds(2 * (1 - core), 2)]
            return [send(c, 0, given, from_core.at[lax.rem(c, RING)], core_peer)]
        if stage == 1:
            return [
                send(c, 1, part.at[lane_a, 1 - column], from_first_a.at[c], column_peer),
                send(c, 2, part.at[lane_b, :, given_row], from_first_b.at[c], row_peer),
            ]
        if stage == 2:
            return [
                send(c, 3, part.at[lane_a, column, given_row], from_second_a.at[c], row_peer),
                send(c, 4, part.at[lane_b, 1 - column, kept_row], from_second_b.at[c], column_peer),
            ]
        if stage == 3:
            given = part.at[own, column, 2 * row + 1 - high]
            return [send(c, 5, given, from_line.at[c], cross_peer)]
        if stage == 4:
            block = results.at[pair, both, own, column, 2 * row + high]
            return [
                send(
                    c,
                    5 + step,
                    block,
                    block,
                    {"dp": 2 * lax.rem(plane + step, planes) + column},
                )
                for step in range(1, planes)
            ]
        if stage == 5:
            block_a = results.at[:, both, lane_a, column, kept_row]
            block_b = results.at[:, both, lane_b, column, kept_row]
            return [
                send(c, 9, block_a, block_a, row_peer),
                send(c, 10, block_b, block_b, column_peer),
            ]
        if stage == 6:
            block_a = results.at[:, both, lane_a, column]
            block_b = results.at[:, both, lane_b, :, kept_row]
            return [
                send(c, 11, block_a, block_a, column_peer),
                send(c, 12, block_b, block_b, row_peer),
            ]
        block = results.at[:, both, own]
        return [send(c, 13, block, block, core_peer)]

    def stage_of(c, stage):
        if stage > 0:
            for copy in copies_of(c, stage - 1):
                copy.wait()
        if stage == 1:
            grads[c, own] = grads[c, own] + from_core[lax.rem(c, RING)]
        if stage == 2:
            grads[c, lane_a, column] = grads[c, lane_a, column] + from_first_a[c]
            grads[c, lane_b, :, kept_row] = grads[c, lane_b, :, kept_row] + from_first_b[c]
        if stage == 3:
            grads[c, lane_a, column, kept_row] = grads[c, lane_a, column, kept_row] + from_second_a[c]
            grads[c, lane_b, column, kept_row] = grads[c, lane_b, column, kept_row] + from_second_b[c]
        if stage == 4:
            mine = 2 * row + high
            grads[c, own, column, mine] = grads[c, own, column, mine] + from_line[c]
            for unit in range(PAIR):
                results[pair, PAIR * c + unit, own, column, mine] = grads[
                    c, own, column, mine, 8 * unit : 8 * unit + 8
                ]
        if stage < len(LAGS) - 1:
            for copy in copies_of(c, stage):
                copy.start()

    per_weight = units // PAIR

    def slot(at):
        if not reduce_here:
            return
        for stage, lag in enumerate(LAGS):
            entry = at - lag
            if isinstance(at, int):
                c = entry if entry < per_weight else max(entry - GAP, per_weight - 1)
                if 0 <= entry < chunks + GAP and (c == entry or entry >= per_weight + GAP):
                    stage_of(c, stage)
                continue
            second = entry >= per_weight + GAP

            @pl.when(
                ((entry >= 0) & (entry < per_weight)) | (second & (entry < chunks + GAP))
            )
            def _():
                stage_of(entry - GAP * second.astype(jnp.int32), stage)

    def slot_after(at, steps_with, first_slot):
        if isinstance(at, int):
            if at in steps_with:
                slot(first_slot + steps_with.index(at))
            return
        wanted, number = False, first_slot
        for step in steps_with:
            wanted = wanted | (at == step)
            number = number + (at > step).astype(jnp.int32)

        @pl.when(wanted)
        def _():
            slot(number)

    def swap(at, source, target):
        return pltpu.make_async_remote_copy(
            src_ref=source,
            dst_ref=target,
            send_sem=swap_send.at[at],
            recv_sem=swap_recv.at[at],
            device_id=pair_peer,
            device_id_type=MESH,
        )

    def swap_rows(at):
        return swap(at, swap_out.at[(at + 1) % 2], swap_in.at[at])

    places = nb_rows[...]
    codes = jnp.where(places < BLOCK, places, jnp.where(places < rows, BLOCK - 1 - places, 4 * BLOCK))
    side[...] = jnp.zeros_like(side)
    side[:offsets, :] = codes.astype(jnp.float32)
    side[offsets : offsets + down_offsets, :] = down_rows_ref[...].astype(jnp.float32)
    side_cols[...] = side[...].T
    nb_own[...] = jnp.full_like(nb_own, rows)
    nb_own[:offsets, :] = nb_rows[...]
    swap_neighbours = swap(4, nb_own, nb_pair)
    for weight in (w_mid, w_out):
        weight[offsets:] = jnp.zeros_like(weight[offsets:])

    def widen(here, first, carry):
        spread_fine[here, :] = fine_ref[here, :].astype(jnp.float32)
        return carry

    over_rows(widen, tile=128, all_rows=fine_rows)
    for k in range(down_offsets):
        child = spread_fine[pl.ds(k % children, rows, stride=children), :]
        there = side_cols[:, offsets + k : offsets + k + 1] < fine_rows
        cols_down[:, k * in_width : (k + 1) * in_width] = jnp.where(there, child, 0.0).astype(
            jnp.bfloat16
        )
    loads[0].wait()
    hid_one[...] = dot(cols_down[...], w_down[...].reshape(down_offsets * in_width, width))

    def spread_neighbours():
        def spread(here, first, carry):
            for k in range(offsets):
                nb_cols[k, here, :] = jnp.broadcast_to(
                    side_cols[here, k : k + 1], (64, 128)
                ).astype(jnp.bfloat16)
            return carry

        over_rows(spread)

    pl.semaphore_wait(barrier, len(peers))

    swap_one = swap(0, hid_one, swap_in.at[0])
    swap_two = swap(1, hid_two, swap_in.at[1])

    def start_one():
        swap_neighbours.start()
        swap_one.start()

    def start_two():
        swap_two.start()

    beside = (spread_neighbours, start_one if reduce_here else None)
    center_one, scale_one, total = norm_stats(0, hid_one, beside)

    def normed_one(here, hidden=hid_one):
        return (hidden[here, :] - center_one) * scale_one

    def pre_one(normed):
        return normed * gain_ref[0:1, :] + bias_ref[0:1, :]

    def activate_one(here, first, carry):
        pre = pre_one(normed_one(here))
        value = jnp.where(live_rows(first), pre * sigmoid(pre), 0.0)
        act_one[here, :] = value
        act_one_b[here, :] = value.astype(jnp.bfloat16)
        return carry

    over_rows(activate_one)
    loads[1].wait()
    convolve(act_one_b, w_mid, hid_two)
    center_two, scale_two, _ = norm_stats(
        1, hid_two, (None, start_two if reduce_here else None)
    )

    def normed_two(here, hidden=hid_two):
        return (hidden[here, :] - center_two) * scale_two

    def pre_two(normed):
        return normed * gain_ref[1:2, :] + bias_ref[1:2, :]

    def activate_two(here, first, carry):
        pre = pre_two(normed_two(here))
        act_two_b[here, :] = jnp.where(live_rows(first), pre * sigmoid(pre), 0.0).astype(
            jnp.bfloat16
        )
        return carry

    over_rows(activate_two)
    loads[2].wait()
    convolve(act_two_b, w_out, hid_three)

    def turn(source):
        def part(here, first, carry):
            source_t[:, here] = source[here, :].T
            return carry

        over_rows(part, tile=128)

    center_three, scale_three, _ = norm_stats(
        2, hid_three, (lambda: turn(act_two_b), None)
    )

    def normed_three(here):
        return (hid_three[here, :] - center_three) * scale_three

    def top(here, first, sums):
        normed, alive = normed_three(here), live_rows(first)
        pre = normed * gain_ref[2:3, :] + bias_ref[2:3, :]
        summed = jnp.where(alive, pre, 0.0) + act_one[here, :]
        sigma = sigmoid(summed)
        features_ref[here, :] = jnp.where(alive, summed * sigma, 0.0).astype(jnp.bfloat16)
        slope = sigma * (1.0 + summed * (1.0 - sigma))
        grad = jnp.where(alive, cotangent_ref[here, :].astype(jnp.float32) * slope, 0.0)
        act_one[here, :] = grad
        return add_to(sums[0], grad), add_to(sums[1], grad * normed)

    sums = over_rows(top, (no_sum, no_sum))

    def pair_source(swapped, source_at, normed_of, pre_of):
        swapped.wait()

        def part(here, first, carry):
            pre = pre_of(normed_of(here, swap_in.at[source_at]))
            pair_source_t[:, here] = (pre * sigmoid(pre)).astype(jnp.bfloat16).T
            return carry

        over_rows(part, tile=128)

    def pair_hidden(hidden_at):
        swap_rows(hidden_at).wait()

        def part(here, first, carry):
            held[here, :] = swap_in[hidden_at, here, :].astype(jnp.bfloat16)
            return carry

        over_rows(part)

    def source_two():
        if reduce_here:
            pair_source(swap_two, 1, normed_two, pre_two)

    norm_grad(
        3,
        2,
        sums,
        act_one,
        normed_three,
        scale_three,
        total,
        lambda here: jnp.zeros((64, width), jnp.float32),
        (source_two, None),
    )
    if reduce_here:
        swap_rows(2).start()
    steps = units // PAIR

    def pair_halves(first_unit, at_slot):
        middle = (steps + 1) // 2
        return (
            lambda: convolve_pair(first_unit, 0, middle, at_slot),
            lambda: convolve_pair(first_unit, middle, steps, at_slot),
        )

    def through_silu(normed_of, pre_of):
        def part(here, first, sums):
            normed = normed_of(here)
            grad = grad_act[here, :] * silu_slope(pre_of(normed))
            grad = jnp.where(live_rows(first), grad, 0.0)
            grad_act[here, :] = grad
            return add_to(sums[0], grad), add_to(sums[1], grad * normed)

        return over_rows(part, (no_sum, no_sum))

    nothing = (None, None)
    convolve_back(w_out, grad_act, 0, no_slot, no_slot)
    sums = through_silu(normed_two, pre_two)
    if reduce_here:
        swap_neighbours.wait()
        pair_hidden(2)
    after = lambda at: slot_after(at, (1, 3, 4, 6), 0)
    norm_grad(
        4,
        1,
        sums,
        grad_act,
        normed_two,
        scale_two,
        total,
        lambda here: act_one[here, :],
        pair_halves(0, after) if reduce_here else nothing,
    )
    if reduce_here:
        swap_rows(3).start()
    turn(act_one_b)
    convolve_back(
        w_mid,
        grad_act,
        units,
        lambda at: slot_after(at, (0, 5), 4),
        lambda at: slot_after(at, (1, 3, 5), 6),
    )
    sums = through_silu(normed_one, pre_one)
    if reduce_here:
        pair_source(swap_one, 0, normed_one, pre_one)
        pair_hidden(3)
    after = lambda at: slot_after(at, (0, 3, 5, 6), 9)
    norm_grad(
        5,
        0,
        sums,
        grad_act,
        normed_one,
        scale_one,
        total,
        None,
        pair_halves(units, after) if reduce_here else nothing,
    )
    down_rows = down_offsets * in_width
    if reduce_here:
        down_all[...] = dot(cols_down[...].T, grad_hidden[...])
        kept = down_rows // 2
        swap_down = swap(
            5, down_all.at[pl.ds(pl.multiple_of(kept * (1 - pair), kept), kept), :], down_got
        )
        swap_down.start()
    else:
        grads[2 * units * width :, :] = dot(cols_down[...].T, grad_hidden[...])
    for child in range(children):
        total_child = jnp.zeros((rows, in_width), jnp.float32)
        for k in range(child, down_offsets, children):
            there = side_cols[:, offsets + k : offsets + k + 1] < fine_rows
            total_child += jnp.where(there, dot_last(grad_hidden[...], w_down[k]), 0.0)
        spread_fine[pl.ds(child, rows, stride=children), :] = total_child
    fine_grad_ref[...] = spread_fine[...].astype(jnp.bfloat16)

    if reduce_here:

        def rest(at, carry):
            slot(at)
            return carry

        lax.fori_loop(13, chunks - 1 + GAP, rest, 0)
        swap_down.wait()
        for part in range(PAIR):
            total_down = (
                down_all[pl.ds(pl.multiple_of(kept * pair + part * width, width), width), :]
                + down_got[part * width : (part + 1) * width, :]
            )
            grads[chunks - 1, :, :, :, 8 * part : 8 * part + 8] = total_down.reshape(
                grads.shape[1:4] + (8, width)
            )
        lax.fori_loop(chunks - 1 + GAP, chunks + GAP + LAGS[-1], rest, 0)
    else:
        store = pltpu.make_async_copy(grads, results, load_sem.at[0])
        store.start()
        store.wait()


def place_kernel(
    features_ref,
    fine_grad_ref,
    grads_ref,
    gain_ref,
    bias_ref,
    features_out,
    fine_grad_out,
    grad_down_out,
    grad_mid_out,
    grad_out_out,
    gain_out,
    bias_out,
    sem,
):
    offsets = grad_mid_out.shape[0]
    units = (offsets + 1) // 2
    piece = (units + 1) // 2
    moves = []
    for pair in range(2):
        for at, target in enumerate((grad_out_out, grad_mid_out)):
            for first in range(0, units, piece):
                count = min(piece, offsets - units * pair - first, units - first)
                here = grads_ref.at[pair, pl.ds(at * units + first, count)]
                moves.append((here, target.at[pl.ds(units * pair + first, count)]))
        down_units = grad_down_out.shape[0] // 2
        here = grads_ref.at[pair, pl.ds(2 * units, down_units)]
        moves.append((here, grad_down_out.at[pl.ds(pair * down_units, down_units)]))
    copies = [
        pltpu.make_async_copy(source, target, sem.at[at])
        for at, (source, target) in enumerate(moves)
    ]
    for copy in copies:
        copy.start()
    features_out[...] = features_ref[...]
    fine_grad_out[...] = fine_grad_ref[...]
    gain_out[...] = gain_ref[...]
    bias_out[...] = bias_ref[...]
    for copy in copies:
        copy.wait()


def per_device(
    dp_size,
    group_size,
    fine_features,
    down_map,
    neighbours,
    voxel_counts,
    down_weight,
    mid_weight,
    out_weight,
    norm_gain,
    norm_bias,
    cotangent,
):
    rows, width = cotangent.shape
    fine_rows, in_width = fine_features.shape
    offsets = neighbours.shape[1]
    down_offsets = down_map.shape[1]
    f32, bf16, i32 = jnp.float32, jnp.bfloat16, jnp.int32
    vmem = pl.BlockSpec(memory_space=pltpu.VMEM)
    hbm = pl.BlockSpec(memory_space=pl.ANY)
    shape = jax.ShapeDtypeStruct
    reduce_here = dp_size == 8 and group_size == 4
    result = pltpu.VMEM if reduce_here else shape
    near_size, far_size = (dp_size * group_size, 1) if reduce_here else (group_size, dp_size)
    share = 2 if reduce_here else 1
    units = (offsets + 1) // 2 * 2 // share
    all_units = 2 * units + down_offsets * in_width // (share * width)
    grad_rows = all_units * width
    chunks = all_units // PAIR
    padded = (offsets + 1) // 2 * 2
    features, fine_grad, grads, gain_grad, bias_grad = pl.pallas_call(
        functools.partial(kernel, dp_size, group_size, reduce_here),
        out_shape=(
            result((rows, width), bf16),
            result((fine_rows, in_width), bf16),
            pltpu.VMEM((2, all_units, *GROUPS, 8, width), f32)
            if reduce_here
            else shape((grad_rows, width), f32),
            result(norm_gain.shape, f32),
            result(norm_bias.shape, f32),
        ),
        in_specs=[vmem, vmem, vmem, vmem, hbm, hbm, hbm, vmem, vmem, vmem],
        out_specs=(vmem, vmem, vmem if reduce_here else hbm, vmem, vmem),
        scratch_shapes=[
            pltpu.VMEM(down_weight.shape, bf16),
            pltpu.VMEM((padded, width, width), bf16),
            pltpu.VMEM((padded, width, width), bf16),
            pltpu.VMEM((fine_rows, in_width), f32),
            pltpu.VMEM((rows, down_offsets * in_width), bf16),
            pltpu.VMEM((offsets, rows, 128), bf16),
            pltpu.VMEM((2, GROUP * rows, rows), bf16),
            pltpu.VMEM((2, rows, GROUP * width), bf16),
            pltpu.VMEM((BLOCK, 2 * width), bf16),
            pltpu.VMEM((rows, width), f32),
            pltpu.VMEM((rows, width), bf16),
            pltpu.VMEM((rows, width), bf16),
            pltpu.VMEM((rows, width), f32),
            pltpu.VMEM((rows, width), f32),
            pltpu.VMEM((rows, width), f32),
            pltpu.VMEM((rows, width), bf16),
            pltpu.VMEM((rows, width), bf16),
            pltpu.VMEM((width, rows), bf16),
            pltpu.VMEM((width, rows), bf16),
            pltpu.VMEM((rows, width), f32),
            pltpu.VMEM((128, rows), f32),
            pltpu.VMEM((rows, 128), f32),
            pltpu.VMEM((padded, rows), i32),
            pltpu.VMEM((padded, rows), i32),
            pltpu.VMEM((2, rows, width), f32),
            pltpu.VMEM((4, rows, width), f32),
            pltpu.VMEM((down_offsets * in_width, width), f32),
            pltpu.VMEM((down_offsets * in_width // 2, width), f32),
            pltpu.VMEM(
                (chunks, *GROUPS, 8 * PAIR, width) if reduce_here else (grad_rows, width), f32
            ),
            pltpu.VMEM((RING, 2, *GROUPS[1:], 8 * PAIR, width), f32),
            pltpu.VMEM((chunks, GROUPS[2], 8 * PAIR, width), f32),
            pltpu.VMEM((chunks, GROUPS[1], 2, 8 * PAIR, width), f32),
            pltpu.VMEM((chunks, 2, 8 * PAIR, width), f32),
            pltpu.VMEM((chunks, 2, 8 * PAIR, width), f32),
            pltpu.VMEM((chunks, 2, 8 * PAIR, width), f32),
            pltpu.VMEM((6, near_size, 8, width // 2), f32),
            pltpu.VMEM((6, far_size, 8, width // 2), f32),
            pltpu.SemaphoreType.DMA((3,)),
            pltpu.SemaphoreType.DMA((RING, COPIES)),
            pltpu.SemaphoreType.DMA((RING, COPIES)),
            pltpu.SemaphoreType.DMA((6,)),
            pltpu.SemaphoreType.DMA((6,)),
            pltpu.SemaphoreType.DMA((6, group_size - 1)),
            pltpu.SemaphoreType.DMA((6, group_size - 1)),
            pltpu.SemaphoreType.DMA((6, far_size)),
            pltpu.SemaphoreType.DMA((6, far_size)),
        ],
        compiler_params=pltpu.CompilerParams(
            collective_id=0, has_side_effects=True, vmem_limit_bytes=(46 if reduce_here else 60) * 1024 * 1024
        ),
    )(
        fine_features,
        down_map.T,
        neighbours.T,
        voxel_counts.reshape(1, 1),
        down_weight,
        mid_weight,
        out_weight,
        norm_gain,
        norm_bias,
        cotangent,
    )
    if not reduce_here:
        grads = lax.psum(grads, ("dp", "group"))
        middle, end = offsets * width, 2 * padded * width
        grad_out = grads[:middle].reshape(out_weight.shape)
        grad_mid = grads[padded * width : padded * width + middle].reshape(mid_weight.shape)
        grad_down = grads[end:].reshape(down_weight.shape)
        return (features, fine_grad, grad_down, grad_mid, grad_out, gain_grad, bias_grad)
    held = [
        pltpu.with_memory_space_constraint(value, pltpu.VMEM)
        for value in (features, fine_grad, grads, gain_grad, bias_grad)
    ]
    features, fine_grad, grad_down, grad_mid, grad_out, gain_grad, bias_grad = pl.pallas_call(
        place_kernel,
        out_shape=(
            shape(features.shape, bf16),
            shape(fine_grad.shape, bf16),
            shape((down_offsets * in_width // width, *GROUPS, 8, width), f32),
            shape((offsets, *GROUPS, 8, width), f32),
            shape((offsets, *GROUPS, 8, width), f32),
            shape(norm_gain.shape, f32),
            shape(norm_bias.shape, f32),
        ),
        in_specs=[vmem] * 5,
        out_specs=(vmem, vmem, hbm, hbm, hbm, vmem, vmem),
        scratch_shapes=[pltpu.SemaphoreType.DMA((10,))],
        compiler_params=pltpu.CompilerParams(vmem_limit_bytes=8 * 1024 * 1024),
    )(*held)
    grad_down = grad_down.reshape(down_weight.shape)
    grad_mid = grad_mid.reshape(mid_weight.shape)
    grad_out = grad_out.reshape(out_weight.shape)
    return (features, fine_grad, grad_down, grad_mid, grad_out, gain_grad, bias_grad)


def solution(mesh):
    in_specs = (
        P(("dp", "group"), None),
        P(("dp", "group"), None),
        P(("dp", "group"), None),
        P(("dp", "group")),
        P(),
        P(),
        P(),
        P(),
        P(),
        P(("dp", "group"), None),
    )
    out_specs = (P(("dp", "group"), None), P(("dp", "group"), None), P(), P(), P(), P(), P())
    return jax.shard_map(
        functools.partial(per_device, mesh.shape["dp"], mesh.shape["group"]),
        mesh=mesh,
        in_specs=in_specs,
        out_specs=out_specs,
        check_vma=False,
    )
```

```python
import functools

import jax
import jax.numpy as jnp
from jax import lax
from jax.experimental import pallas as pl
from jax.experimental.pallas import tpu as pltpu
from jax.sharding import PartitionSpec as P

eps_norm = 1e-05
MESH = pl.DeviceIdType.MESH
GROUP = 3
BLOCK = 256
PAIR = 2
COPIES = 14
GROUPS = (4, 2, 4)
GAP = 3
LAGS = (0, 1, 2, 3, 5, 7, 8, 10, 11)
RING = 8


def sigmoid(value):
    return 1.0 / (1.0 + jnp.exp(-value))


def silu_slope(value):
    sigma = sigmoid(value)
    return sigma * (1.0 + value * (1.0 - sigma))


def dot(left, right):
    return jnp.dot(left, right, preferred_element_type=jnp.float32)


def dot_last(left, right):
    return lax.dot_general(
        left, right, (((1,), (1,)), ((), ())), preferred_element_type=jnp.float32
    )


def kernel(
    dp_size,
    group_size,
    reduce_here,
    fine_ref,
    down_rows_ref,
    nb_rows,
    count_ref,
    down_hbm,
    mid_hbm,
    out_hbm,
    gain_ref,
    bias_ref,
    cotangent_ref,
    features_ref,
    fine_grad_ref,
    results,
    gain_grad_ref,
    bias_grad_ref,
    w_down,
    w_mid,
    w_out,
    spread_fine,
    cols_down,
    nb_cols,
    pickers,
    columns,
    side_by_side,
    act_one,
    act_one_b,
    act_two_b,
    hid_one,
    hid_two,
    hid_three,
    held,
    grad_hidden,
    source_t,
    pair_source_t,
    grad_act,
    side,
    side_cols,
    nb_own,
    nb_pair,
    swap_out,
    swap_in,
    down_all,
    down_got,
    grads,
    from_core,
    from_first_a,
    from_first_b,
    from_second_a,
    from_second_b,
    from_line,
    near,
    far,
    load_sem,
    sum_send,
    sum_recv,
    swap_send,
    swap_recv,
    near_send,
    near_recv,
    far_send,
    far_recv,
):
    rows, width = cotangent_ref.shape
    offsets = nb_rows.shape[0]
    fine_rows, in_width = fine_ref.shape
    children = fine_rows // rows
    down_offsets = down_rows_ref.shape[0]
    units = (offsets + 1) // 2 * (1 if reduce_here else 2)
    chunks = grads.shape[0]
    dp_me = lax.axis_index("dp")
    group_me = lax.axis_index("group")

    loads = [
        pltpu.make_async_copy(source, target, load_sem.at[at])
        for at, (source, target) in enumerate(
            (
                (down_hbm, w_down),
                (mid_hbm, w_mid.at[pl.ds(0, offsets)]),
                (out_hbm, w_out.at[pl.ds(0, offsets)]),
            )
        )
    ]
    for load in loads:
        load.start()

    direct = reduce_here
    peers = [
        {
            "dp": lax.rem(dp_me + dp_step, dp_size),
            "group": lax.rem(group_me + group_step, group_size),
        }
        for dp_step in reversed(range(dp_size))
        for group_step in reversed(range(group_size))
        if (dp_step or group_step) and (direct or not dp_step or not group_step)
    ]
    barrier = pltpu.get_barrier_semaphore()
    for peer in peers:
        pl.semaphore_signal(barrier, inc=1, device_id=peer, device_id_type=MESH)

    def share(at, axis, me, size, slots, send, recv):
        copies = []
        for step in range(1, size):
            copies.append(
                pltpu.make_async_remote_copy(
                    src_ref=slots.at[at, me],
                    dst_ref=slots.at[at, me],
                    send_sem=send.at[at, step - 1],
                    recv_sem=recv.at[at, step - 1],
                    device_id={axis: lax.rem(me + step, size)},
                    device_id_type=MESH,
                )
            )
        for copy in copies:
            copy.start()
        return copies

    def exchange_direct(at, block, combine, meanwhile):
        me = dp_me * group_size + group_me
        near[at, me] = block
        for peer in peers:
            pltpu.make_async_remote_copy(
                src_ref=near.at[at, me],
                dst_ref=near.at[at, me],
                send_sem=near_send.at[at, 0],
                recv_sem=near_recv.at[at, 0],
                device_id=peer,
                device_id_type=MESH,
            ).start()
        for work in meanwhile:
            if work is not None:
                work()
        others = near.at[at, pl.ds(0, len(peers))]
        for sem in (near_recv, near_send):
            pltpu.make_async_copy(others, others, sem.at[at, 0]).wait()
        return combine([near[at, slot] for slot in range(len(peers) + 1)])

    def exchange(at, block, combine, meanwhile=(None, None)):
        if direct:
            return exchange_direct(at, block, combine, meanwhile)
        near[at, group_me] = block
        copies = share(at, "group", group_me, group_size, near, near_send, near_recv)
        if meanwhile[0] is not None:
            meanwhile[0]()
        for copy in copies:
            copy.wait()
        far[at, dp_me] = combine([near[at, slot] for slot in range(group_size)])
        copies = share(at, "dp", dp_me, dp_size, far, far_send, far_recv)
        if meanwhile[1] is not None:
            meanwhile[1]()
        for copy in copies:
            copy.wait()
        return combine([far[at, slot] for slot in range(dp_size)])

    lanes = width // 2

    def stack(first, second, third):
        filler = jnp.zeros((2, lanes), jnp.float32)
        return jnp.concatenate([first, second, third, filler], axis=0)

    def fold(value):
        return jnp.concatenate([value[:, :lanes], value[:, lanes:]], axis=0)

    def unfold(value):
        return jnp.concatenate([value[0:1], value[1:2]], axis=1)

    def add_all(blocks):
        total = blocks[0]
        for block in blocks[1:]:
            total = total + block
        return total

    def merge_all(blocks):
        count = add_all([block[4:6] for block in blocks])
        center = add_all([block[4:6] * block[0:2] for block in blocks]) / count
        squares = add_all(
            [
                block[2:4] + block[4:6] * (block[0:2] - center) * (block[0:2] - center)
                for block in blocks
            ]
        )
        return stack(center, squares, count)

    count = count_ref[...]
    own_count = jnp.broadcast_to(count.astype(jnp.float32), (1, width))
    live = lax.broadcasted_iota(jnp.int32, (rows, width), 0) < count

    def norm_stats(at, hidden, meanwhile=(None, None)):
        center = jnp.sum(hidden, axis=0, keepdims=True) / own_count
        centered = jnp.where(live, hidden - center, 0.0)
        squares = jnp.sum(centered * centered, axis=0, keepdims=True)
        merged = exchange(
            at, stack(fold(center), fold(squares), fold(own_count)), merge_all, meanwhile
        )
        total = unfold(merged[4:6])
        scale = lax.rsqrt(unfold(merged[2:4]) / total + eps_norm)
        return unfold(merged[0:2]), scale, total

    def norm_grad(at, norm, incoming, normed, scale, total, meanwhile=(None, None)):
        shift_sum = fold(jnp.sum(incoming, axis=0, keepdims=True))
        scale_sum = fold(jnp.sum(incoming * normed, axis=0, keepdims=True))
        summed = exchange(
            at, stack(shift_sum, scale_sum, jnp.zeros_like(shift_sum)), add_all, meanwhile
        )
        shift_sum, scale_sum = unfold(summed[0:2]), unfold(summed[2:4])
        bias_grad_ref[norm : norm + 1, :] = shift_sum
        gain_grad_ref[norm : norm + 1, :] = scale_sum

        def grad(incoming, normed):
            return (
                scale
                * gain_ref[norm : norm + 1, :]
                * (incoming - shift_sum / total - normed * (scale_sum / total))
            )

        hidden_grad = jnp.where(live, grad(incoming, normed), 0.0).astype(jnp.bfloat16)
        return hidden_grad, grad

    def pick(mask):
        return jnp.where(mask, jnp.bfloat16(1), jnp.bfloat16(0))

    def counting(shape, axis):
        return lax.broadcasted_iota(jnp.int32, shape, axis).astype(jnp.float32).astype(jnp.bfloat16)

    def place_spread(turn, step):
        picked = dot(pickers[turn, : PAIR * rows, :], held[...]).astype(jnp.bfloat16)
        for part in range(PAIR):
            columns[turn, :, part * width : (part + 1) * width] = picked[
                part * rows : (part + 1) * rows
            ]

    def run_steps(first, last, build, place, use, after):
        build(first % 2, first)

        def one(turn, step, more):
            place(turn, step)
            if more:
                build(1 - turn, step + 1)
            use(turn, step)

        bodies = (last - first - 1) // 2

        def body(at, carry):
            for turn in range(2):
                one((first + turn) % 2, first + 2 * at + turn, True)
            after(first + 2 * at, 2)
            return carry

        lax.fori_loop(0, bodies, body, 0)
        for step in range(first + 2 * bodies, last):
            one(step % 2, step, step + 1 < last)
            after(step, 1)

    def convolve(source, weight, hidden):
        places = counting((rows, BLOCK), 1)
        hidden[...] = jnp.zeros_like(hidden)
        for block in range(2):
            side_by_side[:, block * width : (block + 1) * width] = source[
                block * BLOCK : (block + 1) * BLOCK, :
            ]

        def build(turn, step):
            for part in range(GROUP):
                code = nb_cols[step * GROUP + part]
                wanted = jnp.concatenate([jnp.maximum(code, -1 - code)] * (BLOCK // 128), axis=1)
                pickers[turn, part * rows : (part + 1) * rows, :BLOCK] = pick(wanted == places)

        def use(turn, step):
            weights = weight[pl.ds(step * GROUP, GROUP)].reshape(GROUP * width, width)
            hidden[...] += dot(columns[turn], weights)

        def place(turn, step):
            for part in range(GROUP):
                found = dot(
                    pickers[turn, part * rows : (part + 1) * rows, :BLOCK], side_by_side[...]
                )
                code = nb_cols[step * GROUP + part].astype(jnp.float32)
                second = jnp.concatenate([code] * (width // 128), axis=1) < 0
                columns[turn, :, part * width : (part + 1) * width] = jnp.where(
                    second, found[:, width:], found[:, :width]
                ).astype(jnp.bfloat16)

        run_steps(0, offsets // GROUP, build, place, use, no_slot)

    def build_spread(neighbours, first_offset):
        places = counting((BLOCK, rows), 0)

        def build(turn, step):
            for part in range(PAIR):
                wanted = neighbours[pl.ds(first_offset + PAIR * step + part, 1), :]
                wanted = wanted.astype(jnp.float32)
                for first in range(0, rows, BLOCK):
                    here = jnp.broadcast_to(wanted - first, (16, rows)).astype(jnp.bfloat16)
                    pickers[turn, part * rows + first : part * rows + first + BLOCK, :] = pick(
                        jnp.concatenate([here] * (BLOCK // 16), axis=0) == places
                    )

        return build

    def no_slot(at, count):
        pass

    def put(first_unit, at, product, more):
        for part in range(PAIR):
            value = product[:, part * width : (part + 1) * width]
            if reduce_here:
                c = first_unit // PAIR + at
                value = value.reshape(grads.shape[1:4] + (8, width))
                here_rows = slice(8 * part, 8 * part + 8)
                if more:
                    value = value + grads[c, :, :, :, here_rows]
                grads[c, :, :, :, here_rows] = value
            else:
                unit = pl.multiple_of((first_unit + PAIR * at + part) * width, width)
                grads[pl.ds(unit, width), :] = value

    def convolve_back(weight, act_grad, first_unit, own_slot, other_slot):
        def use_of(first_offset, weigh):
            def use(turn, step):
                spread = columns[turn, :, : PAIR * width]
                k = first_offset + PAIR * step
                weights = jnp.concatenate([weight[k + part] for part in range(PAIR)], axis=1)
                act_grad[...] += dot_last(spread, weights)
                if weigh:
                    put(first_unit, step, dot(source_t[...], spread), False)

            return use

        steps = units // PAIR
        build = build_spread(nb_own, own_offset)
        run_steps(0, steps, build, place_spread, use_of(own_offset, True), own_slot)
        if reduce_here:
            build = build_spread(nb_own, other_offset)
            run_steps(0, steps, build, place_spread, use_of(other_offset, False), other_slot)

    def convolve_pair(first_unit, first_step, last_step, at_slot):
        def use(turn, step):
            spread = columns[turn, :, : PAIR * width]
            put(first_unit, step, dot(pair_source_t[...], spread), True)

        build = build_spread(nb_pair, own_offset)
        run_steps(first_step, last_step, build, place_spread, use, at_slot)

    core, row = lax.rem(group_me, 2), group_me // 2
    column, plane = lax.rem(dp_me, 2), dp_me // 2
    pair, high = lax.rem(plane, 2), plane // 2
    planes = 4
    core_peer = {"group": group_me + 1 - 2 * core}
    row_peer = {"group": group_me + 2 - 4 * row}
    column_peer = {"dp": dp_me + 1 - 2 * column}
    pair_peer = {"dp": dp_me + 2 - 4 * pair}
    cross_peer = {"dp": dp_me + 4 - 8 * high}
    own_offset = units * pair if reduce_here else 0
    other_offset = units * (1 - pair)
    own = pl.ds(2 * core, 2)
    lane_a, lane_b = 2 * core, 2 * core + 1
    kept_row, given_row = pl.ds(2 * row, 2), pl.ds(2 * (1 - row), 2)

    def send(c, number, source, target, peer):
        turn = lax.rem(c, RING)
        return pltpu.make_async_remote_copy(
            src_ref=source,
            dst_ref=target,
            send_sem=sum_send.at[turn, number],
            recv_sem=sum_recv.at[turn, number],
            device_id=peer,
            device_id_type=MESH,
        )

    def copies_of(c, stage):
        part, both = grads.at[c], pl.ds(PAIR * c, PAIR)
        if stage == 0:
            given = part.at[pl.ds(2 * (1 - core), 2)]
            return [send(c, 0, given, from_core.at[lax.rem(c, RING)], core_peer)]
        if stage == 1:
            return [
                send(c, 1, part.at[lane_a, 1 - column], from_first_a.at[c], column_peer),
                send(c, 2, part.at[lane_b, :, given_row], from_first_b.at[c], row_peer),
            ]
        if stage == 2:
            return [
                send(c, 3, part.at[lane_a, column, given_row], from_second_a.at[c], row_peer),
                send(c, 4, part.at[lane_b, 1 - column, kept_row], from_second_b.at[c], column_peer),
            ]
        if stage == 3:
            given = part.at[own, column, 2 * row + 1 - high]
            return [send(c, 5, given, from_line.at[c], cross_peer)]
        if stage == 4:
            block = results.at[pair, both, own, column, 2 * row + high]
            return [
                send(
                    c,
                    5 + step,
                    block,
                    block,
                    {"dp": 2 * lax.rem(plane + step, planes) + column},
                )
                for step in range(1, planes)
            ]
        if stage == 5:
            block_a = results.at[:, both, lane_a, column, kept_row]
            block_b = results.at[:, both, lane_b, column, kept_row]
            return [
                send(c, 9, block_a, block_a, row_peer),
                send(c, 10, block_b, block_b, column_peer),
            ]
        if stage == 6:
            block_a = results.at[:, both, lane_a, column]
            block_b = results.at[:, both, lane_b, :, kept_row]
            return [
                send(c, 11, block_a, block_a, column_peer),
                send(c, 12, block_b, block_b, row_peer),
            ]
        block = results.at[:, both, own]
        return [send(c, 13, block, block, core_peer)]

    def stage_of(c, stage):
        if stage > 0:
            for copy in copies_of(c, stage - 1):
                copy.wait()
        if stage == 1:
            grads[c, own] = grads[c, own] + from_core[lax.rem(c, RING)]
        if stage == 2:
            grads[c, lane_a, column] = grads[c, lane_a, column] + from_first_a[c]
            grads[c, lane_b, :, kept_row] = grads[c, lane_b, :, kept_row] + from_first_b[c]
        if stage == 3:
            grads[c, lane_a, column, kept_row] = grads[c, lane_a, column, kept_row] + from_second_a[c]
            grads[c, lane_b, column, kept_row] = grads[c, lane_b, column, kept_row] + from_second_b[c]
        if stage == 4:
            mine = 2 * row + high
            grads[c, own, column, mine] = grads[c, own, column, mine] + from_line[c]
            for unit in range(PAIR):
                results[pair, PAIR * c + unit, own, column, mine] = grads[
                    c, own, column, mine, 8 * unit : 8 * unit + 8
                ]
        if stage < len(LAGS) - 1:
            for copy in copies_of(c, stage):
                copy.start()

    per_weight = units // PAIR

    def slot(at):
        if not reduce_here:
            return
        for stage, lag in enumerate(LAGS):
            entry = at - lag
            if isinstance(at, int):
                c = entry if entry < per_weight else max(entry - GAP, per_weight - 1)
                if 0 <= entry < chunks + GAP and (c == entry or entry >= per_weight + GAP):
                    stage_of(c, stage)
                continue
            second = entry >= per_weight + GAP

            @pl.when(
                ((entry >= 0) & (entry < per_weight)) | (second & (entry < chunks + GAP))
            )
            def _():
                stage_of(entry - GAP * second.astype(jnp.int32), stage)

    def slot_after(at, count, steps_with, first_slot):
        if isinstance(at, int):
            for number, step in enumerate(steps_with):
                if at <= step < at + count:
                    slot(first_slot + number)
            return
        start, end = first_slot, first_slot
        for step in steps_with:
            start = start + (at > step).astype(jnp.int32)
            end = end + (at + count > step).astype(jnp.int32)

        def one(number, carry):
            slot(number)
            return carry

        lax.fori_loop(start, end, one, 0)

    def swap(at, source, target):
        return pltpu.make_async_remote_copy(
            src_ref=source,
            dst_ref=target,
            send_sem=swap_send.at[at],
            recv_sem=swap_recv.at[at],
            device_id=pair_peer,
            device_id_type=MESH,
        )

    def swap_in_place(at, source):
        return swap(at, source, swap_in.at[at])

    cuts = (0, rows // 4, rows // 2, rows)
    swap_cotangent = [
        swap(
            6 + at,
            swap_out.at[0, pl.ds(cuts[at], cuts[at + 1] - cuts[at])],
            swap_in.at[4, pl.ds(cuts[at], cuts[at + 1] - cuts[at])],
        )
        for at in range(3)
    ]

    places = nb_rows[...]
    codes = jnp.where(places < BLOCK, places, jnp.where(places < rows, BLOCK - 1 - places, 4 * BLOCK))
    side[...] = jnp.zeros_like(side)
    side[:offsets, :] = codes.astype(jnp.float32)
    side[offsets : offsets + down_offsets, :] = down_rows_ref[...].astype(jnp.float32)
    side_cols[...] = side[...].T
    nb_own[...] = jnp.full_like(nb_own, rows)
    nb_own[:offsets, :] = nb_rows[...]
    swap_neighbours = swap(4, nb_own, nb_pair)
    swap_out[0] = cotangent_ref[...].astype(jnp.float32)
    for weight in (w_mid, w_out):
        weight[offsets:] = jnp.zeros_like(weight[offsets:])

    spread_fine[...] = fine_ref[...].astype(jnp.float32)
    for k in range(down_offsets):
        child = spread_fine[pl.ds(k % children, rows, stride=children), :]
        there = side_cols[:, offsets + k : offsets + k + 1] < fine_rows
        cols_down[:, k * in_width : (k + 1) * in_width] = jnp.where(there, child, 0.0).astype(
            jnp.bfloat16
        )
    loads[0].wait()
    hid_one[...] = dot(cols_down[...], w_down[...].reshape(down_offsets * in_width, width))

    def spread_neighbours():
        for k in range(offsets):
            nb_cols[k] = jnp.broadcast_to(side_cols[:, k : k + 1], (rows, 128)).astype(jnp.bfloat16)

    pl.semaphore_wait(barrier, len(peers))

    swap_one, swap_two = swap_in_place(0, hid_one), swap_in_place(1, hid_two)
    swap_three, swap_incoming = swap_in_place(2, hid_three), swap_in_place(3, swap_out.at[1])

    def start(*swaps):
        def run():
            for each in swaps:
                each.start()

        return run if reduce_here else None

    beside = (spread_neighbours, start(swap_neighbours, swap_one, swap_cotangent[0]))
    center_one, scale_one, total = norm_stats(0, hid_one[...], beside)

    def pre_one(hidden=hid_one):
        normed = (hidden[...] - center_one) * scale_one
        return normed, normed * gain_ref[0:1, :] + bias_ref[0:1, :]

    _, pre = pre_one()
    act_one[...] = jnp.where(live, pre * sigmoid(pre), 0.0)
    act_one_b[...] = act_one[...].astype(jnp.bfloat16)
    loads[1].wait()
    convolve(act_one_b, w_mid, hid_two)
    center_two, scale_two, _ = norm_stats(
        1, hid_two[...], (None, start(swap_two, swap_cotangent[1]))
    )

    def pre_two(hidden=hid_two):
        normed = (hidden[...] - center_two) * scale_two
        return normed, normed * gain_ref[1:2, :] + bias_ref[1:2, :]

    _, pre = pre_two()
    act_two_b[...] = jnp.where(live, pre * sigmoid(pre), 0.0).astype(jnp.bfloat16)
    loads[2].wait()
    convolve(act_two_b, w_out, hid_three)
    center_three, scale_three, _ = norm_stats(
        2, hid_three[...], (None, start(swap_cotangent[2]))
    )
    normed_three = (hid_three[...] - center_three) * scale_three
    summed = (
        jnp.where(live, normed_three * gain_ref[2:3, :] + bias_ref[2:3, :], 0.0) + act_one[...]
    )
    sigma = sigmoid(summed)
    features_ref[...] = jnp.where(live, summed * sigma, 0.0).astype(jnp.bfloat16)

    slope = sigma * (1.0 + summed * (1.0 - sigma))
    act_one[...] = jnp.where(live, cotangent_ref[...].astype(jnp.float32) * slope, 0.0)
    grad_hidden[...], grad_three = norm_grad(
        3, 2, act_one[...], normed_three, scale_three, total, (start(swap_three), None)
    )
    held[...] = grad_hidden[...]
    grad_act[...] = jnp.zeros_like(grad_act)
    steps = units // PAIR

    def pair_out():
        for each in (swap_neighbours, swap_one, swap_two, swap_three, *swap_cotangent):
            each.wait()
        _, pre = pre_two(swap_in.at[1])
        pair_source_t[...] = (pre * sigmoid(pre)).astype(jnp.bfloat16).T
        _, pre = pre_one(swap_in.at[0])
        normed = (swap_in[2] - center_three) * scale_three
        summed = normed * gain_ref[2:3, :] + bias_ref[2:3, :] + pre * sigmoid(pre)
        held[...] = grad_three(swap_in[4] * silu_slope(summed), normed).astype(jnp.bfloat16)

    def pair_mid():
        _, pre = pre_one(swap_in.at[0])
        pair_source_t[...] = (pre * sigmoid(pre)).astype(jnp.bfloat16).T
        normed, _ = pre_two(swap_in.at[1])
        swap_incoming.wait()
        held[...] = grad_two(swap_in[3], normed).astype(jnp.bfloat16)

    def pair_halves(first_unit, at_slot):
        middle = (steps + 1) // 2
        return (
            lambda: convolve_pair(first_unit, 0, middle, at_slot),
            lambda: convolve_pair(first_unit, middle, steps, at_slot),
        )

    nothing = (None, None)
    source_t[...] = act_two_b[...].T
    convolve_back(w_out, grad_act, 0, no_slot, no_slot)
    normed, pre = pre_two()
    incoming = jnp.where(live, grad_act[...] * silu_slope(pre), 0.0)
    if reduce_here:
        swap_out[1] = incoming
        pair_out()
    after = lambda at, count: slot_after(at, count, (1, 3, 4, 4, 5, 6), 0)
    beside = (start(swap_incoming), *pair_halves(0, after)) if reduce_here else nothing
    grad_hidden[...], grad_two = norm_grad(4, 1, incoming, normed, scale_two, total, beside)
    held[...] = grad_hidden[...]
    grad_act[...] = act_one[...]
    source_t[...] = act_one_b[...].T
    convolve_back(
        w_mid,
        grad_act,
        units,
        lambda at, count: slot_after(at, count, (0, 5), 6),
        lambda at, count: slot_after(at, count, (1, 3), 8),
    )
    normed, pre = pre_one()
    incoming = jnp.where(live, grad_act[...] * silu_slope(pre), 0.0)
    if reduce_here:
        pair_mid()
    after = lambda at, count: slot_after(at, count, (0, 3, 6, 6), 10)
    beside = pair_halves(units, after) if reduce_here else nothing
    grad_hidden[...], _ = norm_grad(5, 0, incoming, normed, scale_one, total, beside)
    down_rows = down_offsets * in_width
    if reduce_here:
        down_all[...] = dot(cols_down[...].T, grad_hidden[...])
        kept = down_rows // 2
        swap_down = swap(
            5, down_all.at[pl.ds(pl.multiple_of(kept * (1 - pair), kept), kept), :], down_got
        )
        swap_down.start()
    else:
        grads[2 * units * width :, :] = dot(cols_down[...].T, grad_hidden[...])
    for child in range(children):
        total_child = jnp.zeros((rows, in_width), jnp.float32)
        for k in range(child, down_offsets, children):
            there = side_cols[:, offsets + k : offsets + k + 1] < fine_rows
            total_child += jnp.where(there, dot_last(grad_hidden[...], w_down[k]), 0.0)
        spread_fine[pl.ds(child, rows, stride=children), :] = total_child
    fine_grad_ref[...] = spread_fine[...].astype(jnp.bfloat16)

    if reduce_here:

        def rest(at, carry):
            slot(at)
            return carry

        lax.fori_loop(14, chunks - 1 + GAP, rest, 0)
        swap_down.wait()
        for part in range(PAIR):
            total_down = (
                down_all[pl.ds(pl.multiple_of(kept * pair + part * width, width), width), :]
                + down_got[part * width : (part + 1) * width, :]
            )
            grads[chunks - 1, :, :, :, 8 * part : 8 * part + 8] = total_down.reshape(
                grads.shape[1:4] + (8, width)
            )
        lax.fori_loop(chunks - 1 + GAP, chunks + GAP + LAGS[-1], rest, 0)
    else:
        store = pltpu.make_async_copy(grads, results, load_sem.at[0])
        store.start()
        store.wait()


def place_kernel(
    features_ref,
    fine_grad_ref,
    grads_ref,
    gain_ref,
    bias_ref,
    features_out,
    fine_grad_out,
    grad_down_out,
    grad_mid_out,
    grad_out_out,
    gain_out,
    bias_out,
    sem,
):
    offsets = grad_mid_out.shape[0]
    units = (offsets + 1) // 2
    piece = (units + 1) // 2
    moves = []
    for pair in range(2):
        for at, target in enumerate((grad_out_out, grad_mid_out)):
            for first in range(0, units, piece):
                count = min(piece, offsets - units * pair - first, units - first)
                here = grads_ref.at[pair, pl.ds(at * units + first, count)]
                moves.append((here, target.at[pl.ds(units * pair + first, count)]))
        down_units = grad_down_out.shape[0] // 2
        here = grads_ref.at[pair, pl.ds(2 * units, down_units)]
        moves.append((here, grad_down_out.at[pl.ds(pair * down_units, down_units)]))
    copies = [
        pltpu.make_async_copy(source, target, sem.at[at])
        for at, (source, target) in enumerate(moves)
    ]
    for copy in copies:
        copy.start()
    features_out[...] = features_ref[...]
    fine_grad_out[...] = fine_grad_ref[...]
    gain_out[...] = gain_ref[...]
    bias_out[...] = bias_ref[...]
    for copy in copies:
        copy.wait()


def per_device(
    dp_size,
    group_size,
    fine_features,
    down_map,
    neighbours,
    voxel_counts,
    down_weight,
    mid_weight,
    out_weight,
    norm_gain,
    norm_bias,
    cotangent,
):
    rows, width = cotangent.shape
    fine_rows, in_width = fine_features.shape
    offsets = neighbours.shape[1]
    down_offsets = down_map.shape[1]
    f32, bf16, i32 = jnp.float32, jnp.bfloat16, jnp.int32
    vmem = pl.BlockSpec(memory_space=pltpu.VMEM)
    hbm = pl.BlockSpec(memory_space=pl.ANY)
    shape = jax.ShapeDtypeStruct
    reduce_here = dp_size == 8 and group_size == 4
    result = pltpu.VMEM if reduce_here else shape
    near_size, far_size = (dp_size * group_size, 1) if reduce_here else (group_size, dp_size)
    share = 2 if reduce_here else 1
    units = (offsets + 1) // 2 * 2 // share
    all_units = 2 * units + down_offsets * in_width // (share * width)
    grad_rows = all_units * width
    chunks = all_units // PAIR
    padded = (offsets + 1) // 2 * 2
    features, fine_grad, grads, gain_grad, bias_grad = pl.pallas_call(
        functools.partial(kernel, dp_size, group_size, reduce_here),
        out_shape=(
            result((rows, width), bf16),
            result((fine_rows, in_width), bf16),
            pltpu.VMEM((2, all_units, *GROUPS, 8, width), f32)
            if reduce_here
            else shape((grad_rows, width), f32),
            result(norm_gain.shape, f32),
            result(norm_bias.shape, f32),
        ),
        in_specs=[vmem, vmem, vmem, vmem, hbm, hbm, hbm, vmem, vmem, vmem],
        out_specs=(vmem, vmem, vmem if reduce_here else hbm, vmem, vmem),
        scratch_shapes=[
            pltpu.VMEM(down_weight.shape, bf16),
            pltpu.VMEM((padded, width, width), bf16),
            pltpu.VMEM((padded, width, width), bf16),
            pltpu.VMEM((fine_rows, in_width), f32),
            pltpu.VMEM((rows, down_offsets * in_width), bf16),
            pltpu.VMEM((offsets, rows, 128), bf16),
            pltpu.VMEM((2, GROUP * rows, rows), bf16),
            pltpu.VMEM((2, rows, GROUP * width), bf16),
            pltpu.VMEM((BLOCK, 2 * width), bf16),
            pltpu.VMEM((rows, width), f32),
            pltpu.VMEM((rows, width), bf16),
            pltpu.VMEM((rows, width), bf16),
            pltpu.VMEM((rows, width), f32),
            pltpu.VMEM((rows, width), f32),
            pltpu.VMEM((rows, width), f32),
            pltpu.VMEM((rows, width), bf16),
            pltpu.VMEM((rows, width), bf16),
            pltpu.VMEM((width, rows), bf16),
            pltpu.VMEM((width, rows), bf16),
            pltpu.VMEM((rows, width), f32),
            pltpu.VMEM((128, rows), f32),
            pltpu.VMEM((rows, 128), f32),
            pltpu.VMEM((padded, rows), i32),
            pltpu.VMEM((padded, rows), i32),
            pltpu.VMEM((2, rows, width), f32),
            pltpu.VMEM((5, rows, width), f32),
            pltpu.VMEM((down_offsets * in_width, width), f32),
            pltpu.VMEM((down_offsets * in_width // 2, width), f32),
            pltpu.VMEM(
                (chunks, *GROUPS, 8 * PAIR, width) if reduce_here else (grad_rows, width), f32
            ),
            pltpu.VMEM((RING, 2, *GROUPS[1:], 8 * PAIR, width), f32),
            pltpu.VMEM((chunks, GROUPS[2], 8 * PAIR, width), f32),
            pltpu.VMEM((chunks, GROUPS[1], 2, 8 * PAIR, width), f32),
            pltpu.VMEM((chunks, 2, 8 * PAIR, width), f32),
            pltpu.VMEM((chunks, 2, 8 * PAIR, width), f32),
            pltpu.VMEM((chunks, 2, 8 * PAIR, width), f32),
            pltpu.VMEM((6, near_size, 8, width // 2), f32),
            pltpu.VMEM((6, far_size, 8, width // 2), f32),
            pltpu.SemaphoreType.DMA((3,)),
            pltpu.SemaphoreType.DMA((RING, COPIES)),
            pltpu.SemaphoreType.DMA((RING, COPIES)),
            pltpu.SemaphoreType.DMA((9,)),
            pltpu.SemaphoreType.DMA((9,)),
            pltpu.SemaphoreType.DMA((6, group_size - 1)),
            pltpu.SemaphoreType.DMA((6, group_size - 1)),
            pltpu.SemaphoreType.DMA((6, far_size)),
            pltpu.SemaphoreType.DMA((6, far_size)),
        ],
        compiler_params=pltpu.CompilerParams(
            collective_id=0, has_side_effects=True, vmem_limit_bytes=(46 if reduce_here else 60) * 1024 * 1024
        ),
    )(
        fine_features,
        down_map.T,
        neighbours.T,
        voxel_counts.reshape(1, 1),
        down_weight,
        mid_weight,
        out_weight,
        norm_gain,
        norm_bias,
        cotangent,
    )
    if not reduce_here:
        grads = lax.psum(grads, ("dp", "group"))
        middle, end = offsets * width, 2 * padded * width
        grad_out = grads[:middle].reshape(out_weight.shape)
        grad_mid = grads[padded * width : padded * width + middle].reshape(mid_weight.shape)
        grad_down = grads[end:].reshape(down_weight.shape)
        return (features, fine_grad, grad_down, grad_mid, grad_out, gain_grad, bias_grad)
    held = [
        pltpu.with_memory_space_constraint(value, pltpu.VMEM)
        for value in (features, fine_grad, grads, gain_grad, bias_grad)
    ]
    features, fine_grad, grad_down, grad_mid, grad_out, gain_grad, bias_grad = pl.pallas_call(
        place_kernel,
        out_shape=(
            shape(features.shape, bf16),
            shape(fine_grad.shape, bf16),
            shape((down_offsets * in_width // width, *GROUPS, 8, width), f32),
            shape((offsets, *GROUPS, 8, width), f32),
            shape((offsets, *GROUPS, 8, width), f32),
            shape(norm_gain.shape, f32),
            shape(norm_bias.shape, f32),
        ),
        in_specs=[vmem] * 5,
        out_specs=(vmem, vmem, hbm, hbm, hbm, vmem, vmem),
        scratch_shapes=[pltpu.SemaphoreType.DMA((10,))],
        compiler_params=pltpu.CompilerParams(vmem_limit_bytes=8 * 1024 * 1024),
    )(*held)
    grad_down = grad_down.reshape(down_weight.shape)
    grad_mid = grad_mid.reshape(mid_weight.shape)
    grad_out = grad_out.reshape(out_weight.shape)
    return (features, fine_grad, grad_down, grad_mid, grad_out, gain_grad, bias_grad)


def solution(mesh):
    in_specs = (
        P(("dp", "group"), None),
        P(("dp", "group"), None),
        P(("dp", "group"), None),
        P(("dp", "group")),
        P(),
        P(),
        P(),
        P(),
        P(),
        P(("dp", "group"), None),
    )
    out_specs = (P(("dp", "group"), None), P(("dp", "group"), None), P(), P(), P(), P(), P())
    return jax.shard_map(
        functools.partial(per_device, mesh.shape["dp"], mesh.shape["group"]),
        mesh=mesh,
        in_specs=in_specs,
        out_specs=out_specs,
        check_vma=False,
    )
```

```python
import functools

import jax
import jax.numpy as jnp
from jax import lax
from jax.experimental import pallas as pl
from jax.experimental.pallas import tpu as pltpu
from jax.sharding import PartitionSpec as P

eps_norm = 1e-05
MESH = pl.DeviceIdType.MESH
GROUP = 3
BLOCK = 256
PAIR = 2
COPIES = 14
GROUPS = (4, 2, 4)
GAP = 3
LAGS = (0, 1, 2, 3, 5, 7, 8, 11, 12)
RING = 8


def sigmoid(value):
    return 1.0 / (1.0 + jnp.exp(-value))


def silu_slope(value):
    sigma = sigmoid(value)
    return sigma * (1.0 + value * (1.0 - sigma))


def dot(left, right):
    return jnp.dot(left, right, preferred_element_type=jnp.float32)


def dot_last(left, right):
    return lax.dot_general(
        left, right, (((1,), (1,)), ((), ())), preferred_element_type=jnp.float32
    )


def kernel(
    dp_size,
    group_size,
    reduce_here,
    fine_ref,
    down_rows_ref,
    nb_rows,
    count_ref,
    down_hbm,
    mid_hbm,
    out_hbm,
    gain_ref,
    bias_ref,
    cotangent_ref,
    features_ref,
    fine_grad_ref,
    results,
    gain_grad_ref,
    bias_grad_ref,
    w_down,
    w_mid,
    w_out,
    spread_fine,
    cols_down,
    nb_cols,
    pickers,
    columns,
    side_by_side,
    act_one,
    act_one_b,
    act_two_b,
    hid_one,
    hid_two,
    hid_three,
    held,
    grad_hidden,
    source_t,
    pair_source_t,
    grad_act,
    side,
    side_cols,
    nb_own,
    nb_pair,
    swap_out,
    swap_in,
    down_all,
    down_got,
    grads,
    from_core,
    from_first_a,
    from_first_b,
    from_second_a,
    from_second_b,
    from_line,
    near,
    far,
    load_sem,
    sum_send,
    sum_recv,
    swap_send,
    swap_recv,
    near_send,
    near_recv,
    far_send,
    far_recv,
):
    rows, width = cotangent_ref.shape
    offsets = nb_rows.shape[0]
    fine_rows, in_width = fine_ref.shape
    children = fine_rows // rows
    down_offsets = down_rows_ref.shape[0]
    units = (offsets + 1) // 2 * (1 if reduce_here else 2)
    chunks = grads.shape[0]
    dp_me = lax.axis_index("dp")
    group_me = lax.axis_index("group")

    loads = [
        pltpu.make_async_copy(source, target, load_sem.at[at])
        for at, (source, target) in enumerate(
            (
                (down_hbm, w_down),
                (mid_hbm, w_mid.at[pl.ds(0, offsets)]),
                (out_hbm, w_out.at[pl.ds(0, offsets)]),
            )
        )
    ]
    for load in loads:
        load.start()

    direct = reduce_here
    peers = [
        {
            "dp": lax.rem(dp_me + dp_step, dp_size),
            "group": lax.rem(group_me + group_step, group_size),
        }
        for dp_step in reversed(range(dp_size))
        for group_step in reversed(range(group_size))
        if (dp_step or group_step) and (direct or not dp_step or not group_step)
    ]
    barrier = pltpu.get_barrier_semaphore()
    for peer in peers:
        pl.semaphore_signal(barrier, inc=1, device_id=peer, device_id_type=MESH)

    def share(at, axis, me, size, slots, send, recv):
        copies = []
        for step in range(1, size):
            copies.append(
                pltpu.make_async_remote_copy(
                    src_ref=slots.at[at, me],
                    dst_ref=slots.at[at, me],
                    send_sem=send.at[at, step - 1],
                    recv_sem=recv.at[at, step - 1],
                    device_id={axis: lax.rem(me + step, size)},
                    device_id_type=MESH,
                )
            )
        for copy in copies:
            copy.start()
        return copies

    def exchange_direct(at, block, combine, meanwhile):
        me = dp_me * group_size + group_me
        near[at, me] = block
        for peer in peers:
            pltpu.make_async_remote_copy(
                src_ref=near.at[at, me],
                dst_ref=near.at[at, me],
                send_sem=near_send.at[at, 0],
                recv_sem=near_recv.at[at, 0],
                device_id=peer,
                device_id_type=MESH,
            ).start()
        for work in meanwhile:
            if work is not None:
                work()
        others = near.at[at, pl.ds(0, len(peers))]
        for sem in (near_recv, near_send):
            pltpu.make_async_copy(others, others, sem.at[at, 0]).wait()
        return combine([near[at, slot] for slot in range(len(peers) + 1)])

    def exchange(at, block, combine, meanwhile=(None, None)):
        if direct:
            return exchange_direct(at, block, combine, meanwhile)
        near[at, group_me] = block
        copies = share(at, "group", group_me, group_size, near, near_send, near_recv)
        if meanwhile[0] is not None:
            meanwhile[0]()
        for copy in copies:
            copy.wait()
        far[at, dp_me] = combine([near[at, slot] for slot in range(group_size)])
        copies = share(at, "dp", dp_me, dp_size, far, far_send, far_recv)
        if meanwhile[1] is not None:
            meanwhile[1]()
        for copy in copies:
            copy.wait()
        return combine([far[at, slot] for slot in range(dp_size)])

    lanes = width // 2

    def stack(first, second, third):
        filler = jnp.zeros((2, lanes), jnp.float32)
        return jnp.concatenate([first, second, third, filler], axis=0)

    def fold(value):
        return jnp.concatenate([value[:, :lanes], value[:, lanes:]], axis=0)

    def unfold(value):
        return jnp.concatenate([value[0:1], value[1:2]], axis=1)

    def add_all(blocks):
        total = blocks[0]
        for block in blocks[1:]:
            total = total + block
        return total

    def merge_all(blocks):
        count = add_all([block[4:6] for block in blocks])
        center = add_all([block[4:6] * block[0:2] for block in blocks]) / count
        squares = add_all(
            [
                block[2:4] + block[4:6] * (block[0:2] - center) * (block[0:2] - center)
                for block in blocks
            ]
        )
        return stack(center, squares, count)

    count = count_ref[...]
    own_count = jnp.broadcast_to(count.astype(jnp.float32), (1, width))
    live = lax.broadcasted_iota(jnp.int32, (rows, width), 0) < count

    def norm_stats(at, hidden, meanwhile=(None, None)):
        center = jnp.sum(hidden, axis=0, keepdims=True) / own_count
        centered = jnp.where(live, hidden - center, 0.0)
        squares = jnp.sum(centered * centered, axis=0, keepdims=True)
        merged = exchange(
            at, stack(fold(center), fold(squares), fold(own_count)), merge_all, meanwhile
        )
        total = unfold(merged[4:6])
        scale = lax.rsqrt(unfold(merged[2:4]) / total + eps_norm)
        return unfold(merged[0:2]), scale, total

    def norm_grad(at, norm, incoming, normed, scale, total, meanwhile=(None, None)):
        shift_sum = fold(jnp.sum(incoming, axis=0, keepdims=True))
        scale_sum = fold(jnp.sum(incoming * normed, axis=0, keepdims=True))
        summed = exchange(
            at, stack(shift_sum, scale_sum, jnp.zeros_like(shift_sum)), add_all, meanwhile
        )
        shift_sum, scale_sum = unfold(summed[0:2]), unfold(summed[2:4])
        bias_grad_ref[norm : norm + 1, :] = shift_sum
        gain_grad_ref[norm : norm + 1, :] = scale_sum
        hidden_grad = (
            scale
            * gain_ref[norm : norm + 1, :]
            * (incoming - shift_sum / total - normed * (scale_sum / total))
        )
        return jnp.where(live, hidden_grad, 0.0).astype(jnp.bfloat16)

    def pick(mask):
        return jnp.where(mask, jnp.bfloat16(1), jnp.bfloat16(0))

    def counting(shape, axis):
        return lax.broadcasted_iota(jnp.int32, shape, axis).astype(jnp.float32).astype(jnp.bfloat16)

    def place_spread(turn, step):
        picked = dot(pickers[turn, : PAIR * rows, :], held[...]).astype(jnp.bfloat16)
        for part in range(PAIR):
            columns[turn, :, part * width : (part + 1) * width] = picked[
                part * rows : (part + 1) * rows
            ]

    def run_steps(first, last, build, place, use, after):
        build(first % 2, first)

        def one(turn, step, more):
            place(turn, step)
            if more:
                build(1 - turn, step + 1)
            use(turn, step)

        bodies = (last - first - 1) // 2

        def body(at, carry):
            for turn in range(2):
                one((first + turn) % 2, first + 2 * at + turn, True)
            after(first + 2 * at, 2)
            return carry

        lax.fori_loop(0, bodies, body, 0)
        for step in range(first + 2 * bodies, last):
            one(step % 2, step, step + 1 < last)
            after(step, 1)

    def convolve(source, weight, hidden):
        places = counting((rows, BLOCK), 1)
        hidden[...] = jnp.zeros_like(hidden)
        for block in range(2):
            side_by_side[:, block * width : (block + 1) * width] = source[
                block * BLOCK : (block + 1) * BLOCK, :
            ]

        def build(turn, step):
            for part in range(GROUP):
                code = nb_cols[step * GROUP + part]
                wanted = jnp.concatenate([jnp.maximum(code, -1 - code)] * (BLOCK // 128), axis=1)
                pickers[turn, part * rows : (part + 1) * rows, :BLOCK] = pick(wanted == places)

        def use(turn, step):
            weights = weight[pl.ds(step * GROUP, GROUP)].reshape(GROUP * width, width)
            hidden[...] += dot(columns[turn], weights)

        def place(turn, step):
            for part in range(GROUP):
                found = dot(
                    pickers[turn, part * rows : (part + 1) * rows, :BLOCK], side_by_side[...]
                )
                code = nb_cols[step * GROUP + part].astype(jnp.float32)
                second = jnp.concatenate([code] * (width // 128), axis=1) < 0
                columns[turn, :, part * width : (part + 1) * width] = jnp.where(
                    second, found[:, width:], found[:, :width]
                ).astype(jnp.bfloat16)

        run_steps(0, offsets // GROUP, build, place, use, no_slot)

    def build_spread(neighbours, offset_of):
        places = counting((BLOCK, rows), 0)

        def build(turn, step):
            for part in range(PAIR):
                wanted = neighbours[pl.ds(offset_of(PAIR * step + part), 1), :]
                wanted = wanted.astype(jnp.float32)
                for first in range(0, rows, BLOCK):
                    here = jnp.broadcast_to(wanted - first, (16, rows)).astype(jnp.bfloat16)
                    pickers[turn, part * rows + first : part * rows + first + BLOCK, :] = pick(
                        jnp.concatenate([here] * (BLOCK // 16), axis=0) == places
                    )

        return build

    def no_slot(at, count):
        pass

    def own_of(second):
        if not reduce_here:
            return lambda at: at
        extra = 14 * pair if second else 14 - 14 * pair
        return lambda at: 14 * pair + at + (extra - 14 * pair) * (jnp.int32(at) == 13)

    def put(second, at, product, more):
        for part in range(PAIR):
            value = product[:, part * width : (part + 1) * width]
            if not reduce_here:
                unit = pl.multiple_of((units * second + PAIR * at + part) * width, width)
                grads[pl.ds(unit, width), :] = value
                continue
            c, half = at, part
            if second:
                c, half = units // PAIR - 1 + at + part, 1 - part
            if isinstance(at, int) and PAIR * at + part == units - 1:
                empty = pair if second else 1 - pair
                c, half = chunks - 2 + empty, empty
            value = value.reshape(grads.shape[1:4] + (8, width))
            here_rows = pl.ds(8 * half, 8)
            if more:
                value = value + grads[c, :, :, :, here_rows]
            grads[c, :, :, :, here_rows] = value

    def convolve_back(weight, act_grad, second, own_slot, other_slot):
        def use_of(offset_of, weigh):
            def use(turn, step):
                spread = columns[turn, :, : PAIR * width]
                weights = jnp.concatenate(
                    [weight[offset_of(PAIR * step + part)] for part in range(PAIR)], axis=1
                )
                act_grad[...] += dot_last(spread, weights)
                if weigh:
                    put(second, step, dot(source_t[...], spread), False)

            return use

        steps = units // PAIR
        offset_of = own_of(second)
        build = build_spread(nb_own, offset_of)
        run_steps(0, steps, build, place_spread, use_of(offset_of, True), own_slot)
        if reduce_here:
            if second:
                offset_of = lambda at: 14 - 14 * pair + at
            else:
                offset_of = lambda at: 13 - 13 * pair + at + 14 * pair * (jnp.int32(at) == 13)
            build = build_spread(nb_own, offset_of)
            run_steps(0, steps, build, place_spread, use_of(offset_of, False), other_slot)

    def convolve_pair(second, first_step, last_step, at_slot):
        def use(turn, step):
            spread = columns[turn, :, : PAIR * width]
            put(second, step, dot(pair_source_t[...], spread), True)

        build = build_spread(nb_pair, own_of(second))
        run_steps(first_step, last_step, build, place_spread, use, at_slot)

    core, row = lax.rem(group_me, 2), group_me // 2
    column, plane = lax.rem(dp_me, 2), dp_me // 2
    pair, high = lax.rem(plane, 2), plane // 2
    planes = 4
    core_peer = {"group": group_me + 1 - 2 * core}
    row_peer = {"group": group_me + 2 - 4 * row}
    column_peer = {"dp": dp_me + 1 - 2 * column}
    pair_peer = {"dp": dp_me + 2 - 4 * pair}
    cross_peer = {"dp": dp_me + 4 - 8 * high}
    own = pl.ds(2 * core, 2)
    lane_a, lane_b = 2 * core, 2 * core + 1
    kept_row, given_row = pl.ds(2 * row, 2), pl.ds(2 * (1 - row), 2)

    def send(c, number, source, target, peer):
        turn = lax.rem(c, RING)
        return pltpu.make_async_remote_copy(
            src_ref=source,
            dst_ref=target,
            send_sem=sum_send.at[turn, number],
            recv_sem=sum_recv.at[turn, number],
            device_id=peer,
            device_id_type=MESH,
        )

    def copies_of(c, stage, size):
        both, some = pl.ds(PAIR * c, size), pl.ds(0, 8 * size)
        part = grads.at[c, :, :, :, some]

        def landing(ref, at):
            return ref.at[(at, *[slice(None)] * (len(ref.shape) - 3), some)]

        if stage == 0:
            given = part.at[pl.ds(2 * (1 - core), 2)]
            return [send(c, 0, given, landing(from_core, lax.rem(c, RING)), core_peer)]
        if stage == 1:
            return [
                send(c, 1, part.at[lane_a, 1 - column], landing(from_first_a, c), column_peer),
                send(c, 2, part.at[lane_b, :, given_row], landing(from_first_b, c), row_peer),
            ]
        if stage == 2:
            return [
                send(c, 3, part.at[lane_a, column, given_row], landing(from_second_a, c), row_peer),
                send(c, 4, part.at[lane_b, 1 - column, kept_row], landing(from_second_b, c), column_peer),
            ]
        if stage == 3:
            given = part.at[own, column, 2 * row + 1 - high]
            return [send(c, 5, given, landing(from_line, c), cross_peer)]
        if stage == 4:
            block = results.at[pair, both, own, column, 2 * row + high]
            return [
                send(
                    c,
                    5 + step,
                    block,
                    block,
                    {"dp": 2 * lax.rem(plane + step, planes) + column},
                )
                for step in range(1, planes)
            ]
        if stage == 5:
            block_a = results.at[:, both, lane_a, column, kept_row]
            block_b = results.at[:, both, lane_b, column, kept_row]
            return [
                send(c, 9, block_a, block_a, row_peer),
                send(c, 10, block_b, block_b, column_peer),
            ]
        if stage == 6:
            block_a = results.at[:, both, lane_a, column]
            block_b = results.at[:, both, lane_b, :, kept_row]
            return [
                send(c, 11, block_a, block_a, column_peer),
                send(c, 12, block_b, block_b, row_peer),
            ]
        block = results.at[:, both, own]
        return [send(c, 13, block, block, core_peer)]

    def stage_of(c, stage, size=PAIR):
        if stage > 0:
            for copy in copies_of(c, stage - 1, size):
                copy.wait()
        some = slice(0, 8 * size)

        def add(lanes, columns_of, rows_of, landed):
            here_rows = (c, lanes, columns_of, rows_of, some)
            grads[here_rows] = grads[here_rows] + landed

        every = slice(None)
        if stage == 1:
            add(own, every, every, from_core[lax.rem(c, RING), :, :, :, some])
        if stage == 2:
            add(lane_a, column, every, from_first_a[c, :, some])
            add(lane_b, every, kept_row, from_first_b[c, :, :, some])
        if stage == 3:
            add(lane_a, column, kept_row, from_second_a[c, :, some])
            add(lane_b, column, kept_row, from_second_b[c, :, some])
        if stage == 4:
            mine = 2 * row + high
            add(own, column, mine, from_line[c, :, some])
            for unit in range(size):
                results[pair, PAIR * c + unit, own, column, mine] = grads[
                    c, own, column, mine, 8 * unit : 8 * unit + 8
                ]
        if stage < len(LAGS) - 1:
            for copy in copies_of(c, stage, size):
                copy.start()

    early = units // PAIR - 1

    def slot(at, last=False):
        if not reduce_here:
            return
        for stage, lag in enumerate(LAGS):
            entry = at - lag
            if isinstance(at, int):
                c = entry if entry < early else max(entry - GAP, early - 1)
                if 0 <= entry < chunks - 1 + GAP and (c == entry or entry >= early + GAP):
                    stage_of(c, stage)
                continue
            second = entry >= early + GAP

            @pl.when(
                ((entry >= 0) & (entry < early)) | (second & (entry < chunks - 1 + GAP))
            )
            def _():
                stage_of(entry - GAP * second.astype(jnp.int32), stage)

            if last:

                @pl.when(entry == chunks - 1 + GAP)
                def _():
                    stage_of(chunks - 1, stage, 1)

    def slot_after(at, count, steps_with, first_slot):
        if isinstance(at, int):
            for number, step in enumerate(steps_with):
                if at <= step < at + count:
                    slot(first_slot + number)
            return
        start, end = first_slot, first_slot
        for step in steps_with:
            start = start + (at > step).astype(jnp.int32)
            end = end + (at + count > step).astype(jnp.int32)

        def one(number, carry):
            slot(number)
            return carry

        lax.fori_loop(start, end, one, 0)

    def swap(at, source, target):
        return pltpu.make_async_remote_copy(
            src_ref=source,
            dst_ref=target,
            send_sem=swap_send.at[at],
            recv_sem=swap_recv.at[at],
            device_id=pair_peer,
            device_id_type=MESH,
        )

    def swap_rows(at):
        return swap(at, swap_out.at[at % 2], swap_in.at[at])

    def start_rows(at, value):
        if reduce_here:
            swap_out[at % 2] = value.astype(jnp.float32)
            swap_rows(at).start()

    places = nb_rows[...]
    codes = jnp.where(places < BLOCK, places, jnp.where(places < rows, BLOCK - 1 - places, 4 * BLOCK))
    side[...] = jnp.zeros_like(side)
    side[:offsets, :] = codes.astype(jnp.float32)
    side[offsets : offsets + down_offsets, :] = down_rows_ref[...].astype(jnp.float32)
    side_cols[...] = side[...].T
    nb_own[...] = jnp.full_like(nb_own, rows)
    nb_own[:offsets, :] = nb_rows[...]
    swap_neighbours = swap(4, nb_own, nb_pair)
    for weight in (w_mid, w_out):
        weight[offsets:] = jnp.zeros_like(weight[offsets:])

    spread_fine[...] = fine_ref[...].astype(jnp.float32)
    for k in range(down_offsets):
        child = spread_fine[pl.ds(k % children, rows, stride=children), :]
        there = side_cols[:, offsets + k : offsets + k + 1] < fine_rows
        cols_down[:, k * in_width : (k + 1) * in_width] = jnp.where(there, child, 0.0).astype(
            jnp.bfloat16
        )
    loads[0].wait()
    hid_one[...] = dot(cols_down[...], w_down[...].reshape(down_offsets * in_width, width))

    def spread_neighbours():
        for k in range(offsets):
            nb_cols[k] = jnp.broadcast_to(side_cols[:, k : k + 1], (rows, 128)).astype(jnp.bfloat16)

    pl.semaphore_wait(barrier, len(peers))

    swap_one = swap(0, hid_one, swap_in.at[0])
    swap_two = swap(1, hid_two, swap_in.at[1])

    def start_one():
        swap_neighbours.start()
        swap_one.start()

    def start_two():
        swap_two.start()

    beside = (spread_neighbours, start_one if reduce_here else None)
    center_one, scale_one, total = norm_stats(0, hid_one[...], beside)

    def pre_one(hidden=hid_one):
        normed = (hidden[...] - center_one) * scale_one
        return normed, normed * gain_ref[0:1, :] + bias_ref[0:1, :]

    _, pre = pre_one()
    act_one[...] = jnp.where(live, pre * sigmoid(pre), 0.0)
    act_one_b[...] = act_one[...].astype(jnp.bfloat16)
    loads[1].wait()
    convolve(act_one_b, w_mid, hid_two)
    center_two, scale_two, _ = norm_stats(
        1, hid_two[...], (None, start_two if reduce_here else None)
    )

    def pre_two(hidden=hid_two):
        normed = (hidden[...] - center_two) * scale_two
        return normed, normed * gain_ref[1:2, :] + bias_ref[1:2, :]

    _, pre = pre_two()
    act_two_b[...] = jnp.where(live, pre * sigmoid(pre), 0.0).astype(jnp.bfloat16)
    loads[2].wait()
    convolve(act_two_b, w_out, hid_three)
    def turn_two():
        source_t[...] = act_two_b[...].T

    center_three, scale_three, _ = norm_stats(2, hid_three[...], (turn_two, None))
    normed_three = (hid_three[...] - center_three) * scale_three
    summed = (
        jnp.where(live, normed_three * gain_ref[2:3, :] + bias_ref[2:3, :], 0.0) + act_one[...]
    )
    sigma = sigmoid(summed)
    features_ref[...] = jnp.where(live, summed * sigma, 0.0).astype(jnp.bfloat16)

    def pair_source(swapped, pre_of, source_at):
        swapped.wait()
        _, pre = pre_of(swap_in.at[source_at])
        pair_source_t[...] = (pre * sigmoid(pre)).astype(jnp.bfloat16).T

    def pair_two():
        if reduce_here:
            pair_source(swap_two, pre_two, 1)

    slope = sigma * (1.0 + summed * (1.0 - sigma))
    act_one[...] = jnp.where(live, cotangent_ref[...].astype(jnp.float32) * slope, 0.0)
    grad_hidden[...] = norm_grad(
        3, 2, act_one[...], normed_three, scale_three, total, (pair_two, None)
    )
    start_rows(2, grad_hidden[...])
    held[...] = grad_hidden[...]
    grad_act[...] = jnp.zeros_like(grad_act)
    steps = units // PAIR

    def receive(hidden_at):
        swap_rows(hidden_at).wait()
        held[...] = swap_in[hidden_at].astype(jnp.bfloat16)

    def pair_halves(second, at_slot):
        middle = (steps + 1) // 2
        return (
            lambda: convolve_pair(second, 0, middle, at_slot),
            lambda: convolve_pair(second, middle, steps, at_slot),
        )

    nothing = (None, None)
    convolve_back(w_out, grad_act, 0, no_slot, no_slot)
    normed, pre = pre_two()
    incoming = jnp.where(live, grad_act[...] * silu_slope(pre), 0.0)
    if reduce_here:
        swap_neighbours.wait()
        receive(2)
    after = lambda at, count: slot_after(at, count, (1, 3, 4, 6), 0)
    beside = pair_halves(0, after) if reduce_here else nothing
    grad_hidden[...] = norm_grad(4, 1, incoming, normed, scale_two, total, beside)
    start_rows(3, grad_hidden[...])
    held[...] = grad_hidden[...]
    grad_act[...] = act_one[...]
    source_t[...] = act_one_b[...].T
    convolve_back(
        w_mid,
        grad_act,
        1,
        lambda at, count: slot_after(at, count, (0, 5), 4),
        lambda at, count: slot_after(at, count, (1, 3, 5), 6),
    )
    normed, pre = pre_one()
    incoming = jnp.where(live, grad_act[...] * silu_slope(pre), 0.0)
    if reduce_here:
        pair_source(swap_one, pre_one, 0)
        receive(3)
    after = lambda at, count: slot_after(at, count, (0, 3, 5, 6), 9)
    beside = pair_halves(1, after) if reduce_here else nothing
    grad_hidden[...] = norm_grad(5, 0, incoming, normed, scale_one, total, beside)
    down_rows = down_offsets * in_width
    if reduce_here:
        down_all[...] = dot(cols_down[...].T, grad_hidden[...])
        kept = down_rows // 2
        swap_down = swap(
            5, down_all.at[pl.ds(pl.multiple_of(kept * (1 - pair), kept), kept), :], down_got
        )
        swap_down.start()
    else:
        grads[2 * units * width :, :] = dot(cols_down[...].T, grad_hidden[...])
    for child in range(children):
        total_child = jnp.zeros((rows, in_width), jnp.float32)
        for k in range(child, down_offsets, children):
            there = side_cols[:, offsets + k : offsets + k + 1] < fine_rows
            total_child += jnp.where(there, dot_last(grad_hidden[...], w_down[k]), 0.0)
        spread_fine[pl.ds(child, rows, stride=children), :] = total_child
    fine_grad_ref[...] = spread_fine[...].astype(jnp.bfloat16)

    if reduce_here:

        def rest(at, carry):
            slot(at)
            return carry

        def final(at, carry):
            slot(at, True)
            return carry

        lax.fori_loop(13, chunks - 2 + GAP, rest, 0)
        swap_down.wait()
        for part in range(PAIR):
            total_down = (
                down_all[pl.ds(pl.multiple_of(kept * pair + part * width, width), width), :]
                + down_got[part * width : (part + 1) * width, :]
            )
            half = 1 - part
            grads[chunks - 2 + part, :, :, :, 8 * half : 8 * half + 8] = total_down.reshape(
                grads.shape[1:4] + (8, width)
            )
        lax.fori_loop(chunks - 2 + GAP, chunks + GAP + LAGS[-1], final, 0)
    else:
        store = pltpu.make_async_copy(grads, results, load_sem.at[0])
        store.start()
        store.wait()


def place_kernel(
    features_ref,
    fine_grad_ref,
    grads_ref,
    gain_ref,
    bias_ref,
    features_out,
    fine_grad_out,
    grad_down_out,
    grad_mid_out,
    grad_out_out,
    gain_out,
    bias_out,
    sem,
):
    half = grad_mid_out.shape[0] // 2
    moves = []
    for at, target in enumerate((grad_out_out, grad_mid_out)):
        for pair in range(2):
            for first in range(0, half, 3):
                count = min(3, half - first)
                here = grads_ref.at[pair, pl.ds(at * half + first, count)]
                moves.append((here, target.at[pl.ds((half + 1) * pair + first, count)]))
        moves.append((grads_ref.at[1 - at, pl.ds(2 * half, 1)], target.at[pl.ds(half, 1)]))
    for pair in range(2):
        down_units = grad_down_out.shape[0] // 2
        here = grads_ref.at[pair, pl.ds(2 * half + 1, down_units)]
        moves.append((here, grad_down_out.at[pl.ds(pair * down_units, down_units)]))
    copies = [
        pltpu.make_async_copy(source, target, sem.at[at])
        for at, (source, target) in enumerate(moves)
    ]
    for copy in copies:
        copy.start()
    features_out[...] = features_ref[...]
    fine_grad_out[...] = fine_grad_ref[...]
    gain_out[...] = gain_ref[...]
    bias_out[...] = bias_ref[...]
    for copy in copies:
        copy.wait()


def per_device(
    dp_size,
    group_size,
    fine_features,
    down_map,
    neighbours,
    voxel_counts,
    down_weight,
    mid_weight,
    out_weight,
    norm_gain,
    norm_bias,
    cotangent,
):
    rows, width = cotangent.shape
    fine_rows, in_width = fine_features.shape
    offsets = neighbours.shape[1]
    down_offsets = down_map.shape[1]
    f32, bf16, i32 = jnp.float32, jnp.bfloat16, jnp.int32
    vmem = pl.BlockSpec(memory_space=pltpu.VMEM)
    hbm = pl.BlockSpec(memory_space=pl.ANY)
    shape = jax.ShapeDtypeStruct
    reduce_here = dp_size == 8 and group_size == 4
    result = pltpu.VMEM if reduce_here else shape
    near_size, far_size = (dp_size * group_size, 1) if reduce_here else (group_size, dp_size)
    share = 2 if reduce_here else 1
    units = (offsets + 1) // 2 * 2 // share
    all_units = 2 * units + down_offsets * in_width // (share * width)
    grad_rows = all_units * width
    chunks = all_units // PAIR
    padded = (offsets + 1) // 2 * 2
    features, fine_grad, grads, gain_grad, bias_grad = pl.pallas_call(
        functools.partial(kernel, dp_size, group_size, reduce_here),
        out_shape=(
            result((rows, width), bf16),
            result((fine_rows, in_width), bf16),
            pltpu.VMEM((2, all_units, *GROUPS, 8, width), f32)
            if reduce_here
            else shape((grad_rows, width), f32),
            result(norm_gain.shape, f32),
            result(norm_bias.shape, f32),
        ),
        in_specs=[vmem, vmem, vmem, vmem, hbm, hbm, hbm, vmem, vmem, vmem],
        out_specs=(vmem, vmem, vmem if reduce_here else hbm, vmem, vmem),
        scratch_shapes=[
            pltpu.VMEM(down_weight.shape, bf16),
            pltpu.VMEM((padded, width, width), bf16),
            pltpu.VMEM((padded, width, width), bf16),
            pltpu.VMEM((fine_rows, in_width), f32),
            pltpu.VMEM((rows, down_offsets * in_width), bf16),
            pltpu.VMEM((offsets, rows, 128), bf16),
            pltpu.VMEM((2, GROUP * rows, rows), bf16),
            pltpu.VMEM((2, rows, GROUP * width), bf16),
            pltpu.VMEM((BLOCK, 2 * width), bf16),
            pltpu.VMEM((rows, width), f32),
            pltpu.VMEM((rows, width), bf16),
            pltpu.VMEM((rows, width), bf16),
            pltpu.VMEM((rows, width), f32),
            pltpu.VMEM((rows, width), f32),
            pltpu.VMEM((rows, width), f32),
            pltpu.VMEM((rows, width), bf16),
            pltpu.VMEM((rows, width), bf16),
            pltpu.VMEM((width, rows), bf16),
            pltpu.VMEM((width, rows), bf16),
            pltpu.VMEM((rows, width), f32),
            pltpu.VMEM((128, rows), f32),
            pltpu.VMEM((rows, 128), f32),
            pltpu.VMEM((padded, rows), i32),
            pltpu.VMEM((padded, rows), i32),
            pltpu.VMEM((2, rows, width), f32),
            pltpu.VMEM((4, rows, width), f32),
            pltpu.VMEM((down_offsets * in_width, width), f32),
            pltpu.VMEM((down_offsets * in_width // 2, width), f32),
            pltpu.VMEM(
                (chunks, *GROUPS, 8 * PAIR, width) if reduce_here else (grad_rows, width), f32
            ),
            pltpu.VMEM((RING, 2, *GROUPS[1:], 8 * PAIR, width), f32),
            pltpu.VMEM((chunks, GROUPS[2], 8 * PAIR, width), f32),
            pltpu.VMEM((chunks, GROUPS[1], 2, 8 * PAIR, width), f32),
            pltpu.VMEM((chunks, 2, 8 * PAIR, width), f32),
            pltpu.VMEM((chunks, 2, 8 * PAIR, width), f32),
            pltpu.VMEM((chunks, 2, 8 * PAIR, width), f32),
            pltpu.VMEM((6, near_size, 8, width // 2), f32),
            pltpu.VMEM((6, far_size, 8, width // 2), f32),
            pltpu.SemaphoreType.DMA((3,)),
            pltpu.SemaphoreType.DMA((RING, COPIES)),
            pltpu.SemaphoreType.DMA((RING, COPIES)),
            pltpu.SemaphoreType.DMA((6,)),
            pltpu.SemaphoreType.DMA((6,)),
            pltpu.SemaphoreType.DMA((6, group_size - 1)),
            pltpu.SemaphoreType.DMA((6, group_size - 1)),
            pltpu.SemaphoreType.DMA((6, far_size)),
            pltpu.SemaphoreType.DMA((6, far_size)),
        ],
        compiler_params=pltpu.CompilerParams(
            collective_id=0, has_side_effects=True, vmem_limit_bytes=(46 if reduce_here else 60) * 1024 * 1024
        ),
    )(
        fine_features,
        down_map.T,
        neighbours.T,
        voxel_counts.reshape(1, 1),
        down_weight,
        mid_weight,
        out_weight,
        norm_gain,
        norm_bias,
        cotangent,
    )
    if not reduce_here:
        grads = lax.psum(grads, ("dp", "group"))
        middle, end = offsets * width, 2 * padded * width
        grad_out = grads[:middle].reshape(out_weight.shape)
        grad_mid = grads[padded * width : padded * width + middle].reshape(mid_weight.shape)
        grad_down = grads[end:].reshape(down_weight.shape)
        return (features, fine_grad, grad_down, grad_mid, grad_out, gain_grad, bias_grad)
    held = [
        pltpu.with_memory_space_constraint(value, pltpu.VMEM)
        for value in (features, fine_grad, grads, gain_grad, bias_grad)
    ]
    features, fine_grad, grad_down, grad_mid, grad_out, gain_grad, bias_grad = pl.pallas_call(
        place_kernel,
        out_shape=(
            shape(features.shape, bf16),
            shape(fine_grad.shape, bf16),
            shape((down_offsets * in_width // width, *GROUPS, 8, width), f32),
            shape((offsets, *GROUPS, 8, width), f32),
            shape((offsets, *GROUPS, 8, width), f32),
            shape(norm_gain.shape, f32),
            shape(norm_bias.shape, f32),
        ),
        in_specs=[vmem] * 5,
        out_specs=(vmem, vmem, hbm, hbm, hbm, vmem, vmem),
        scratch_shapes=[pltpu.SemaphoreType.DMA((24,))],
        compiler_params=pltpu.CompilerParams(vmem_limit_bytes=8 * 1024 * 1024),
    )(*held)
    grad_down = grad_down.reshape(down_weight.shape)
    grad_mid = grad_mid.reshape(mid_weight.shape)
    grad_out = grad_out.reshape(out_weight.shape)
    return (features, fine_grad, grad_down, grad_mid, grad_out, gain_grad, bias_grad)


def solution(mesh):
    in_specs = (
        P(("dp", "group"), None),
        P(("dp", "group"), None),
        P(("dp", "group"), None),
        P(("dp", "group")),
        P(),
        P(),
        P(),
        P(),
        P(),
        P(("dp", "group"), None),
    )
    out_specs = (P(("dp", "group"), None), P(("dp", "group"), None), P(), P(), P(), P(), P())
    return jax.shard_map(
        functools.partial(per_device, mesh.shape["dp"], mesh.shape["group"]),
        mesh=mesh,
        in_specs=in_specs,
        out_specs=out_specs,
        check_vma=False,
    )
```

```python
import functools

import jax
import jax.numpy as jnp
from jax import lax
from jax.experimental import pallas as pl
from jax.experimental.pallas import tpu as pltpu
from jax.sharding import PartitionSpec as P

eps_norm = 1e-05
MESH = pl.DeviceIdType.MESH
GROUP = 3
BLOCK = 256
PAIR = 2
COPIES = 14
GROUPS = (4, 2, 4)
GAP = 1
LAGS = (0, 1, 2, 3, 5, 7, 8, 10, 11)
RING = 8


def sigmoid(value):
    return 1.0 / (1.0 + jnp.exp(-value))


def silu_slope(value):
    sigma = sigmoid(value)
    return sigma * (1.0 + value * (1.0 - sigma))


def dot(left, right):
    return jnp.dot(left, right, preferred_element_type=jnp.float32)


def dot_last(left, right):
    return lax.dot_general(
        left, right, (((1,), (1,)), ((), ())), preferred_element_type=jnp.float32
    )


def kernel(
    dp_size,
    group_size,
    reduce_here,
    fine_ref,
    down_rows_ref,
    nb_rows,
    count_ref,
    down_hbm,
    mid_hbm,
    out_hbm,
    gain_ref,
    bias_ref,
    cotangent_ref,
    features_ref,
    fine_grad_ref,
    results,
    gain_grad_ref,
    bias_grad_ref,
    w_down,
    w_mid,
    w_out,
    spread_fine,
    cols_down,
    nb_cols,
    pickers,
    columns,
    side_by_side,
    act_one,
    act_one_b,
    act_two_b,
    hid_one,
    hid_two,
    hid_three,
    held,
    grad_hidden,
    source_t,
    pair_source_t,
    grad_act,
    side,
    side_cols,
    nb_own,
    nb_pair,
    swap_out,
    swap_in,
    down_all,
    down_got,
    grads,
    from_core,
    from_first_a,
    from_first_b,
    from_second_a,
    from_second_b,
    from_line,
    near,
    far,
    load_sem,
    sum_send,
    sum_recv,
    swap_send,
    swap_recv,
    near_send,
    near_recv,
    far_send,
    far_recv,
):
    rows, width = cotangent_ref.shape
    offsets = nb_rows.shape[0]
    fine_rows, in_width = fine_ref.shape
    children = fine_rows // rows
    down_offsets = down_rows_ref.shape[0]
    units = (offsets + 1) // 2 * (1 if reduce_here else 2)
    chunks = grads.shape[0]
    dp_me = lax.axis_index("dp")
    group_me = lax.axis_index("group")

    loads = [
        pltpu.make_async_copy(source, target, load_sem.at[at])
        for at, (source, target) in enumerate(
            (
                (down_hbm, w_down),
                (mid_hbm, w_mid.at[pl.ds(0, offsets)]),
                (out_hbm, w_out.at[pl.ds(0, offsets)]),
            )
        )
    ]
    for load in loads:
        load.start()

    direct = reduce_here
    peers = [
        {
            "dp": lax.rem(dp_me + dp_step, dp_size),
            "group": lax.rem(group_me + group_step, group_size),
        }
        for dp_step in reversed(range(dp_size))
        for group_step in reversed(range(group_size))
        if (dp_step or group_step) and (direct or not dp_step or not group_step)
    ]
    barrier = pltpu.get_barrier_semaphore()
    for peer in peers:
        pl.semaphore_signal(barrier, inc=1, device_id=peer, device_id_type=MESH)

    def share(at, axis, me, size, slots, send, recv):
        copies = []
        for step in range(1, size):
            copies.append(
                pltpu.make_async_remote_copy(
                    src_ref=slots.at[at, me],
                    dst_ref=slots.at[at, me],
                    send_sem=send.at[at, step - 1],
                    recv_sem=recv.at[at, step - 1],
                    device_id={axis: lax.rem(me + step, size)},
                    device_id_type=MESH,
                )
            )
        for copy in copies:
            copy.start()
        return copies

    def exchange_direct(at, block, combine, meanwhile):
        me = dp_me * group_size + group_me
        near[at, me] = block
        for peer in peers:
            pltpu.make_async_remote_copy(
                src_ref=near.at[at, me],
                dst_ref=near.at[at, me],
                send_sem=near_send.at[at, 0],
                recv_sem=near_recv.at[at, 0],
                device_id=peer,
                device_id_type=MESH,
            ).start()
        for work in meanwhile:
            if work is not None:
                work()
        others = near.at[at, pl.ds(0, len(peers))]
        for sem in (near_recv, near_send):
            pltpu.make_async_copy(others, others, sem.at[at, 0]).wait()
        return combine([near[at, slot] for slot in range(len(peers) + 1)])

    def exchange(at, block, combine, meanwhile=(None, None)):
        if direct:
            return exchange_direct(at, block, combine, meanwhile)
        near[at, group_me] = block
        copies = share(at, "group", group_me, group_size, near, near_send, near_recv)
        if meanwhile[0] is not None:
            meanwhile[0]()
        for copy in copies:
            copy.wait()
        far[at, dp_me] = combine([near[at, slot] for slot in range(group_size)])
        copies = share(at, "dp", dp_me, dp_size, far, far_send, far_recv)
        if meanwhile[1] is not None:
            meanwhile[1]()
        for copy in copies:
            copy.wait()
        return combine([far[at, slot] for slot in range(dp_size)])

    lanes = width // 2

    def stack(first, second, third):
        filler = jnp.zeros((2, lanes), jnp.float32)
        return jnp.concatenate([first, second, third, filler], axis=0)

    def fold(value):
        return jnp.concatenate([value[:, :lanes], value[:, lanes:]], axis=0)

    def unfold(value):
        return jnp.concatenate([value[0:1], value[1:2]], axis=1)

    def add_all(blocks):
        total = blocks[0]
        for block in blocks[1:]:
            total = total + block
        return total

    def merge_all(blocks):
        count = add_all([block[4:6] for block in blocks])
        center = add_all([block[4:6] * block[0:2] for block in blocks]) / count
        squares = add_all(
            [
                block[2:4] + block[4:6] * (block[0:2] - center) * (block[0:2] - center)
                for block in blocks
            ]
        )
        return stack(center, squares, count)

    count = count_ref[...]
    own_count = jnp.broadcast_to(count.astype(jnp.float32), (1, width))
    live = lax.broadcasted_iota(jnp.int32, (rows, width), 0) < count

    def norm_stats(at, hidden, meanwhile=(None, None)):
        center = jnp.sum(hidden, axis=0, keepdims=True) / own_count
        centered = jnp.where(live, hidden - center, 0.0)
        squares = jnp.sum(centered * centered, axis=0, keepdims=True)
        merged = exchange(
            at, stack(fold(center), fold(squares), fold(own_count)), merge_all, meanwhile
        )
        total = unfold(merged[4:6])
        scale = lax.rsqrt(unfold(merged[2:4]) / total + eps_norm)
        return unfold(merged[0:2]), scale, total

    def norm_grad(at, norm, incoming, normed, scale, total, meanwhile=(None, None)):
        shift_sum = fold(jnp.sum(incoming, axis=0, keepdims=True))
        scale_sum = fold(jnp.sum(incoming * normed, axis=0, keepdims=True))
        summed = exchange(
            at, stack(shift_sum, scale_sum, jnp.zeros_like(shift_sum)), add_all, meanwhile
        )
        shift_sum, scale_sum = unfold(summed[0:2]), unfold(summed[2:4])
        bias_grad_ref[norm : norm + 1, :] = shift_sum
        gain_grad_ref[norm : norm + 1, :] = scale_sum
        hidden_grad = (
            scale
            * gain_ref[norm : norm + 1, :]
            * (incoming - shift_sum / total - normed * (scale_sum / total))
        )
        return jnp.where(live, hidden_grad, 0.0).astype(jnp.bfloat16)

    def pick(mask):
        return jnp.where(mask, jnp.bfloat16(1), jnp.bfloat16(0))

    def counting(shape, axis):
        return lax.broadcasted_iota(jnp.int32, shape, axis).astype(jnp.float32).astype(jnp.bfloat16)

    def place_spread(turn, step):
        picked = dot(pickers[turn, : PAIR * rows, :], held[...]).astype(jnp.bfloat16)
        for part in range(PAIR):
            columns[turn, :, part * width : (part + 1) * width] = picked[
                part * rows : (part + 1) * rows
            ]

    def run_steps(first, last, build, place, use, after):
        build(first % 2, first)

        def one(turn, step, more):
            place(turn, step)
            if more:
                build(1 - turn, step + 1)
            use(turn, step)

        bodies = (last - first - 1) // 2

        def body(at, carry):
            for turn in range(2):
                one((first + turn) % 2, first + 2 * at + turn, True)
            after(first + 2 * at, 2)
            return carry

        lax.fori_loop(0, bodies, body, 0)
        for step in range(first + 2 * bodies, last):
            one(step % 2, step, step + 1 < last)
            after(step, 1)

    def convolve(source, weight, hidden):
        places = counting((rows, BLOCK), 1)
        hidden[...] = jnp.zeros_like(hidden)
        for block in range(2):
            side_by_side[:, block * width : (block + 1) * width] = source[
                block * BLOCK : (block + 1) * BLOCK, :
            ]

        def build(turn, step):
            for part in range(GROUP):
                code = nb_cols[step * GROUP + part]
                wanted = jnp.concatenate([jnp.maximum(code, -1 - code)] * (BLOCK // 128), axis=1)
                pickers[turn, part * rows : (part + 1) * rows, :BLOCK] = pick(wanted == places)

        def use(turn, step):
            weights = weight[pl.ds(step * GROUP, GROUP)].reshape(GROUP * width, width)
            hidden[...] += dot(columns[turn], weights)

        def place(turn, step):
            for part in range(GROUP):
                found = dot(
                    pickers[turn, part * rows : (part + 1) * rows, :BLOCK], side_by_side[...]
                )
                code = nb_cols[step * GROUP + part].astype(jnp.float32)
                second = jnp.concatenate([code] * (width // 128), axis=1) < 0
                columns[turn, :, part * width : (part + 1) * width] = jnp.where(
                    second, found[:, width:], found[:, :width]
                ).astype(jnp.bfloat16)

        run_steps(0, offsets // GROUP, build, place, use, no_slot)

    def build_spread(neighbours, offset_of):
        places = counting((BLOCK, rows), 0)

        def build(turn, step):
            for part in range(PAIR):
                wanted = neighbours[pl.ds(offset_of(PAIR * step + part), 1), :]
                wanted = wanted.astype(jnp.float32)
                for first in range(0, rows, BLOCK):
                    here = jnp.broadcast_to(wanted - first, (16, rows)).astype(jnp.bfloat16)
                    pickers[turn, part * rows + first : part * rows + first + BLOCK, :] = pick(
                        jnp.concatenate([here] * (BLOCK // 16), axis=0) == places
                    )

        return build

    def no_slot(at, count):
        pass

    def own_of(second):
        if not reduce_here:
            return lambda at: at
        extra = 14 * pair if second else 14 - 14 * pair
        return lambda at: 14 * pair + at + (extra - 14 * pair) * (jnp.int32(at) == 13)

    def put(second, at, product, more):
        for part in range(PAIR):
            value = product[:, part * width : (part + 1) * width]
            if not reduce_here:
                unit = pl.multiple_of((units * second + PAIR * at + part) * width, width)
                grads[pl.ds(unit, width), :] = value
                continue
            c, half = at, part
            if second:
                c, half = units // PAIR - 1 + at + part, 1 - part
            if isinstance(at, int) and PAIR * at + part == units - 1:
                empty = pair if second else 1 - pair
                c, half = chunks - 2 + empty, empty
            value = value.reshape(grads.shape[1:4] + (8, width))
            here_rows = pl.ds(8 * half, 8)
            if more:
                value = value + grads[c, :, :, :, here_rows]
            grads[c, :, :, :, here_rows] = value

    def convolve_back(weight, act_grad, second, own_slot, other_slot):
        def use_of(offset_of, weigh):
            def use(turn, step):
                spread = columns[turn, :, : PAIR * width]
                weights = jnp.concatenate(
                    [weight[offset_of(PAIR * step + part)] for part in range(PAIR)], axis=1
                )
                act_grad[...] += dot_last(spread, weights)
                if weigh:
                    put(second, step, dot(source_t[...], spread), False)

            return use

        steps = units // PAIR
        offset_of = own_of(second)
        build = build_spread(nb_own, offset_of)
        run_steps(0, steps, build, place_spread, use_of(offset_of, True), own_slot)
        if reduce_here:
            if second:
                offset_of = lambda at: 14 - 14 * pair + at
            else:
                offset_of = lambda at: 13 - 13 * pair + at + 14 * pair * (jnp.int32(at) == 13)
            build = build_spread(nb_own, offset_of)
            run_steps(0, steps, build, place_spread, use_of(offset_of, False), other_slot)

    def convolve_pair(second, first_step, last_step, at_slot):
        def use(turn, step):
            spread = columns[turn, :, : PAIR * width]
            put(second, step, dot(pair_source_t[...], spread), True)

        build = build_spread(nb_pair, own_of(second))
        run_steps(first_step, last_step, build, place_spread, use, at_slot)

    core, row = lax.rem(group_me, 2), group_me // 2
    column, plane = lax.rem(dp_me, 2), dp_me // 2
    pair, high = lax.rem(plane, 2), plane // 2
    planes = 4
    core_peer = {"group": group_me + 1 - 2 * core}
    row_peer = {"group": group_me + 2 - 4 * row}
    column_peer = {"dp": dp_me + 1 - 2 * column}
    pair_peer = {"dp": dp_me + 2 - 4 * pair}
    cross_peer = {"dp": dp_me + 4 - 8 * high}
    own = pl.ds(2 * core, 2)
    lane_a, lane_b = 2 * core, 2 * core + 1
    kept_row, given_row = pl.ds(2 * row, 2), pl.ds(2 * (1 - row), 2)

    def send(c, number, source, target, peer):
        turn = lax.rem(c, RING)
        return pltpu.make_async_remote_copy(
            src_ref=source,
            dst_ref=target,
            send_sem=sum_send.at[turn, number],
            recv_sem=sum_recv.at[turn, number],
            device_id=peer,
            device_id_type=MESH,
        )

    def copies_of(c, stage, size):
        both, some = pl.ds(PAIR * c, size), pl.ds(0, 8 * size)
        part = grads.at[c, :, :, :, some]

        def landing(ref, at):
            return ref.at[(at, *[slice(None)] * (len(ref.shape) - 3), some)]

        if stage == 0:
            given = part.at[pl.ds(2 * (1 - core), 2)]
            return [send(c, 0, given, landing(from_core, lax.rem(c, RING)), core_peer)]
        if stage == 1:
            return [
                send(c, 1, part.at[lane_a, 1 - column], landing(from_first_a, c), column_peer),
                send(c, 2, part.at[lane_b, :, given_row], landing(from_first_b, c), row_peer),
            ]
        if stage == 2:
            return [
                send(c, 3, part.at[lane_a, column, given_row], landing(from_second_a, c), row_peer),
                send(c, 4, part.at[lane_b, 1 - column, kept_row], landing(from_second_b, c), column_peer),
            ]
        if stage == 3:
            given = part.at[own, column, 2 * row + 1 - high]
            return [send(c, 5, given, landing(from_line, c), cross_peer)]
        if stage == 4:
            block = results.at[pair, both, own, column, 2 * row + high]
            return [
                send(
                    c,
                    5 + step,
                    block,
                    block,
                    {"dp": 2 * lax.rem(plane + step, planes) + column},
                )
                for step in range(1, planes)
            ]
        if stage == 5:
            block_a = results.at[:, both, lane_a, column, kept_row]
            block_b = results.at[:, both, lane_b, column, kept_row]
            return [
                send(c, 9, block_a, block_a, row_peer),
                send(c, 10, block_b, block_b, column_peer),
            ]
        if stage == 6:
            block_a = results.at[:, both, lane_a, column]
            block_b = results.at[:, both, lane_b, :, kept_row]
            return [
                send(c, 11, block_a, block_a, column_peer),
                send(c, 12, block_b, block_b, row_peer),
            ]
        block = results.at[:, both, own]
        return [send(c, 13, block, block, core_peer)]

    def stage_of(c, stage, size=PAIR):
        if stage > 0:
            for copy in copies_of(c, stage - 1, size):
                copy.wait()
        some = slice(0, 8 * size)

        def add(lanes, columns_of, rows_of, landed):
            here_rows = (c, lanes, columns_of, rows_of, some)
            grads[here_rows] = grads[here_rows] + landed

        every = slice(None)
        if stage == 1:
            add(own, every, every, from_core[lax.rem(c, RING), :, :, :, some])
        if stage == 2:
            add(lane_a, column, every, from_first_a[c, :, some])
            add(lane_b, every, kept_row, from_first_b[c, :, :, some])
        if stage == 3:
            add(lane_a, column, kept_row, from_second_a[c, :, some])
            add(lane_b, column, kept_row, from_second_b[c, :, some])
        if stage == 4:
            mine = 2 * row + high
            add(own, column, mine, from_line[c, :, some])
            for unit in range(size):
                results[pair, PAIR * c + unit, own, column, mine] = grads[
                    c, own, column, mine, 8 * unit : 8 * unit + 8
                ]
        if stage < len(LAGS) - 1:
            for copy in copies_of(c, stage, size):
                copy.start()

    early = units // PAIR - 1

    def slot(at, last=False):
        if not reduce_here:
            return
        for stage, lag in enumerate(LAGS):
            entry = at - lag
            if isinstance(at, int):
                c = entry if entry < early else max(entry - GAP, early - 1)
                if 0 <= entry < chunks - 1 + GAP and (c == entry or entry >= early + GAP):
                    stage_of(c, stage)
                continue
            second = entry >= early + GAP

            @pl.when(
                ((entry >= 0) & (entry < early)) | (second & (entry < chunks - 1 + GAP))
            )
            def _():
                stage_of(entry - GAP * second.astype(jnp.int32), stage)

            if last:

                @pl.when(entry == chunks - 1 + GAP)
                def _():
                    stage_of(chunks - 1, stage, 1)

    def slot_after(at, count, steps_with, first_slot):
        if isinstance(at, int):
            for number, step in enumerate(steps_with):
                if at <= step < at + count:
                    slot(first_slot + number)
            return
        start, end = first_slot, first_slot
        for step in steps_with:
            start = start + (at > step).astype(jnp.int32)
            end = end + (at + count > step).astype(jnp.int32)

        def one(number, carry):
            slot(number)
            return carry

        lax.fori_loop(start, end, one, 0)

    def swap(at, source, target):
        return pltpu.make_async_remote_copy(
            src_ref=source,
            dst_ref=target,
            send_sem=swap_send.at[at],
            recv_sem=swap_recv.at[at],
            device_id=pair_peer,
            device_id_type=MESH,
        )

    def swap_rows(at):
        return swap(at, swap_out.at[at % 2], swap_in.at[at])

    def start_rows(at, value):
        if reduce_here:
            swap_out[at % 2] = value.astype(jnp.float32)
            swap_rows(at).start()

    places = nb_rows[...]
    codes = jnp.where(places < BLOCK, places, jnp.where(places < rows, BLOCK - 1 - places, 4 * BLOCK))
    side[...] = jnp.zeros_like(side)
    side[:offsets, :] = codes.astype(jnp.float32)
    side[offsets : offsets + down_offsets, :] = down_rows_ref[...].astype(jnp.float32)
    side_cols[...] = side[...].T
    nb_own[...] = jnp.full_like(nb_own, rows)
    nb_own[:offsets, :] = nb_rows[...]
    swap_neighbours = swap(4, nb_own, nb_pair)
    for weight in (w_mid, w_out):
        weight[offsets:] = jnp.zeros_like(weight[offsets:])

    spread_fine[...] = fine_ref[...].astype(jnp.float32)
    for k in range(down_offsets):
        child = spread_fine[pl.ds(k % children, rows, stride=children), :]
        there = side_cols[:, offsets + k : offsets + k + 1] < fine_rows
        cols_down[:, k * in_width : (k + 1) * in_width] = jnp.where(there, child, 0.0).astype(
            jnp.bfloat16
        )
    loads[0].wait()
    hid_one[...] = dot(cols_down[...], w_down[...].reshape(down_offsets * in_width, width))

    def spread_neighbours():
        for k in range(offsets):
            nb_cols[k] = jnp.broadcast_to(side_cols[:, k : k + 1], (rows, 128)).astype(jnp.bfloat16)

    pl.semaphore_wait(barrier, len(peers))

    swap_one = swap(0, hid_one, swap_in.at[0])
    swap_two = swap(1, hid_two, swap_in.at[1])

    def start_one():
        swap_neighbours.start()
        swap_one.start()

    def start_two():
        swap_two.start()

    beside = (spread_neighbours, start_one if reduce_here else None)
    center_one, scale_one, total = norm_stats(0, hid_one[...], beside)

    def pre_one(hidden=hid_one):
        normed = (hidden[...] - center_one) * scale_one
        return normed, normed * gain_ref[0:1, :] + bias_ref[0:1, :]

    _, pre = pre_one()
    act_one[...] = jnp.where(live, pre * sigmoid(pre), 0.0)
    act_one_b[...] = act_one[...].astype(jnp.bfloat16)
    loads[1].wait()
    convolve(act_one_b, w_mid, hid_two)
    center_two, scale_two, _ = norm_stats(
        1, hid_two[...], (None, start_two if reduce_here else None)
    )

    def pre_two(hidden=hid_two):
        normed = (hidden[...] - center_two) * scale_two
        return normed, normed * gain_ref[1:2, :] + bias_ref[1:2, :]

    _, pre = pre_two()
    act_two_b[...] = jnp.where(live, pre * sigmoid(pre), 0.0).astype(jnp.bfloat16)
    loads[2].wait()
    convolve(act_two_b, w_out, hid_three)
    def turn_two():
        source_t[...] = act_two_b[...].T

    center_three, scale_three, _ = norm_stats(2, hid_three[...], (turn_two, None))
    normed_three = (hid_three[...] - center_three) * scale_three
    summed = (
        jnp.where(live, normed_three * gain_ref[2:3, :] + bias_ref[2:3, :], 0.0) + act_one[...]
    )
    sigma = sigmoid(summed)
    features_ref[...] = jnp.where(live, summed * sigma, 0.0).astype(jnp.bfloat16)

    def pair_source(swapped, pre_of, source_at):
        swapped.wait()
        _, pre = pre_of(swap_in.at[source_at])
        pair_source_t[...] = (pre * sigmoid(pre)).astype(jnp.bfloat16).T

    def pair_two():
        if reduce_here:
            pair_source(swap_two, pre_two, 1)

    slope = sigma * (1.0 + summed * (1.0 - sigma))
    act_one[...] = jnp.where(live, cotangent_ref[...].astype(jnp.float32) * slope, 0.0)
    grad_hidden[...] = norm_grad(
        3, 2, act_one[...], normed_three, scale_three, total, (pair_two, None)
    )
    start_rows(2, grad_hidden[...])
    held[...] = grad_hidden[...]
    grad_act[...] = jnp.zeros_like(grad_act)
    steps = units // PAIR

    def receive(hidden_at):
        swap_rows(hidden_at).wait()
        held[...] = swap_in[hidden_at].astype(jnp.bfloat16)

    def pair_halves(second, at_slot):
        middle = (steps + 1) // 2
        return (
            lambda: convolve_pair(second, 0, middle, at_slot),
            lambda: convolve_pair(second, middle, steps, at_slot),
        )

    nothing = (None, None)
    convolve_back(w_out, grad_act, 0, no_slot, no_slot)
    normed, pre = pre_two()
    incoming = jnp.where(live, grad_act[...] * silu_slope(pre), 0.0)
    if reduce_here:
        swap_neighbours.wait()
        receive(2)
    after = lambda at, count: slot_after(at, count, (0, 4), 0)
    beside = pair_halves(0, after) if reduce_here else nothing
    grad_hidden[...] = norm_grad(4, 1, incoming, normed, scale_two, total, beside)
    start_rows(3, grad_hidden[...])
    held[...] = grad_hidden[...]
    grad_act[...] = act_one[...]
    source_t[...] = act_one_b[...].T
    convolve_back(
        w_mid,
        grad_act,
        1,
        lambda at, count: slot_after(at, count, (0, 5), 2),
        lambda at, count: slot_after(at, count, (1, 3, 5), 4),
    )
    normed, pre = pre_one()
    incoming = jnp.where(live, grad_act[...] * silu_slope(pre), 0.0)
    if reduce_here:
        pair_source(swap_one, pre_one, 0)
        receive(3)
    after = lambda at, count: slot_after(at, count, (0, 1, 3, 5, 6), 7)
    beside = pair_halves(1, after) if reduce_here else nothing
    grad_hidden[...] = norm_grad(5, 0, incoming, normed, scale_one, total, beside)
    down_rows = down_offsets * in_width
    if reduce_here:
        down_all[...] = dot(cols_down[...].T, grad_hidden[...])
        kept = down_rows // 2
        swap_down = swap(
            5, down_all.at[pl.ds(pl.multiple_of(kept * (1 - pair), kept), kept), :], down_got
        )
        swap_down.start()
    else:
        grads[2 * units * width :, :] = dot(cols_down[...].T, grad_hidden[...])
    slot(12)
    for child in range(children):
        total_child = jnp.zeros((rows, in_width), jnp.float32)
        for k in range(child, down_offsets, children):
            there = side_cols[:, offsets + k : offsets + k + 1] < fine_rows
            total_child += jnp.where(there, dot_last(grad_hidden[...], w_down[k]), 0.0)
        spread_fine[pl.ds(child, rows, stride=children), :] = total_child
    fine_grad_ref[...] = spread_fine[...].astype(jnp.bfloat16)
    slot(13)

    if reduce_here:

        def final(at, carry):
            slot(at, True)
            return carry

        swap_down.wait()
        for part in range(PAIR):
            total_down = (
                down_all[pl.ds(pl.multiple_of(kept * pair + part * width, width), width), :]
                + down_got[part * width : (part + 1) * width, :]
            )
            half = 1 - part
            grads[chunks - 2 + part, :, :, :, 8 * half : 8 * half + 8] = total_down.reshape(
                grads.shape[1:4] + (8, width)
            )
        lax.fori_loop(chunks - 2 + GAP, chunks + GAP + LAGS[-1], final, 0)
    else:
        store = pltpu.make_async_copy(grads, results, load_sem.at[0])
        store.start()
        store.wait()


def place_kernel(
    features_ref,
    fine_grad_ref,
    grads_ref,
    gain_ref,
    bias_ref,
    features_out,
    fine_grad_out,
    grad_down_out,
    grad_mid_out,
    grad_out_out,
    gain_out,
    bias_out,
    sem,
):
    half = grad_mid_out.shape[0] // 2
    moves = []
    for at, target in enumerate((grad_out_out, grad_mid_out)):
        for pair in range(2):
            for first in range(0, half, 3):
                count = min(3, half - first)
                here = grads_ref.at[pair, pl.ds(at * half + first, count)]
                moves.append((here, target.at[pl.ds((half + 1) * pair + first, count)]))
        moves.append((grads_ref.at[1 - at, pl.ds(2 * half, 1)], target.at[pl.ds(half, 1)]))
    for pair in range(2):
        down_units = grad_down_out.shape[0] // 2
        here = grads_ref.at[pair, pl.ds(2 * half + 1, down_units)]
        moves.append((here, grad_down_out.at[pl.ds(pair * down_units, down_units)]))
    copies = [
        pltpu.make_async_copy(source, target, sem.at[at])
        for at, (source, target) in enumerate(moves)
    ]
    for copy in copies:
        copy.start()
    features_out[...] = features_ref[...]
    fine_grad_out[...] = fine_grad_ref[...]
    gain_out[...] = gain_ref[...]
    bias_out[...] = bias_ref[...]
    for copy in copies:
        copy.wait()


def per_device(
    dp_size,
    group_size,
    fine_features,
    down_map,
    neighbours,
    voxel_counts,
    down_weight,
    mid_weight,
    out_weight,
    norm_gain,
    norm_bias,
    cotangent,
):
    rows, width = cotangent.shape
    fine_rows, in_width = fine_features.shape
    offsets = neighbours.shape[1]
    down_offsets = down_map.shape[1]
    f32, bf16, i32 = jnp.float32, jnp.bfloat16, jnp.int32
    vmem = pl.BlockSpec(memory_space=pltpu.VMEM)
    hbm = pl.BlockSpec(memory_space=pl.ANY)
    shape = jax.ShapeDtypeStruct
    reduce_here = dp_size == 8 and group_size == 4
    result = pltpu.VMEM if reduce_here else shape
    near_size, far_size = (dp_size * group_size, 1) if reduce_here else (group_size, dp_size)
    share = 2 if reduce_here else 1
    units = (offsets + 1) // 2 * 2 // share
    all_units = 2 * units + down_offsets * in_width // (share * width)
    grad_rows = all_units * width
    chunks = all_units // PAIR
    padded = (offsets + 1) // 2 * 2
    features, fine_grad, grads, gain_grad, bias_grad = pl.pallas_call(
        functools.partial(kernel, dp_size, group_size, reduce_here),
        out_shape=(
            result((rows, width), bf16),
            result((fine_rows, in_width), bf16),
            pltpu.VMEM((2, all_units, *GROUPS, 8, width), f32)
            if reduce_here
            else shape((grad_rows, width), f32),
            result(norm_gain.shape, f32),
            result(norm_bias.shape, f32),
        ),
        in_specs=[vmem, vmem, vmem, vmem, hbm, hbm, hbm, vmem, vmem, vmem],
        out_specs=(vmem, vmem, vmem if reduce_here else hbm, vmem, vmem),
        scratch_shapes=[
            pltpu.VMEM(down_weight.shape, bf16),
            pltpu.VMEM((padded, width, width), bf16),
            pltpu.VMEM((padded, width, width), bf16),
            pltpu.VMEM((fine_rows, in_width), f32),
            pltpu.VMEM((rows, down_offsets * in_width), bf16),
            pltpu.VMEM((offsets, rows, 128), bf16),
            pltpu.VMEM((2, GROUP * rows, rows), bf16),
            pltpu.VMEM((2, rows, GROUP * width), bf16),
            pltpu.VMEM((BLOCK, 2 * width), bf16),
            pltpu.VMEM((rows, width), f32),
            pltpu.VMEM((rows, width), bf16),
            pltpu.VMEM((rows, width), bf16),
            pltpu.VMEM((rows, width), f32),
            pltpu.VMEM((rows, width), f32),
            pltpu.VMEM((rows, width), f32),
            pltpu.VMEM((rows, width), bf16),
            pltpu.VMEM((rows, width), bf16),
            pltpu.VMEM((width, rows), bf16),
            pltpu.VMEM((width, rows), bf16),
            pltpu.VMEM((rows, width), f32),
            pltpu.VMEM((128, rows), f32),
            pltpu.VMEM((rows, 128), f32),
            pltpu.VMEM((padded, rows), i32),
            pltpu.VMEM((padded, rows), i32),
            pltpu.VMEM((2, rows, width), f32),
            pltpu.VMEM((4, rows, width), f32),
            pltpu.VMEM((down_offsets * in_width, width), f32),
            pltpu.VMEM((down_offsets * in_width // 2, width), f32),
            pltpu.VMEM(
                (chunks, *GROUPS, 8 * PAIR, width) if reduce_here else (grad_rows, width), f32
            ),
            pltpu.VMEM((RING, 2, *GROUPS[1:], 8 * PAIR, width), f32),
            pltpu.VMEM((chunks, GROUPS[2], 8 * PAIR, width), f32),
            pltpu.VMEM((chunks, GROUPS[1], 2, 8 * PAIR, width), f32),
            pltpu.VMEM((chunks, 2, 8 * PAIR, width), f32),
            pltpu.VMEM((chunks, 2, 8 * PAIR, width), f32),
            pltpu.VMEM((chunks, 2, 8 * PAIR, width), f32),
            pltpu.VMEM((6, near_size, 8, width // 2), f32),
            pltpu.VMEM((6, far_size, 8, width // 2), f32),
            pltpu.SemaphoreType.DMA((3,)),
            pltpu.SemaphoreType.DMA((RING, COPIES)),
            pltpu.SemaphoreType.DMA((RING, COPIES)),
            pltpu.SemaphoreType.DMA((6,)),
            pltpu.SemaphoreType.DMA((6,)),
            pltpu.SemaphoreType.DMA((6, group_size - 1)),
            pltpu.SemaphoreType.DMA((6, group_size - 1)),
            pltpu.SemaphoreType.DMA((6, far_size)),
            pltpu.SemaphoreType.DMA((6, far_size)),
        ],
        compiler_params=pltpu.CompilerParams(
            collective_id=0, has_side_effects=True, vmem_limit_bytes=(46 if reduce_here else 60) * 1024 * 1024
        ),
    )(
        fine_features,
        down_map.T,
        neighbours.T,
        voxel_counts.reshape(1, 1),
        down_weight,
        mid_weight,
        out_weight,
        norm_gain,
        norm_bias,
        cotangent,
    )
    if not reduce_here:
        grads = lax.psum(grads, ("dp", "group"))
        middle, end = offsets * width, 2 * padded * width
        grad_out = grads[:middle].reshape(out_weight.shape)
        grad_mid = grads[padded * width : padded * width + middle].reshape(mid_weight.shape)
        grad_down = grads[end:].reshape(down_weight.shape)
        return (features, fine_grad, grad_down, grad_mid, grad_out, gain_grad, bias_grad)
    held = [
        pltpu.with_memory_space_constraint(value, pltpu.VMEM)
        for value in (features, fine_grad, grads, gain_grad, bias_grad)
    ]
    features, fine_grad, grad_down, grad_mid, grad_out, gain_grad, bias_grad = pl.pallas_call(
        place_kernel,
        out_shape=(
            shape(features.shape, bf16),
            shape(fine_grad.shape, bf16),
            shape((down_offsets * in_width // width, *GROUPS, 8, width), f32),
            shape((offsets, *GROUPS, 8, width), f32),
            shape((offsets, *GROUPS, 8, width), f32),
            shape(norm_gain.shape, f32),
            shape(norm_bias.shape, f32),
        ),
        in_specs=[vmem] * 5,
        out_specs=(vmem, vmem, hbm, hbm, hbm, vmem, vmem),
        scratch_shapes=[pltpu.SemaphoreType.DMA((24,))],
        compiler_params=pltpu.CompilerParams(vmem_limit_bytes=8 * 1024 * 1024),
    )(*held)
    grad_down = grad_down.reshape(down_weight.shape)
    grad_mid = grad_mid.reshape(mid_weight.shape)
    grad_out = grad_out.reshape(out_weight.shape)
    return (features, fine_grad, grad_down, grad_mid, grad_out, gain_grad, bias_grad)


def solution(mesh):
    in_specs = (
        P(("dp", "group"), None),
        P(("dp", "group"), None),
        P(("dp", "group"), None),
        P(("dp", "group")),
        P(),
        P(),
        P(),
        P(),
        P(),
        P(("dp", "group"), None),
    )
    out_specs = (P(("dp", "group"), None), P(("dp", "group"), None), P(), P(), P(), P(), P())
    return jax.shard_map(
        functools.partial(per_device, mesh.shape["dp"], mesh.shape["group"]),
        mesh=mesh,
        in_specs=in_specs,
        out_specs=out_specs,
        check_vma=False,
    )
```

```python
import functools

import jax
import jax.numpy as jnp
from jax import lax
from jax.experimental import pallas as pl
from jax.experimental.pallas import tpu as pltpu
from jax.sharding import PartitionSpec as P

eps_norm = 1e-05
MESH = pl.DeviceIdType.MESH
GROUP = 3
BLOCK = 256
PAIR = 2
GROUPS = (4, 2, 4)
GAP = 1
LAGS = (0, 1, 2, 3, 5, 7, 8, 10, 11)
RING = 16
CORE_RING = 8


def sigmoid(value):
    return 0.5 + 0.5 * jnp.tanh(0.5 * value)


def silu_slope(value):
    sigma = sigmoid(value)
    return sigma * (1.0 + value * (1.0 - sigma))


def dot(left, right):
    return jnp.dot(left, right, preferred_element_type=jnp.float32)


def dot_last(left, right):
    return lax.dot_general(
        left, right, (((1,), (1,)), ((), ())), preferred_element_type=jnp.float32
    )


def kernel(
    dp_size,
    group_size,
    reduce_here,
    fine_ref,
    down_rows_ref,
    nb_rows,
    count_ref,
    down_hbm,
    mid_hbm,
    out_hbm,
    gain_ref,
    bias_ref,
    cotangent_ref,
    features_ref,
    fine_grad_ref,
    results,
    gain_grad_ref,
    bias_grad_ref,
    w_down,
    w_mid,
    w_out,
    spread_fine,
    cols_down,
    nb_cols,
    pickers,
    columns,
    side_by_side,
    act_one,
    act_one_b,
    act_two_b,
    hid_one,
    hid_two,
    hid_three,
    held,
    grad_hidden,
    source_t,
    pair_source_t,
    grad_act,
    side,
    side_cols,
    nb_own,
    nb_pair,
    swap_out,
    swap_in,
    down_all,
    down_got,
    grads,
    from_core,
    from_first_a,
    from_first_b,
    from_second_a,
    from_second_b,
    from_line,
    near,
    far,
    load_sem,
    sum_send,
    sum_recv,
    swap_send,
    swap_recv,
    near_send,
    near_recv,
    far_send,
    far_recv,
):
    rows, width = cotangent_ref.shape
    offsets = nb_rows.shape[0]
    fine_rows, in_width = fine_ref.shape
    children = fine_rows // rows
    down_offsets = down_rows_ref.shape[0]
    units = (offsets + 1) // 2 * (1 if reduce_here else 2)
    chunks = grads.shape[0]
    dp_me = lax.axis_index("dp")
    group_me = lax.axis_index("group")

    loads = [
        pltpu.make_async_copy(source, target, load_sem.at[at])
        for at, (source, target) in enumerate(
            (
                (down_hbm, w_down),
                (mid_hbm, w_mid.at[pl.ds(0, offsets)]),
                (out_hbm, w_out.at[pl.ds(0, offsets)]),
            )
        )
    ]
    for load in loads:
        load.start()

    direct = reduce_here
    peers = [
        {
            "dp": lax.rem(dp_me + dp_step, dp_size),
            "group": lax.rem(group_me + group_step, group_size),
        }
        for dp_step in reversed(range(dp_size))
        for group_step in reversed(range(group_size))
        if (dp_step or group_step) and (direct or not dp_step or not group_step)
    ]
    barrier = pltpu.get_barrier_semaphore()
    for peer in peers:
        pl.semaphore_signal(barrier, inc=1, device_id=peer, device_id_type=MESH)

    def share(at, axis, me, size, slots, send, recv):
        copies = []
        for step in range(1, size):
            copies.append(
                pltpu.make_async_remote_copy(
                    src_ref=slots.at[at, me],
                    dst_ref=slots.at[at, me],
                    send_sem=send.at[at, step - 1],
                    recv_sem=recv.at[at, step - 1],
                    device_id={axis: lax.rem(me + step, size)},
                    device_id_type=MESH,
                )
            )
        for copy in copies:
            copy.start()
        return copies

    def exchange_direct(at, block, combine, meanwhile):
        me = dp_me * group_size + group_me
        near[at, me] = block
        for peer in peers:
            pltpu.make_async_remote_copy(
                src_ref=near.at[at, me],
                dst_ref=near.at[at, me],
                send_sem=near_send.at[at, 0],
                recv_sem=near_recv.at[at, 0],
                device_id=peer,
                device_id_type=MESH,
            ).start()
        for work in meanwhile:
            if work is not None:
                work()
        others = near.at[at, pl.ds(0, len(peers))]
        for sem in (near_recv, near_send):
            pltpu.make_async_copy(others, others, sem.at[at, 0]).wait()
        return combine([near[at, slot] for slot in range(len(peers) + 1)])

    def exchange(at, block, combine, meanwhile=(None, None)):
        if direct:
            return exchange_direct(at, block, combine, meanwhile)
        near[at, group_me] = block
        copies = share(at, "group", group_me, group_size, near, near_send, near_recv)
        if meanwhile[0] is not None:
            meanwhile[0]()
        for copy in copies:
            copy.wait()
        far[at, dp_me] = combine([near[at, slot] for slot in range(group_size)])
        copies = share(at, "dp", dp_me, dp_size, far, far_send, far_recv)
        if meanwhile[1] is not None:
            meanwhile[1]()
        for copy in copies:
            copy.wait()
        return combine([far[at, slot] for slot in range(dp_size)])

    lanes = width // 2

    def stack(first, second, third):
        filler = jnp.zeros((2, lanes), jnp.float32)
        return jnp.concatenate([first, second, third, filler], axis=0)

    def fold(value):
        return jnp.concatenate([value[:, :lanes], value[:, lanes:]], axis=0)

    def unfold(value):
        return jnp.concatenate([value[0:1], value[1:2]], axis=1)

    def add_all(blocks):
        total = blocks[0]
        for block in blocks[1:]:
            total = total + block
        return total

    def merge_all(blocks):
        count = add_all([block[4:6] for block in blocks])
        center = add_all([block[4:6] * block[0:2] for block in blocks]) / count
        squares = add_all(
            [
                block[2:4] + block[4:6] * (block[0:2] - center) * (block[0:2] - center)
                for block in blocks
            ]
        )
        return stack(center, squares, count)

    count = count_ref[...]
    own_count = jnp.broadcast_to(count.astype(jnp.float32), (1, width))
    live = lax.broadcasted_iota(jnp.int32, (rows, width), 0) < count

    def norm_stats(at, hidden, meanwhile=(None, None)):
        center = jnp.sum(hidden, axis=0, keepdims=True) / own_count
        centered = jnp.where(live, hidden - center, 0.0)
        squares = jnp.sum(centered * centered, axis=0, keepdims=True)
        merged = exchange(
            at, stack(fold(center), fold(squares), fold(own_count)), merge_all, meanwhile
        )
        total = unfold(merged[4:6])
        scale = lax.rsqrt(unfold(merged[2:4]) / total + eps_norm)
        return unfold(merged[0:2]), scale, total

    def norm_grad(at, norm, incoming, normed, scale, total, meanwhile=(None, None)):
        shift_sum = fold(jnp.sum(incoming, axis=0, keepdims=True))
        scale_sum = fold(jnp.sum(incoming * normed, axis=0, keepdims=True))
        summed = exchange(
            at, stack(shift_sum, scale_sum, jnp.zeros_like(shift_sum)), add_all, meanwhile
        )
        shift_sum, scale_sum = unfold(summed[0:2]), unfold(summed[2:4])
        bias_grad_ref[norm : norm + 1, :] = shift_sum
        gain_grad_ref[norm : norm + 1, :] = scale_sum
        hidden_grad = (
            scale
            * gain_ref[norm : norm + 1, :]
            * (incoming - shift_sum / total - normed * (scale_sum / total))
        )
        return jnp.where(live, hidden_grad, 0.0).astype(jnp.bfloat16)

    def pick(mask):
        return jnp.where(mask, jnp.bfloat16(1), jnp.bfloat16(0))

    def counting(shape, axis):
        return lax.broadcasted_iota(jnp.int32, shape, axis).astype(jnp.float32).astype(jnp.bfloat16)

    def place_spread(turn, step):
        picked = dot(pickers[turn, : PAIR * rows, :], held[...]).astype(jnp.bfloat16)
        for part in range(PAIR):
            columns[turn, :, part * width : (part + 1) * width] = picked[
                part * rows : (part + 1) * rows
            ]

    def run_steps(first, last, build, place, use, after):
        build(first % 2, first)

        def one(turn, step, more):
            place(turn, step)
            if more:
                build(1 - turn, step + 1)
            use(turn, step)

        bodies = (last - first - 1) // 2

        def body(at, carry):
            for turn in range(2):
                one((first + turn) % 2, first + 2 * at + turn, True)
            after(first + 2 * at, 2)
            return carry

        lax.fori_loop(0, bodies, body, 0)
        for step in range(first + 2 * bodies, last):
            one(step % 2, step, step + 1 < last)
            after(step, 1)

    def convolve(source, weight, hidden):
        places = counting((rows, BLOCK), 1)
        hidden[...] = jnp.zeros_like(hidden)
        for block in range(2):
            side_by_side[:, block * width : (block + 1) * width] = source[
                block * BLOCK : (block + 1) * BLOCK, :
            ]

        def build(turn, step):
            for part in range(GROUP):
                code = nb_cols[step * GROUP + part]
                wanted = jnp.concatenate([jnp.maximum(code, -1 - code)] * (BLOCK // 128), axis=1)
                pickers[turn, part * rows : (part + 1) * rows, :BLOCK] = pick(wanted == places)

        def use(turn, step):
            weights = weight[pl.ds(step * GROUP, GROUP)].reshape(GROUP * width, width)
            hidden[...] += dot(columns[turn], weights)

        def place(turn, step):
            for part in range(GROUP):
                found = dot(
                    pickers[turn, part * rows : (part + 1) * rows, :BLOCK], side_by_side[...]
                )
                code = nb_cols[step * GROUP + part].astype(jnp.float32)
                second = jnp.concatenate([code] * (width // 128), axis=1) < 0
                columns[turn, :, part * width : (part + 1) * width] = jnp.where(
                    second, found[:, width:], found[:, :width]
                ).astype(jnp.bfloat16)

        run_steps(0, offsets // GROUP, build, place, use, no_slot)

    def build_spread(neighbours, offset_of):
        places = counting((BLOCK, rows), 0)

        def build(turn, step):
            for part in range(PAIR):
                wanted = neighbours[pl.ds(offset_of(PAIR * step + part), 1), :]
                wanted = wanted.astype(jnp.float32)
                for first in range(0, rows, BLOCK):
                    here = jnp.broadcast_to(wanted - first, (16, rows)).astype(jnp.bfloat16)
                    pickers[turn, part * rows + first : part * rows + first + BLOCK, :] = pick(
                        jnp.concatenate([here] * (BLOCK // 16), axis=0) == places
                    )

        return build

    def no_slot(at, count):
        pass

    def own_of(second):
        if not reduce_here:
            return lambda at: at
        extra = 14 * pair if second else 14 - 14 * pair
        return lambda at: 14 * pair + at + (extra - 14 * pair) * (jnp.int32(at) == 13)

    def put(second, at, product, more):
        for part in range(PAIR):
            value = product[:, part * width : (part + 1) * width]
            if not reduce_here:
                unit = pl.multiple_of((units * second + PAIR * at + part) * width, width)
                grads[pl.ds(unit, width), :] = value
                continue
            c, half = at, part
            if second:
                c, half = units // PAIR - 1 + at + part, 1 - part
            if isinstance(at, int) and PAIR * at + part == units - 1:
                empty = pair if second else 1 - pair
                c, half = chunks - 2 + empty, empty
            value = value.reshape(grads.shape[1:4] + (8, width))
            here_rows = pl.ds(8 * half, 8)
            if more:
                value = value + grads[c, :, :, :, here_rows]
            grads[c, :, :, :, here_rows] = value

    def convolve_back(weight, act_grad, second, own_slot, other_slot):
        def use_of(offset_of, weigh):
            def use(turn, step):
                spread = columns[turn, :, : PAIR * width]
                weights = jnp.concatenate(
                    [weight[offset_of(PAIR * step + part)] for part in range(PAIR)], axis=1
                )
                act_grad[...] += dot_last(spread, weights)
                if weigh:
                    put(second, step, dot(source_t[...], spread), False)

            return use

        steps = units // PAIR
        offset_of = own_of(second)
        build = build_spread(nb_own, offset_of)
        run_steps(0, steps, build, place_spread, use_of(offset_of, True), own_slot)
        if reduce_here:
            if second:
                offset_of = lambda at: 14 - 14 * pair + at
            else:
                offset_of = lambda at: 13 - 13 * pair + at + 14 * pair * (jnp.int32(at) == 13)
            build = build_spread(nb_own, offset_of)
            run_steps(0, steps, build, place_spread, use_of(offset_of, False), other_slot)

    def convolve_pair(second, first_step, last_step, at_slot):
        def use(turn, step):
            spread = columns[turn, :, : PAIR * width]
            put(second, step, dot(pair_source_t[...], spread), True)

        build = build_spread(nb_pair, own_of(second))
        run_steps(first_step, last_step, build, place_spread, use, at_slot)

    core, row = lax.rem(group_me, 2), group_me // 2
    column, plane = lax.rem(dp_me, 2), dp_me // 2
    pair, high = lax.rem(plane, 2), plane // 2
    planes = 4
    core_peer = {"group": group_me + 1 - 2 * core}
    row_peer = {"group": group_me + 2 - 4 * row}
    column_peer = {"dp": dp_me + 1 - 2 * column}
    pair_peer = {"dp": dp_me + 2 - 4 * pair}
    cross_peer = {"dp": dp_me + 4 - 8 * high}
    own = pl.ds(2 * core, 2)
    lane_a, lane_b = 2 * core, 2 * core + 1
    kept_row, given_row = pl.ds(2 * row, 2), pl.ds(2 * (1 - row), 2)

    def send(c, stage, source, target, peer):
        turn = lax.rem(c, RING)
        return pltpu.make_async_remote_copy(
            src_ref=source,
            dst_ref=target,
            send_sem=sum_send.at[turn],
            recv_sem=sum_recv.at[turn, stage],
            device_id=peer,
            device_id_type=MESH,
        )

    def copies_of(c, stage, size):
        both, some = pl.ds(PAIR * c, size), pl.ds(0, 8 * size)
        part = grads.at[c, :, :, :, some]

        def landing(ref, at):
            return ref.at[(at, *[slice(None)] * (len(ref.shape) - 3), some)]

        if stage == 0:
            given = part.at[pl.ds(2 * (1 - core), 2)]
            return [send(c, stage, given, landing(from_core, lax.rem(c, CORE_RING)), core_peer)]
        if stage == 1:
            return [
                send(c, stage, part.at[lane_a, 1 - column], landing(from_first_a, c), column_peer),
                send(c, stage, part.at[lane_b, :, given_row], landing(from_first_b, c), row_peer),
            ]
        if stage == 2:
            return [
                send(c, stage, part.at[lane_a, column, given_row], landing(from_second_a, c), row_peer),
                send(c, stage, part.at[lane_b, 1 - column, kept_row], landing(from_second_b, c), column_peer),
            ]
        if stage == 3:
            given = part.at[own, column, 2 * row + 1 - high]
            return [send(c, stage, given, landing(from_line, c), cross_peer)]
        if stage == 4:
            block = results.at[pair, both, own, column, 2 * row + high]
            return [
                send(
                    c,
                    stage,
                    block,
                    block,
                    {"dp": 2 * lax.rem(plane + step, planes) + column},
                )
                for step in range(1, planes)
            ]
        if stage == 5:
            block_a = results.at[:, both, lane_a, column, kept_row]
            block_b = results.at[:, both, lane_b, column, kept_row]
            return [
                send(c, stage, block_a, block_a, row_peer),
                send(c, stage, block_b, block_b, column_peer),
            ]
        if stage == 6:
            block_a = results.at[:, both, lane_a, column]
            block_b = results.at[:, both, lane_b, :, kept_row]
            return [
                send(c, stage, block_a, block_a, column_peer),
                send(c, stage, block_b, block_b, row_peer),
            ]
        block = results.at[:, both, own]
        return [send(c, stage, block, block, core_peer)]

    def wait_bytes(sem, like):
        pltpu.make_async_copy(like, like, sem).wait()

    def wait_arrived(c, stage, size):
        some = pl.ds(0, 8 * size)
        like = (
            from_core.at[0, :, :, :, some],
            grads.at[c, 0, :, :, some],
            grads.at[c, 0, 0, :, some],
            from_line.at[c, :, some],
            results.at[0, pl.ds(0, 3 * size), 0, 0, pl.ds(0, 2)],
            grads.at[c, 0, :, :, some],
            grads.at[c, pl.ds(0, 2), :, :, some],
            grads.at[c, :, :, :, some],
        )[stage]
        wait_bytes(sum_recv.at[lax.rem(c, RING), stage], like)

    def wait_sent(c, size):
        like = results.at[0, pl.ds(0, 23), 0, pl.ds(0, size)]
        wait_bytes(sum_send.at[lax.rem(c, RING)], like)

    def stage_of(c, stage, size=PAIR):
        if stage > 0:
            wait_arrived(c, stage - 1, size)
        some = slice(0, 8 * size)

        def add(lanes, columns_of, rows_of, landed):
            here_rows = (c, lanes, columns_of, rows_of, some)
            grads[here_rows] = grads[here_rows] + landed

        every = slice(None)
        if stage == 1:
            add(own, every, every, from_core[lax.rem(c, CORE_RING), :, :, :, some])
        if stage == 2:
            add(lane_a, column, every, from_first_a[c, :, some])
            add(lane_b, every, kept_row, from_first_b[c, :, :, some])
        if stage == 3:
            add(lane_a, column, kept_row, from_second_a[c, :, some])
            add(lane_b, column, kept_row, from_second_b[c, :, some])
        if stage == 4:
            mine = 2 * row + high
            add(own, column, mine, from_line[c, :, some])
            for unit in range(size):
                results[pair, PAIR * c + unit, own, column, mine] = grads[
                    c, own, column, mine, 8 * unit : 8 * unit + 8
                ]
        if stage < len(LAGS) - 1:
            for copy in copies_of(c, stage, size):
                copy.start()
        else:
            wait_sent(c, size)

    early = units // PAIR - 1

    def slot(at, last=False):
        if not reduce_here:
            return
        for stage, lag in enumerate(LAGS):
            entry = at - lag
            if isinstance(at, int):
                c = entry if entry < early else max(entry - GAP, early - 1)
                if 0 <= entry < chunks - 1 + GAP and (c == entry or entry >= early + GAP):
                    stage_of(c, stage)
                continue
            second = entry >= early + GAP

            @pl.when(
                ((entry >= 0) & (entry < early)) | (second & (entry < chunks - 1 + GAP))
            )
            def _():
                stage_of(entry - GAP * second.astype(jnp.int32), stage)

            if last:

                @pl.when(entry == chunks - 1 + GAP)
                def _():
                    stage_of(chunks - 1, stage, 1)

    def slot_after(at, count, steps_with, first_slot):
        if isinstance(at, int):
            for number, step in enumerate(steps_with):
                if at <= step < at + count:
                    slot(first_slot + number)
            return
        start, end = first_slot, first_slot
        for step in steps_with:
            start = start + (at > step).astype(jnp.int32)
            end = end + (at + count > step).astype(jnp.int32)

        def one(number, carry):
            slot(number)
            return carry

        lax.fori_loop(start, end, one, 0)

    def swap(at, source, target):
        return pltpu.make_async_remote_copy(
            src_ref=source,
            dst_ref=target,
            send_sem=swap_send.at[at],
            recv_sem=swap_recv.at[at],
            device_id=pair_peer,
            device_id_type=MESH,
        )

    def swap_rows(at):
        return swap(at, swap_out.at[at % 2], swap_in.at[at])

    def start_rows(at, value):
        if reduce_here:
            swap_out[at % 2] = value.astype(jnp.float32)
            swap_rows(at).start()

    places = nb_rows[...]
    codes = jnp.where(places < BLOCK, places, jnp.where(places < rows, BLOCK - 1 - places, 4 * BLOCK))
    side[...] = jnp.zeros_like(side)
    side[:offsets, :] = codes.astype(jnp.float32)
    side[offsets : offsets + down_offsets, :] = down_rows_ref[...].astype(jnp.float32)
    side_cols[...] = side[...].T
    nb_own[...] = jnp.full_like(nb_own, rows)
    nb_own[:offsets, :] = nb_rows[...]
    swap_neighbours = swap(4, nb_own, nb_pair)
    for weight in (w_mid, w_out):
        weight[offsets:] = jnp.zeros_like(weight[offsets:])

    spread_fine[...] = fine_ref[...].astype(jnp.float32)
    for k in range(down_offsets):
        child = spread_fine[pl.ds(k % children, rows, stride=children), :]
        there = side_cols[:, offsets + k : offsets + k + 1] < fine_rows
        cols_down[:, k * in_width : (k + 1) * in_width] = jnp.where(there, child, 0.0).astype(
            jnp.bfloat16
        )
    loads[0].wait()
    hid_one[...] = dot(cols_down[...], w_down[...].reshape(down_offsets * in_width, width))

    def spread_neighbours():
        for k in range(offsets):
            nb_cols[k] = jnp.broadcast_to(side_cols[:, k : k + 1], (rows, 128)).astype(jnp.bfloat16)

    pl.semaphore_wait(barrier, len(peers))

    swap_one = swap(0, hid_one, swap_in.at[0])
    swap_two = swap(1, hid_two, swap_in.at[1])

    def start_one():
        swap_neighbours.start()
        swap_one.start()

    def start_two():
        swap_two.start()

    beside = (spread_neighbours, start_one if reduce_here else None)
    center_one, scale_one, total = norm_stats(0, hid_one[...], beside)

    def pre_one(hidden=hid_one):
        normed = (hidden[...] - center_one) * scale_one
        return normed, normed * gain_ref[0:1, :] + bias_ref[0:1, :]

    _, pre = pre_one()
    act_one[...] = jnp.where(live, pre * sigmoid(pre), 0.0)
    act_one_b[...] = act_one[...].astype(jnp.bfloat16)
    loads[1].wait()
    convolve(act_one_b, w_mid, hid_two)
    center_two, scale_two, _ = norm_stats(
        1, hid_two[...], (None, start_two if reduce_here else None)
    )

    def pre_two(hidden=hid_two):
        normed = (hidden[...] - center_two) * scale_two
        return normed, normed * gain_ref[1:2, :] + bias_ref[1:2, :]

    _, pre = pre_two()
    act_two_b[...] = jnp.where(live, pre * sigmoid(pre), 0.0).astype(jnp.bfloat16)
    loads[2].wait()
    convolve(act_two_b, w_out, hid_three)
    def turn_two():
        source_t[...] = act_two_b[...].T

    center_three, scale_three, _ = norm_stats(2, hid_three[...], (turn_two, None))
    normed_three = (hid_three[...] - center_three) * scale_three
    summed = (
        jnp.where(live, normed_three * gain_ref[2:3, :] + bias_ref[2:3, :], 0.0) + act_one[...]
    )
    sigma = sigmoid(summed)
    features_ref[...] = jnp.where(live, summed * sigma, 0.0).astype(jnp.bfloat16)

    def pair_source(swapped, pre_of, source_at):
        swapped.wait()
        _, pre = pre_of(swap_in.at[source_at])
        pair_source_t[...] = (pre * sigmoid(pre)).astype(jnp.bfloat16).T

    def pair_two():
        if reduce_here:
            pair_source(swap_two, pre_two, 1)

    slope = sigma * (1.0 + summed * (1.0 - sigma))
    act_one[...] = jnp.where(live, cotangent_ref[...].astype(jnp.float32) * slope, 0.0)
    grad_hidden[...] = norm_grad(
        3, 2, act_one[...], normed_three, scale_three, total, (pair_two, None)
    )
    start_rows(2, grad_hidden[...])
    held[...] = grad_hidden[...]
    grad_act[...] = jnp.zeros_like(grad_act)
    steps = units // PAIR

    def receive(hidden_at):
        swap_rows(hidden_at).wait()
        held[...] = swap_in[hidden_at].astype(jnp.bfloat16)

    def pair_halves(second, at_slot):
        middle = (steps + 1) // 2
        return (
            lambda: convolve_pair(second, 0, middle, at_slot),
            lambda: convolve_pair(second, middle, steps, at_slot),
        )

    nothing = (None, None)
    convolve_back(w_out, grad_act, 0, no_slot, no_slot)
    normed, pre = pre_two()
    incoming = jnp.where(live, grad_act[...] * silu_slope(pre), 0.0)
    if reduce_here:
        swap_neighbours.wait()
        receive(2)
    after = lambda at, count: slot_after(at, count, (0, 4), 0)
    beside = pair_halves(0, after) if reduce_here else nothing
    grad_hidden[...] = norm_grad(4, 1, incoming, normed, scale_two, total, beside)
    start_rows(3, grad_hidden[...])
    held[...] = grad_hidden[...]
    grad_act[...] = act_one[...]
    source_t[...] = act_one_b[...].T
    convolve_back(
        w_mid,
        grad_act,
        1,
        lambda at, count: slot_after(at, count, (0, 5), 2),
        lambda at, count: slot_after(at, count, (1, 3, 5), 4),
    )
    normed, pre = pre_one()
    incoming = jnp.where(live, grad_act[...] * silu_slope(pre), 0.0)
    if reduce_here:
        pair_source(swap_one, pre_one, 0)
        receive(3)
    after = lambda at, count: slot_after(at, count, (0, 1, 3, 5, 6), 7)
    beside = pair_halves(1, after) if reduce_here else nothing
    grad_hidden[...] = norm_grad(5, 0, incoming, normed, scale_one, total, beside)
    down_rows = down_offsets * in_width
    if reduce_here:
        down_all[...] = dot(cols_down[...].T, grad_hidden[...])
        kept = down_rows // 2
        swap_down = swap(
            5, down_all.at[pl.ds(pl.multiple_of(kept * (1 - pair), kept), kept), :], down_got
        )
        swap_down.start()
    else:
        grads[2 * units * width :, :] = dot(cols_down[...].T, grad_hidden[...])
    slot(12)
    for child in range(children):
        total_child = jnp.zeros((rows, in_width), jnp.float32)
        for k in range(child, down_offsets, children):
            there = side_cols[:, offsets + k : offsets + k + 1] < fine_rows
            total_child += jnp.where(there, dot_last(grad_hidden[...], w_down[k]), 0.0)
        spread_fine[pl.ds(child, rows, stride=children), :] = total_child
    fine_grad_ref[...] = spread_fine[...].astype(jnp.bfloat16)
    slot(13)

    if reduce_here:

        def final(at, carry):
            slot(at, True)
            return carry

        swap_down.wait()
        for part in range(PAIR):
            total_down = (
                down_all[pl.ds(pl.multiple_of(kept * pair + part * width, width), width), :]
                + down_got[part * width : (part + 1) * width, :]
            )
            half = 1 - part
            grads[chunks - 2 + part, :, :, :, 8 * half : 8 * half + 8] = total_down.reshape(
                grads.shape[1:4] + (8, width)
            )
        lax.fori_loop(chunks - 2 + GAP, chunks + GAP + LAGS[-1], final, 0)
    else:
        store = pltpu.make_async_copy(grads, results, load_sem.at[0])
        store.start()
        store.wait()


def place_kernel(
    features_ref,
    fine_grad_ref,
    grads_ref,
    gain_ref,
    bias_ref,
    features_out,
    fine_grad_out,
    grad_down_out,
    grad_mid_out,
    grad_out_out,
    gain_out,
    bias_out,
    sem,
):
    half = grad_mid_out.shape[0] // 2
    moves = []
    for at, target in enumerate((grad_out_out, grad_mid_out)):
        for pair in range(2):
            for first in range(0, half, 3):
                count = min(3, half - first)
                here = grads_ref.at[pair, pl.ds(at * half + first, count)]
                moves.append((here, target.at[pl.ds((half + 1) * pair + first, count)]))
        moves.append((grads_ref.at[1 - at, pl.ds(2 * half, 1)], target.at[pl.ds(half, 1)]))
    for pair in range(2):
        down_units = grad_down_out.shape[0] // 2
        here = grads_ref.at[pair, pl.ds(2 * half + 1, down_units)]
        moves.append((here, grad_down_out.at[pl.ds(pair * down_units, down_units)]))
    copies = [
        pltpu.make_async_copy(source, target, sem.at[at])
        for at, (source, target) in enumerate(moves)
    ]
    for copy in copies:
        copy.start()
    features_out[...] = features_ref[...]
    fine_grad_out[...] = fine_grad_ref[...]
    gain_out[...] = gain_ref[...]
    bias_out[...] = bias_ref[...]
    for copy in copies:
        copy.wait()


def per_device(
    dp_size,
    group_size,
    fine_features,
    down_map,
    neighbours,
    voxel_counts,
    down_weight,
    mid_weight,
    out_weight,
    norm_gain,
    norm_bias,
    cotangent,
):
    rows, width = cotangent.shape
    fine_rows, in_width = fine_features.shape
    offsets = neighbours.shape[1]
    down_offsets = down_map.shape[1]
    f32, bf16, i32 = jnp.float32, jnp.bfloat16, jnp.int32
    vmem = pl.BlockSpec(memory_space=pltpu.VMEM)
    hbm = pl.BlockSpec(memory_space=pl.ANY)
    shape = jax.ShapeDtypeStruct
    reduce_here = dp_size == 8 and group_size == 4
    result = pltpu.VMEM if reduce_here else shape
    near_size, far_size = (dp_size * group_size, 1) if reduce_here else (group_size, dp_size)
    share = 2 if reduce_here else 1
    units = (offsets + 1) // 2 * 2 // share
    all_units = 2 * units + down_offsets * in_width // (share * width)
    grad_rows = all_units * width
    chunks = all_units // PAIR
    padded = (offsets + 1) // 2 * 2
    features, fine_grad, grads, gain_grad, bias_grad = pl.pallas_call(
        functools.partial(kernel, dp_size, group_size, reduce_here),
        out_shape=(
            result((rows, width), bf16),
            result((fine_rows, in_width), bf16),
            pltpu.VMEM((2, all_units, *GROUPS, 8, width), f32)
            if reduce_here
            else shape((grad_rows, width), f32),
            result(norm_gain.shape, f32),
            result(norm_bias.shape, f32),
        ),
        in_specs=[vmem, vmem, vmem, vmem, hbm, hbm, hbm, vmem, vmem, vmem],
        out_specs=(vmem, vmem, vmem if reduce_here else hbm, vmem, vmem),
        scratch_shapes=[
            pltpu.VMEM(down_weight.shape, bf16),
            pltpu.VMEM((padded, width, width), bf16),
            pltpu.VMEM((padded, width, width), bf16),
            pltpu.VMEM((fine_rows, in_width), f32),
            pltpu.VMEM((rows, down_offsets * in_width), bf16),
            pltpu.VMEM((offsets, rows, 128), bf16),
            pltpu.VMEM((2, GROUP * rows, rows), bf16),
            pltpu.VMEM((2, rows, GROUP * width), bf16),
            pltpu.VMEM((BLOCK, 2 * width), bf16),
            pltpu.VMEM((rows, width), f32),
            pltpu.VMEM((rows, width), bf16),
            pltpu.VMEM((rows, width), bf16),
            pltpu.VMEM((rows, width), f32),
            pltpu.VMEM((rows, width), f32),
            pltpu.VMEM((rows, width), f32),
            pltpu.VMEM((rows, width), bf16),
            pltpu.VMEM((rows, width), bf16),
            pltpu.VMEM((width, rows), bf16),
            pltpu.VMEM((width, rows), bf16),
            pltpu.VMEM((rows, width), f32),
            pltpu.VMEM((128, rows), f32),
            pltpu.VMEM((rows, 128), f32),
            pltpu.VMEM((padded, rows), i32),
            pltpu.VMEM((padded, rows), i32),
            pltpu.VMEM((2, rows, width), f32),
            pltpu.VMEM((4, rows, width), f32),
            pltpu.VMEM((down_offsets * in_width, width), f32),
            pltpu.VMEM((down_offsets * in_width // 2, width), f32),
            pltpu.VMEM(
                (chunks, *GROUPS, 8 * PAIR, width) if reduce_here else (grad_rows, width), f32
            ),
            pltpu.VMEM((CORE_RING, 2, *GROUPS[1:], 8 * PAIR, width), f32),
            pltpu.VMEM((chunks, GROUPS[2], 8 * PAIR, width), f32),
            pltpu.VMEM((chunks, GROUPS[1], 2, 8 * PAIR, width), f32),
            pltpu.VMEM((chunks, 2, 8 * PAIR, width), f32),
            pltpu.VMEM((chunks, 2, 8 * PAIR, width), f32),
            pltpu.VMEM((chunks, 2, 8 * PAIR, width), f32),
            pltpu.VMEM((6, near_size, 8, width // 2), f32),
            pltpu.VMEM((6, far_size, 8, width // 2), f32),
            pltpu.SemaphoreType.DMA((3,)),
            pltpu.SemaphoreType.DMA((RING,)),
            pltpu.SemaphoreType.DMA((RING, len(LAGS) - 1)),
            pltpu.SemaphoreType.DMA((6,)),
            pltpu.SemaphoreType.DMA((6,)),
            pltpu.SemaphoreType.DMA((6, group_size - 1)),
            pltpu.SemaphoreType.DMA((6, group_size - 1)),
            pltpu.SemaphoreType.DMA((6, far_size)),
            pltpu.SemaphoreType.DMA((6, far_size)),
        ],
        compiler_params=pltpu.CompilerParams(
            collective_id=0, has_side_effects=True, vmem_limit_bytes=(46 if reduce_here else 60) * 1024 * 1024
        ),
    )(
        fine_features,
        down_map.T,
        neighbours.T,
        voxel_counts.reshape(1, 1),
        down_weight,
        mid_weight,
        out_weight,
        norm_gain,
        norm_bias,
        cotangent,
    )
    if not reduce_here:
        grads = lax.psum(grads, ("dp", "group"))
        middle, end = offsets * width, 2 * padded * width
        grad_out = grads[:middle].reshape(out_weight.shape)
        grad_mid = grads[padded * width : padded * width + middle].reshape(mid_weight.shape)
        grad_down = grads[end:].reshape(down_weight.shape)
        return (features, fine_grad, grad_down, grad_mid, grad_out, gain_grad, bias_grad)
    held = [
        pltpu.with_memory_space_constraint(value, pltpu.VMEM)
        for value in (features, fine_grad, grads, gain_grad, bias_grad)
    ]
    features, fine_grad, grad_down, grad_mid, grad_out, gain_grad, bias_grad = pl.pallas_call(
        place_kernel,
        out_shape=(
            shape(features.shape, bf16),
            shape(fine_grad.shape, bf16),
            shape((down_offsets * in_width // width, *GROUPS, 8, width), f32),
            shape((offsets, *GROUPS, 8, width), f32),
            shape((offsets, *GROUPS, 8, width), f32),
            shape(norm_gain.shape, f32),
            shape(norm_bias.shape, f32),
        ),
        in_specs=[vmem] * 5,
        out_specs=(vmem, vmem, hbm, hbm, hbm, vmem, vmem),
        scratch_shapes=[pltpu.SemaphoreType.DMA((24,))],
        compiler_params=pltpu.CompilerParams(vmem_limit_bytes=8 * 1024 * 1024),
    )(*held)
    grad_down = grad_down.reshape(down_weight.shape)
    grad_mid = grad_mid.reshape(mid_weight.shape)
    grad_out = grad_out.reshape(out_weight.shape)
    return (features, fine_grad, grad_down, grad_mid, grad_out, gain_grad, bias_grad)


def solution(mesh):
    in_specs = (
        P(("dp", "group"), None),
        P(("dp", "group"), None),
        P(("dp", "group"), None),
        P(("dp", "group")),
        P(),
        P(),
        P(),
        P(),
        P(),
        P(("dp", "group"), None),
    )
    out_specs = (P(("dp", "group"), None), P(("dp", "group"), None), P(), P(), P(), P(), P())
    return jax.shard_map(
        functools.partial(per_device, mesh.shape["dp"], mesh.shape["group"]),
        mesh=mesh,
        in_specs=in_specs,
        out_specs=out_specs,
        check_vma=False,
    )
```

```python
import functools

import jax
import jax.numpy as jnp
from jax import lax
from jax.experimental import pallas as pl
from jax.experimental.pallas import tpu as pltpu
from jax.sharding import PartitionSpec as P

eps_norm = 1e-05
MESH = pl.DeviceIdType.MESH
GROUP = 3
BLOCK = 256
PAIR = 2
GROUPS = (4, 2, 4)
GAP = 1
LAGS = (0, 1, 2, 3, 5, 7, 8, 10, 11)
RING = 16
CORE_RING = 8


def sigmoid(value):
    return 0.5 + 0.5 * jnp.tanh(0.5 * value)


def silu_slope(value):
    sigma = sigmoid(value)
    return sigma * (1.0 + value * (1.0 - sigma))


def dot(left, right):
    return jnp.dot(left, right, preferred_element_type=jnp.float32)


def dot_last(left, right):
    return lax.dot_general(
        left, right, (((1,), (1,)), ((), ())), preferred_element_type=jnp.float32
    )


def kernel(
    dp_size,
    group_size,
    reduce_here,
    fine_ref,
    down_rows_ref,
    nb_rows,
    count_ref,
    down_hbm,
    mid_hbm,
    out_hbm,
    gain_ref,
    bias_ref,
    cotangent_hbm,
    features_ref,
    fine_grad_ref,
    results,
    gain_grad_ref,
    bias_grad_ref,
    w_down,
    w_mid,
    w_out,
    cotangent_ref,
    spread_fine,
    cols_down,
    nb_cols,
    pickers,
    columns,
    side_by_side,
    act_one,
    act_one_b,
    act_two_b,
    hid_one,
    hid_two,
    hid_three,
    held,
    grad_hidden,
    source_t,
    pair_source_t,
    grad_act,
    side,
    side_cols,
    nb_own,
    nb_pair,
    swap_out,
    swap_in,
    down_all,
    down_got,
    grads,
    from_core,
    from_first_a,
    from_first_b,
    from_second_a,
    from_second_b,
    from_line,
    near,
    far,
    load_sem,
    sum_send,
    sum_recv,
    swap_send,
    swap_recv,
    near_send,
    near_recv,
    far_send,
    far_recv,
):
    rows, width = cotangent_hbm.shape
    offsets = nb_rows.shape[0]
    fine_rows, in_width = fine_ref.shape
    children = fine_rows // rows
    down_offsets = down_rows_ref.shape[0]
    units = (offsets + 1) // 2 * (1 if reduce_here else 2)
    chunks = grads.shape[0]
    dp_me = lax.axis_index("dp")
    group_me = lax.axis_index("group")

    loads = [
        pltpu.make_async_copy(source, target, load_sem.at[at])
        for at, (source, target) in enumerate(
            (
                (down_hbm, w_down),
                (mid_hbm, w_mid.at[pl.ds(0, offsets)]),
                (out_hbm, w_out.at[pl.ds(0, offsets)]),
                (cotangent_hbm, cotangent_ref),
            )
        )
    ]
    for load in loads:
        load.start()

    direct = reduce_here
    peers = [
        {
            "dp": lax.rem(dp_me + dp_step, dp_size),
            "group": lax.rem(group_me + group_step, group_size),
        }
        for dp_step in reversed(range(dp_size))
        for group_step in reversed(range(group_size))
        if (dp_step or group_step) and (direct or not dp_step or not group_step)
    ]
    barrier = pltpu.get_barrier_semaphore()
    for peer in peers:
        pl.semaphore_signal(barrier, inc=1, device_id=peer, device_id_type=MESH)

    def share(at, axis, me, size, slots, send, recv):
        copies = []
        for step in range(1, size):
            copies.append(
                pltpu.make_async_remote_copy(
                    src_ref=slots.at[at, me],
                    dst_ref=slots.at[at, me],
                    send_sem=send.at[at, step - 1],
                    recv_sem=recv.at[at, step - 1],
                    device_id={axis: lax.rem(me + step, size)},
                    device_id_type=MESH,
                )
            )
        for copy in copies:
            copy.start()
        return copies

    def exchange_direct(at, block, combine, meanwhile):
        me = dp_me * group_size + group_me
        near[at, me] = block
        for peer in peers:
            pltpu.make_async_remote_copy(
                src_ref=near.at[at, me],
                dst_ref=near.at[at, me],
                send_sem=near_send.at[at, 0],
                recv_sem=near_recv.at[at, 0],
                device_id=peer,
                device_id_type=MESH,
            ).start()
        for work in meanwhile:
            if work is not None:
                work()
        others = near.at[at, pl.ds(0, len(peers))]
        for sem in (near_recv, near_send):
            pltpu.make_async_copy(others, others, sem.at[at, 0]).wait()
        return combine([near[at, slot] for slot in range(len(peers) + 1)])

    def exchange(at, block, combine, meanwhile=(None, None)):
        if direct:
            return exchange_direct(at, block, combine, meanwhile)
        near[at, group_me] = block
        copies = share(at, "group", group_me, group_size, near, near_send, near_recv)
        if meanwhile[0] is not None:
            meanwhile[0]()
        for copy in copies:
            copy.wait()
        far[at, dp_me] = combine([near[at, slot] for slot in range(group_size)])
        copies = share(at, "dp", dp_me, dp_size, far, far_send, far_recv)
        if meanwhile[1] is not None:
            meanwhile[1]()
        for copy in copies:
            copy.wait()
        return combine([far[at, slot] for slot in range(dp_size)])

    lanes = width // 2

    def stack(first, second, third):
        filler = jnp.zeros((2, lanes), jnp.float32)
        return jnp.concatenate([first, second, third, filler], axis=0)

    def fold(value):
        return jnp.concatenate([value[:, :lanes], value[:, lanes:]], axis=0)

    def unfold(value):
        return jnp.concatenate([value[0:1], value[1:2]], axis=1)

    def add_all(blocks):
        total = blocks[0]
        for block in blocks[1:]:
            total = total + block
        return total

    def merge_all(blocks):
        count = add_all([block[4:6] for block in blocks])
        center = add_all([block[4:6] * block[0:2] for block in blocks]) / count
        squares = add_all(
            [
                block[2:4] + block[4:6] * (block[0:2] - center) * (block[0:2] - center)
                for block in blocks
            ]
        )
        return stack(center, squares, count)

    count = count_ref[0]
    own_count = jnp.full((1, width), count.astype(jnp.float32))
    live = lax.broadcasted_iota(jnp.int32, (rows, width), 0) < count

    def norm_stats(at, hidden, meanwhile=(None, None)):
        center = jnp.sum(hidden, axis=0, keepdims=True) / own_count
        centered = jnp.where(live, hidden - center, 0.0)
        squares = jnp.sum(centered * centered, axis=0, keepdims=True)
        merged = exchange(
            at, stack(fold(center), fold(squares), fold(own_count)), merge_all, meanwhile
        )
        total = unfold(merged[4:6])
        scale = lax.rsqrt(unfold(merged[2:4]) / total + eps_norm)
        return unfold(merged[0:2]), scale, total

    def norm_grad(at, norm, incoming, normed, scale, total, meanwhile=(None, None)):
        shift_sum = fold(jnp.sum(incoming, axis=0, keepdims=True))
        scale_sum = fold(jnp.sum(incoming * normed, axis=0, keepdims=True))
        summed = exchange(
            at, stack(shift_sum, scale_sum, jnp.zeros_like(shift_sum)), add_all, meanwhile
        )
        shift_sum, scale_sum = unfold(summed[0:2]), unfold(summed[2:4])
        bias_grad_ref[norm : norm + 1, :] = shift_sum
        gain_grad_ref[norm : norm + 1, :] = scale_sum
        hidden_grad = (
            scale
            * gain_ref[norm : norm + 1, :]
            * (incoming - shift_sum / total - normed * (scale_sum / total))
        )
        return jnp.where(live, hidden_grad, 0.0).astype(jnp.bfloat16)

    def pick(mask):
        return jnp.where(mask, jnp.bfloat16(1), jnp.bfloat16(0))

    def counting(shape, axis):
        return lax.broadcasted_iota(jnp.int32, shape, axis).astype(jnp.float32).astype(jnp.bfloat16)

    def place_spread(turn, step):
        picked = dot(pickers[turn, : PAIR * rows, :], held[...]).astype(jnp.bfloat16)
        for part in range(PAIR):
            columns[turn, :, part * width : (part + 1) * width] = picked[
                part * rows : (part + 1) * rows
            ]

    def run_steps(first, last, build, place, use, after):
        build(first % 2, first)

        def one(turn, step, more):
            place(turn, step)
            if more:
                build(1 - turn, step + 1)
            use(turn, step)

        bodies = (last - first - 1) // 2

        def body(at, carry):
            for turn in range(2):
                one((first + turn) % 2, first + 2 * at + turn, True)
            after(first + 2 * at, 2)
            return carry

        lax.fori_loop(0, bodies, body, 0)
        for step in range(first + 2 * bodies, last):
            one(step % 2, step, step + 1 < last)
            after(step, 1)

    def convolve(source, weight, hidden):
        places = counting((rows, BLOCK), 1)
        hidden[...] = jnp.zeros_like(hidden)
        for block in range(2):
            side_by_side[:, block * width : (block + 1) * width] = source[
                block * BLOCK : (block + 1) * BLOCK, :
            ]

        def build(turn, step):
            for part in range(GROUP):
                code = nb_cols[step * GROUP + part]
                wanted = jnp.concatenate([jnp.maximum(code, -1 - code)] * (BLOCK // 128), axis=1)
                pickers[turn, part * rows : (part + 1) * rows, :BLOCK] = pick(wanted == places)

        def use(turn, step):
            weights = weight[pl.ds(step * GROUP, GROUP)].reshape(GROUP * width, width)
            hidden[...] += dot(columns[turn], weights)

        def place(turn, step):
            for part in range(GROUP):
                found = dot(
                    pickers[turn, part * rows : (part + 1) * rows, :BLOCK], side_by_side[...]
                )
                code = nb_cols[step * GROUP + part].astype(jnp.float32)
                second = jnp.concatenate([code] * (width // 128), axis=1) < 0
                columns[turn, :, part * width : (part + 1) * width] = jnp.where(
                    second, found[:, width:], found[:, :width]
                ).astype(jnp.bfloat16)

        run_steps(0, offsets // GROUP, build, place, use, no_slot)

    def build_spread(neighbours, offset_of):
        places = counting((BLOCK, rows), 0)

        def build(turn, step):
            for part in range(PAIR):
                wanted = neighbours[pl.ds(offset_of(PAIR * step + part), 1), :]
                wanted = wanted.astype(jnp.float32)
                for first in range(0, rows, BLOCK):
                    here = jnp.broadcast_to(wanted - first, (16, rows)).astype(jnp.bfloat16)
                    pickers[turn, part * rows + first : part * rows + first + BLOCK, :] = pick(
                        jnp.concatenate([here] * (BLOCK // 16), axis=0) == places
                    )

        return build

    def no_slot(at, count):
        pass

    def own_of(second):
        if not reduce_here:
            return lambda at: at
        extra = 14 * pair if second else 14 - 14 * pair
        return lambda at: 14 * pair + at + (extra - 14 * pair) * (jnp.int32(at) == 13)

    def put(second, at, product, more):
        for part in range(PAIR):
            value = product[:, part * width : (part + 1) * width]
            if not reduce_here:
                unit = pl.multiple_of((units * second + PAIR * at + part) * width, width)
                grads[pl.ds(unit, width), :] = value
                continue
            c, half = at, part
            if second:
                c, half = units // PAIR - 1 + at + part, 1 - part
            if isinstance(at, int) and PAIR * at + part == units - 1:
                empty = pair if second else 1 - pair
                c, half = chunks - 2 + empty, empty
            value = value.reshape(grads.shape[1:4] + (8, width))
            here_rows = pl.ds(8 * half, 8)
            if more:
                value = value + grads[c, :, :, :, here_rows]
            grads[c, :, :, :, here_rows] = value

    def convolve_back(weight, act_grad, second, own_slot, other_slot):
        def use_of(offset_of, weigh):
            def use(turn, step):
                spread = columns[turn, :, : PAIR * width]
                weights = jnp.concatenate(
                    [weight[offset_of(PAIR * step + part)] for part in range(PAIR)], axis=1
                )
                act_grad[...] += dot_last(spread, weights)
                if weigh:
                    put(second, step, dot(source_t[...], spread), False)

            return use

        steps = units // PAIR
        offset_of = own_of(second)
        build = build_spread(nb_own, offset_of)
        run_steps(0, steps, build, place_spread, use_of(offset_of, True), own_slot)
        if reduce_here:
            if second:
                offset_of = lambda at: 14 - 14 * pair + at
            else:
                offset_of = lambda at: 13 - 13 * pair + at + 14 * pair * (jnp.int32(at) == 13)
            build = build_spread(nb_own, offset_of)
            run_steps(0, steps, build, place_spread, use_of(offset_of, False), other_slot)

    def convolve_pair(second, first_step, last_step, at_slot):
        def use(turn, step):
            spread = columns[turn, :, : PAIR * width]
            put(second, step, dot(pair_source_t[...], spread), True)

        build = build_spread(nb_pair, own_of(second))
        run_steps(first_step, last_step, build, place_spread, use, at_slot)

    core, row = lax.rem(group_me, 2), group_me // 2
    column, plane = lax.rem(dp_me, 2), dp_me // 2
    pair, high = lax.rem(plane, 2), plane // 2
    planes = 4
    core_peer = {"group": group_me + 1 - 2 * core}
    row_peer = {"group": group_me + 2 - 4 * row}
    column_peer = {"dp": dp_me + 1 - 2 * column}
    pair_peer = {"dp": dp_me + 2 - 4 * pair}
    cross_peer = {"dp": dp_me + 4 - 8 * high}
    own = pl.ds(2 * core, 2)
    lane_a, lane_b = 2 * core, 2 * core + 1
    kept_row, given_row = pl.ds(2 * row, 2), pl.ds(2 * (1 - row), 2)

    def send(c, stage, source, target, peer):
        turn = lax.rem(c, RING)
        return pltpu.make_async_remote_copy(
            src_ref=source,
            dst_ref=target,
            send_sem=sum_send.at[turn],
            recv_sem=sum_recv.at[turn, stage],
            device_id=peer,
            device_id_type=MESH,
        )

    def copies_of(c, stage, size):
        both, some = pl.ds(PAIR * c, size), pl.ds(0, 8 * size)
        part = grads.at[c, :, :, :, some]

        def landing(ref, at):
            return ref.at[(at, *[slice(None)] * (len(ref.shape) - 3), some)]

        if stage == 0:
            given = part.at[pl.ds(2 * (1 - core), 2)]
            return [send(c, stage, given, landing(from_core, lax.rem(c, CORE_RING)), core_peer)]
        if stage == 1:
            return [
                send(c, stage, part.at[lane_a, 1 - column], landing(from_first_a, c), column_peer),
                send(c, stage, part.at[lane_b, :, given_row], landing(from_first_b, c), row_peer),
            ]
        if stage == 2:
            return [
                send(c, stage, part.at[lane_a, column, given_row], landing(from_second_a, c), row_peer),
                send(c, stage, part.at[lane_b, 1 - column, kept_row], landing(from_second_b, c), column_peer),
            ]
        if stage == 3:
            given = part.at[own, column, 2 * row + 1 - high]
            return [send(c, stage, given, landing(from_line, c), cross_peer)]
        if stage == 4:
            block = results.at[pair, both, own, column, 2 * row + high]
            return [
                send(
                    c,
                    stage,
                    block,
                    block,
                    {"dp": 2 * lax.rem(plane + step, planes) + column},
                )
                for step in range(1, planes)
            ]
        if stage == 5:
            block_a = results.at[:, both, lane_a, column, kept_row]
            block_b = results.at[:, both, lane_b, column, kept_row]
            return [
                send(c, stage, block_a, block_a, row_peer),
                send(c, stage, block_b, block_b, column_peer),
            ]
        if stage == 6:
            block_a = results.at[:, both, lane_a, column]
            block_b = results.at[:, both, lane_b, :, kept_row]
            return [
                send(c, stage, block_a, block_a, column_peer),
                send(c, stage, block_b, block_b, row_peer),
            ]
        block = results.at[:, both, own]
        return [send(c, stage, block, block, core_peer)]

    def wait_bytes(sem, like):
        pltpu.make_async_copy(like, like, sem).wait()

    def wait_arrived(c, stage, size):
        some = pl.ds(0, 8 * size)
        like = (
            from_core.at[0, :, :, :, some],
            grads.at[c, 0, :, :, some],
            grads.at[c, 0, 0, :, some],
            from_line.at[c, :, some],
            results.at[0, pl.ds(0, 3 * size), 0, 0, pl.ds(0, 2)],
            grads.at[c, 0, :, :, some],
            grads.at[c, pl.ds(0, 2), :, :, some],
            grads.at[c, :, :, :, some],
        )[stage]
        wait_bytes(sum_recv.at[lax.rem(c, RING), stage], like)

    def wait_sent(c, size):
        like = results.at[0, pl.ds(0, 23), 0, pl.ds(0, size)]
        wait_bytes(sum_send.at[lax.rem(c, RING)], like)

    def stage_of(c, stage, size=PAIR):
        if stage > 0:
            wait_arrived(c, stage - 1, size)
        some = slice(0, 8 * size)

        def add(lanes, columns_of, rows_of, landed):
            here_rows = (c, lanes, columns_of, rows_of, some)
            grads[here_rows] = grads[here_rows] + landed

        every = slice(None)
        if stage == 1:
            add(own, every, every, from_core[lax.rem(c, CORE_RING), :, :, :, some])
        if stage == 2:
            add(lane_a, column, every, from_first_a[c, :, some])
            add(lane_b, every, kept_row, from_first_b[c, :, :, some])
        if stage == 3:
            add(lane_a, column, kept_row, from_second_a[c, :, some])
            add(lane_b, column, kept_row, from_second_b[c, :, some])
        if stage == 4:
            mine = 2 * row + high
            add(own, column, mine, from_line[c, :, some])
            for unit in range(size):
                results[pair, PAIR * c + unit, own, column, mine] = grads[
                    c, own, column, mine, 8 * unit : 8 * unit + 8
                ]
        if stage < len(LAGS) - 1:
            for copy in copies_of(c, stage, size):
                copy.start()
        else:
            wait_sent(c, size)

    early = units // PAIR - 1

    def slot(at, last=False):
        if not reduce_here:
            return
        for stage, lag in enumerate(LAGS):
            entry = at - lag
            if isinstance(at, int):
                c = entry if entry < early else max(entry - GAP, early - 1)
                if 0 <= entry < chunks - 1 + GAP and (c == entry or entry >= early + GAP):
                    stage_of(c, stage)
                continue
            second = entry >= early + GAP

            @pl.when(
                ((entry >= 0) & (entry < early)) | (second & (entry < chunks - 1 + GAP))
            )
            def _():
                stage_of(entry - GAP * second.astype(jnp.int32), stage)

            if last:

                @pl.when(entry == chunks - 1 + GAP)
                def _():
                    stage_of(chunks - 1, stage, 1)

    def slot_after(at, count, steps_with, first_slot):
        if isinstance(at, int):
            for number, step in enumerate(steps_with):
                if at <= step < at + count:
                    slot(first_slot + number)
            return
        start, end = first_slot, first_slot
        for step in steps_with:
            start = start + (at > step).astype(jnp.int32)
            end = end + (at + count > step).astype(jnp.int32)

        def one(number, carry):
            slot(number)
            return carry

        lax.fori_loop(start, end, one, 0)

    def swap(at, source, target):
        return pltpu.make_async_remote_copy(
            src_ref=source,
            dst_ref=target,
            send_sem=swap_send.at[at],
            recv_sem=swap_recv.at[at],
            device_id=pair_peer,
            device_id_type=MESH,
        )

    def swap_rows(at):
        return swap(at, swap_out.at[at % 2], swap_in.at[at])

    def start_rows(at, value):
        if reduce_here:
            swap_out[at % 2] = value.astype(jnp.float32)
            swap_rows(at).start()

    places = nb_rows[...]
    codes = jnp.where(places < BLOCK, places, jnp.where(places < rows, BLOCK - 1 - places, 4 * BLOCK))
    side[...] = jnp.zeros_like(side)
    side[:offsets, :] = codes.astype(jnp.float32)
    side[offsets : offsets + down_offsets, :] = down_rows_ref[...].astype(jnp.float32)
    side_cols[...] = side[...].T
    swap_neighbours = swap(4, nb_own, nb_pair)

    spread_fine[...] = fine_ref[...].astype(jnp.float32)
    for k in range(down_offsets):
        child = spread_fine[pl.ds(k % children, rows, stride=children), :]
        there = side_cols[:, offsets + k : offsets + k + 1] < fine_rows
        cols_down[:, k * in_width : (k + 1) * in_width] = jnp.where(there, child, 0.0).astype(
            jnp.bfloat16
        )
    loads[0].wait()
    hid_one[...] = dot(cols_down[...], w_down[...].reshape(down_offsets * in_width, width))

    def spread_neighbours():
        for k in range(offsets):
            nb_cols[k] = jnp.broadcast_to(side_cols[:, k : k + 1], (rows, 128)).astype(jnp.bfloat16)

    pl.semaphore_wait(barrier, len(peers))

    swap_one = swap(0, hid_one, swap_in.at[0])
    swap_two = swap(1, hid_two, swap_in.at[1])

    def start_one():
        nb_own[...] = jnp.full_like(nb_own, rows)
        nb_own[:offsets, :] = nb_rows[...]
        for weight in (w_mid, w_out):
            weight[offsets:] = jnp.zeros_like(weight[offsets:])
        if not reduce_here:
            return
        swap_neighbours.start()
        swap_one.start()

    def start_two():
        swap_two.start()

    beside = (start_one, spread_neighbours)
    center_one, scale_one, total = norm_stats(0, hid_one[...], beside)

    def pre_one(hidden=hid_one):
        normed = (hidden[...] - center_one) * scale_one
        return normed, normed * gain_ref[0:1, :] + bias_ref[0:1, :]

    _, pre = pre_one()
    act_one[...] = jnp.where(live, pre * sigmoid(pre), 0.0)
    act_one_b[...] = act_one[...].astype(jnp.bfloat16)
    loads[1].wait()
    convolve(act_one_b, w_mid, hid_two)
    center_two, scale_two, _ = norm_stats(
        1, hid_two[...], (None, start_two if reduce_here else None)
    )

    def pre_two(hidden=hid_two):
        normed = (hidden[...] - center_two) * scale_two
        return normed, normed * gain_ref[1:2, :] + bias_ref[1:2, :]

    _, pre = pre_two()
    act_two_b[...] = jnp.where(live, pre * sigmoid(pre), 0.0).astype(jnp.bfloat16)
    loads[2].wait()
    convolve(act_two_b, w_out, hid_three)
    def turn_two():
        source_t[...] = act_two_b[...].T

    center_three, scale_three, _ = norm_stats(2, hid_three[...], (turn_two, None))
    loads[3].wait()
    normed_three = (hid_three[...] - center_three) * scale_three
    summed = (
        jnp.where(live, normed_three * gain_ref[2:3, :] + bias_ref[2:3, :], 0.0) + act_one[...]
    )
    sigma = sigmoid(summed)
    features_ref[...] = jnp.where(live, summed * sigma, 0.0).astype(jnp.bfloat16)

    def pair_source(swapped, pre_of, source_at):
        swapped.wait()
        _, pre = pre_of(swap_in.at[source_at])
        pair_source_t[...] = (pre * sigmoid(pre)).astype(jnp.bfloat16).T

    def pair_two():
        if reduce_here:
            pair_source(swap_two, pre_two, 1)

    slope = sigma * (1.0 + summed * (1.0 - sigma))
    act_one[...] = jnp.where(live, cotangent_ref[...].astype(jnp.float32) * slope, 0.0)
    grad_hidden[...] = norm_grad(
        3, 2, act_one[...], normed_three, scale_three, total, (pair_two, None)
    )
    start_rows(2, grad_hidden[...])
    held[...] = grad_hidden[...]
    grad_act[...] = jnp.zeros_like(grad_act)
    steps = units // PAIR

    def receive(hidden_at):
        swap_rows(hidden_at).wait()
        held[...] = swap_in[hidden_at].astype(jnp.bfloat16)

    def pair_halves(second, at_slot):
        middle = (steps + 1) // 2
        return (
            lambda: convolve_pair(second, 0, middle, at_slot),
            lambda: convolve_pair(second, middle, steps, at_slot),
        )

    nothing = (None, None)
    convolve_back(w_out, grad_act, 0, no_slot, no_slot)
    normed, pre = pre_two()
    incoming = jnp.where(live, grad_act[...] * silu_slope(pre), 0.0)
    if reduce_here:
        swap_neighbours.wait()
        receive(2)
    after = lambda at, count: slot_after(at, count, (0, 4), 0)
    beside = pair_halves(0, after) if reduce_here else nothing
    grad_hidden[...] = norm_grad(4, 1, incoming, normed, scale_two, total, beside)
    start_rows(3, grad_hidden[...])
    held[...] = grad_hidden[...]
    grad_act[...] = act_one[...]
    source_t[...] = act_one_b[...].T
    convolve_back(
        w_mid,
        grad_act,
        1,
        lambda at, count: slot_after(at, count, (0, 5), 2),
        lambda at, count: slot_after(at, count, (1, 3, 5), 4),
    )
    normed, pre = pre_one()
    incoming = jnp.where(live, grad_act[...] * silu_slope(pre), 0.0)
    if reduce_here:
        pair_source(swap_one, pre_one, 0)
        receive(3)
    after = lambda at, count: slot_after(at, count, (0, 1, 3, 5, 6), 7)
    beside = pair_halves(1, after) if reduce_here else nothing
    grad_hidden[...] = norm_grad(5, 0, incoming, normed, scale_one, total, beside)
    down_rows = down_offsets * in_width
    if reduce_here:
        down_all[...] = dot(cols_down[...].T, grad_hidden[...])
        kept = down_rows // 2
        swap_down = swap(
            5, down_all.at[pl.ds(pl.multiple_of(kept * (1 - pair), kept), kept), :], down_got
        )
        swap_down.start()
    else:
        grads[2 * units * width :, :] = dot(cols_down[...].T, grad_hidden[...])
    slot(12)
    for child in range(children):
        total_child = jnp.zeros((rows, in_width), jnp.float32)
        for k in range(child, down_offsets, children):
            there = side_cols[:, offsets + k : offsets + k + 1] < fine_rows
            total_child += jnp.where(there, dot_last(grad_hidden[...], w_down[k]), 0.0)
        spread_fine[pl.ds(child, rows, stride=children), :] = total_child
    fine_grad_ref[...] = spread_fine[...].astype(jnp.bfloat16)
    slot(13)

    if reduce_here:

        def final(at, carry):
            slot(at, True)
            return carry

        swap_down.wait()
        for part in range(PAIR):
            total_down = (
                down_all[pl.ds(pl.multiple_of(kept * pair + part * width, width), width), :]
                + down_got[part * width : (part + 1) * width, :]
            )
            half = 1 - part
            grads[chunks - 2 + part, :, :, :, 8 * half : 8 * half + 8] = total_down.reshape(
                grads.shape[1:4] + (8, width)
            )
        lax.fori_loop(chunks - 2 + GAP, chunks + GAP + LAGS[-1], final, 0)
    else:
        store = pltpu.make_async_copy(grads, results, load_sem.at[0])
        store.start()
        store.wait()


def place_kernel(
    features_ref,
    fine_grad_ref,
    grads_ref,
    gain_ref,
    bias_ref,
    features_out,
    fine_grad_out,
    grad_down_out,
    grad_mid_out,
    grad_out_out,
    gain_out,
    bias_out,
    sem,
):
    half = grad_mid_out.shape[0] // 2
    moves = []
    for at, target in enumerate((grad_out_out, grad_mid_out)):
        for pair in range(2):
            for first in range(0, half, 3):
                count = min(3, half - first)
                here = grads_ref.at[pair, pl.ds(at * half + first, count)]
                moves.append((here, target.at[pl.ds((half + 1) * pair + first, count)]))
        moves.append((grads_ref.at[1 - at, pl.ds(2 * half, 1)], target.at[pl.ds(half, 1)]))
    for pair in range(2):
        down_units = grad_down_out.shape[0] // 2
        here = grads_ref.at[pair, pl.ds(2 * half + 1, down_units)]
        moves.append((here, grad_down_out.at[pl.ds(pair * down_units, down_units)]))
    copies = [
        pltpu.make_async_copy(source, target, sem.at[at])
        for at, (source, target) in enumerate(moves)
    ]
    for copy in copies:
        copy.start()
    features_out[...] = features_ref[...]
    fine_grad_out[...] = fine_grad_ref[...]
    gain_out[...] = gain_ref[...]
    bias_out[...] = bias_ref[...]
    for copy in copies:
        copy.wait()


def per_device(
    dp_size,
    group_size,
    fine_features,
    down_map,
    neighbours,
    voxel_counts,
    down_weight,
    mid_weight,
    out_weight,
    norm_gain,
    norm_bias,
    cotangent,
):
    rows, width = cotangent.shape
    fine_rows, in_width = fine_features.shape
    offsets = neighbours.shape[1]
    down_offsets = down_map.shape[1]
    f32, bf16, i32 = jnp.float32, jnp.bfloat16, jnp.int32
    vmem = pl.BlockSpec(memory_space=pltpu.VMEM)
    smem = pl.BlockSpec(memory_space=pltpu.SMEM)
    hbm = pl.BlockSpec(memory_space=pl.ANY)
    shape = jax.ShapeDtypeStruct
    reduce_here = dp_size == 8 and group_size == 4
    result = pltpu.VMEM if reduce_here else shape
    near_size, far_size = (dp_size * group_size, 1) if reduce_here else (group_size, dp_size)
    share = 2 if reduce_here else 1
    units = (offsets + 1) // 2 * 2 // share
    all_units = 2 * units + down_offsets * in_width // (share * width)
    grad_rows = all_units * width
    chunks = all_units // PAIR
    padded = (offsets + 1) // 2 * 2
    features, fine_grad, grads, gain_grad, bias_grad = pl.pallas_call(
        functools.partial(kernel, dp_size, group_size, reduce_here),
        out_shape=(
            result((rows, width), bf16),
            result((fine_rows, in_width), bf16),
            pltpu.VMEM((2, all_units, *GROUPS, 8, width), f32)
            if reduce_here
            else shape((grad_rows, width), f32),
            result(norm_gain.shape, f32),
            result(norm_bias.shape, f32),
        ),
        in_specs=[vmem, vmem, vmem, smem, hbm, hbm, hbm, vmem, vmem, hbm],
        out_specs=(vmem, vmem, vmem if reduce_here else hbm, vmem, vmem),
        scratch_shapes=[
            pltpu.VMEM(down_weight.shape, bf16),
            pltpu.VMEM((padded, width, width), bf16),
            pltpu.VMEM((padded, width, width), bf16),
            pltpu.VMEM((rows, width), bf16),
            pltpu.VMEM((fine_rows, in_width), f32),
            pltpu.VMEM((rows, down_offsets * in_width), bf16),
            pltpu.VMEM((offsets, rows, 128), bf16),
            pltpu.VMEM((2, GROUP * rows, rows), bf16),
            pltpu.VMEM((2, rows, GROUP * width), bf16),
            pltpu.VMEM((BLOCK, 2 * width), bf16),
            pltpu.VMEM((rows, width), f32),
            pltpu.VMEM((rows, width), bf16),
            pltpu.VMEM((rows, width), bf16),
            pltpu.VMEM((rows, width), f32),
            pltpu.VMEM((rows, width), f32),
            pltpu.VMEM((rows, width), f32),
            pltpu.VMEM((rows, width), bf16),
            pltpu.VMEM((rows, width), bf16),
            pltpu.VMEM((width, rows), bf16),
            pltpu.VMEM((width, rows), bf16),
            pltpu.VMEM((rows, width), f32),
            pltpu.VMEM((128, rows), f32),
            pltpu.VMEM((rows, 128), f32),
            pltpu.VMEM((padded, rows), i32),
            pltpu.VMEM((padded, rows), i32),
            pltpu.VMEM((2, rows, width), f32),
            pltpu.VMEM((4, rows, width), f32),
            pltpu.VMEM((down_offsets * in_width, width), f32),
            pltpu.VMEM((down_offsets * in_width // 2, width), f32),
            pltpu.VMEM(
                (chunks, *GROUPS, 8 * PAIR, width) if reduce_here else (grad_rows, width), f32
            ),
            pltpu.VMEM((CORE_RING, 2, *GROUPS[1:], 8 * PAIR, width), f32),
            pltpu.VMEM((chunks, GROUPS[2], 8 * PAIR, width), f32),
            pltpu.VMEM((chunks, GROUPS[1], 2, 8 * PAIR, width), f32),
            pltpu.VMEM((chunks, 2, 8 * PAIR, width), f32),
            pltpu.VMEM((chunks, 2, 8 * PAIR, width), f32),
            pltpu.VMEM((chunks, 2, 8 * PAIR, width), f32),
            pltpu.VMEM((6, near_size, 8, width // 2), f32),
            pltpu.VMEM((6, far_size, 8, width // 2), f32),
            pltpu.SemaphoreType.DMA((4,)),
            pltpu.SemaphoreType.DMA((RING,)),
            pltpu.SemaphoreType.DMA((RING, len(LAGS) - 1)),
            pltpu.SemaphoreType.DMA((6,)),
            pltpu.SemaphoreType.DMA((6,)),
            pltpu.SemaphoreType.DMA((6, group_size - 1)),
            pltpu.SemaphoreType.DMA((6, group_size - 1)),
            pltpu.SemaphoreType.DMA((6, far_size)),
            pltpu.SemaphoreType.DMA((6, far_size)),
        ],
        compiler_params=pltpu.CompilerParams(
            collective_id=0, has_side_effects=True, vmem_limit_bytes=(46 if reduce_here else 60) * 1024 * 1024
        ),
    )(
        fine_features,
        down_map.T,
        neighbours.T,
        voxel_counts,
        down_weight,
        mid_weight,
        out_weight,
        norm_gain,
        norm_bias,
        cotangent,
    )
    if not reduce_here:
        grads = lax.psum(grads, ("dp", "group"))
        middle, end = offsets * width, 2 * padded * width
        grad_out = grads[:middle].reshape(out_weight.shape)
        grad_mid = grads[padded * width : padded * width + middle].reshape(mid_weight.shape)
        grad_down = grads[end:].reshape(down_weight.shape)
        return (features, fine_grad, grad_down, grad_mid, grad_out, gain_grad, bias_grad)
    held = [
        pltpu.with_memory_space_constraint(value, pltpu.VMEM)
        for value in (features, fine_grad, grads, gain_grad, bias_grad)
    ]
    features, fine_grad, grad_down, grad_mid, grad_out, gain_grad, bias_grad = pl.pallas_call(
        place_kernel,
        out_shape=(
            shape(features.shape, bf16),
            shape(fine_grad.shape, bf16),
            shape((down_offsets * in_width // width, *GROUPS, 8, width), f32),
            shape((offsets, *GROUPS, 8, width), f32),
            shape((offsets, *GROUPS, 8, width), f32),
            shape(norm_gain.shape, f32),
            shape(norm_bias.shape, f32),
        ),
        in_specs=[vmem] * 5,
        out_specs=(vmem, vmem, hbm, hbm, hbm, vmem, vmem),
        scratch_shapes=[pltpu.SemaphoreType.DMA((24,))],
        compiler_params=pltpu.CompilerParams(vmem_limit_bytes=8 * 1024 * 1024),
    )(*held)
    grad_down = grad_down.reshape(down_weight.shape)
    grad_mid = grad_mid.reshape(mid_weight.shape)
    grad_out = grad_out.reshape(out_weight.shape)
    return (features, fine_grad, grad_down, grad_mid, grad_out, gain_grad, bias_grad)


def solution(mesh):
    in_specs = (
        P(("dp", "group"), None),
        P(("dp", "group"), None),
        P(("dp", "group"), None),
        P(("dp", "group")),
        P(),
        P(),
        P(),
        P(),
        P(),
        P(("dp", "group"), None),
    )
    out_specs = (P(("dp", "group"), None), P(("dp", "group"), None), P(), P(), P(), P(), P())
    return jax.shard_map(
        functools.partial(per_device, mesh.shape["dp"], mesh.shape["group"]),
        mesh=mesh,
        in_specs=in_specs,
        out_specs=out_specs,
        check_vma=False,
    )
```

```python
import functools

import jax
import jax.numpy as jnp
from jax import lax
from jax.experimental import pallas as pl
from jax.experimental.pallas import tpu as pltpu
from jax.sharding import PartitionSpec as P

eps_norm = 1e-05
MESH = pl.DeviceIdType.MESH
GROUP = 3
BLOCK = 256
PAIR = 2
GROUPS = (4, 2, 4)
GAP = 1
LAGS = (0, 1, 2, 3, 5, 7, 8, 10, 11)
RING = 16
CORE_RING = 8


def sigmoid(value):
    return 0.5 + 0.5 * jnp.tanh(0.5 * value)


def silu_slope(value):
    sigma = sigmoid(value)
    return sigma * (1.0 + value * (1.0 - sigma))


def dot(left, right):
    return jnp.dot(left, right, preferred_element_type=jnp.float32)


def dot_last(left, right):
    return lax.dot_general(
        left, right, (((1,), (1,)), ((), ())), preferred_element_type=jnp.float32
    )


def kernel(
    dp_size,
    group_size,
    reduce_here,
    fine_ref,
    down_rows_ref,
    nb_rows,
    count_ref,
    down_hbm,
    mid_hbm,
    out_hbm,
    gain_ref,
    bias_ref,
    cotangent_hbm,
    features_ref,
    fine_grad_ref,
    results,
    gain_grad_ref,
    bias_grad_ref,
    w_down,
    w_mid,
    w_out,
    cotangent_ref,
    spread_fine,
    cols_down,
    nb_cols,
    pickers,
    columns,
    side_by_side,
    act_one,
    act_one_b,
    act_two_b,
    hid_one,
    hid_two,
    hid_three,
    held,
    grad_hidden,
    source_t,
    pair_source_t,
    grad_act,
    side,
    side_cols,
    nb_own,
    nb_pair,
    swap_out,
    swap_in,
    down_all,
    down_got,
    grads,
    from_core,
    from_first_a,
    from_first_b,
    from_second_a,
    from_second_b,
    from_line,
    near,
    far,
    load_sem,
    sum_send,
    sum_recv,
    swap_send,
    swap_recv,
    near_send,
    near_recv,
    far_send,
    far_recv,
):
    rows, width = cotangent_hbm.shape
    offsets = nb_rows.shape[0]
    fine_rows, in_width = fine_ref.shape
    children = fine_rows // rows
    down_offsets = down_rows_ref.shape[0]
    units = (offsets + 1) // 2 * (1 if reduce_here else 2)
    chunks = grads.shape[0]
    dp_me = lax.axis_index("dp")
    group_me = lax.axis_index("group")

    loads = [
        pltpu.make_async_copy(source, target, load_sem.at[at])
        for at, (source, target) in enumerate(
            (
                (down_hbm, w_down),
                (mid_hbm, w_mid.at[pl.ds(0, offsets)]),
                (out_hbm, w_out.at[pl.ds(0, offsets)]),
                (cotangent_hbm, cotangent_ref),
            )
        )
    ]
    for load in loads:
        load.start()

    direct = reduce_here
    peers = [
        {
            "dp": lax.rem(dp_me + dp_step, dp_size),
            "group": lax.rem(group_me + group_step, group_size),
        }
        for dp_step in reversed(range(dp_size))
        for group_step in reversed(range(group_size))
        if (dp_step or group_step) and (direct or not dp_step or not group_step)
    ]
    barrier = pltpu.get_barrier_semaphore()
    for peer in peers:
        pl.semaphore_signal(barrier, inc=1, device_id=peer, device_id_type=MESH)

    def share(at, axis, me, size, slots, send, recv):
        copies = []
        for step in range(1, size):
            copies.append(
                pltpu.make_async_remote_copy(
                    src_ref=slots.at[at, me],
                    dst_ref=slots.at[at, me],
                    send_sem=send.at[at, step - 1],
                    recv_sem=recv.at[at, step - 1],
                    device_id={axis: lax.rem(me + step, size)},
                    device_id_type=MESH,
                )
            )
        for copy in copies:
            copy.start()
        return copies

    def exchange_direct(at, block, combine, meanwhile):
        me = dp_me * group_size + group_me
        near[at, me] = block
        for peer in peers:
            pltpu.make_async_remote_copy(
                src_ref=near.at[at, me],
                dst_ref=near.at[at, me],
                send_sem=near_send.at[at, 0],
                recv_sem=near_recv.at[at, 0],
                device_id=peer,
                device_id_type=MESH,
            ).start()
        for work in meanwhile:
            if work is not None:
                work()
        others = near.at[at, pl.ds(0, len(peers))]
        for sem in (near_recv, near_send):
            pltpu.make_async_copy(others, others, sem.at[at, 0]).wait()
        return combine([near[at, slot] for slot in range(len(peers) + 1)])

    def exchange(at, block, combine, meanwhile=(None, None)):
        if direct and at < 4:
            return exchange_direct(at, block, combine, meanwhile)
        near[at, group_me] = block
        copies = share(at, "group", group_me, group_size, near, near_send, near_recv)
        if meanwhile[0] is not None:
            meanwhile[0]()
        for copy in copies:
            copy.wait()
        far[at, dp_me] = combine([near[at, slot] for slot in range(group_size)])
        copies = share(at, "dp", dp_me, dp_size, far, far_send, far_recv)
        if meanwhile[1] is not None:
            meanwhile[1]()
        for copy in copies:
            copy.wait()
        return combine([far[at, slot] for slot in range(dp_size)])

    lanes = width // 2

    def stack(first, second, third):
        filler = jnp.zeros((2, lanes), jnp.float32)
        return jnp.concatenate([first, second, third, filler], axis=0)

    def fold(value):
        return jnp.concatenate([value[:, :lanes], value[:, lanes:]], axis=0)

    def unfold(value):
        return jnp.concatenate([value[0:1], value[1:2]], axis=1)

    def add_all(blocks):
        total = blocks[0]
        for block in blocks[1:]:
            total = total + block
        return total

    def merge_all(blocks):
        count = add_all([block[4:6] for block in blocks])
        center = add_all([block[4:6] * block[0:2] for block in blocks]) / count
        squares = add_all(
            [
                block[2:4] + block[4:6] * (block[0:2] - center) * (block[0:2] - center)
                for block in blocks
            ]
        )
        return stack(center, squares, count)

    count = count_ref[0]
    own_count = jnp.full((1, width), count.astype(jnp.float32))
    live = lax.broadcasted_iota(jnp.int32, (rows, width), 0) < count

    def norm_stats(at, hidden, meanwhile=(None, None)):
        center = jnp.sum(hidden, axis=0, keepdims=True) / own_count
        centered = jnp.where(live, hidden - center, 0.0)
        squares = jnp.sum(centered * centered, axis=0, keepdims=True)
        merged = exchange(
            at, stack(fold(center), fold(squares), fold(own_count)), merge_all, meanwhile
        )
        total = unfold(merged[4:6])
        scale = lax.rsqrt(unfold(merged[2:4]) / total + eps_norm)
        return unfold(merged[0:2]), scale, total

    def norm_grad(at, norm, incoming, normed, scale, total, meanwhile=(None, None)):
        shift_sum = fold(jnp.sum(incoming, axis=0, keepdims=True))
        scale_sum = fold(jnp.sum(incoming * normed, axis=0, keepdims=True))
        summed = exchange(
            at, stack(shift_sum, scale_sum, jnp.zeros_like(shift_sum)), add_all, meanwhile
        )
        shift_sum, scale_sum = unfold(summed[0:2]), unfold(summed[2:4])
        bias_grad_ref[norm : norm + 1, :] = shift_sum
        gain_grad_ref[norm : norm + 1, :] = scale_sum
        hidden_grad = (
            scale
            * gain_ref[norm : norm + 1, :]
            * (incoming - shift_sum / total - normed * (scale_sum / total))
        )
        return jnp.where(live, hidden_grad, 0.0).astype(jnp.bfloat16)

    def pick(mask):
        return jnp.where(mask, jnp.bfloat16(1), jnp.bfloat16(0))

    def counting(shape, axis):
        return lax.broadcasted_iota(jnp.int32, shape, axis).astype(jnp.float32).astype(jnp.bfloat16)

    def place_spread(turn, step):
        picked = dot(pickers[turn, : PAIR * rows, :], held[...]).astype(jnp.bfloat16)
        for part in range(PAIR):
            columns[turn, :, part * width : (part + 1) * width] = picked[
                part * rows : (part + 1) * rows
            ]

    def run_steps(first, last, build, place, use, after):
        build(first % 2, first)

        def one(turn, step, more):
            place(turn, step)
            if more:
                build(1 - turn, step + 1)
            use(turn, step)

        bodies = (last - first - 1) // 2

        def body(at, carry):
            for turn in range(2):
                one((first + turn) % 2, first + 2 * at + turn, True)
            after(first + 2 * at, 2)
            return carry

        lax.fori_loop(0, bodies, body, 0)
        for step in range(first + 2 * bodies, last):
            one(step % 2, step, step + 1 < last)
            after(step, 1)

    def convolve(source, weight, hidden):
        places = counting((rows, BLOCK), 1)
        hidden[...] = jnp.zeros_like(hidden)
        for block in range(2):
            side_by_side[:, block * width : (block + 1) * width] = source[
                block * BLOCK : (block + 1) * BLOCK, :
            ]

        def build(turn, step):
            for part in range(GROUP):
                code = nb_cols[step * GROUP + part]
                wanted = jnp.concatenate([jnp.maximum(code, -1 - code)] * (BLOCK // 128), axis=1)
                pickers[turn, part * rows : (part + 1) * rows, :BLOCK] = pick(wanted == places)

        def use(turn, step):
            weights = weight[pl.ds(step * GROUP, GROUP)].reshape(GROUP * width, width)
            hidden[...] += dot(columns[turn], weights)

        def place(turn, step):
            for part in range(GROUP):
                found = dot(
                    pickers[turn, part * rows : (part + 1) * rows, :BLOCK], side_by_side[...]
                )
                code = nb_cols[step * GROUP + part].astype(jnp.float32)
                second = jnp.concatenate([code] * (width // 128), axis=1) < 0
                columns[turn, :, part * width : (part + 1) * width] = jnp.where(
                    second, found[:, width:], found[:, :width]
                ).astype(jnp.bfloat16)

        run_steps(0, offsets // GROUP, build, place, use, no_slot)

    def build_spread(neighbours, offset_of):
        places = counting((BLOCK, rows), 0)

        def build(turn, step):
            for part in range(PAIR):
                wanted = neighbours[pl.ds(offset_of(PAIR * step + part), 1), :]
                wanted = wanted.astype(jnp.float32)
                for first in range(0, rows, BLOCK):
                    here = jnp.broadcast_to(wanted - first, (16, rows)).astype(jnp.bfloat16)
                    pickers[turn, part * rows + first : part * rows + first + BLOCK, :] = pick(
                        jnp.concatenate([here] * (BLOCK // 16), axis=0) == places
                    )

        return build

    def no_slot(at, count):
        pass

    def own_of(second):
        if not reduce_here:
            return lambda at: at
        extra = 14 * pair if second else 14 - 14 * pair
        return lambda at: 14 * pair + at + (extra - 14 * pair) * (jnp.int32(at) == 13)

    def put(second, at, product, more):
        for part in range(PAIR):
            value = product[:, part * width : (part + 1) * width]
            if not reduce_here:
                unit = pl.multiple_of((units * second + PAIR * at + part) * width, width)
                grads[pl.ds(unit, width), :] = value
                continue
            c, half = at, part
            if second:
                c, half = units // PAIR - 1 + at + part, 1 - part
            if isinstance(at, int) and PAIR * at + part == units - 1:
                empty = pair if second else 1 - pair
                c, half = chunks - 2 + empty, empty
            value = value.reshape(grads.shape[1:4] + (8, width))
            here_rows = pl.ds(8 * half, 8)
            if more:
                value = value + grads[c, :, :, :, here_rows]
            grads[c, :, :, :, here_rows] = value

    def convolve_back(weight, act_grad, second, own_slot, other_slot):
        def use_of(offset_of, weigh):
            def use(turn, step):
                spread = columns[turn, :, : PAIR * width]
                weights = jnp.concatenate(
                    [weight[offset_of(PAIR * step + part)] for part in range(PAIR)], axis=1
                )
                act_grad[...] += dot_last(spread, weights)
                if weigh:
                    put(second, step, dot(source_t[...], spread), False)

            return use

        steps = units // PAIR
        offset_of = own_of(second)
        build = build_spread(nb_own, offset_of)
        run_steps(0, steps, build, place_spread, use_of(offset_of, True), own_slot)
        if reduce_here:
            if second:
                offset_of = lambda at: 14 - 14 * pair + at
            else:
                offset_of = lambda at: 13 - 13 * pair + at + 14 * pair * (jnp.int32(at) == 13)
            build = build_spread(nb_own, offset_of)
            run_steps(0, steps, build, place_spread, use_of(offset_of, False), other_slot)

    def convolve_pair(second, first_step, last_step, at_slot):
        def use(turn, step):
            spread = columns[turn, :, : PAIR * width]
            put(second, step, dot(pair_source_t[...], spread), True)

        build = build_spread(nb_pair, own_of(second))
        run_steps(first_step, last_step, build, place_spread, use, at_slot)

    core, row = lax.rem(group_me, 2), group_me // 2
    column, plane = lax.rem(dp_me, 2), dp_me // 2
    pair, high = lax.rem(plane, 2), plane // 2
    planes = 4
    core_peer = {"group": group_me + 1 - 2 * core}
    row_peer = {"group": group_me + 2 - 4 * row}
    column_peer = {"dp": dp_me + 1 - 2 * column}
    pair_peer = {"dp": dp_me + 2 - 4 * pair}
    cross_peer = {"dp": dp_me + 4 - 8 * high}
    own = pl.ds(2 * core, 2)
    lane_a, lane_b = 2 * core, 2 * core + 1
    kept_row, given_row = pl.ds(2 * row, 2), pl.ds(2 * (1 - row), 2)

    def send(c, stage, source, target, peer):
        turn = lax.rem(c, RING)
        return pltpu.make_async_remote_copy(
            src_ref=source,
            dst_ref=target,
            send_sem=sum_send.at[turn],
            recv_sem=sum_recv.at[turn, stage],
            device_id=peer,
            device_id_type=MESH,
        )

    def copies_of(c, stage, size):
        both, some = pl.ds(PAIR * c, size), pl.ds(0, 8 * size)
        part = grads.at[c, :, :, :, some]

        def landing(ref, at):
            return ref.at[(at, *[slice(None)] * (len(ref.shape) - 3), some)]

        if stage == 0:
            given = part.at[pl.ds(2 * (1 - core), 2)]
            return [send(c, stage, given, landing(from_core, lax.rem(c, CORE_RING)), core_peer)]
        if stage == 1:
            return [
                send(c, stage, part.at[lane_a, 1 - column], landing(from_first_a, c), column_peer),
                send(c, stage, part.at[lane_b, :, given_row], landing(from_first_b, c), row_peer),
            ]
        if stage == 2:
            return [
                send(c, stage, part.at[lane_a, column, given_row], landing(from_second_a, c), row_peer),
                send(c, stage, part.at[lane_b, 1 - column, kept_row], landing(from_second_b, c), column_peer),
            ]
        if stage == 3:
            given = part.at[own, column, 2 * row + 1 - high]
            return [send(c, stage, given, landing(from_line, c), cross_peer)]
        if stage == 4:
            block = results.at[pair, both, own, column, 2 * row + high]
            return [
                send(
                    c,
                    stage,
                    block,
                    block,
                    {"dp": 2 * lax.rem(plane + step, planes) + column},
                )
                for step in range(1, planes)
            ]
        if stage == 5:
            block_a = results.at[:, both, lane_a, column, kept_row]
            block_b = results.at[:, both, lane_b, column, kept_row]
            return [
                send(c, stage, block_a, block_a, row_peer),
                send(c, stage, block_b, block_b, column_peer),
            ]
        if stage == 6:
            block_a = results.at[:, both, lane_a, column]
            block_b = results.at[:, both, lane_b, :, kept_row]
            return [
                send(c, stage, block_a, block_a, column_peer),
                send(c, stage, block_b, block_b, row_peer),
            ]
        block = results.at[:, both, own]
        return [send(c, stage, block, block, core_peer)]

    def wait_bytes(sem, like):
        pltpu.make_async_copy(like, like, sem).wait()

    def wait_arrived(c, stage, size):
        some = pl.ds(0, 8 * size)
        like = (
            from_core.at[0, :, :, :, some],
            grads.at[c, 0, :, :, some],
            grads.at[c, 0, 0, :, some],
            from_line.at[c, :, some],
            results.at[0, pl.ds(0, 3 * size), 0, 0, pl.ds(0, 2)],
            grads.at[c, 0, :, :, some],
            grads.at[c, pl.ds(0, 2), :, :, some],
            grads.at[c, :, :, :, some],
        )[stage]
        wait_bytes(sum_recv.at[lax.rem(c, RING), stage], like)

    def wait_sent(c, size):
        like = results.at[0, pl.ds(0, 23), 0, pl.ds(0, size)]
        wait_bytes(sum_send.at[lax.rem(c, RING)], like)

    def stage_of(c, stage, size=PAIR):
        if stage > 0:
            wait_arrived(c, stage - 1, size)
        some = slice(0, 8 * size)

        def add(lanes, columns_of, rows_of, landed):
            here_rows = (c, lanes, columns_of, rows_of, some)
            grads[here_rows] = grads[here_rows] + landed

        every = slice(None)
        if stage == 1:
            add(own, every, every, from_core[lax.rem(c, CORE_RING), :, :, :, some])
        if stage == 2:
            add(lane_a, column, every, from_first_a[c, :, some])
            add(lane_b, every, kept_row, from_first_b[c, :, :, some])
        if stage == 3:
            add(lane_a, column, kept_row, from_second_a[c, :, some])
            add(lane_b, column, kept_row, from_second_b[c, :, some])
        if stage == 4:
            mine = 2 * row + high
            add(own, column, mine, from_line[c, :, some])
            for unit in range(size):
                results[pair, PAIR * c + unit, own, column, mine] = grads[
                    c, own, column, mine, 8 * unit : 8 * unit + 8
                ]
        if stage < len(LAGS) - 1:
            for copy in copies_of(c, stage, size):
                copy.start()
        else:
            wait_sent(c, size)

    early = units // PAIR - 1

    def slot(at, last=False):
        if not reduce_here:
            return
        for stage, lag in enumerate(LAGS):
            entry = at - lag
            if isinstance(at, int):
                c = entry if entry < early else max(entry - GAP, early - 1)
                if 0 <= entry < chunks - 1 + GAP and (c == entry or entry >= early + GAP):
                    stage_of(c, stage)
                continue
            second = entry >= early + GAP

            @pl.when(
                ((entry >= 0) & (entry < early)) | (second & (entry < chunks - 1 + GAP))
            )
            def _():
                stage_of(entry - GAP * second.astype(jnp.int32), stage)

            if last:

                @pl.when(entry == chunks - 1 + GAP)
                def _():
                    stage_of(chunks - 1, stage, 1)

    def slot_after(at, count, steps_with, first_slot):
        if isinstance(at, int):
            for number, step in enumerate(steps_with):
                if at <= step < at + count:
                    slot(first_slot + number)
            return
        start, end = first_slot, first_slot
        for step in steps_with:
            start = start + (at > step).astype(jnp.int32)
            end = end + (at + count > step).astype(jnp.int32)

        def one(number, carry):
            slot(number)
            return carry

        lax.fori_loop(start, end, one, 0)

    def swap(at, source, target):
        return pltpu.make_async_remote_copy(
            src_ref=source,
            dst_ref=target,
            send_sem=swap_send.at[at],
            recv_sem=swap_recv.at[at],
            device_id=pair_peer,
            device_id_type=MESH,
        )

    def swap_rows(at):
        return swap(at, swap_out.at[at % 2], swap_in.at[at])

    def start_rows(at, value):
        if reduce_here:
            swap_out[at % 2] = value.astype(jnp.float32)
            swap_rows(at).start()

    places = nb_rows[...]
    codes = jnp.where(places < BLOCK, places, jnp.where(places < rows, BLOCK - 1 - places, 4 * BLOCK))
    side[...] = jnp.zeros_like(side)
    side[:offsets, :] = codes.astype(jnp.float32)
    side[offsets : offsets + down_offsets, :] = down_rows_ref[...].astype(jnp.float32)
    side_cols[...] = side[...].T
    swap_neighbours = swap(4, nb_own, nb_pair)

    spread_fine[...] = fine_ref[...].astype(jnp.float32)
    for k in range(down_offsets):
        child = spread_fine[pl.ds(k % children, rows, stride=children), :]
        there = side_cols[:, offsets + k : offsets + k + 1] < fine_rows
        cols_down[:, k * in_width : (k + 1) * in_width] = jnp.where(there, child, 0.0).astype(
            jnp.bfloat16
        )
    loads[0].wait()
    hid_one[...] = dot(cols_down[...], w_down[...].reshape(down_offsets * in_width, width))

    def spread_neighbours():
        for k in range(offsets):
            nb_cols[k] = jnp.broadcast_to(side_cols[:, k : k + 1], (rows, 128)).astype(jnp.bfloat16)

    pl.semaphore_wait(barrier, len(peers))

    swap_one = swap(0, hid_one, swap_in.at[0])
    swap_two = swap(1, hid_two, swap_in.at[1])

    def start_one():
        nb_own[...] = jnp.full_like(nb_own, rows)
        nb_own[:offsets, :] = nb_rows[...]
        for weight in (w_mid, w_out):
            weight[offsets:] = jnp.zeros_like(weight[offsets:])
        if not reduce_here:
            return
        swap_neighbours.start()
        swap_one.start()

    def start_two():
        swap_two.start()

    beside = (start_one, spread_neighbours)
    center_one, scale_one, total = norm_stats(0, hid_one[...], beside)

    def pre_one(hidden=hid_one):
        normed = (hidden[...] - center_one) * scale_one
        return normed, normed * gain_ref[0:1, :] + bias_ref[0:1, :]

    _, pre = pre_one()
    act_one[...] = jnp.where(live, pre * sigmoid(pre), 0.0)
    act_one_b[...] = act_one[...].astype(jnp.bfloat16)
    loads[1].wait()
    convolve(act_one_b, w_mid, hid_two)
    center_two, scale_two, _ = norm_stats(
        1, hid_two[...], (None, start_two if reduce_here else None)
    )

    def pre_two(hidden=hid_two):
        normed = (hidden[...] - center_two) * scale_two
        return normed, normed * gain_ref[1:2, :] + bias_ref[1:2, :]

    _, pre = pre_two()
    act_two_b[...] = jnp.where(live, pre * sigmoid(pre), 0.0).astype(jnp.bfloat16)
    loads[2].wait()
    convolve(act_two_b, w_out, hid_three)
    def turn_two():
        source_t[...] = act_two_b[...].T

    center_three, scale_three, _ = norm_stats(2, hid_three[...], (turn_two, None))
    loads[3].wait()
    normed_three = (hid_three[...] - center_three) * scale_three
    summed = (
        jnp.where(live, normed_three * gain_ref[2:3, :] + bias_ref[2:3, :], 0.0) + act_one[...]
    )
    sigma = sigmoid(summed)
    features_ref[...] = jnp.where(live, summed * sigma, 0.0).astype(jnp.bfloat16)

    def pair_source(swapped, pre_of, source_at):
        swapped.wait()
        _, pre = pre_of(swap_in.at[source_at])
        pair_source_t[...] = (pre * sigmoid(pre)).astype(jnp.bfloat16).T

    def pair_two():
        if reduce_here:
            pair_source(swap_two, pre_two, 1)

    slope = sigma * (1.0 + summed * (1.0 - sigma))
    act_one[...] = jnp.where(live, cotangent_ref[...].astype(jnp.float32) * slope, 0.0)
    grad_hidden[...] = norm_grad(
        3, 2, act_one[...], normed_three, scale_three, total, (pair_two, None)
    )
    start_rows(2, grad_hidden[...])
    held[...] = grad_hidden[...]
    grad_act[...] = jnp.zeros_like(grad_act)
    steps = units // PAIR

    def receive(hidden_at):
        swap_rows(hidden_at).wait()
        held[...] = swap_in[hidden_at].astype(jnp.bfloat16)

    def pair_halves(second, at_slot):
        middle = (steps + 1) // 2
        return (
            lambda: convolve_pair(second, 0, middle, at_slot),
            lambda: convolve_pair(second, middle, steps, at_slot),
        )

    nothing = (None, None)
    convolve_back(w_out, grad_act, 0, no_slot, no_slot)
    normed, pre = pre_two()
    incoming = jnp.where(live, grad_act[...] * silu_slope(pre), 0.0)
    if reduce_here:
        swap_neighbours.wait()
        receive(2)
    after = lambda at, count: slot_after(at, count, (0, 4), 0)
    beside = pair_halves(0, after) if reduce_here else nothing
    grad_hidden[...] = norm_grad(4, 1, incoming, normed, scale_two, total, beside)
    start_rows(3, grad_hidden[...])
    held[...] = grad_hidden[...]
    grad_act[...] = act_one[...]
    source_t[...] = act_one_b[...].T
    convolve_back(
        w_mid,
        grad_act,
        1,
        lambda at, count: slot_after(at, count, (0, 5), 2),
        lambda at, count: slot_after(at, count, (1, 3, 5), 4),
    )
    normed, pre = pre_one()
    incoming = jnp.where(live, grad_act[...] * silu_slope(pre), 0.0)
    if reduce_here:
        pair_source(swap_one, pre_one, 0)
        receive(3)
    after = lambda at, count: slot_after(at, count, (0, 1, 3, 5, 6), 7)
    beside = pair_halves(1, after) if reduce_here else nothing
    grad_hidden[...] = norm_grad(5, 0, incoming, normed, scale_one, total, beside)
    down_rows = down_offsets * in_width
    if reduce_here:
        down_all[...] = dot(cols_down[...].T, grad_hidden[...])
        kept = down_rows // 2
        swap_down = swap(
            5, down_all.at[pl.ds(pl.multiple_of(kept * (1 - pair), kept), kept), :], down_got
        )
        swap_down.start()
    else:
        grads[2 * units * width :, :] = dot(cols_down[...].T, grad_hidden[...])
    slot(12)
    for child in range(children):
        total_child = jnp.zeros((rows, in_width), jnp.float32)
        for k in range(child, down_offsets, children):
            there = side_cols[:, offsets + k : offsets + k + 1] < fine_rows
            total_child += jnp.where(there, dot_last(grad_hidden[...], w_down[k]), 0.0)
        spread_fine[pl.ds(child, rows, stride=children), :] = total_child
    fine_grad_ref[...] = spread_fine[...].astype(jnp.bfloat16)
    slot(13)

    if reduce_here:

        def final(at, carry):
            slot(at, True)
            return carry

        swap_down.wait()
        for part in range(PAIR):
            total_down = (
                down_all[pl.ds(pl.multiple_of(kept * pair + part * width, width), width), :]
                + down_got[part * width : (part + 1) * width, :]
            )
            half = 1 - part
            grads[chunks - 2 + part, :, :, :, 8 * half : 8 * half + 8] = total_down.reshape(
                grads.shape[1:4] + (8, width)
            )
        lax.fori_loop(chunks - 2 + GAP, chunks + GAP + LAGS[-1], final, 0)
    else:
        store = pltpu.make_async_copy(grads, results, load_sem.at[0])
        store.start()
        store.wait()


def place_kernel(
    features_ref,
    fine_grad_ref,
    grads_ref,
    gain_ref,
    bias_ref,
    features_out,
    fine_grad_out,
    grad_down_out,
    grad_mid_out,
    grad_out_out,
    gain_out,
    bias_out,
    sem,
):
    half = grad_mid_out.shape[0] // 2
    moves = []
    for at, target in enumerate((grad_out_out, grad_mid_out)):
        for pair in range(2):
            for first in range(0, half, 3):
                count = min(3, half - first)
                here = grads_ref.at[pair, pl.ds(at * half + first, count)]
                moves.append((here, target.at[pl.ds((half + 1) * pair + first, count)]))
        moves.append((grads_ref.at[1 - at, pl.ds(2 * half, 1)], target.at[pl.ds(half, 1)]))
    for pair in range(2):
        down_units = grad_down_out.shape[0] // 2
        here = grads_ref.at[pair, pl.ds(2 * half + 1, down_units)]
        moves.append((here, grad_down_out.at[pl.ds(pair * down_units, down_units)]))
    copies = [
        pltpu.make_async_copy(source, target, sem.at[at])
        for at, (source, target) in enumerate(moves)
    ]
    for copy in copies:
        copy.start()
    features_out[...] = features_ref[...]
    fine_grad_out[...] = fine_grad_ref[...]
    gain_out[...] = gain_ref[...]
    bias_out[...] = bias_ref[...]
    for copy in copies:
        copy.wait()


def per_device(
    dp_size,
    group_size,
    fine_features,
    down_map,
    neighbours,
    voxel_counts,
    down_weight,
    mid_weight,
    out_weight,
    norm_gain,
    norm_bias,
    cotangent,
):
    rows, width = cotangent.shape
    fine_rows, in_width = fine_features.shape
    offsets = neighbours.shape[1]
    down_offsets = down_map.shape[1]
    f32, bf16, i32 = jnp.float32, jnp.bfloat16, jnp.int32
    vmem = pl.BlockSpec(memory_space=pltpu.VMEM)
    smem = pl.BlockSpec(memory_space=pltpu.SMEM)
    hbm = pl.BlockSpec(memory_space=pl.ANY)
    shape = jax.ShapeDtypeStruct
    reduce_here = dp_size == 8 and group_size == 4
    result = pltpu.VMEM if reduce_here else shape
    near_size = dp_size * group_size if reduce_here else group_size
    share = 2 if reduce_here else 1
    units = (offsets + 1) // 2 * 2 // share
    all_units = 2 * units + down_offsets * in_width // (share * width)
    grad_rows = all_units * width
    chunks = all_units // PAIR
    padded = (offsets + 1) // 2 * 2
    features, fine_grad, grads, gain_grad, bias_grad = pl.pallas_call(
        functools.partial(kernel, dp_size, group_size, reduce_here),
        out_shape=(
            result((rows, width), bf16),
            result((fine_rows, in_width), bf16),
            pltpu.VMEM((2, all_units, *GROUPS, 8, width), f32)
            if reduce_here
            else shape((grad_rows, width), f32),
            result(norm_gain.shape, f32),
            result(norm_bias.shape, f32),
        ),
        in_specs=[vmem, vmem, vmem, smem, hbm, hbm, hbm, vmem, vmem, hbm],
        out_specs=(vmem, vmem, vmem if reduce_here else hbm, vmem, vmem),
        scratch_shapes=[
            pltpu.VMEM(down_weight.shape, bf16),
            pltpu.VMEM((padded, width, width), bf16),
            pltpu.VMEM((padded, width, width), bf16),
            pltpu.VMEM((rows, width), bf16),
            pltpu.VMEM((fine_rows, in_width), f32),
            pltpu.VMEM((rows, down_offsets * in_width), bf16),
            pltpu.VMEM((offsets, rows, 128), bf16),
            pltpu.VMEM((2, GROUP * rows, rows), bf16),
            pltpu.VMEM((2, rows, GROUP * width), bf16),
            pltpu.VMEM((BLOCK, 2 * width), bf16),
            pltpu.VMEM((rows, width), f32),
            pltpu.VMEM((rows, width), bf16),
            pltpu.VMEM((rows, width), bf16),
            pltpu.VMEM((rows, width), f32),
            pltpu.VMEM((rows, width), f32),
            pltpu.VMEM((rows, width), f32),
            pltpu.VMEM((rows, width), bf16),
            pltpu.VMEM((rows, width), bf16),
            pltpu.VMEM((width, rows), bf16),
            pltpu.VMEM((width, rows), bf16),
            pltpu.VMEM((rows, width), f32),
            pltpu.VMEM((128, rows), f32),
            pltpu.VMEM((rows, 128), f32),
            pltpu.VMEM((padded, rows), i32),
            pltpu.VMEM((padded, rows), i32),
            pltpu.VMEM((2, rows, width), f32),
            pltpu.VMEM((4, rows, width), f32),
            pltpu.VMEM((down_offsets * in_width, width), f32),
            pltpu.VMEM((down_offsets * in_width // 2, width), f32),
            pltpu.VMEM(
                (chunks, *GROUPS, 8 * PAIR, width) if reduce_here else (grad_rows, width), f32
            ),
            pltpu.VMEM((CORE_RING, 2, *GROUPS[1:], 8 * PAIR, width), f32),
            pltpu.VMEM((chunks, GROUPS[2], 8 * PAIR, width), f32),
            pltpu.VMEM((chunks, GROUPS[1], 2, 8 * PAIR, width), f32),
            pltpu.VMEM((chunks, 2, 8 * PAIR, width), f32),
            pltpu.VMEM((chunks, 2, 8 * PAIR, width), f32),
            pltpu.VMEM((chunks, 2, 8 * PAIR, width), f32),
            pltpu.VMEM((6, near_size, 8, width // 2), f32),
            pltpu.VMEM((6, dp_size, 8, width // 2), f32),
            pltpu.SemaphoreType.DMA((4,)),
            pltpu.SemaphoreType.DMA((RING,)),
            pltpu.SemaphoreType.DMA((RING, len(LAGS) - 1)),
            pltpu.SemaphoreType.DMA((6,)),
            pltpu.SemaphoreType.DMA((6,)),
            pltpu.SemaphoreType.DMA((6, group_size - 1)),
            pltpu.SemaphoreType.DMA((6, group_size - 1)),
            pltpu.SemaphoreType.DMA((6, dp_size - 1)),
            pltpu.SemaphoreType.DMA((6, dp_size - 1)),
        ],
        compiler_params=pltpu.CompilerParams(
            collective_id=0, has_side_effects=True, vmem_limit_bytes=(46 if reduce_here else 60) * 1024 * 1024
        ),
    )(
        fine_features,
        down_map.T,
        neighbours.T,
        voxel_counts,
        down_weight,
        mid_weight,
        out_weight,
        norm_gain,
        norm_bias,
        cotangent,
    )
    if not reduce_here:
        grads = lax.psum(grads, ("dp", "group"))
        middle, end = offsets * width, 2 * padded * width
        grad_out = grads[:middle].reshape(out_weight.shape)
        grad_mid = grads[padded * width : padded * width + middle].reshape(mid_weight.shape)
        grad_down = grads[end:].reshape(down_weight.shape)
        return (features, fine_grad, grad_down, grad_mid, grad_out, gain_grad, bias_grad)
    held = [
        pltpu.with_memory_space_constraint(value, pltpu.VMEM)
        for value in (features, fine_grad, grads, gain_grad, bias_grad)
    ]
    features, fine_grad, grad_down, grad_mid, grad_out, gain_grad, bias_grad = pl.pallas_call(
        place_kernel,
        out_shape=(
            shape(features.shape, bf16),
            shape(fine_grad.shape, bf16),
            shape((down_offsets * in_width // width, *GROUPS, 8, width), f32),
            shape((offsets, *GROUPS, 8, width), f32),
            shape((offsets, *GROUPS, 8, width), f32),
            shape(norm_gain.shape, f32),
            shape(norm_bias.shape, f32),
        ),
        in_specs=[vmem] * 5,
        out_specs=(vmem, vmem, hbm, hbm, hbm, vmem, vmem),
        scratch_shapes=[pltpu.SemaphoreType.DMA((24,))],
        compiler_params=pltpu.CompilerParams(vmem_limit_bytes=8 * 1024 * 1024),
    )(*held)
    grad_down = grad_down.reshape(down_weight.shape)
    grad_mid = grad_mid.reshape(mid_weight.shape)
    grad_out = grad_out.reshape(out_weight.shape)
    return (features, fine_grad, grad_down, grad_mid, grad_out, gain_grad, bias_grad)


def solution(mesh):
    in_specs = (
        P(("dp", "group"), None),
        P(("dp", "group"), None),
        P(("dp", "group"), None),
        P(("dp", "group")),
        P(),
        P(),
        P(),
        P(),
        P(),
        P(("dp", "group"), None),
    )
    out_specs = (P(("dp", "group"), None), P(("dp", "group"), None), P(), P(), P(), P(), P())
    return jax.shard_map(
        functools.partial(per_device, mesh.shape["dp"], mesh.shape["group"]),
        mesh=mesh,
        in_specs=in_specs,
        out_specs=out_specs,
        check_vma=False,
    )
```

```python
import functools

import jax
import jax.numpy as jnp
from jax import lax
from jax.experimental import pallas as pl
from jax.experimental.pallas import tpu as pltpu
from jax.sharding import PartitionSpec as P

eps_norm = 1e-05
MESH = pl.DeviceIdType.MESH
GROUP = 3
BLOCK = 256
PAIR = 2
GROUPS = (4, 2, 4)
GAP = 1
LAGS = (0, 1, 2, 4, 6, 8, 9, 11, 12)
RING = 16
CORE_RING = 8


def sigmoid(value):
    return 0.5 + 0.5 * jnp.tanh(0.5 * value)


def silu_slope(value):
    sigma = sigmoid(value)
    return sigma * (1.0 + value * (1.0 - sigma))


def dot(left, right):
    return jnp.dot(left, right, preferred_element_type=jnp.float32)


def dot_last(left, right):
    return lax.dot_general(
        left, right, (((1,), (1,)), ((), ())), preferred_element_type=jnp.float32
    )


def kernel(
    dp_size,
    group_size,
    reduce_here,
    fine_ref,
    down_rows_ref,
    nb_rows,
    count_ref,
    down_hbm,
    mid_hbm,
    out_hbm,
    gain_ref,
    bias_ref,
    cotangent_hbm,
    features_ref,
    fine_grad_ref,
    results,
    gain_grad_ref,
    bias_grad_ref,
    w_down,
    w_mid,
    w_out,
    cotangent_ref,
    spread_fine,
    cols_down,
    nb_cols,
    pickers,
    columns,
    side_by_side,
    act_one,
    act_one_b,
    act_two_b,
    hid_one,
    hid_two,
    hid_three,
    held,
    grad_hidden,
    source_t,
    pair_source_t,
    grad_act,
    side,
    side_cols,
    nb_own,
    nb_pair,
    swap_out,
    swap_in,
    down_all,
    down_got,
    grads,
    from_core,
    from_first_a,
    from_first_b,
    from_second_a,
    from_second_b,
    from_line,
    near,
    far,
    load_sem,
    sum_send,
    sum_recv,
    swap_send,
    swap_recv,
    near_send,
    near_recv,
    far_send,
    far_recv,
):
    rows, width = cotangent_hbm.shape
    offsets = nb_rows.shape[0]
    fine_rows, in_width = fine_ref.shape
    children = fine_rows // rows
    down_offsets = down_rows_ref.shape[0]
    units = (offsets + 1) // 2 * (1 if reduce_here else 2)
    chunks = grads.shape[0]
    dp_me = lax.axis_index("dp")
    group_me = lax.axis_index("group")

    loads = [
        pltpu.make_async_copy(source, target, load_sem.at[at])
        for at, (source, target) in enumerate(
            (
                (down_hbm, w_down),
                (mid_hbm, w_mid.at[pl.ds(0, offsets)]),
                (out_hbm, w_out.at[pl.ds(0, offsets)]),
                (cotangent_hbm, cotangent_ref),
            )
        )
    ]
    for load in loads:
        load.start()

    direct = reduce_here
    peers = [
        {
            "dp": lax.rem(dp_me + dp_step, dp_size),
            "group": lax.rem(group_me + group_step, group_size),
        }
        for dp_step in reversed(range(dp_size))
        for group_step in reversed(range(group_size))
        if (dp_step or group_step) and (direct or not dp_step or not group_step)
    ]
    barrier = pltpu.get_barrier_semaphore()
    for peer in peers:
        pl.semaphore_signal(barrier, inc=1, device_id=peer, device_id_type=MESH)

    def share(at, axis, me, size, slots, send, recv):
        copies = []
        for step in range(1, size):
            copies.append(
                pltpu.make_async_remote_copy(
                    src_ref=slots.at[at, me],
                    dst_ref=slots.at[at, me],
                    send_sem=send.at[at, step - 1],
                    recv_sem=recv.at[at, step - 1],
                    device_id={axis: lax.rem(me + step, size)},
                    device_id_type=MESH,
                )
            )
        for copy in copies:
            copy.start()
        return copies

    def exchange_direct(at, block, combine, meanwhile):
        me = dp_me * group_size + group_me
        near[at, me] = block
        for peer in peers:
            pltpu.make_async_remote_copy(
                src_ref=near.at[at, me],
                dst_ref=near.at[at, me],
                send_sem=near_send.at[at, 0],
                recv_sem=near_recv.at[at, 0],
                device_id=peer,
                device_id_type=MESH,
            ).start()
        for work in meanwhile:
            if work is not None:
                work()
        others = near.at[at, pl.ds(0, len(peers))]
        for sem in (near_recv, near_send):
            pltpu.make_async_copy(others, others, sem.at[at, 0]).wait()
        return combine([near[at, slot] for slot in range(len(peers) + 1)])

    def exchange(at, block, combine, meanwhile=(None, None)):
        if direct and at < 4:
            return exchange_direct(at, block, combine, meanwhile)
        near[at, group_me] = block
        copies = share(at, "group", group_me, group_size, near, near_send, near_recv)
        if meanwhile[0] is not None:
            meanwhile[0]()
        for copy in copies:
            copy.wait()
        far[at, dp_me] = combine([near[at, slot] for slot in range(group_size)])
        copies = share(at, "dp", dp_me, dp_size, far, far_send, far_recv)
        if meanwhile[1] is not None:
            meanwhile[1]()
        for copy in copies:
            copy.wait()
        return combine([far[at, slot] for slot in range(dp_size)])

    lanes = width // 2

    def stack(first, second, third):
        filler = jnp.zeros((2, lanes), jnp.float32)
        return jnp.concatenate([first, second, third, filler], axis=0)

    def fold(value):
        return jnp.concatenate([value[:, :lanes], value[:, lanes:]], axis=0)

    def unfold(value):
        return jnp.concatenate([value[0:1], value[1:2]], axis=1)

    def add_all(blocks):
        total = blocks[0]
        for block in blocks[1:]:
            total = total + block
        return total

    def merge_all(blocks):
        count = add_all([block[4:6] for block in blocks])
        center = add_all([block[4:6] * block[0:2] for block in blocks]) / count
        squares = add_all(
            [
                block[2:4] + block[4:6] * (block[0:2] - center) * (block[0:2] - center)
                for block in blocks
            ]
        )
        return stack(center, squares, count)

    count = count_ref[0]
    own_count = jnp.full((1, width), count.astype(jnp.float32))
    live = lax.broadcasted_iota(jnp.int32, (rows, width), 0) < count

    def norm_stats(at, hidden, meanwhile=(None, None)):
        center = jnp.sum(hidden, axis=0, keepdims=True) / own_count
        centered = jnp.where(live, hidden - center, 0.0)
        squares = jnp.sum(centered * centered, axis=0, keepdims=True)
        merged = exchange(
            at, stack(fold(center), fold(squares), fold(own_count)), merge_all, meanwhile
        )
        total = unfold(merged[4:6])
        scale = lax.rsqrt(unfold(merged[2:4]) / total + eps_norm)
        return unfold(merged[0:2]), scale, total

    def norm_grad(at, norm, incoming, normed, scale, total, meanwhile=(None, None)):
        shift_sum = fold(jnp.sum(incoming, axis=0, keepdims=True))
        scale_sum = fold(jnp.sum(incoming * normed, axis=0, keepdims=True))
        summed = exchange(
            at, stack(shift_sum, scale_sum, jnp.zeros_like(shift_sum)), add_all, meanwhile
        )
        shift_sum, scale_sum = unfold(summed[0:2]), unfold(summed[2:4])
        bias_grad_ref[norm : norm + 1, :] = shift_sum
        gain_grad_ref[norm : norm + 1, :] = scale_sum
        hidden_grad = (
            scale
            * gain_ref[norm : norm + 1, :]
            * (incoming - shift_sum / total - normed * (scale_sum / total))
        )
        return jnp.where(live, hidden_grad, 0.0).astype(jnp.bfloat16)

    def pick(mask):
        return jnp.where(mask, jnp.bfloat16(1), jnp.bfloat16(0))

    def counting(shape, axis):
        return lax.broadcasted_iota(jnp.int32, shape, axis).astype(jnp.float32).astype(jnp.bfloat16)

    def place_spread(turn, step):
        picked = dot(pickers[turn, : PAIR * rows, :], held[...]).astype(jnp.bfloat16)
        for part in range(PAIR):
            columns[turn, :, part * width : (part + 1) * width] = picked[
                part * rows : (part + 1) * rows
            ]

    def run_steps(first, last, build, place, use, after):
        build(first % 2, first)

        def one(turn, step, more):
            place(turn, step)
            if more:
                build(1 - turn, step + 1)
            use(turn, step)

        bodies = (last - first - 1) // 2

        def body(at, carry):
            for turn in range(2):
                one((first + turn) % 2, first + 2 * at + turn, True)
            after(first + 2 * at, 2)
            return carry

        lax.fori_loop(0, bodies, body, 0)
        for step in range(first + 2 * bodies, last):
            one(step % 2, step, step + 1 < last)
            after(step, 1)

    def convolve(source, weight, hidden):
        places = counting((rows, BLOCK), 1)
        hidden[...] = jnp.zeros_like(hidden)
        for block in range(2):
            side_by_side[:, block * width : (block + 1) * width] = source[
                block * BLOCK : (block + 1) * BLOCK, :
            ]

        def build(turn, step):
            for part in range(GROUP):
                code = nb_cols[step * GROUP + part]
                wanted = jnp.concatenate([jnp.maximum(code, -1 - code)] * (BLOCK // 128), axis=1)
                pickers[turn, part * rows : (part + 1) * rows, :BLOCK] = pick(wanted == places)

        def use(turn, step):
            weights = weight[pl.ds(step * GROUP, GROUP)].reshape(GROUP * width, width)
            hidden[...] += dot(columns[turn], weights)

        def place(turn, step):
            for part in range(GROUP):
                found = dot(
                    pickers[turn, part * rows : (part + 1) * rows, :BLOCK], side_by_side[...]
                )
                code = nb_cols[step * GROUP + part].astype(jnp.float32)
                second = jnp.concatenate([code] * (width // 128), axis=1) < 0
                columns[turn, :, part * width : (part + 1) * width] = jnp.where(
                    second, found[:, width:], found[:, :width]
                ).astype(jnp.bfloat16)

        run_steps(0, offsets // GROUP, build, place, use, no_slot)

    def build_spread(neighbours, offset_of):
        places = counting((BLOCK, rows), 0)

        def build(turn, step):
            for part in range(PAIR):
                wanted = neighbours[pl.ds(offset_of(PAIR * step + part), 1), :]
                wanted = wanted.astype(jnp.float32)
                for first in range(0, rows, BLOCK):
                    here = jnp.broadcast_to(wanted - first, (16, rows)).astype(jnp.bfloat16)
                    pickers[turn, part * rows + first : part * rows + first + BLOCK, :] = pick(
                        jnp.concatenate([here] * (BLOCK // 16), axis=0) == places
                    )

        return build

    def no_slot(at, count):
        pass

    def own_of(second):
        if not reduce_here:
            return lambda at: at
        extra = 14 * pair if second else 14 - 14 * pair
        return lambda at: 14 * pair + at + (extra - 14 * pair) * (jnp.int32(at) == 13)

    def put(second, at, product, more):
        for part in range(PAIR):
            value = product[:, part * width : (part + 1) * width]
            if not reduce_here:
                unit = pl.multiple_of((units * second + PAIR * at + part) * width, width)
                grads[pl.ds(unit, width), :] = value
                continue
            c, half = at, part
            if second:
                c, half = units // PAIR - 1 + at + part, 1 - part
            if isinstance(at, int) and PAIR * at + part == units - 1:
                empty = pair if second else 1 - pair
                c, half = chunks - 2 + empty, empty
            value = value.reshape(grads.shape[1:4] + (8, width))
            here_rows = pl.ds(8 * half, 8)
            if more:
                value = value + grads[c, :, :, :, here_rows]
            grads[c, :, :, :, here_rows] = value

    def convolve_back(weight, act_grad, second, own_slot, other_slot):
        def use_of(offset_of, weigh):
            def use(turn, step):
                spread = columns[turn, :, : PAIR * width]
                weights = jnp.concatenate(
                    [weight[offset_of(PAIR * step + part)] for part in range(PAIR)], axis=1
                )
                act_grad[...] += dot_last(spread, weights)
                if weigh:
                    put(second, step, dot(source_t[...], spread), False)

            return use

        steps = units // PAIR
        offset_of = own_of(second)
        build = build_spread(nb_own, offset_of)
        run_steps(0, steps, build, place_spread, use_of(offset_of, True), own_slot)
        if reduce_here:
            if second:
                offset_of = lambda at: 14 - 14 * pair + at
            else:
                offset_of = lambda at: 13 - 13 * pair + at + 14 * pair * (jnp.int32(at) == 13)
            build = build_spread(nb_own, offset_of)
            run_steps(0, steps, build, place_spread, use_of(offset_of, False), other_slot)

    def convolve_pair(second, first_step, last_step, at_slot):
        def use(turn, step):
            spread = columns[turn, :, : PAIR * width]
            put(second, step, dot(pair_source_t[...], spread), True)

        build = build_spread(nb_pair, own_of(second))
        run_steps(first_step, last_step, build, place_spread, use, at_slot)

    core, row = lax.rem(group_me, 2), group_me // 2
    column, plane = lax.rem(dp_me, 2), dp_me // 2
    pair, high = lax.rem(plane, 2), plane // 2
    planes = 4
    core_peer = {"group": group_me + 1 - 2 * core}
    row_peer = {"group": group_me + 2 - 4 * row}
    column_peer = {"dp": dp_me + 1 - 2 * column}
    pair_peer = {"dp": dp_me + 2 - 4 * pair}
    cross_peer = {"dp": dp_me + 4 - 8 * high}
    own = pl.ds(2 * core, 2)
    lane_a, lane_b = 2 * core, 2 * core + 1
    kept_row, given_row = pl.ds(2 * row, 2), pl.ds(2 * (1 - row), 2)

    def send(c, stage, source, target, peer):
        turn = lax.rem(c, RING)
        return pltpu.make_async_remote_copy(
            src_ref=source,
            dst_ref=target,
            send_sem=sum_send.at[turn],
            recv_sem=sum_recv.at[turn, stage],
            device_id=peer,
            device_id_type=MESH,
        )

    def copies_of(c, stage, size):
        both, some = pl.ds(PAIR * c, size), pl.ds(0, 8 * size)
        part = grads.at[c, :, :, :, some]

        def landing(ref, at):
            return ref.at[(at, *[slice(None)] * (len(ref.shape) - 3), some)]

        if stage == 0:
            given = part.at[pl.ds(2 * (1 - core), 2)]
            return [send(c, stage, given, landing(from_core, lax.rem(c, CORE_RING)), core_peer)]
        if stage == 1:
            return [
                send(c, stage, part.at[lane_a, 1 - column], landing(from_first_a, c), column_peer),
                send(c, stage, part.at[lane_b, :, given_row], landing(from_first_b, c), row_peer),
            ]
        if stage == 2:
            return [
                send(c, stage, part.at[lane_a, column, given_row], landing(from_second_a, c), row_peer),
                send(c, stage, part.at[lane_b, 1 - column, kept_row], landing(from_second_b, c), column_peer),
            ]
        if stage == 3:
            given = part.at[own, column, 2 * row + 1 - high]
            return [send(c, stage, given, landing(from_line, c), cross_peer)]
        if stage == 4:
            block = results.at[pair, both, own, column, 2 * row + high]
            return [
                send(
                    c,
                    stage,
                    block,
                    block,
                    {"dp": 2 * lax.rem(plane + step, planes) + column},
                )
                for step in range(1, planes)
            ]
        if stage == 5:
            block_a = results.at[:, both, lane_a, column, kept_row]
            block_b = results.at[:, both, lane_b, column, kept_row]
            return [
                send(c, stage, block_a, block_a, row_peer),
                send(c, stage, block_b, block_b, column_peer),
            ]
        if stage == 6:
            block_a = results.at[:, both, lane_a, column]
            block_b = results.at[:, both, lane_b, :, kept_row]
            return [
                send(c, stage, block_a, block_a, column_peer),
                send(c, stage, block_b, block_b, row_peer),
            ]
        block = results.at[:, both, own]
        return [send(c, stage, block, block, core_peer)]

    def wait_bytes(sem, like):
        pltpu.make_async_copy(like, like, sem).wait()

    def wait_arrived(c, stage, size):
        some = pl.ds(0, 8 * size)
        like = (
            from_core.at[0, :, :, :, some],
            grads.at[c, 0, :, :, some],
            grads.at[c, 0, 0, :, some],
            from_line.at[c, :, some],
            results.at[0, pl.ds(0, 3 * size), 0, 0, pl.ds(0, 2)],
            grads.at[c, 0, :, :, some],
            grads.at[c, pl.ds(0, 2), :, :, some],
            grads.at[c, :, :, :, some],
        )[stage]
        wait_bytes(sum_recv.at[lax.rem(c, RING), stage], like)

    def wait_sent(c, size):
        like = results.at[0, pl.ds(0, 23), 0, pl.ds(0, size)]
        wait_bytes(sum_send.at[lax.rem(c, RING)], like)

    def stage_of(c, stage, size=PAIR):
        if stage > 0:
            wait_arrived(c, stage - 1, size)
        some = slice(0, 8 * size)

        def add(lanes, columns_of, rows_of, landed):
            here_rows = (c, lanes, columns_of, rows_of, some)
            grads[here_rows] = grads[here_rows] + landed

        every = slice(None)
        if stage == 1:
            add(own, every, every, from_core[lax.rem(c, CORE_RING), :, :, :, some])
        if stage == 2:
            add(lane_a, column, every, from_first_a[c, :, some])
            add(lane_b, every, kept_row, from_first_b[c, :, :, some])
        if stage == 3:
            add(lane_a, column, kept_row, from_second_a[c, :, some])
            add(lane_b, column, kept_row, from_second_b[c, :, some])
        if stage == 4:
            mine = 2 * row + high
            add(own, column, mine, from_line[c, :, some])
            for unit in range(size):
                results[pair, PAIR * c + unit, own, column, mine] = grads[
                    c, own, column, mine, 8 * unit : 8 * unit + 8
                ]
        if stage < len(LAGS) - 1:
            for copy in copies_of(c, stage, size):
                copy.start()
        else:
            wait_sent(c, size)

    early = units // PAIR - 1

    def slot(at, last=False):
        if not reduce_here:
            return
        for stage, lag in enumerate(LAGS):
            entry = at - lag
            if isinstance(at, int):
                c = entry if entry < early else max(entry - GAP, early - 1)
                if 0 <= entry < chunks - 1 + GAP and (c == entry or entry >= early + GAP):
                    stage_of(c, stage)
                continue
            second = entry >= early + GAP

            @pl.when(
                ((entry >= 0) & (entry < early)) | (second & (entry < chunks - 1 + GAP))
            )
            def _():
                stage_of(entry - GAP * second.astype(jnp.int32), stage)

            if last:

                @pl.when(entry == chunks - 1 + GAP)
                def _():
                    stage_of(chunks - 1, stage, 1)

    def slot_after(at, count, steps_with, first_slot):
        if isinstance(at, int):
            for number, step in enumerate(steps_with):
                if at <= step < at + count:
                    slot(first_slot + number)
            return
        start, end = first_slot, first_slot
        for step in steps_with:
            start = start + (at > step).astype(jnp.int32)
            end = end + (at + count > step).astype(jnp.int32)

        def one(number, carry):
            slot(number)
            return carry

        lax.fori_loop(start, end, one, 0)

    def swap(at, source, target):
        return pltpu.make_async_remote_copy(
            src_ref=source,
            dst_ref=target,
            send_sem=swap_send.at[at],
            recv_sem=swap_recv.at[at],
            device_id=pair_peer,
            device_id_type=MESH,
        )

    def swap_rows(at):
        return swap(at, swap_out.at[at % 2], swap_in.at[at])

    def start_rows(at, value):
        if reduce_here:
            swap_out[at % 2] = value.astype(jnp.float32)
            swap_rows(at).start()

    places = nb_rows[...]
    codes = jnp.where(places < BLOCK, places, jnp.where(places < rows, BLOCK - 1 - places, 4 * BLOCK))
    side[...] = jnp.zeros_like(side)
    side[:offsets, :] = codes.astype(jnp.float32)
    side[offsets : offsets + down_offsets, :] = down_rows_ref[...].astype(jnp.float32)
    side_cols[...] = side[...].T
    swap_neighbours = swap(4, nb_own, nb_pair)

    spread_fine[...] = fine_ref[...].astype(jnp.float32)
    for k in range(down_offsets):
        child = spread_fine[pl.ds(k % children, rows, stride=children), :]
        there = side_cols[:, offsets + k : offsets + k + 1] < fine_rows
        cols_down[:, k * in_width : (k + 1) * in_width] = jnp.where(there, child, 0.0).astype(
            jnp.bfloat16
        )
    loads[0].wait()
    hid_one[...] = dot(cols_down[...], w_down[...].reshape(down_offsets * in_width, width))

    def spread_neighbours():
        for k in range(offsets):
            nb_cols[k] = jnp.broadcast_to(side_cols[:, k : k + 1], (rows, 128)).astype(jnp.bfloat16)

    pl.semaphore_wait(barrier, len(peers))

    swap_one = swap(0, hid_one, swap_in.at[0])
    swap_two = swap(1, hid_two, swap_in.at[1])

    def start_one():
        nb_own[...] = jnp.full_like(nb_own, rows)
        nb_own[:offsets, :] = nb_rows[...]
        for weight in (w_mid, w_out):
            weight[offsets:] = jnp.zeros_like(weight[offsets:])
        if not reduce_here:
            return
        swap_neighbours.start()
        swap_one.start()

    def start_two():
        swap_two.start()

    beside = (start_one, spread_neighbours)
    center_one, scale_one, total = norm_stats(0, hid_one[...], beside)

    def pre_one(hidden=hid_one):
        normed = (hidden[...] - center_one) * scale_one
        return normed, normed * gain_ref[0:1, :] + bias_ref[0:1, :]

    _, pre = pre_one()
    act_one[...] = jnp.where(live, pre * sigmoid(pre), 0.0)
    act_one_b[...] = act_one[...].astype(jnp.bfloat16)
    loads[1].wait()
    convolve(act_one_b, w_mid, hid_two)
    center_two, scale_two, _ = norm_stats(
        1, hid_two[...], (None, start_two if reduce_here else None)
    )

    def pre_two(hidden=hid_two):
        normed = (hidden[...] - center_two) * scale_two
        return normed, normed * gain_ref[1:2, :] + bias_ref[1:2, :]

    _, pre = pre_two()
    act_two_b[...] = jnp.where(live, pre * sigmoid(pre), 0.0).astype(jnp.bfloat16)
    loads[2].wait()
    convolve(act_two_b, w_out, hid_three)
    def turn_two():
        source_t[...] = act_two_b[...].T

    center_three, scale_three, _ = norm_stats(2, hid_three[...], (turn_two, None))
    loads[3].wait()
    normed_three = (hid_three[...] - center_three) * scale_three
    summed = (
        jnp.where(live, normed_three * gain_ref[2:3, :] + bias_ref[2:3, :], 0.0) + act_one[...]
    )
    sigma = sigmoid(summed)
    features_ref[...] = jnp.where(live, summed * sigma, 0.0).astype(jnp.bfloat16)

    def pair_source(swapped, pre_of, source_at):
        swapped.wait()
        _, pre = pre_of(swap_in.at[source_at])
        pair_source_t[...] = (pre * sigmoid(pre)).astype(jnp.bfloat16).T

    def pair_two():
        if reduce_here:
            pair_source(swap_two, pre_two, 1)

    slope = sigma * (1.0 + summed * (1.0 - sigma))
    act_one[...] = jnp.where(live, cotangent_ref[...].astype(jnp.float32) * slope, 0.0)
    grad_hidden[...] = norm_grad(
        3, 2, act_one[...], normed_three, scale_three, total, (pair_two, None)
    )
    start_rows(2, grad_hidden[...])
    held[...] = grad_hidden[...]
    grad_act[...] = jnp.zeros_like(grad_act)
    steps = units // PAIR

    def receive(hidden_at):
        swap_rows(hidden_at).wait()
        held[...] = swap_in[hidden_at].astype(jnp.bfloat16)

    def pair_halves(second, at_slot):
        middle = (steps + 1) // 2
        return (
            lambda: convolve_pair(second, 0, middle, at_slot),
            lambda: convolve_pair(second, middle, steps, at_slot),
        )

    nothing = (None, None)
    convolve_back(w_out, grad_act, 0, no_slot, no_slot)
    normed, pre = pre_two()
    incoming = jnp.where(live, grad_act[...] * silu_slope(pre), 0.0)
    if reduce_here:
        swap_neighbours.wait()
        receive(2)
    after = lambda at, count: slot_after(at, count, (0, 4), 0)
    beside = pair_halves(0, after) if reduce_here else nothing
    grad_hidden[...] = norm_grad(4, 1, incoming, normed, scale_two, total, beside)
    start_rows(3, grad_hidden[...])
    held[...] = grad_hidden[...]
    grad_act[...] = act_one[...]
    source_t[...] = act_one_b[...].T
    convolve_back(
        w_mid,
        grad_act,
        1,
        lambda at, count: slot_after(at, count, (0, 3, 5), 2),
        lambda at, count: slot_after(at, count, (1, 5), 5),
    )
    normed, pre = pre_one()
    incoming = jnp.where(live, grad_act[...] * silu_slope(pre), 0.0)
    if reduce_here:
        pair_source(swap_one, pre_one, 0)
        receive(3)
    after = lambda at, count: slot_after(at, count, (0, 1, 3, 5, 6), 7)
    beside = pair_halves(1, after) if reduce_here else nothing
    grad_hidden[...] = norm_grad(5, 0, incoming, normed, scale_one, total, beside)
    down_rows = down_offsets * in_width
    if reduce_here:
        down_all[...] = dot(cols_down[...].T, grad_hidden[...])
        kept = down_rows // 2
        swap_down = swap(
            5, down_all.at[pl.ds(pl.multiple_of(kept * (1 - pair), kept), kept), :], down_got
        )
        swap_down.start()
    else:
        grads[2 * units * width :, :] = dot(cols_down[...].T, grad_hidden[...])
    slot(12)
    for child in range(children):
        total_child = jnp.zeros((rows, in_width), jnp.float32)
        for k in range(child, down_offsets, children):
            there = side_cols[:, offsets + k : offsets + k + 1] < fine_rows
            total_child += jnp.where(there, dot_last(grad_hidden[...], w_down[k]), 0.0)
        spread_fine[pl.ds(child, rows, stride=children), :] = total_child
    fine_grad_ref[...] = spread_fine[...].astype(jnp.bfloat16)
    slot(13)

    if reduce_here:

        def final(at, carry):
            slot(at, True)
            return carry

        swap_down.wait()
        for part in range(PAIR):
            total_down = (
                down_all[pl.ds(pl.multiple_of(kept * pair + part * width, width), width), :]
                + down_got[part * width : (part + 1) * width, :]
            )
            half = 1 - part
            grads[chunks - 2 + part, :, :, :, 8 * half : 8 * half + 8] = total_down.reshape(
                grads.shape[1:4] + (8, width)
            )
        lax.fori_loop(chunks - 2 + GAP, chunks + GAP + LAGS[-1], final, 0)
    else:
        store = pltpu.make_async_copy(grads, results, load_sem.at[0])
        store.start()
        store.wait()


def place_kernel(
    features_ref,
    fine_grad_ref,
    grads_ref,
    gain_ref,
    bias_ref,
    features_out,
    fine_grad_out,
    grad_down_out,
    grad_mid_out,
    grad_out_out,
    gain_out,
    bias_out,
    sem,
):
    half = grad_mid_out.shape[0] // 2
    moves = []
    for at, target in enumerate((grad_out_out, grad_mid_out)):
        for pair in range(2):
            for first in range(0, half, 3):
                count = min(3, half - first)
                here = grads_ref.at[pair, pl.ds(at * half + first, count)]
                moves.append((here, target.at[pl.ds((half + 1) * pair + first, count)]))
        moves.append((grads_ref.at[1 - at, pl.ds(2 * half, 1)], target.at[pl.ds(half, 1)]))
    for pair in range(2):
        down_units = grad_down_out.shape[0] // 2
        here = grads_ref.at[pair, pl.ds(2 * half + 1, down_units)]
        moves.append((here, grad_down_out.at[pl.ds(pair * down_units, down_units)]))
    copies = [
        pltpu.make_async_copy(source, target, sem.at[at])
        for at, (source, target) in enumerate(moves)
    ]
    for copy in copies:
        copy.start()
    features_out[...] = features_ref[...]
    fine_grad_out[...] = fine_grad_ref[...]
    gain_out[...] = gain_ref[...]
    bias_out[...] = bias_ref[...]
    for copy in copies:
        copy.wait()


def per_device(
    dp_size,
    group_size,
    fine_features,
    down_map,
    neighbours,
    voxel_counts,
    down_weight,
    mid_weight,
    out_weight,
    norm_gain,
    norm_bias,
    cotangent,
):
    rows, width = cotangent.shape
    fine_rows, in_width = fine_features.shape
    offsets = neighbours.shape[1]
    down_offsets = down_map.shape[1]
    f32, bf16, i32 = jnp.float32, jnp.bfloat16, jnp.int32
    vmem = pl.BlockSpec(memory_space=pltpu.VMEM)
    smem = pl.BlockSpec(memory_space=pltpu.SMEM)
    hbm = pl.BlockSpec(memory_space=pl.ANY)
    shape = jax.ShapeDtypeStruct
    reduce_here = dp_size == 8 and group_size == 4
    result = pltpu.VMEM if reduce_here else shape
    near_size = dp_size * group_size if reduce_here else group_size
    share = 2 if reduce_here else 1
    units = (offsets + 1) // 2 * 2 // share
    all_units = 2 * units + down_offsets * in_width // (share * width)
    grad_rows = all_units * width
    chunks = all_units // PAIR
    padded = (offsets + 1) // 2 * 2
    features, fine_grad, grads, gain_grad, bias_grad = pl.pallas_call(
        functools.partial(kernel, dp_size, group_size, reduce_here),
        out_shape=(
            result((rows, width), bf16),
            result((fine_rows, in_width), bf16),
            pltpu.VMEM((2, all_units, *GROUPS, 8, width), f32)
            if reduce_here
            else shape((grad_rows, width), f32),
            result(norm_gain.shape, f32),
            result(norm_bias.shape, f32),
        ),
        in_specs=[vmem, vmem, vmem, smem, hbm, hbm, hbm, vmem, vmem, hbm],
        out_specs=(vmem, vmem, vmem if reduce_here else hbm, vmem, vmem),
        scratch_shapes=[
            pltpu.VMEM(down_weight.shape, bf16),
            pltpu.VMEM((padded, width, width), bf16),
            pltpu.VMEM((padded, width, width), bf16),
            pltpu.VMEM((rows, width), bf16),
            pltpu.VMEM((fine_rows, in_width), f32),
            pltpu.VMEM((rows, down_offsets * in_width), bf16),
            pltpu.VMEM((offsets, rows, 128), bf16),
            pltpu.VMEM((2, GROUP * rows, rows), bf16),
            pltpu.VMEM((2, rows, GROUP * width), bf16),
            pltpu.VMEM((BLOCK, 2 * width), bf16),
            pltpu.VMEM((rows, width), f32),
            pltpu.VMEM((rows, width), bf16),
            pltpu.VMEM((rows, width), bf16),
            pltpu.VMEM((rows, width), f32),
            pltpu.VMEM((rows, width), f32),
            pltpu.VMEM((rows, width), f32),
            pltpu.VMEM((rows, width), bf16),
            pltpu.VMEM((rows, width), bf16),
            pltpu.VMEM((width, rows), bf16),
            pltpu.VMEM((width, rows), bf16),
            pltpu.VMEM((rows, width), f32),
            pltpu.VMEM((128, rows), f32),
            pltpu.VMEM((rows, 128), f32),
            pltpu.VMEM((padded, rows), i32),
            pltpu.VMEM((padded, rows), i32),
            pltpu.VMEM((2, rows, width), f32),
            pltpu.VMEM((4, rows, width), f32),
            pltpu.VMEM((down_offsets * in_width, width), f32),
            pltpu.VMEM((down_offsets * in_width // 2, width), f32),
            pltpu.VMEM(
                (chunks, *GROUPS, 8 * PAIR, width) if reduce_here else (grad_rows, width), f32
            ),
            pltpu.VMEM((CORE_RING, 2, *GROUPS[1:], 8 * PAIR, width), f32),
            pltpu.VMEM((chunks, GROUPS[2], 8 * PAIR, width), f32),
            pltpu.VMEM((chunks, GROUPS[1], 2, 8 * PAIR, width), f32),
            pltpu.VMEM((chunks, 2, 8 * PAIR, width), f32),
            pltpu.VMEM((chunks, 2, 8 * PAIR, width), f32),
            pltpu.VMEM((chunks, 2, 8 * PAIR, width), f32),
            pltpu.VMEM((6, near_size, 8, width // 2), f32),
            pltpu.VMEM((6, dp_size, 8, width // 2), f32),
            pltpu.SemaphoreType.DMA((4,)),
            pltpu.SemaphoreType.DMA((RING,)),
            pltpu.SemaphoreType.DMA((RING, len(LAGS) - 1)),
            pltpu.SemaphoreType.DMA((6,)),
            pltpu.SemaphoreType.DMA((6,)),
            pltpu.SemaphoreType.DMA((6, group_size - 1)),
            pltpu.SemaphoreType.DMA((6, group_size - 1)),
            pltpu.SemaphoreType.DMA((6, dp_size - 1)),
            pltpu.SemaphoreType.DMA((6, dp_size - 1)),
        ],
        compiler_params=pltpu.CompilerParams(
            collective_id=0, has_side_effects=True, vmem_limit_bytes=(46 if reduce_here else 60) * 1024 * 1024
        ),
    )(
        fine_features,
        down_map.T,
        neighbours.T,
        voxel_counts,
        down_weight,
        mid_weight,
        out_weight,
        norm_gain,
        norm_bias,
        cotangent,
    )
    if not reduce_here:
        grads = lax.psum(grads, ("dp", "group"))
        middle, end = offsets * width, 2 * padded * width
        grad_out = grads[:middle].reshape(out_weight.shape)
        grad_mid = grads[padded * width : padded * width + middle].reshape(mid_weight.shape)
        grad_down = grads[end:].reshape(down_weight.shape)
        return (features, fine_grad, grad_down, grad_mid, grad_out, gain_grad, bias_grad)
    held = [
        pltpu.with_memory_space_constraint(value, pltpu.VMEM)
        for value in (features, fine_grad, grads, gain_grad, bias_grad)
    ]
    features, fine_grad, grad_down, grad_mid, grad_out, gain_grad, bias_grad = pl.pallas_call(
        place_kernel,
        out_shape=(
            shape(features.shape, bf16),
            shape(fine_grad.shape, bf16),
            shape((down_offsets * in_width // width, *GROUPS, 8, width), f32),
            shape((offsets, *GROUPS, 8, width), f32),
            shape((offsets, *GROUPS, 8, width), f32),
            shape(norm_gain.shape, f32),
            shape(norm_bias.shape, f32),
        ),
        in_specs=[vmem] * 5,
        out_specs=(vmem, vmem, hbm, hbm, hbm, vmem, vmem),
        scratch_shapes=[pltpu.SemaphoreType.DMA((24,))],
        compiler_params=pltpu.CompilerParams(vmem_limit_bytes=8 * 1024 * 1024),
    )(*held)
    grad_down = grad_down.reshape(down_weight.shape)
    grad_mid = grad_mid.reshape(mid_weight.shape)
    grad_out = grad_out.reshape(out_weight.shape)
    return (features, fine_grad, grad_down, grad_mid, grad_out, gain_grad, bias_grad)


def solution(mesh):
    in_specs = (
        P(("dp", "group"), None),
        P(("dp", "group"), None),
        P(("dp", "group"), None),
        P(("dp", "group")),
        P(),
        P(),
        P(),
        P(),
        P(),
        P(("dp", "group"), None),
    )
    out_specs = (P(("dp", "group"), None), P(("dp", "group"), None), P(), P(), P(), P(), P())
    return jax.shard_map(
        functools.partial(per_device, mesh.shape["dp"], mesh.shape["group"]),
        mesh=mesh,
        in_specs=in_specs,
        out_specs=out_specs,
        check_vma=False,
    )
```
